32 devices in a mesh: ulysses: 4 (over y, x), blk: 8 (over z, core).
Axes of the slice: x: 2, y: 2, z: 4, core: 2. Of those that a mesh axis runs over, the one named last changes fastest.
Arguments:
- tokens: int32 [4, 2048], P(None, 'blk'), may hold values from 0 to 151935
- lengths: int32 [4], replicated, may hold values from 1024 to 2048, as said below
- picked: int32 [4, 128], P(None, 'blk'), may hold values from 0 to 2047, as said below
- targets: int32 [4, 128], P(None, 'blk'), may hold values from 0 to 151935
- advantages: float32 [4, 128], P(None, 'blk'), may hold values from -6 to 6
- step_count: int32 [1], replicated, may hold values from 1 to 20
- embedding: float32 [151936, 1024], P(('ulysses', 'blk')), may hold values from -0.54 to 0.54
- first_embedding: float32 [151936, 1024], P(('ulysses', 'blk')), may hold values from -1.0161426e-06 to 1.0161426e-06
- second_embedding: float32 [151936, 1024], P(('ulysses', 'blk')), may hold values from 8.697458e-15 to 8.6974574e-13
- inflow: float32 [1024, 4096], P(('ulysses', 'blk')), may hold values from -0.1875 to 0.1875
- inflow_first_moment: float32 [1024, 4096], P(('ulysses', 'blk')), may hold values from -3.010227e-06 to 3.010227e-06
- inflow_second_moment: float32 [1024, 4096], P(('ulysses', 'blk')), may hold values from 7.588386e-14 to 7.588386e-12
- outflow: float32 [2048, 1024], P(('ulysses', 'blk')), may hold values from -3 to 3
- first_outflow: float32 [2048, 1024], P(('ulysses', 'blk')), may hold values from -1.9711639e-07 to 1.9711639e-07
- second_outflow: float32 [2048, 1024], P(('ulysses', 'blk')), may hold values from 3.268843e-16 to 3.268843e-14
- expand: float32 [1024, 6144], P(('ulysses', 'blk')), may hold values from -0.1875 to 0.1875
- first_expand: float32 [1024, 6144], P(('ulysses', 'blk')), may hold values from -5.0883534e-07 to 5.0883534e-07
- second_expand: float32 [1024, 6144], P(('ulysses', 'blk')), may hold values from 2.177283e-15 to 2.177283e-13
- contract: float32 [3072, 1024], P(('ulysses', 'blk')), may hold values from -0.109375 to 0.109375
- first_contract: float32 [3072, 1024], P(('ulysses', 'blk')), may hold values from -5.0883534e-07 to 5.0883534e-07
- second_contract: float32 [3072, 1024], P(('ulysses', 'blk')), may hold values from 2.177283e-15 to 2.177283e-13
- scales: float32 [3328], P(('ulysses', 'blk')), may hold values from 0.5 to 1.5
- first_scales: float32 [3328], P(('ulysses', 'blk')), may hold values from -4.461859e-06 to 4.461859e-06
- second_scales: float32 [3328], P(('ulysses', 'blk')), may hold values from 1.6752821e-13 to 1.6752821e-11
Outputs:
- policy_loss: float32 [], replicated
- gradient_norm: float32 [], replicated
- change_embedding: float32 [151936, 1024], P(('ulysses', 'blk'))
- mean_embedding: float32 [151936, 1024], P(('ulysses', 'blk'))
- square_embedding: float32 [151936, 1024], P(('ulysses', 'blk'))
- change_inflow: float32 [1024, 4096], P(('ulysses', 'blk'))
- mean_inflow: float32 [1024, 4096], P(('ulysses', 'blk'))
- square_inflow: float32 [1024, 4096], P(('ulysses', 'blk'))
- change_outflow: float32 [2048, 1024], P(('ulysses', 'blk'))
- mean_outflow: float32 [2048, 1024], P(('ulysses', 'blk'))
- square_outflow: float32 [2048, 1024], P(('ulysses', 'blk'))
- change_expand: float32 [1024, 6144], P(('ulysses', 'blk'))
- mean_expand: float32 [1024, 6144], P(('ulysses', 'blk'))
- square_expand: float32 [1024, 6144], P(('ulysses', 'blk'))
- change_contract: float32 [3072, 1024], P(('ulysses', 'blk'))
- mean_contract: float32 [3072, 1024], P(('ulysses', 'blk'))
- square_contract: float32 [3072, 1024], P(('ulysses', 'blk'))
- change_scales: float32 [3328], P(('ulysses', 'blk'))
- mean_scales: float32 [3328], P(('ulysses', 'blk'))
- square_scales: float32 [3328], P(('ulysses', 'blk'))
The draws below stay inside these ranges and needn't reach their ends.
Inputs may be any that keep to these rules, and one draw needn't show every extreme that they name: lengths[s] counts the valid leading positions of slot s; later positions are padding. Some slot has exactly 2048. `picked`: the entries in columns k * 16 to (k + 1) * 16 - 1 are positions k * 256 to (k + 1) * 256 - 1 of the slot; a position may repeat.
All inputs are finite; a program needn't handle non-finite values.
Results may differ from the reference program's by a relative error of at most 0.03.
The reference program's roundings to bfloat16 on the way count: a program that leaves them out, or rounds other values in their place, can miss the bound.
Values may be sent and summed in bfloat16 or wider, within the bound.
A program may use at most 832 MiB of HBM per device.

```python
import math
import jax
import jax.numpy as jnp
import numpy as np
from jax import lax

MODEL_WIDTH = 1024
QUERY_HEADS = 16
KEY_VALUE_HEADS = 8
HEAD_WIDTH = 128
FF = 3072
VOCAB = 151936
LEN_DEV = 256
PICK_DEV = 16
SLOTS = 4
SLOT_LENGTH = 2048
PICKS = 128
GAINS = 3328
ENTRIES = 171314432


def draw_lengths(key, part):
    first_key, second_key = jax.random.split(key)
    drawn = jax.random.randint(first_key, (SLOTS,), SLOT_LENGTH // 2, SLOT_LENGTH + 1)
    full_slot = jax.random.randint(second_key, (), 0, SLOTS)
    return jnp.where(jnp.arange(SLOTS) == full_slot, SLOT_LENGTH, drawn).astype(jnp.int32)


def draw_picked(key, part):
    offsets = jax.random.randint(key, (SLOTS, PICKS), 0, LEN_DEV)
    offsets = offsets.at[0, 0].set(0)
    offsets = offsets.at[0, PICKS - 1].set(LEN_DEV - 1)
    starts = jnp.arange(PICKS) // PICK_DEV * LEN_DEV
    return (offsets + starts[None, :]).astype(jnp.int32)


def draw_embedding(key, part):
    key = jax.random.fold_in(key, 11)
    noise_key = jax.random.fold_in(key, 0)
    return jnp.clip(0.09 * jax.random.normal(noise_key, (VOCAB, MODEL_WIDTH), jnp.float32), -0.54, 0.54)


def place_ends(entries, key, low, largest):
    extent = entries.shape
    spot = [jax.random.randint(jax.random.fold_in(key, axis), (), 0, extent[axis]) for axis in range(len(extent))]
    entries = entries.at[tuple(spot)].set(low)
    longest = extent.index(max(extent))
    spot[longest] = (spot[longest] + 1) % extent[longest]
    return entries.at[tuple(spot)].set(largest)


def level_of(key, shape, pieces, low, top_value):
    def one(dim, parts):
        steps = jax.random.uniform(jax.random.fold_in(jax.random.fold_in(key, 6), dim), (parts,), jnp.float32, low / len(pieces), top_value / len(pieces))
        return jnp.repeat(jnp.exp(steps), shape[dim] // parts).reshape((-1,) + (1,) * (len(shape) - dim - 1))

    level = one(*pieces[0])
    for cut in pieces[1:]:
        level = level * one(*cut)
    return level


def wide_ids(rng, dims, amount, skew):
    weights = [min(1 << octave, amount + 1 - (1 << octave)) * (1 << 20) // math.isqrt((1 << octave) ** skew) + 1 for octave in range((amount + 1).bit_length()) if 1 << octave <= amount]
    scale = 1 + sum(weights) // (1 << 30)
    grid = np.cumsum(np.array([max(1, weight // scale) for weight in weights]))
    ticket = jax.random.randint(jax.random.fold_in(rng, 1), dims, 0, int(grid[len(weights) - 1]))
    start = jnp.left_shift(1, jnp.searchsorted(jnp.asarray(grid, jnp.int32), ticket, side="right").astype(jnp.int32))
    rank = start - 1 + jax.random.randint(jax.random.fold_in(rng, 4), dims, 0, 1 << 30) % jnp.minimum(start, amount + 1 - start)
    return jax.random.permutation(jax.random.fold_in(rng, 2), amount)[rank].astype(jnp.int32)


def gaussian(key, extent, width, bound, cuts=(), kind=jnp.bfloat16):
    entries = width * jax.random.normal(key, extent, jnp.float32)
    if cuts:
        entries = entries * level_of(key, extent, cuts, -0.22, 0.18)
    return jnp.clip(entries, -bound, bound).astype(kind)


def setup_inputs(seed: int = 0) -> dict:
    key_of = jax.random.split(jax.random.key(seed), 25)
    return {
        "tokens": place_ends(wide_ids(key_of[0], (SLOTS, SLOT_LENGTH), VOCAB, 1), jax.random.fold_in(key_of[0], 3), 0, VOCAB - 1).astype(jnp.int32),
        "lengths": draw_lengths(jax.random.fold_in(key_of[24], 71), 0),
        "picked": draw_picked(jax.random.fold_in(key_of[24], 71), 0),
        "targets": place_ends(wide_ids(key_of[3], (SLOTS, PICKS), VOCAB, 1), jax.random.fold_in(key_of[3], 3), 0, VOCAB - 1).astype(jnp.int32),
        "advantages": gaussian(key_of[4], (SLOTS, PICKS), 1.0, 6.0, ((1, 8),), jnp.float32),
        "step_count": jax.random.randint(key_of[5], (1,), 1, 21).astype(jnp.int32),
        "embedding": draw_embedding(jax.random.fold_in(key_of[24], 71), 0),
        "first_embedding": gaussian(key_of[7], (VOCAB, MODEL_WIDTH), (0.00222 / ENTRIES ** 0.5), 1.0161426189370104e-06, ((0, 32),), jnp.float32),
        "second_embedding": jnp.clip(jnp.exp(math.log(8.697457359353733e-13) - 4.6051701 * jax.random.uniform(key_of[8], (VOCAB, MODEL_WIDTH), jnp.float32) ** level_of(key_of[8], (VOCAB, MODEL_WIDTH), ((0, 32),), -0.2, 0.2)), 8.697457969217455e-15, 8.697457359353733e-13),
        "inflow": gaussian(key_of[9], (MODEL_WIDTH, (QUERY_HEADS + 2 * KEY_VALUE_HEADS) * HEAD_WIDTH), MODEL_WIDTH ** -0.5, 0.1875, ((0, 32),), jnp.float32),
        "inflow_first_moment": gaussian(key_of[10], (MODEL_WIDTH, (QUERY_HEADS + 2 * KEY_VALUE_HEADS) * HEAD_WIDTH), (0.00657 / ENTRIES ** 0.5), 3.0102269192866515e-06, ((0, 32),), jnp.float32),
        "inflow_second_moment": jnp.clip(jnp.exp(math.log(7.588385649015539e-12) - 4.6051702 * jax.random.uniform(key_of[11], (MODEL_WIDTH, (QUERY_HEADS + 2 * KEY_VALUE_HEADS) * HEAD_WIDTH), jnp.float32) ** level_of(key_of[11], (MODEL_WIDTH, (QUERY_HEADS + 2 * KEY_VALUE_HEADS) * HEAD_WIDTH), ((0, 32),), -0.2, 0.2)), 7.588385892961028e-14, 7.588385649015539e-12),
        "outflow": gaussian(key_of[12], (QUERY_HEADS * HEAD_WIDTH, MODEL_WIDTH), (QUERY_HEADS * HEAD_WIDTH * 4 // SLOT_LENGTH) ** -0.5, 3.0, ((0, 32),), jnp.float32),
        "first_outflow": gaussian(key_of[13], (QUERY_HEADS * HEAD_WIDTH, MODEL_WIDTH), (0.00043 / ENTRIES ** 0.5), 1.9711639254182955e-07, ((0, 32),), jnp.float32),
        "second_outflow": jnp.clip(jnp.exp(math.log(3.2688431226158415e-14) - 4.6051702 * jax.random.uniform(key_of[14], (QUERY_HEADS * HEAD_WIDTH, MODEL_WIDTH), jnp.float32) ** level_of(key_of[14], (QUERY_HEADS * HEAD_WIDTH, MODEL_WIDTH), ((0, 32),), -0.2, 0.2)), 3.268843080264194e-16, 3.2688431226158415e-14),
        "expand": gaussian(key_of[15], (MODEL_WIDTH, 2 * FF), MODEL_WIDTH ** -0.5, 0.1875, ((0, 32),), jnp.float32),
        "first_expand": gaussian(key_of[16], (MODEL_WIDTH, 2 * FF), (0.00111 / ENTRIES ** 0.5), 5.088353418614133e-07, ((0, 32),), jnp.float32),
        "second_expand": jnp.clip(jnp.exp(math.log(2.1772830120867642e-13) - 4.6051702 * jax.random.uniform(key_of[17], (MODEL_WIDTH, 2 * FF), jnp.float32) ** level_of(key_of[17], (MODEL_WIDTH, 2 * FF), ((0, 32),), -0.2, 0.2)), 2.1772829443241284e-15, 2.1772830120867642e-13),
        "contract": gaussian(key_of[18], (FF, MODEL_WIDTH), FF ** -0.5, 0.109375, ((0, 32),), jnp.float32),
        "first_contract": gaussian(key_of[19], (FF, MODEL_WIDTH), (0.00111 / ENTRIES ** 0.5), 5.088353418614133e-07, ((0, 32),), jnp.float32),
        "second_contract": jnp.clip(jnp.exp(math.log(2.1772830120867642e-13) - 4.6051702 * jax.random.uniform(key_of[20], (FF, MODEL_WIDTH), jnp.float32) ** level_of(key_of[20], (FF, MODEL_WIDTH), ((0, 32),), -0.2, 0.2)), 2.1772829443241284e-15, 2.1772830120867642e-13),
        "scales": jnp.clip(1.0 + 0.1 * jax.random.normal(key_of[21], (GAINS,), jnp.float32), 0.5, 1.5),
        "first_scales": gaussian(key_of[22], (GAINS,), (0.00974 / ENTRIES ** 0.5), 4.461859134607948e-06, ((0, 32),), jnp.float32),
        "second_scales": jnp.clip(jnp.exp(math.log(1.6752821352383762e-11) - 4.6051702 * jax.random.uniform(key_of[23], (GAINS,), jnp.float32) ** level_of(key_of[23], (GAINS,), ((0, 32),), -0.2, 0.2)), 1.6752820918702893e-13, 1.6752821352383762e-11),
    }


norm_eps = 1e-06
rope_base = 1000000.0
clip_limit = 0.01
beta_first = 0.9
beta_second = 0.95
adam_eps = 1e-08
learning_rates = (0.01, 0.003, 0.07, 0.003, 0.002, 0.01)
weight_decays = (0.1, 0.1, 0.1, 0.1, 0.1, 0.0)
highest = lax.Precision.HIGHEST

@jax.custom_vjp
def low(v):
    return lax.optimization_barrier(v.astype(jnp.bfloat16)).astype(jnp.float32)

@jax.custom_vjp
def low_back(v):
    return v

def low_keep(v):
    return (low(v), None)

def low_pass(kept, grad):
    return (grad,)

def back_keep(v):
    return (v, None)

def back_low(kept, grad):
    return (low(grad),)
low.defvjp(low_keep, low_pass)
low_back.defvjp(back_keep, back_low)

def rms(values, gain_vec):
    return values * lax.rsqrt(lax.optimization_barrier(jnp.mean(values * values, axis=-1, keepdims=True)) + norm_eps) * gain_vec

def rope_angles(positions):
    half_width = HEAD_WIDTH // 2
    frequency = rope_base ** (-(jnp.arange(half_width, dtype=jnp.int32).astype(jnp.float32) * 2.0 / HEAD_WIDTH))
    angles = positions.astype(jnp.float32)[:, None] * frequency[None, :]
    return (jnp.cos(angles), jnp.sin(angles))

def rotate(values, cosine_table, sine_table):
    half_width = values.shape[-1] // 2
    front_half = values[..., :half_width]
    back_half = values[..., half_width:]
    cosine_part = cosine_table[:, None, :]
    sine_part = sine_table[:, None, :]
    return jnp.concatenate([front_half * cosine_part - back_half * sine_part, back_half * cosine_part + front_half * sine_part], axis=-1)

def attention(query_rot, rotated_key, value_reduced, length):
    heads_of_keys = jnp.repeat(rotated_key, QUERY_HEADS // KEY_VALUE_HEADS, axis=1)
    heads_of_values = jnp.repeat(value_reduced, QUERY_HEADS // KEY_VALUE_HEADS, axis=1)
    block_rows = math.gcd(SLOT_LENGTH, 512)
    key_pos = jnp.arange(SLOT_LENGTH, dtype=jnp.int32)
    score_scale = HEAD_WIDTH ** (-0.5)

    def one_block(block_index):
        start_row = (block_index * block_rows).astype(jnp.int32)
        query_part = lax.dynamic_slice_in_dim(query_rot, start_row, block_rows, 0)
        query_pos = start_row + jnp.arange(block_rows, dtype=jnp.int32)
        raw_scores = jnp.einsum('qhd,khd->hqk', query_part, heads_of_keys, precision=highest)
        scores = low_back(raw_scores) * score_scale
        allowed = ((key_pos[None, :] <= query_pos[:, None]) & (key_pos[None, :] < length))[None, :, :]
        masked = jnp.where(allowed, scores, -1e+30)
        row_max = lax.optimization_barrier(jnp.max(masked, axis=-1, keepdims=True))
        weights = jnp.where(allowed, jnp.exp(masked - row_max), 0.0)
        attn_probs = weights / lax.optimization_barrier(jnp.sum(weights, axis=-1, keepdims=True))
        return jnp.einsum('hqk,khd->qhd', low(attn_probs), heads_of_values, precision=highest)
    blocks = lax.map(jax.checkpoint(one_block), jnp.arange(SLOT_LENGTH // block_rows, dtype=jnp.int32))
    return blocks.reshape(SLOT_LENGTH, QUERY_HEADS, HEAD_WIDTH)

def slot_loss(lowered, inputs):
    table, weight_in, weight_out, weight_expand, weight_contract, gains_low = lowered
    sequence, length, chosen, target, advantage = inputs
    gain_attn = gains_low[:MODEL_WIDTH]
    gain_mlp = gains_low[MODEL_WIDTH:2 * MODEL_WIDTH]
    gain_final = gains_low[2 * MODEL_WIDTH:3 * MODEL_WIDTH]
    gain_query = gains_low[3 * MODEL_WIDTH:3 * MODEL_WIDTH + HEAD_WIDTH]
    gain_key = gains_low[3 * MODEL_WIDTH + HEAD_WIDTH:]
    embedded = low_back(jnp.take(table, sequence, axis=0))
    normed_in = low(rms(embedded, gain_attn))
    blended_rows = low_back(jnp.dot(normed_in, weight_in, precision=highest))
    queries = blended_rows[:, :QUERY_HEADS * HEAD_WIDTH].reshape(SLOT_LENGTH, QUERY_HEADS, HEAD_WIDTH)
    key_portion = blended_rows[:, QUERY_HEADS * HEAD_WIDTH:(QUERY_HEADS + KEY_VALUE_HEADS) * HEAD_WIDTH].reshape(SLOT_LENGTH, KEY_VALUE_HEADS, HEAD_WIDTH)
    value_portion = blended_rows[:, (QUERY_HEADS + KEY_VALUE_HEADS) * HEAD_WIDTH:].reshape(SLOT_LENGTH, KEY_VALUE_HEADS, HEAD_WIDTH)
    cosine_table, sine_table = rope_angles(jnp.arange(SLOT_LENGTH, dtype=jnp.int32))
    query_rot = low(low_back(rotate(rms(queries, gain_query), cosine_table, sine_table)))
    rotated_key = low(low_back(rotate(rms(key_portion, gain_key), cosine_table, sine_table)))
    value_reduced = low(low_back(value_portion))
    attended = low(low_back(attention(query_rot, rotated_key, value_reduced, length)))
    branch = low_back(jnp.dot(attended.reshape(SLOT_LENGTH, QUERY_HEADS * HEAD_WIDTH), weight_out, precision=highest))
    after_attn = embedded + branch
    normed_mlp = low(rms(after_attn, gain_mlp))
    gate_up = jnp.dot(normed_mlp, weight_expand, precision=highest)
    gate_part = low_back(gate_up[:, :FF])
    up_part = low_back(gate_up[:, FF:])
    activated = low(jax.nn.silu(gate_part) * up_part)
    after_mlp = after_attn + low_back(jnp.dot(activated, weight_contract, precision=highest))
    final_rows = low(jnp.take(rms(after_mlp, gain_final), chosen, axis=0))
    logits = low_back(jnp.dot(final_rows, table.T, precision=highest))
    row_max = lax.optimization_barrier(jnp.max(logits, axis=1, keepdims=True))
    log_norm = row_max[:, 0] + jnp.log(lax.optimization_barrier(jnp.sum(jnp.exp(logits - row_max), axis=1)))
    target_logit = jnp.take_along_axis(logits, target[:, None], axis=1)[:, 0]
    is_valid = chosen < length
    return -jnp.sum(jnp.where(is_valid, advantage * (target_logit - log_norm), 0.0))

def adam_update(weight_now, first_now, second_now, gradient, rate_value, decay_value, step_float):
    new_first = beta_first * first_now + (1.0 - beta_first) * gradient
    new_second = beta_second * second_now + (1.0 - beta_second) * gradient * gradient
    first_hat = new_first / (1.0 - beta_first ** step_float)
    second_hat = new_second / (1.0 - beta_second ** step_float)
    change = -rate_value * (first_hat / (jnp.sqrt(second_hat) + adam_eps) + decay_value * weight_now)
    return (change, new_first, new_second)

def reference(tokens, lengths, picked, targets, advantages, step_count, embedding, first_embedding, second_embedding, inflow, inflow_first_moment, inflow_second_moment, outflow, first_outflow, second_outflow, expand, first_expand, second_expand, contract, first_contract, second_contract, scales, first_scales, second_scales):
    params = (embedding, inflow, outflow, expand, contract, scales)
    firsts = (first_embedding, inflow_first_moment, first_outflow, first_expand, first_contract, first_scales)
    seconds = (second_embedding, inflow_second_moment, second_outflow, second_expand, second_contract, second_scales)

    def total_loss(weights):
        lowered = tuple((low(weight_item) for weight_item in weights))
        checked = jax.checkpoint(slot_loss)

        def scan_step(running, inputs):
            return (running + checked(lowered, inputs), None)
        result, _ = lax.scan(scan_step, jnp.zeros((), jnp.float32), (tokens, lengths, picked, targets, advantages))
        return result
    raw_loss, pullback = jax.vjp(total_loss, params)
    gradients = pullback(jnp.ones_like(raw_loss))[0]
    valid_count = jnp.sum((picked < lengths[:, None]).astype(jnp.float32))
    squares = jnp.zeros((), jnp.float32)
    for gradient in gradients:
        squares = squares + jnp.sum(gradient * gradient)
    gradient_norm = jnp.sqrt(squares) / valid_count
    factor = jnp.minimum(1.0, clip_limit / gradient_norm) / valid_count
    step_float = step_count[0].astype(jnp.float32)
    outputs = [raw_loss / valid_count, gradient_norm]
    for position in range(6):
        change, new_first, new_second = adam_update(params[position], firsts[position], seconds[position], gradients[position] * factor, learning_rates[position], weight_decays[position], step_float)
        outputs = outputs + [change, new_first, new_second]
    return tuple(outputs)
```

```python
import functools
import math

import jax
import jax.numpy as jnp
from jax import lax
from jax.experimental import pallas as pl
from jax.experimental.pallas import tpu as pltpu
from jax.sharding import PartitionSpec as P

MODEL_WIDTH = 1024
QUERY_HEADS = 16
KEY_VALUE_HEADS = 8
HEAD_WIDTH = 128
FF = 3072
QUERY_WIDTH = QUERY_HEADS * HEAD_WIDTH

norm_eps = 1e-06
rope_base = 1000000.0
clip_limit = 0.01
beta_first = 0.9
beta_second = 0.95
adam_eps = 1e-08
learning_rates = (0.01, 0.003, 0.07, 0.003, 0.002, 0.01)
weight_decays = (0.1, 0.1, 0.1, 0.1, 0.1, 0.0)
masked_score = -1e30

bf16 = jnp.bfloat16
f32 = jnp.float32
BOTH = ("ulysses", "blk")


def inverse_root(values):
    return lax.rsqrt(jnp.mean(values * values, axis=-1, keepdims=True) + norm_eps)


def norm_back(inputs, gain_vec, upstream):
    root_scale = inverse_root(inputs)
    unit_rows = inputs * root_scale
    weighted = upstream * gain_vec
    grad_inputs = root_scale * (
        weighted - unit_rows * jnp.mean(weighted * unit_rows, axis=-1, keepdims=True)
    )
    grad_gain = jnp.sum((upstream * unit_rows).reshape(-1, gain_vec.shape[-1]), axis=0)
    return (grad_inputs, grad_gain)


def rope_angles(positions):
    half_width = HEAD_WIDTH // 2
    frequency = rope_base ** (
        -(jnp.arange(half_width, dtype=jnp.int32).astype(f32) * 2.0 / HEAD_WIDTH)
    )
    angles = positions.astype(f32)[:, None] * frequency[None, :]
    return (jnp.cos(angles), jnp.sin(angles))


def rotate(values, tables, sign_value):
    half_width = values.shape[-1] // 2
    front_half = values[..., :half_width]
    back_half = values[..., half_width:]
    cosine_part = tables[0][:, None, :]
    sine_part = tables[1][:, None, :] * sign_value
    return jnp.concatenate(
        [
            front_half * cosine_part - back_half * sine_part,
            back_half * cosine_part + front_half * sine_part,
        ],
        axis=-1,
    )


def mm(left, right):
    return lax.dot_general(left, right, (((1,), (0,)), ((), ())), preferred_element_type=f32)


def mm_outer(left, right):
    return lax.dot_general(left, right, (((0,), (0,)), ((), ())), preferred_element_type=f32)


def mm_back(left, right):
    return lax.dot_general(left, right, (((1,), (1,)), ((), ())), preferred_element_type=f32)


def spread_rows(onehot, rows):
    return lax.dot_general(
        onehot.astype(f32),
        rows,
        (((0,), (0,)), ((), ())),
        precision=lax.Precision.HIGHEST,
        preferred_element_type=f32,
    )


def adam_update(weight_now, first_now, second_now, gradient, rate_value, decay_value, step_float):
    new_first = beta_first * first_now + (1.0 - beta_first) * gradient
    new_second = beta_second * second_now + (1.0 - beta_second) * gradient * gradient
    first_hat = new_first / (1.0 - beta_first**step_float)
    second_hat = new_second / (1.0 - beta_second**step_float)
    change = -rate_value * (
        first_hat / (jnp.sqrt(second_hat) + adam_eps) + decay_value * weight_now
    )
    return (change, new_first, new_second)


def exchange_kernel(axis, blk_count, kinds, *refs):
    parts = len(kinds)
    sources, landings = refs[:parts], refs[parts : 2 * parts]
    send_sems, recv_sems, own_sems = refs[2 * parts :]
    row, column = lax.axis_index("ulysses"), lax.axis_index("blk")
    if axis == "all":
        me = row * blk_count + column
    else:
        me = row if axis == "ulysses" else column
    count = landings[0].shape[0]

    def place(peer):
        if axis == "all":
            return {"ulysses": peer // blk_count, "blk": lax.rem(peer, blk_count)}
        return {axis: peer}

    barrier = pltpu.get_barrier_semaphore()

    def greet(step, carry):
        pl.semaphore_signal(
            barrier,
            inc=1,
            device_id=place(lax.rem(me + step, count)),
            device_id_type=pl.DeviceIdType.MESH,
        )
        return carry

    lax.fori_loop(1, count, greet, 0)
    pl.semaphore_wait(barrier, count - 1)

    def copies(step):
        peer = lax.rem(me + step, count)
        return [
            pltpu.make_async_remote_copy(
                src_ref=sources[k].at[peer] if kinds[k] == "s" else sources[k],
                dst_ref=landings[k].at[me],
                send_sem=send_sems.at[k, step],
                recv_sem=recv_sems.at[k, step],
                device_id=place(peer),
                device_id_type=pl.DeviceIdType.MESH,
            )
            for k in range(parts)
        ]

    def send(step, carry):
        for copy in copies(step):
            copy.start()
        return carry

    lax.fori_loop(1, count, send, 0)
    own = [
        pltpu.make_async_copy(
            sources[k].at[me] if kinds[k] == "s" else sources[k],
            landings[k].at[me],
            own_sems.at[k],
        )
        for k in range(parts)
    ]
    for copy in own:
        copy.start()
    for copy in own:
        copy.wait()

    def finish(step, carry):
        for copy in copies(step):
            copy.wait()
        return carry

    lax.fori_loop(1, count, finish, 0)


class Exchanger:
    def __init__(self):
        self.used = 0

    def __call__(self, axis, kinds, *arrays):
        blk_count = lax.axis_size("blk")
        count = lax.axis_size("ulysses") * blk_count if axis == "all" else lax.axis_size(axis)
        shapes = [
            jax.ShapeDtypeStruct(
                array.shape if kind == "s" else (count,) + array.shape, array.dtype
            )
            for kind, array in zip(kinds, arrays)
        ]
        parts = len(arrays)
        collective_id = self.used
        self.used += 1
        return pl.pallas_call(
            functools.partial(exchange_kernel, axis, blk_count, kinds),
            out_shape=shapes,
            in_specs=[pl.BlockSpec(memory_space=pltpu.VMEM)] * parts,
            out_specs=[pl.BlockSpec(memory_space=pltpu.VMEM)] * parts,
            scratch_shapes=[
                pltpu.SemaphoreType.DMA((parts, count)),
                pltpu.SemaphoreType.DMA((parts, count)),
                pltpu.SemaphoreType.DMA((parts,)),
            ],
            compiler_params=pltpu.CompilerParams(
                collective_id=collective_id,
                has_side_effects=True,
                vmem_limit_bytes=32 * 1024 * 1024,
            ),
            name="exchange_" + str(collective_id),
        )(*arrays)


def lookup_kernel(slots, fills_ref, ids_ref, table_ref, rows_ref, wide, sem):
    wide[...] = jnp.zeros_like(wide)

    def row_copy(place, row):
        return pltpu.make_async_copy(
            table_ref.at[pl.ds(row, 1), :], wide.at[pl.ds(place, 1), :], sem
        )

    def of_peer(peer, total):
        fill = fills_ref[peer]

        def fetch(k, carry):
            place = peer * slots + k
            row_copy(place, ids_ref[place]).start()
            return carry

        lax.fori_loop(0, fill, fetch, 0)
        return total + fill

    total = lax.fori_loop(0, fills_ref.shape[0], of_peer, 0)

    def drain(k, carry):
        row_copy(0, 0).wait()
        return carry

    lax.fori_loop(0, total, drain, 0)
    rows_ref[...] = wide[...].astype(rows_ref.dtype)


def lookup(fills, ids, table, slots):
    places = ids.shape[0]
    return pl.pallas_call(
        functools.partial(lookup_kernel, slots),
        out_shape=jax.ShapeDtypeStruct((places, table.shape[1]), bf16),
        in_specs=[
            pl.BlockSpec(memory_space=pltpu.SMEM),
            pl.BlockSpec(memory_space=pltpu.SMEM),
            pl.BlockSpec(memory_space=pl.ANY),
        ],
        out_specs=pl.BlockSpec(memory_space=pltpu.VMEM),
        scratch_shapes=[
            pltpu.VMEM((places, table.shape[1]), f32),
            pltpu.SemaphoreType.DMA,
        ],
        compiler_params=pltpu.CompilerParams(vmem_limit_bytes=40 * 1024 * 1024),
        name="lookup",
    )(fills, ids, table)


def local(
    tokens,
    lengths,
    picked,
    targets,
    advantages,
    step_count,
    embedding,
    first_embedding,
    second_embedding,
    inflow,
    inflow_first_moment,
    inflow_second_moment,
    outflow,
    first_outflow,
    second_outflow,
    expand,
    first_expand,
    second_expand,
    contract,
    first_contract,
    second_contract,
    scales,
    first_scales,
    second_scales,
):
    exchange = Exchanger()
    n_u, n_b = lax.axis_size("ulysses"), lax.axis_size("blk")
    n_all = n_u * n_b
    u, b = lax.axis_index("ulysses"), lax.axis_index("blk")
    me = u * n_b + b
    slot_count, block_len = tokens.shape
    assert slot_count == n_u
    picks = picked.shape[1]
    slot_picks = picks * n_b
    all_picks = slot_picks * n_u
    row_share = embedding.shape[0]
    group = QUERY_HEADS // KEY_VALUE_HEADS
    score_scale = HEAD_WIDTH ** (-0.5)
    in_rows, out_share, ff_share = inflow.shape[0], outflow.shape[0], contract.shape[0]
    q_share = QUERY_WIDTH // n_b
    heads_share = q_share // HEAD_WIDTH

    inflow_low = inflow.astype(bf16)
    kv_weight = lax.all_gather(inflow_low[:, QUERY_WIDTH:], BOTH, axis=0, tiled=True)
    q_cols = inflow_low[:, :QUERY_WIDTH].reshape(in_rows, n_b, q_share).transpose(1, 0, 2)
    ff_cols = (
        expand.astype(bf16)
        .reshape(in_rows, 2, n_u, n_b, ff_share)
        .transpose(3, 0, 1, 2, 4)
        .reshape(n_b, in_rows, 2 * n_u * ff_share)
    )
    (split_cols,) = exchange("blk", "s", jnp.concatenate([q_cols, ff_cols], axis=2))
    in_block = n_b * in_rows
    mixed_share = q_share + 2 * n_u * ff_share
    wide_rows = in_block * mixed_share // MODEL_WIDTH
    layer_rows = jnp.concatenate(
        [
            split_cols.reshape(wide_rows, MODEL_WIDTH),
            outflow.astype(bf16),
            contract.astype(bf16),
        ],
        axis=0,
    )
    layer_all = lax.all_gather(layer_rows, "ulysses", axis=0)
    mixed_in = layer_all[:, :wide_rows].reshape(n_u * in_block, mixed_share)
    q_weight = mixed_in[:, :q_share]
    ff_weight = mixed_in[:, q_share:]
    out_weight = layer_all[:, wide_rows : wide_rows + out_share].reshape(n_u * out_share, MODEL_WIDTH)
    contract_weight = layer_all[:, wide_rows + out_share :].reshape(n_u * ff_share, MODEL_WIDTH)

    packed = jnp.concatenate(
        [tokens.astype(f32), targets.astype(f32), picked.astype(f32), advantages], axis=1
    )
    scale_share = scales.shape[0]
    gains_mine = jnp.pad(scales, (0, 128 - scale_share)).reshape(1, 128)
    packed_all, = exchange("blk", "g", packed)
    gains_all, = exchange("all", "g", gains_mine)
    gains_wide = gains_all[:, 0, :scale_share].reshape(-1).astype(bf16).astype(f32)
    gain_attn = gains_wide[:MODEL_WIDTH]
    gain_mlp = gains_wide[MODEL_WIDTH : 2 * MODEL_WIDTH]
    gain_final = gains_wide[2 * MODEL_WIDTH : 3 * MODEL_WIDTH]
    gain_query = gains_wide[3 * MODEL_WIDTH : 3 * MODEL_WIDTH + HEAD_WIDTH]
    gain_key = gains_wide[3 * MODEL_WIDTH + HEAD_WIDTH :]

    wants_count = block_len + picks
    wants = (
        packed_all[:, :, :wants_count]
        .astype(jnp.int32)
        .transpose(1, 0, 2)
        .reshape(n_all, wants_count)
    )
    picked_all = packed_all[:, :, wants_count : wants_count + picks].astype(jnp.int32)
    targets_all = packed_all[:, :, block_len:wants_count].astype(jnp.int32)
    advantages_all = packed_all[:, :, wants_count + picks :]
    valid_all = picked_all < lengths[None, :, None]
    weights_all = jnp.where(valid_all, advantages_all, 0.0)
    my_length = lax.dynamic_index_in_dim(lengths, u, 0, keepdims=False)
    slot_picked = lax.dynamic_index_in_dim(picked_all, u, 1, keepdims=False).reshape(-1)
    my_picked = lax.dynamic_index_in_dim(picked, u, 0, keepdims=False)
    my_valid = my_picked < my_length
    my_weight = jnp.where(
        my_valid, lax.dynamic_index_in_dim(advantages, u, 0, keepdims=False), 0.0
    )

    fill_mean = wants_count / n_all
    slots = -(-int(fill_mean + 8 * math.sqrt(fill_mean)) // 16) * 16
    places = n_all * slots
    owner_all = wants // row_share
    counts = jnp.sum(
        (owner_all[:, None, :] == jnp.arange(n_all, dtype=jnp.int32)[None, :, None]).astype(
            jnp.int32
        ),
        axis=-1,
    )
    rounds = (jnp.max(counts) + slots - 1) // slots
    wants_mine = owner_all == me
    earlier = (
        jnp.arange(wants_count)[:, None] < jnp.arange(wants_count)[None, :]
    ).astype(bf16)
    rank_mine = mm(wants_mine.astype(bf16), earlier).astype(jnp.int32)
    total_mine = jnp.sum(wants_mine.astype(jnp.int32), axis=1)
    rows_mine = jnp.where(wants_mine, wants - me * row_share, 0)
    own_wants = lax.dynamic_index_in_dim(wants, me, 0, keepdims=False)
    own_owner = own_wants // row_share
    same_owner = own_owner[:, None] == own_owner[None, :]
    own_rank = jnp.sum(
        jnp.where(
            same_owner & (jnp.arange(wants_count)[:, None] < jnp.arange(wants_count)[None, :]),
            1,
            0,
        ),
        axis=0,
    )

    def slot_ids(turn):
        slot_rank = turn * slots + jnp.arange(slots, dtype=jnp.int32)
        chosen = wants_mine[:, None, :] & (rank_mine[:, None, :] == slot_rank[None, :, None])
        ids = jnp.sum(jnp.where(chosen, rows_mine[:, None, :], 0), axis=-1)
        fills = jnp.clip(total_mine - turn * slots, 0, slots)
        filled = jnp.arange(slots)[None, :] < fills[:, None]
        return (ids, fills, filled)

    def landing(turn):
        rank = own_rank - turn * slots
        place = jnp.where((rank >= 0) & (rank < slots), own_owner * slots + rank, -1)
        return (place[:, None] == jnp.arange(places, dtype=jnp.int32)[None, :]).astype(bf16)

    rows_out = exchange.used
    exchange.used += 1

    def fetch_turn(state):
        turn, so_far = state
        ids, fills, _ = slot_ids(turn)
        rows = lookup(fills, ids.reshape(-1), embedding, slots)
        mine = Exchanger()
        mine.used = rows_out
        (arrived,) = mine("all", "s", rows.reshape(n_all, slots, MODEL_WIDTH))
        return (turn + 1, so_far + mm(landing(turn), arrived.reshape(places, MODEL_WIDTH)))

    _, fetched = lax.while_loop(
        lambda state: state[0] < rounds,
        fetch_turn,
        (jnp.int32(0), jnp.zeros((wants_count, MODEL_WIDTH), f32)),
    )
    embedded = fetched[:block_len]
    target_rows = fetched[block_len:]

    unit_in = embedded * inverse_root(embedded)
    normed_in = (unit_in * gain_attn).astype(bf16)
    pick_hot = (my_picked - b * block_len)[:, None] == jnp.arange(block_len)[None, :]
    picked_both = mm(
        pick_hot.astype(bf16), jnp.concatenate([embedded.astype(bf16), normed_in], axis=1)
    )
    embedded_picks = picked_both[:, :MODEL_WIDTH]
    (normed_slot,) = exchange("blk", "g", picked_both[:, MODEL_WIDTH:].astype(bf16))
    normed_slot = normed_slot.reshape(slot_picks, MODEL_WIDTH)
    mixed_kv = mm(normed_in, kv_weight)
    key_raw = mixed_kv[:, : KEY_VALUE_HEADS * HEAD_WIDTH].reshape(
        block_len, KEY_VALUE_HEADS, HEAD_WIDTH
    )
    values_low = (
        mixed_kv[:, KEY_VALUE_HEADS * HEAD_WIDTH :]
        .reshape(block_len, KEY_VALUE_HEADS, HEAD_WIDTH)
        .astype(bf16)
        .transpose(1, 0, 2)
    )
    key_pos = b * block_len + jnp.arange(block_len, dtype=jnp.int32)
    key_tables = rope_angles(key_pos)
    key_rot = (
        rotate(key_raw * inverse_root(key_raw) * gain_key, key_tables, 1.0)
        .astype(bf16)
        .transpose(1, 0, 2)
    )

    query_raw = mm(normed_slot, q_weight).reshape(slot_picks, heads_share, HEAD_WIDTH)
    query_tables = rope_angles(slot_picked)
    query_mine = rotate(query_raw * inverse_root(query_raw) * gain_query, query_tables, 1.0)
    (query_all,) = exchange("blk", "g", query_mine.astype(bf16).reshape(slot_picks, q_share))

    def into_groups(array):
        return (
            array.reshape(n_b, slot_picks, heads_share, HEAD_WIDTH)
            .transpose(0, 2, 1, 3)
            .reshape(KEY_VALUE_HEADS, group * slot_picks, HEAD_WIDTH)
        )

    query_groups = into_groups(query_all)
    query_pos = jnp.tile(slot_picked, group)
    allowed = ((key_pos[None, :] <= query_pos[:, None]) & (key_pos[None, :] < my_length))[None]
    scores = (
        jnp.einsum("kqd,kjd->kqj", query_groups, key_rot, preferred_element_type=f32)
        * score_scale
    )
    scores = jnp.where(allowed, scores, masked_score)
    part_max = jnp.max(scores, axis=-1, keepdims=True)
    part_weights = jnp.where(allowed, jnp.exp(scores - part_max), 0.0)
    part_sum = jnp.sum(part_weights, axis=-1)
    part_out = jnp.einsum(
        "kqj,kjd->kqd", part_weights.astype(bf16), values_low, preferred_element_type=f32
    )
    out_cut = QUERY_WIDTH // n_all
    part_send = (
        part_out.astype(bf16)
        .reshape(QUERY_HEADS, slot_picks, HEAD_WIDTH)
        .transpose(1, 0, 2)
        .reshape(slot_picks, n_u, n_b, out_cut)
        .transpose(2, 0, 1, 3)
        .reshape(n_b, slot_picks, n_u * out_cut)
    )
    stats = jnp.stack([part_max[..., 0], part_sum]).reshape(2 * QUERY_HEADS, slot_picks)
    part_got, stats_all = exchange("blk", "sg", part_send, stats)
    stats_all = stats_all.reshape(n_b, 2, QUERY_HEADS, slot_picks)
    full_max = jnp.max(stats_all[:, 0], axis=0)
    shrink = jnp.exp(stats_all[:, 0] - full_max[None])
    full_sum = jnp.sum(stats_all[:, 1] * shrink, axis=0)
    log_total = full_max + jnp.log(full_sum)
    share_of = shrink / full_sum[None]
    heads_row = QUERY_HEADS // n_u
    cut_head = (b * out_cut) // HEAD_WIDTH
    my_share = lax.dynamic_index_in_dim(
        share_of.reshape(n_b, n_u, heads_row, slot_picks), cut_head, 2, keepdims=False
    )
    attended_wide = jnp.sum(
        part_got.astype(f32).reshape(n_b, slot_picks, n_u, out_cut)
        * my_share.transpose(0, 2, 1)[..., None],
        axis=0,
    )
    attended = attended_wide.astype(bf16).reshape(slot_picks, n_u * out_cut)

    def sum_to_picks(partial):
        (got,) = exchange("blk", "s", partial.astype(bf16).reshape(n_b, picks, MODEL_WIDTH))
        return jnp.sum(got.astype(f32), axis=0)

    def to_slot(rows):
        (got,) = exchange("blk", "g", rows)
        return got.reshape(slot_picks, rows.shape[1])

    after_attn = embedded_picks + sum_to_picks(mm(attended, out_weight))
    normed_mlp = to_slot((after_attn * inverse_root(after_attn) * gain_mlp).astype(bf16))
    gate_up = mm(normed_mlp, ff_weight)
    ff_mine = n_u * ff_share
    gate_part, up_part = gate_up[:, :ff_mine], gate_up[:, ff_mine:]
    sigmoid_gate = jax.nn.sigmoid(gate_part)
    activated = (gate_part * sigmoid_gate * up_part).astype(bf16)
    after_mlp = after_attn + sum_to_picks(mm(activated, contract_weight))
    final_rows = (after_mlp * inverse_root(after_mlp) * gain_final).astype(bf16)

    (final_all,) = exchange("ulysses", "g", to_slot(final_rows))
    final_all = final_all.reshape(all_picks, MODEL_WIDTH)
    table_low = embedding.astype(bf16)
    logits = mm_back(final_all, table_low)
    local_max = jnp.max(logits, axis=1)
    head_weights = jnp.exp(logits - local_max[:, None])
    local_sum = jnp.sum(head_weights, axis=1)
    head_rows = mm(head_weights.astype(bf16), table_low).astype(bf16)
    head_stats = jnp.stack([local_max, local_sum], axis=1).reshape(n_u, slot_picks, 2)

    def merge_rows(rows, stats_in):
        top = jnp.max(stats_in[..., 0], axis=0)
        factor = jnp.exp(stats_in[..., 0] - top[None])
        total = jnp.sum(stats_in[..., 1] * factor, axis=0)
        return (jnp.sum(rows.astype(f32) * factor[..., None], axis=0), top, total)

    got_rows, got_stats = exchange(
        "ulysses",
        "ss",
        head_rows.reshape(n_u, slot_picks, MODEL_WIDTH),
        jnp.pad(head_stats, ((0, 0), (0, 0), (0, 126))),
    )
    slot_rows, slot_top, slot_total = merge_rows(got_rows, got_stats)
    slot_stats = jnp.stack([slot_top, slot_total], axis=1).reshape(n_b, picks, 2)
    got_rows, got_stats = exchange(
        "blk",
        "ss",
        slot_rows.astype(bf16).reshape(n_b, picks, MODEL_WIDTH),
        jnp.pad(slot_stats, ((0, 0), (0, 0), (0, 126))),
    )
    mean_rows, top, total = merge_rows(got_rows, got_stats)
    log_norm = top + jnp.log(total)
    target_logit = jnp.sum(final_rows.astype(f32) * target_rows, axis=1)
    loss_local = -jnp.sum(my_weight * (target_logit - log_norm))
    count_local = jnp.sum(my_valid.astype(f32))
    grad_final = my_weight[:, None] * (mean_rows / total[:, None] - target_rows)

    grad_after_mlp, grad_gain_final = norm_back(after_mlp, gain_final, grad_final)
    (got_branch, norms_slot) = exchange(
        "blk",
        "gg",
        grad_after_mlp.astype(bf16),
        jnp.broadcast_to(log_norm[:, None], (picks, 128)),
    )
    grad_branch = got_branch.reshape(slot_picks, MODEL_WIDTH)
    (norms_all,) = exchange("ulysses", "g", norms_slot[:, :, 0].reshape(n_b, picks))
    norms_all = norms_all.reshape(all_picks)
    grad_contract = mm_outer(activated, grad_branch)
    grad_act = mm_back(grad_branch, contract_weight)
    grad_gate = grad_act * up_part * sigmoid_gate * (1.0 + gate_part * (1.0 - sigmoid_gate))
    grad_up = grad_act * gate_part * sigmoid_gate
    grad_gate_up = jnp.concatenate([grad_gate, grad_up], axis=1).astype(bf16)
    grad_expand = mm_outer(normed_mlp, grad_gate_up)
    grad_mid_part, grad_gain_mlp = norm_back(
        after_attn, gain_mlp, sum_to_picks(mm_back(grad_gate_up, ff_weight))
    )
    grad_after_attn = grad_after_mlp + grad_mid_part
    grad_attn_branch = to_slot(grad_after_attn.astype(bf16))
    grad_outflow = mm_outer(attended, grad_attn_branch)
    grad_attended = mm_back(grad_attn_branch, out_weight).astype(bf16)
    delta_part = jnp.sum(
        attended_wide * grad_attended.astype(f32).reshape(slot_picks, n_u, out_cut), axis=-1
    )
    got_attended, got_delta = exchange("blk", "gg", grad_attended, delta_part.T)
    grad_heads = (
        got_attended.reshape(n_b, slot_picks, n_u, out_cut)
        .transpose(1, 2, 0, 3)
        .reshape(slot_picks, QUERY_HEADS, HEAD_WIDTH)
        .transpose(1, 0, 2)
        .reshape(KEY_VALUE_HEADS, group * slot_picks, HEAD_WIDTH)
    )
    row_delta = jnp.sum(
        got_delta.transpose(1, 0, 2).reshape(QUERY_HEADS, HEAD_WIDTH // out_cut, slot_picks), axis=1
    ).reshape(KEY_VALUE_HEADS, group * slot_picks, 1)
    log_groups = log_total.reshape(KEY_VALUE_HEADS, group * slot_picks, 1)
    attn_probs = jnp.where(allowed, jnp.exp(scores - log_groups), 0.0)
    grad_probs = jnp.einsum("kqd,kjd->kqj", grad_heads, values_low, preferred_element_type=f32)
    grad_scores = (attn_probs * (grad_probs - row_delta) * score_scale).astype(bf16)
    grad_query_part = jnp.einsum(
        "kqj,kjd->kqd", grad_scores, key_rot, preferred_element_type=f32
    )
    grad_key_rot = jnp.einsum(
        "kqj,kqd->kjd", grad_scores, query_groups, preferred_element_type=f32
    ).astype(bf16)
    grad_value = jnp.einsum(
        "kqj,kqd->kjd", attn_probs.astype(bf16), grad_heads, preferred_element_type=f32
    ).astype(bf16)
    (got_query,) = exchange(
        "blk",
        "s",
        grad_query_part.astype(bf16)
        .reshape(n_b, heads_share, slot_picks, HEAD_WIDTH)
        .transpose(0, 2, 1, 3)
        .reshape(n_b, slot_picks, q_share),
    )
    grad_query_rot = jnp.sum(got_query.astype(f32), axis=0).astype(bf16).astype(f32)
    grad_query_raw, grad_gain_query = norm_back(
        query_raw,
        gain_query,
        rotate(grad_query_rot.reshape(slot_picks, heads_share, HEAD_WIDTH), query_tables, -1.0),
    )
    grad_query_low = grad_query_raw.reshape(slot_picks, q_share).astype(bf16)
    grad_q_weight = mm_outer(normed_slot, grad_query_low)
    grad_normed_picks = sum_to_picks(mm_back(grad_query_low, q_weight))
    grad_key_raw, grad_gain_key = norm_back(
        key_raw, gain_key, rotate(grad_key_rot.astype(f32).transpose(1, 0, 2), key_tables, -1.0)
    )
    grad_kv = jnp.concatenate(
        [
            grad_key_raw.reshape(block_len, -1).astype(bf16),
            grad_value.transpose(1, 0, 2).reshape(block_len, -1),
        ],
        axis=1,
    )
    grad_kv_weight = mm_outer(normed_in, grad_kv)
    back_both = spread_rows(
        pick_hot, jnp.concatenate([grad_normed_picks, grad_after_attn], axis=1)
    )
    grad_normed = mm_back(grad_kv, kv_weight) + back_both[:, :MODEL_WIDTH]
    grad_embed_part, grad_gain_attn = norm_back(embedded, gain_attn, grad_normed)
    grad_embedded = (back_both[:, MODEL_WIDTH:] + grad_embed_part).astype(bf16)

    grad_layer = jnp.concatenate(
        [
            jnp.concatenate([grad_q_weight, grad_expand], axis=1)
            .astype(bf16)
            .reshape(n_u, wide_rows, MODEL_WIDTH),
            grad_outflow.astype(bf16).reshape(n_u, out_share, MODEL_WIDTH),
            grad_contract.astype(bf16).reshape(n_u, ff_share, MODEL_WIDTH),
        ],
        axis=1,
    )
    got_layer = lax.all_to_all(grad_layer, "ulysses", 0, 0, tiled=True)
    sum_layer = jnp.sum(got_layer.astype(f32), axis=0)
    sum_outflow = sum_layer[wide_rows : wide_rows + out_share]
    sum_contract = sum_layer[wide_rows + out_share :]
    (got_cols,) = exchange("blk", "s", sum_layer[:wide_rows].astype(bf16).reshape(n_b, in_rows, mixed_share))
    got_cols = got_cols.astype(f32)
    sum_q = got_cols[:, :, :q_share].transpose(1, 0, 2).reshape(in_rows, QUERY_WIDTH)
    sum_expand = (
        got_cols[:, :, q_share:]
        .reshape(n_b, in_rows, 2, n_u, ff_share)
        .transpose(1, 2, 3, 0, 4)
        .reshape(in_rows, 2 * FF)
    )
    kv_first = lax.all_to_all(
        grad_kv_weight.astype(bf16).reshape(n_u, in_block, -1), "ulysses", 0, 0, tiled=True
    )
    kv_second = lax.all_to_all(
        jnp.sum(kv_first.astype(f32), axis=0).astype(bf16).reshape(n_b, in_rows, -1),
        "blk",
        0,
        0,
        tiled=True,
    )
    sum_kv = jnp.sum(kv_second.astype(f32), axis=0)
    sum_inflow = jnp.concatenate([sum_q, sum_kv], axis=1)
    grad_scales = jnp.concatenate(
        [grad_gain_attn, grad_gain_mlp, grad_gain_final, grad_gain_query, grad_gain_key]
    )
    (got_scales,) = exchange(
        "all",
        "s",
        jnp.pad(grad_scales.reshape(n_all, scale_share), ((0, 0), (0, 128 - scale_share))).reshape(
            n_all, 1, 128
        ),
    )
    sum_scales = jnp.sum(got_scales, axis=0)[0, :scale_share]

    def flat(array):
        return array.transpose(1, 0, 2).reshape(-1)

    target_local = flat(targets_all) - me * row_share
    is_target = target_local[:, None] == jnp.arange(row_share, dtype=jnp.int32)[None, :]
    grad_logits = (
        flat(weights_all)[:, None]
        * (jnp.exp(logits - norms_all[:, None]) - is_target.astype(f32))
    ).astype(bf16)
    table_head = mm_outer(grad_logits, final_all)
    rows_back = exchange.used
    exchange.used += 1

    def return_turn(state):
        turn, so_far = state
        ids, _, filled = slot_ids(turn)
        sent = mm_outer(landing(turn)[:block_len], grad_embedded).astype(bf16)
        mine = Exchanger()
        mine.used = rows_back
        (arrived,) = mine("all", "s", sent.reshape(n_all, slots, MODEL_WIDTH))
        row_of = jnp.where(filled, ids, -1).reshape(-1)
        hot = (
            jnp.arange(row_share, dtype=jnp.int32)[:, None] == row_of[None, :]
        ).astype(bf16)
        return (turn + 1, so_far + mm(hot, arrived.reshape(places, MODEL_WIDTH)))

    _, table_grad = lax.while_loop(
        lambda state: state[0] < rounds, return_turn, (jnp.int32(0), table_head)
    )

    raw_grads = (table_grad, sum_inflow, sum_outflow, sum_expand, sum_contract, sum_scales)
    squares = jnp.zeros((), f32)
    for grad_piece in raw_grads:
        squares = squares + jnp.sum(grad_piece * grad_piece)
    (totals,) = exchange(
        "all",
        "g",
        jnp.pad(jnp.stack([squares, count_local, loss_local]), (0, 125)).reshape(1, 128),
    )
    totals = jnp.sum(totals, axis=(0, 1))
    square_total, count_total, loss_total = totals[0], totals[1], totals[2]
    gradient_norm = jnp.sqrt(square_total) / count_total
    factor = jnp.minimum(1.0, clip_limit / gradient_norm) / count_total
    step_float = step_count[0].astype(f32)
    weights_now = (embedding, inflow, outflow, expand, contract, scales)
    firsts = (
        first_embedding,
        inflow_first_moment,
        first_outflow,
        first_expand,
        first_contract,
        first_scales,
    )
    seconds = (
        second_embedding,
        inflow_second_moment,
        second_outflow,
        second_expand,
        second_contract,
        second_scales,
    )
    outputs = [loss_total / count_total, gradient_norm]
    for position in range(6):
        change, new_first, new_second = adam_update(
            weights_now[position],
            firsts[position],
            seconds[position],
            raw_grads[position] * factor,
            learning_rates[position],
            weight_decays[position],
            step_float,
        )
        outputs = outputs + [change, new_first, new_second]
    return tuple(outputs)


def solution(mesh):
    rows = P(("ulysses", "blk"), None)
    flat_rows = P(("ulysses", "blk"))
    column = P(None, "blk")
    return jax.shard_map(
        local,
        mesh=mesh,
        in_specs=(column, P(), column, column, column, P()) + (rows,) * 15 + (flat_rows,) * 3,
        out_specs=(P(), P()) + (rows,) * 15 + (flat_rows,) * 3,
        check_vma=False,
    )
```

```python
import functools
import math

import jax
import jax.numpy as jnp
from jax import lax
from jax.experimental import pallas as pl
from jax.experimental.pallas import tpu as pltpu
from jax.sharding import PartitionSpec as P

MODEL_WIDTH = 1024
QUERY_HEADS = 16
KEY_VALUE_HEADS = 8
HEAD_WIDTH = 128
FF = 3072
QUERY_WIDTH = QUERY_HEADS * HEAD_WIDTH

norm_eps = 1e-06
rope_base = 1000000.0
clip_limit = 0.01
beta_first = 0.9
beta_second = 0.95
adam_eps = 1e-08
learning_rates = (0.01, 0.003, 0.07, 0.003, 0.002, 0.01)
weight_decays = (0.1, 0.1, 0.1, 0.1, 0.1, 0.0)
masked_score = -1e30

bf16 = jnp.bfloat16
f32 = jnp.float32
BOTH = ("ulysses", "blk")


def inverse_root(values):
    return lax.rsqrt(jnp.mean(values * values, axis=-1, keepdims=True) + norm_eps)


def norm_back(inputs, gain_vec, upstream):
    root_scale = inverse_root(inputs)
    unit_rows = inputs * root_scale
    weighted = upstream * gain_vec
    grad_inputs = root_scale * (
        weighted - unit_rows * jnp.mean(weighted * unit_rows, axis=-1, keepdims=True)
    )
    grad_gain = jnp.sum((upstream * unit_rows).reshape(-1, gain_vec.shape[-1]), axis=0)
    return (grad_inputs, grad_gain)


def rope_angles(positions):
    half_width = HEAD_WIDTH // 2
    frequency = rope_base ** (
        -(jnp.arange(half_width, dtype=jnp.int32).astype(f32) * 2.0 / HEAD_WIDTH)
    )
    angles = positions.astype(f32)[:, None] * frequency[None, :]
    return (jnp.cos(angles), jnp.sin(angles))


def rotate(values, tables, sign_value):
    half_width = values.shape[-1] // 2
    front_half = values[..., :half_width]
    back_half = values[..., half_width:]
    cosine_part = tables[0][:, None, :]
    sine_part = tables[1][:, None, :] * sign_value
    return jnp.concatenate(
        [
            front_half * cosine_part - back_half * sine_part,
            back_half * cosine_part + front_half * sine_part,
        ],
        axis=-1,
    )


def mm(left, right):
    return lax.dot_general(left, right, (((1,), (0,)), ((), ())), preferred_element_type=f32)


def mm_outer(left, right):
    return lax.dot_general(left, right, (((0,), (0,)), ((), ())), preferred_element_type=f32)


def mm_back(left, right):
    return lax.dot_general(left, right, (((1,), (1,)), ((), ())), preferred_element_type=f32)


def spread_rows(onehot, rows):
    return lax.dot_general(
        onehot.astype(f32),
        rows,
        (((0,), (0,)), ((), ())),
        precision=lax.Precision.HIGHEST,
        preferred_element_type=f32,
    )


def adam_update(weight_now, first_now, second_now, gradient, rate_value, decay_value, step_float):
    new_first = beta_first * first_now + (1.0 - beta_first) * gradient
    new_second = beta_second * second_now + (1.0 - beta_second) * gradient * gradient
    first_hat = new_first / (1.0 - beta_first**step_float)
    second_hat = new_second / (1.0 - beta_second**step_float)
    change = -rate_value * (
        first_hat / (jnp.sqrt(second_hat) + adam_eps) + decay_value * weight_now
    )
    return (change, new_first, new_second)


def place_of(axis, blk_count, peer):
    if axis == "all":
        return {"ulysses": peer // blk_count, "blk": lax.rem(peer, blk_count)}
    return {axis: peer}


def rank_of(axis, blk_count):
    row, column = lax.axis_index("ulysses"), lax.axis_index("blk")
    return {"ulysses": row, "blk": column, "all": row * blk_count + column}[axis]


def greet(axes, blk_count, counts):
    barrier = pltpu.get_barrier_semaphore()
    axes = ("all",) if "all" in axes else tuple(axes)
    total = 0
    for axis in axes:
        me, count = rank_of(axis, blk_count), counts[axis]

        def call(step, carry, axis=axis, me=me, count=count):
            pl.semaphore_signal(
                barrier,
                inc=1,
                device_id=place_of(axis, blk_count, lax.rem(me + step, count)),
                device_id_type=pl.DeviceIdType.MESH,
            )
            return carry

        lax.fori_loop(1, count, call, 0)
        total += count - 1
    pl.semaphore_wait(barrier, total)


def each(count, body, first=0):
    def step(k, carry):
        body(k)
        return carry

    lax.fori_loop(first, count, step, 0)


def remote(source, target, send_sem, recv_sem, device_id):
    return pltpu.make_async_remote_copy(
        src_ref=source,
        dst_ref=target,
        send_sem=send_sem,
        recv_sem=recv_sem,
        device_id=device_id,
        device_id_type=pl.DeviceIdType.MESH,
    )


class Part:
    def __init__(self, axis, kind, source, landing, send_sems, recv_sems, own_sem, blk_count):
        self.axis, self.kind, self.blk_count = axis, kind, blk_count
        self.source, self.landing = source, landing
        self.send_sems, self.recv_sems, self.own_sem = send_sems, recv_sems, own_sem
        self.me, self.count = rank_of(axis, blk_count), landing.shape[0]

    def copy(self, step):
        peer = lax.rem(self.me + step, self.count)
        return remote(
            self.source.at[peer] if self.kind == "s" else self.source,
            self.landing.at[self.me],
            self.send_sems.at[step],
            self.recv_sems.at[step],
            place_of(self.axis, self.blk_count, peer),
        )

    def own(self):
        return pltpu.make_async_copy(
            self.source.at[self.me] if self.kind == "s" else self.source,
            self.landing.at[self.me],
            self.own_sem,
        )

    def start(self):
        each(self.count, lambda step: self.copy(step).start(), 1)
        self.own().start()

    def finish(self):
        self.own().wait()
        each(self.count, lambda step: self.copy(step).wait(), 1)


def sems(count):
    return [
        pltpu.SemaphoreType.DMA((count,)),
        pltpu.SemaphoreType.DMA((count,)),
        pltpu.SemaphoreType.DMA,
    ]


def exchange_kernel(plan, blk_count, counts, *refs):
    parts = len(plan)
    entries = [
        Part(axis, kind, refs[k], refs[parts + k], *refs[2 * parts + 3 * k :][:3], blk_count)
        for k, (axis, kind) in enumerate(plan)
    ]
    greet({axis for axis, _ in plan}, blk_count, counts)
    for entry in entries:
        entry.start()
    for entry in entries:
        entry.finish()


def axis_counts():
    n_u, n_b = lax.axis_size("ulysses"), lax.axis_size("blk")
    return {"ulysses": n_u, "blk": n_b, "all": n_u * n_b}


VMEM = pl.BlockSpec(memory_space=pltpu.VMEM)


def remote_call(kernel, collective_id, shapes, scratch, arrays, name):
    return pl.pallas_call(
        kernel,
        out_shape=shapes,
        in_specs=[VMEM] * len(arrays),
        out_specs=[VMEM] * len(shapes),
        scratch_shapes=scratch,
        compiler_params=pltpu.CompilerParams(
            collective_id=collective_id,
            has_side_effects=True,
            vmem_limit_bytes=40 * 1024 * 1024,
        ),
        name=name,
    )(*arrays)


class Exchanger:
    def __init__(self):
        self.used = 0

    def next_id(self):
        self.used += 1
        return self.used - 1

    def many(self, plan, *arrays, collective_id=None):
        counts = axis_counts()
        shapes = [
            jax.ShapeDtypeStruct(
                array.shape if kind == "s" else (counts[axis],) + array.shape, array.dtype
            )
            for (axis, kind), array in zip(plan, arrays)
        ]
        scratch = []
        for axis, _ in plan:
            scratch += sems(counts[axis])
        if collective_id is None:
            collective_id = self.next_id()
        return remote_call(
            functools.partial(exchange_kernel, plan, counts["blk"], counts),
            collective_id,
            shapes,
            scratch,
            arrays,
            "exchange_" + str(collective_id),
        )

    def __call__(self, axis, kinds, *arrays):
        return self.many(tuple((axis, kind) for kind in kinds), *arrays)


def start_kernel(
    blk_count,
    counts,
    rows_in,
    kv_in,
    q_in,
    ff_in,
    rows_out,
    kv_out,
    q_out,
    ff_out,
    q_split,
    z_send,
    z_recv,
    own_sem,
    xy_send,
    xy_recv,
    core_send,
    core_recv,
    *part_sems,
):
    u, b = lax.axis_index("ulysses"), lax.axis_index("blk")
    n_u, n_z = kv_out.shape[0], kv_out.shape[1]
    z, c = b // 2, lax.rem(b, 2)
    greet({"ulysses", "blk"}, blk_count, counts)
    rows = Part("ulysses", "s", rows_in, rows_out, *part_sems[0:3], blk_count)
    first_q = Part("blk", "s", q_in, q_split, *part_sems[3:6], blk_count)
    then_q = Part("ulysses", "g", q_split, q_out, *part_sems[6:9], blk_count)
    split_ff = Part("blk", "s", ff_in, ff_out, *part_sems[9:12], blk_count)

    def along_z(step):
        mine = kv_out.at[u, z, c]
        return remote(
            kv_in,
            mine,
            z_send.at[step],
            z_recv.at[step],
            {"blk": lax.rem(z + step, n_z) * 2 + c},
        )

    def own_copy():
        return pltpu.make_async_copy(kv_in, kv_out.at[u, z, c], own_sem)

    def block(hop, step):
        return kv_out.at[lax.rem(u - hop + n_u, n_u), lax.rem(z - step + n_z, n_z), c]

    def across(hop, step):
        place = block(0, step)
        return remote(
            place,
            place,
            xy_send.at[hop, step],
            xy_recv.at[hop, step],
            {"ulysses": lax.rem(u + hop, n_u)},
        )

    def to_core(hop, step):
        place = block(hop, step)
        return remote(
            place,
            place,
            core_send.at[hop, step],
            core_recv.at[hop, step],
            {"blk": z * 2 + 1 - c},
        )

    own_copy().start()
    each(n_z, lambda step: along_z(step).start(), 1)
    first_q.start()
    rows.start()
    own_copy().wait()
    each(n_u, lambda hop: across(hop, 0).start(), 1)
    to_core(0, 0).start()
    split_ff.start()

    def pass_on(step):
        along_z(step).wait_recv()
        each(n_u, lambda hop: across(hop, step).start(), 1)
        to_core(0, step).start()

    each(n_z, pass_on, 1)
    first_q.finish()
    then_q.start()

    def share(step):
        def one(hop):
            across(hop, step).wait_recv()
            to_core(hop, step).start()

        each(n_u, one, 1)

    each(n_z, share)
    rows.finish()
    split_ff.finish()
    then_q.finish()
    each(n_z, lambda step: along_z(step).wait_send(), 1)
    each(n_z, lambda step: each(n_u, lambda hop: across(hop, step).wait_send(), 1))
    each(n_z, lambda step: each(n_u, lambda hop: to_core(hop, step).wait()))


def start_call(exchange, rows, kv_low, q_cols, ff_cols):
    counts = axis_counts()
    n_u, n_b = counts["ulysses"], counts["blk"]
    n_z = n_b // 2
    dma = pltpu.SemaphoreType.DMA
    return remote_call(
        functools.partial(start_kernel, n_b, counts),
        exchange.next_id(),
        [
            jax.ShapeDtypeStruct(rows.shape, bf16),
            jax.ShapeDtypeStruct((n_u, n_z, 2) + kv_low.shape, bf16),
            jax.ShapeDtypeStruct((n_u,) + q_cols.shape, bf16),
            jax.ShapeDtypeStruct(ff_cols.shape, bf16),
        ],
        [
            pltpu.VMEM(q_cols.shape, bf16),
            dma((n_z,)),
            dma((n_z,)),
            dma,
            dma((n_u, n_z)),
            dma((n_u, n_z)),
            dma((n_u, n_z)),
            dma((n_u, n_z)),
        ]
        + sems(n_u)
        + sems(n_b)
        + sems(n_u)
        + sems(n_b),
        (rows, kv_low, q_cols, ff_cols),
        "start",
    )


def settle_kernel(
    blk_count,
    counts,
    kv_in,
    rows_in,
    q_in,
    gains_in,
    kv_out,
    rows_out,
    q_out,
    gains_out,
    kv_core,
    kv_pair,
    kv_cross,
    kv_plane,
    kv_line,
    q_got,
    q_sum,
    core_send,
    core_recv,
    xy_send,
    xy_recv,
    z_send,
    z_recv,
    *part_sems,
):
    u, b = lax.axis_index("ulysses"), lax.axis_index("blk")
    n_u, n_z = kv_in.shape[0], kv_in.shape[1]
    z, c = b // 2, lax.rem(b, 2)
    greet({"all"}, blk_count, counts)
    rows = Part("ulysses", "s", rows_in, rows_out, *part_sems[0:3], blk_count)
    first_q = Part("ulysses", "s", q_in, q_got, *part_sems[3:6], blk_count)
    then_q = Part("blk", "s", q_sum, q_out, *part_sems[6:9], blk_count)
    gains = Part("all", "s", gains_in, gains_out, *part_sems[9:12], blk_count)

    def place(hop, step):
        return (lax.rem(u + hop, n_u), lax.rem(z + step, n_z))

    def to_core(hop, step):
        row, line = place(hop, step)
        return remote(
            kv_in.at[row, line, 1 - c],
            kv_core.at[hop, step],
            core_send.at[hop, step],
            core_recv.at[hop, step],
            {"blk": z * 2 + 1 - c},
        )

    def across(hop, step):
        return remote(
            kv_pair.at[hop, step],
            kv_cross.at[hop, step],
            xy_send.at[hop, step],
            xy_recv.at[hop, step],
            {"ulysses": lax.rem(u + hop, n_u)},
        )

    def along_z(step):
        return remote(
            kv_plane.at[step],
            kv_line.at[step],
            z_send.at[step],
            z_recv.at[step],
            {"blk": lax.rem(z + step, n_z) * 2 + c},
        )

    each(n_z, lambda step: each(n_u, lambda hop: to_core(hop, step).start()))
    first_q.start()

    def add_pair(step):
        def one(hop):
            row, line = place(hop, step)
            to_core(hop, step).wait_recv()
            kv_pair[hop, step] = (
                kv_in[row, line, c].astype(f32) + kv_core[hop, step].astype(f32)
            ).astype(bf16)

        def forward(hop):
            one(hop)
            across(hop, step).start()

        one(0)
        each(n_u, forward, 1)

    each(n_z, add_pair, 1)
    add_pair(0)
    rows.start()
    gains.start()
    first_q.finish()
    q_sum[...] = jnp.sum(q_got[...].astype(f32), axis=0).astype(bf16)
    then_q.start()

    def plane_sum(step):
        total = kv_pair[0, step].astype(f32)
        for hop in range(1, n_u):
            across(hop, step).wait_recv()
            total = total + kv_cross[hop, step].astype(f32)
        return total

    def add_plane(step):
        kv_plane[step] = plane_sum(step).astype(bf16)
        along_z(step).start()

    each(n_z, add_plane, 1)
    total = plane_sum(0)
    for step in range(1, n_z):
        along_z(step).wait_recv()
        total = total + kv_line[step].astype(f32)
    kv_out[...] = total
    then_q.finish()
    gains.finish()
    rows.finish()
    each(n_z, lambda step: each(n_u, lambda hop: to_core(hop, step).wait_send()))
    each(n_z, lambda step: each(n_u, lambda hop: across(hop, step).wait_send(), 1))
    each(n_z, lambda step: along_z(step).wait_send(), 1)


def settle_call(exchange, kv_grad, rows, q_grad, gains):
    counts = axis_counts()
    n_u, n_b = counts["ulysses"], counts["blk"]
    n_z = n_b // 2
    block = kv_grad.shape[3:]
    dma = pltpu.SemaphoreType.DMA
    return remote_call(
        functools.partial(settle_kernel, n_b, counts),
        exchange.next_id(),
        [
            jax.ShapeDtypeStruct(block, f32),
            jax.ShapeDtypeStruct(rows.shape, bf16),
            jax.ShapeDtypeStruct(q_grad.shape[1:], bf16),
            jax.ShapeDtypeStruct(gains.shape, f32),
        ],
        [
            pltpu.VMEM((n_u, n_z) + block, bf16),
            pltpu.VMEM((n_u, n_z) + block, bf16),
            pltpu.VMEM((n_u, n_z) + block, bf16),
            pltpu.VMEM((n_z,) + block, bf16),
            pltpu.VMEM((n_z,) + block, bf16),
            pltpu.VMEM(q_grad.shape, bf16),
            pltpu.VMEM(q_grad.shape[1:], bf16),
            dma((n_u, n_z)),
            dma((n_u, n_z)),
            dma((n_u, n_z)),
            dma((n_u, n_z)),
            dma((n_z,)),
            dma((n_z,)),
        ]
        + sems(n_u)
        + sems(n_u)
        + sems(n_b)
        + sems(n_u * n_b),
        (kv_grad, rows, q_grad, gains),
        "settle",
    )


def lookup_kernel(slots, fills_ref, ids_ref, table_ref, rows_ref, wide, sem):
    wide[...] = jnp.zeros_like(wide)

    def row_copy(place, row):
        return pltpu.make_async_copy(
            table_ref.at[pl.ds(row, 1), :], wide.at[pl.ds(place, 1), :], sem
        )

    def of_peer(peer, total):
        fill = fills_ref[peer]

        def fetch(k, carry):
            place = peer * slots + k
            row_copy(place, ids_ref[place]).start()
            return carry

        lax.fori_loop(0, fill, fetch, 0)
        return total + fill

    total = lax.fori_loop(0, fills_ref.shape[0], of_peer, 0)

    def drain(k, carry):
        row_copy(0, 0).wait()
        return carry

    lax.fori_loop(0, total, drain, 0)
    rows_ref[...] = wide[...].astype(rows_ref.dtype)


def lookup(fills, ids, table, slots):
    places = ids.shape[0]
    return pl.pallas_call(
        functools.partial(lookup_kernel, slots),
        out_shape=jax.ShapeDtypeStruct((places, table.shape[1]), bf16),
        in_specs=[
            pl.BlockSpec(memory_space=pltpu.SMEM),
            pl.BlockSpec(memory_space=pltpu.SMEM),
            pl.BlockSpec(memory_space=pl.ANY),
        ],
        out_specs=VMEM,
        scratch_shapes=[
            pltpu.VMEM((places, table.shape[1]), f32),
            pltpu.SemaphoreType.DMA,
        ],
        compiler_params=pltpu.CompilerParams(vmem_limit_bytes=40 * 1024 * 1024),
        name="lookup",
    )(fills, ids, table)


TABLE_TILE = 256


def table_grad_kernel(
    limit, logits, finals, norms, weights, targets, rows, row_ids, grad_out, squares
):
    tile = grad_out.shape[0]
    start = pl.program_id(0) * tile
    ids = start + lax.broadcasted_iota(jnp.int32, (tile, 1), 0)
    grad_logits = (
        weights[...]
        * (jnp.exp(logits[...] - norms[...]) - jnp.where(targets[...] == ids, 1.0, 0.0))
    ).astype(bf16)
    hot = jnp.where(row_ids[...] == ids, 1.0, 0.0).astype(bf16)
    grad = mm(grad_logits, finals[...]) + mm(hot, rows[...])
    grad_out[...] = grad.astype(bf16)

    @pl.when(pl.program_id(0) == 0)
    def _():
        squares[...] = jnp.zeros_like(squares)

    squares[...] += jnp.sum(jnp.where(ids < limit, grad * grad, 0.0), axis=0, keepdims=True)


def table_grad_call(logits, finals, norms, weights, targets, rows, row_ids):
    share, picks = logits.shape
    places, width = rows.shape
    whole = lambda *shape: pl.BlockSpec(shape, lambda i: (0, 0))
    return pl.pallas_call(
        functools.partial(table_grad_kernel, share),
        grid=(pl.cdiv(share, TABLE_TILE),),
        out_shape=[
            jax.ShapeDtypeStruct((share, width), bf16),
            jax.ShapeDtypeStruct((1, width), f32),
        ],
        in_specs=[
            pl.BlockSpec((TABLE_TILE, picks), lambda i: (i, 0)),
            whole(picks, width),
            whole(1, picks),
            whole(1, picks),
            whole(1, picks),
            whole(places, width),
            whole(1, places),
        ],
        out_specs=[
            pl.BlockSpec((TABLE_TILE, width), lambda i: (i, 0)),
            whole(1, width),
        ],
        compiler_params=pltpu.CompilerParams(vmem_limit_bytes=40 * 1024 * 1024),
        cost_estimate=pl.CostEstimate(
            flops=2 * share * width * (picks + places),
            bytes_accessed=share * (4 * picks + 2 * width),
            transcendentals=share * picks,
        ),
        name="table_grad",
    )(logits, finals, norms, weights, targets, rows, row_ids)


def adam_kernel(rate, decay, numbers, weight, first, second, grad, change, new_first, new_second):
    gradient = grad[...].astype(f32) * numbers[0]
    mean = beta_first * first[...] + (1.0 - beta_first) * gradient
    square = beta_second * second[...] + (1.0 - beta_second) * gradient * gradient
    new_first[...] = mean
    new_second[...] = square
    change[...] = -rate * (
        mean * numbers[1] / (jnp.sqrt(square * numbers[2]) + adam_eps) + decay * weight[...]
    )


def adam_call(numbers, weight, first, second, grad, rate, decay):
    share, width = weight.shape
    block = pl.BlockSpec((TABLE_TILE, width), lambda i: (i, 0))
    return pl.pallas_call(
        functools.partial(adam_kernel, rate, decay),
        grid=(pl.cdiv(share, TABLE_TILE),),
        out_shape=[jax.ShapeDtypeStruct((share, width), f32)] * 3,
        in_specs=[pl.BlockSpec(memory_space=pltpu.SMEM)] + [block] * 4,
        out_specs=[block] * 3,
        compiler_params=pltpu.CompilerParams(vmem_limit_bytes=48 * 1024 * 1024),
        name="adam",
    )(numbers, weight, first, second, grad)


def local(
    tokens,
    lengths,
    picked,
    targets,
    advantages,
    step_count,
    embedding,
    first_embedding,
    second_embedding,
    inflow,
    inflow_first_moment,
    inflow_second_moment,
    outflow,
    first_outflow,
    second_outflow,
    expand,
    first_expand,
    second_expand,
    contract,
    first_contract,
    second_contract,
    scales,
    first_scales,
    second_scales,
):
    exchange = Exchanger()
    n_u, n_b = lax.axis_size("ulysses"), lax.axis_size("blk")
    n_all = n_u * n_b
    n_z = n_b // 2
    u, b = lax.axis_index("ulysses"), lax.axis_index("blk")
    me = u * n_b + b
    slot_count, block_len = tokens.shape
    assert slot_count == n_u and n_b % 2 == 0
    picks = picked.shape[1]
    slot_picks = picks * n_b
    all_picks = slot_picks * n_u
    row_share = embedding.shape[0]
    group = QUERY_HEADS // KEY_VALUE_HEADS
    score_scale = HEAD_WIDTH ** (-0.5)
    in_rows, out_share, ff_share = inflow.shape[0], outflow.shape[0], contract.shape[0]
    q_share = QUERY_WIDTH // n_b
    heads_share = q_share // HEAD_WIDTH
    ff_mine = n_u * ff_share
    out_cut = QUERY_WIDTH // n_all
    scale_share = scales.shape[0]

    packed = jnp.concatenate(
        [tokens.astype(f32), targets.astype(f32), picked.astype(f32), advantages], axis=1
    )
    packed_all, gains_all = exchange.many(
        (("blk", "g"), ("all", "g")),
        packed,
        jnp.pad(scales, (0, 128 - scale_share)).reshape(1, 128),
    )
    gains_wide = gains_all[:, 0, :scale_share].reshape(-1).astype(bf16).astype(f32)
    gain_attn = gains_wide[:MODEL_WIDTH]
    gain_mlp = gains_wide[MODEL_WIDTH : 2 * MODEL_WIDTH]
    gain_final = gains_wide[2 * MODEL_WIDTH : 3 * MODEL_WIDTH]
    gain_query = gains_wide[3 * MODEL_WIDTH : 3 * MODEL_WIDTH + HEAD_WIDTH]
    gain_key = gains_wide[3 * MODEL_WIDTH + HEAD_WIDTH :]

    wants_block = block_len + picks
    wants_count = n_b * wants_block
    wants = (
        packed_all[:, :, :wants_block]
        .astype(jnp.int32)
        .transpose(1, 0, 2)
        .reshape(n_u, wants_count)
    )
    picked_all = packed_all[:, :, wants_block : wants_block + picks].astype(jnp.int32)
    targets_all = packed_all[:, :, block_len:wants_block].astype(jnp.int32)
    advantages_all = packed_all[:, :, wants_block + picks :]
    weights_all = jnp.where(picked_all < lengths[None, :, None], advantages_all, 0.0)
    my_length = lax.dynamic_index_in_dim(lengths, u, 0, keepdims=False)
    slot_picked = lax.dynamic_index_in_dim(picked_all, u, 1, keepdims=False).reshape(-1)
    my_picked = lax.dynamic_index_in_dim(picked, u, 0, keepdims=False)
    my_valid = my_picked < my_length
    my_weight = jnp.where(
        my_valid, lax.dynamic_index_in_dim(advantages, u, 0, keepdims=False), 0.0
    )

    fill_mean = wants_count / n_all
    slots = -(-int(fill_mean + 5.2 * math.sqrt(fill_mean)) // 16) * 16
    places = n_u * slots
    owners = wants // row_share
    counts = jnp.sum(
        (owners[:, None, :] == jnp.arange(n_all, dtype=jnp.int32)[None, :, None]).astype(f32),
        axis=-1,
    )
    rounds = (jnp.max(counts).astype(jnp.int32) + slots - 1) // slots
    own_owners = lax.dynamic_index_in_dim(owners, u, 0, keepdims=True)
    sent_mask = owners == me
    got_mask = own_owners == jnp.arange(n_u, dtype=jnp.int32)[:, None] * n_b + b
    masks = jnp.concatenate([sent_mask, got_mask], axis=0)
    totals_sent = jnp.sum(sent_mask.astype(f32), axis=1).astype(jnp.int32)
    lanes = math.gcd(wants_count, 128)
    blocks = masks.astype(bf16).reshape(2 * n_u, wants_count // lanes, lanes)
    before = (jnp.arange(lanes)[:, None] < jnp.arange(lanes)[None, :]).astype(bf16)
    block_sums = jnp.sum(blocks.astype(f32), axis=-1)
    chunk = jnp.arange(wants_count // lanes)
    block_base = mm(block_sums.astype(bf16), (chunk[:, None] < chunk[None, :]).astype(bf16))
    ranks = (
        mm(blocks.reshape(-1, lanes), before).reshape(blocks.shape) + block_base[:, :, None]
    ).reshape(2 * n_u, wants_count)
    ranks = jnp.where(masks, ranks.astype(jnp.int32), -1)
    labels = jnp.concatenate(
        [
            wants - me * row_share,
            jnp.broadcast_to(
                jnp.arange(wants_count, dtype=jnp.int32)[None, :], (n_u, wants_count)
            ),
        ],
        axis=0,
    )

    def slot_tables(turn):
        slot_rank = turn * slots + jnp.arange(slots, dtype=jnp.int32)
        hit = ranks[:, None, :] == slot_rank[None, :, None]
        found = jnp.sum(jnp.where(hit, labels[:, None, :] + 1, 0), axis=-1) - 1
        fills = jnp.clip(totals_sent - turn * slots, 0, slots)
        row_ids = found[:n_u].reshape(-1)
        entry = found[n_u:].reshape(-1)
        block, inside = entry // wants_block, entry % wants_block
        is_token = (entry >= 0) & (inside < block_len)
        key_pos = jnp.where(is_token, block * block_len + inside, 1 << 30)
        target_of = jnp.where(
            (entry >= 0) & (inside >= block_len), block * picks + inside - block_len, -1
        )
        pick_hot = (slot_picked[:, None] == key_pos[None, :]).astype(bf16)
        target_hot = (jnp.arange(slot_picks)[:, None] == target_of[None, :]).astype(bf16)
        return (row_ids, fills, key_pos, pick_hot, target_hot)

    def fetch(fills, row_ids):
        rows = lookup(fills, jnp.maximum(row_ids, 0), embedding, slots)
        return rows.reshape(n_u, slots, MODEL_WIDTH)

    tables = slot_tables(jnp.int32(0))
    row_ids, fills, key_pos, pick_hot, target_hot = tables

    inflow_low = inflow.astype(bf16)
    q_cols = inflow_low[:, :QUERY_WIDTH].reshape(in_rows, n_b, q_share).transpose(1, 0, 2)
    ff_cols = (
        expand.astype(bf16)
        .reshape(in_rows, 2, n_u, n_b, ff_share)
        .transpose(3, 0, 1, 2, 4)
        .reshape(n_b, in_rows, 2 * ff_mine)
    )
    arrived, kv_weight, q_weight, ff_split = start_call(
        exchange, fetch(fills, row_ids), inflow_low[:, QUERY_WIDTH:], q_cols, ff_cols
    )
    arrived = arrived.reshape(places, MODEL_WIDTH)
    kv_weight = kv_weight.reshape(MODEL_WIDTH, -1)
    q_weight = q_weight.reshape(MODEL_WIDTH, q_share)
    in_block = n_b * in_rows
    wide_rows = in_block * 2 * ff_mine // MODEL_WIDTH
    layer_rows = jnp.concatenate(
        [
            ff_split.reshape(wide_rows, MODEL_WIDTH),
            outflow.astype(bf16),
            contract.astype(bf16),
        ],
        axis=0,
    )
    layer_all = lax.all_to_all(
        jnp.broadcast_to(layer_rows[None], (n_u,) + layer_rows.shape), "ulysses", 0, 0, tiled=True
    )
    ff_weight = layer_all[:, :wide_rows].reshape(MODEL_WIDTH, 2 * ff_mine)
    out_weight = layer_all[:, wide_rows : wide_rows + out_share].reshape(
        n_u * out_share, MODEL_WIDTH
    )
    contract_weight = layer_all[:, wide_rows + out_share :].reshape(ff_mine, MODEL_WIDTH)

    def picked_rows(pick_hot, target_hot, arrived):
        return jnp.concatenate([mm(pick_hot, arrived), mm(target_hot, arrived)], axis=1)

    refetch_id = [exchange.next_id() for _ in range(5)]

    def refetch(turn, which):
        tables = slot_tables(turn)
        (got,) = exchange.many(
            (("ulysses", "s"),), fetch(tables[1], tables[0]), collective_id=refetch_id[which]
        )
        return (tables, got.reshape(places, MODEL_WIDTH))

    def more(state):
        return state[0] < rounds

    def picks_turn(state):
        tables, got = refetch(state[0], 0)
        return (state[0] + 1, state[1] + picked_rows(tables[3], tables[4], got))

    pick_part = picked_rows(pick_hot, target_hot, arrived)
    _, pick_part = lax.while_loop(more, picks_turn, (jnp.int32(1), pick_part))
    (got_picks,) = exchange(
        "blk", "s", pick_part.astype(bf16).reshape(n_b, picks, 2 * MODEL_WIDTH)
    )
    got_picks = jnp.sum(got_picks.astype(f32), axis=0)
    embedded_picks, target_rows = got_picks[:, :MODEL_WIDTH], got_picks[:, MODEL_WIDTH:]

    def to_slot(rows):
        (got,) = exchange("blk", "g", rows)
        return got.reshape(slot_picks, rows.shape[1])

    def sum_to_picks(partial):
        (got,) = exchange("blk", "s", partial.astype(bf16).reshape(n_b, picks, MODEL_WIDTH))
        return jnp.sum(got.astype(f32), axis=0)

    normed_slot = to_slot(
        (embedded_picks * inverse_root(embedded_picks) * gain_attn).astype(bf16)
    )

    def keys_of(arrived, key_pos):
        embedded = arrived.astype(f32)
        normed = (embedded * inverse_root(embedded) * gain_attn).astype(bf16)
        mixed = mm(normed, kv_weight)
        half = KEY_VALUE_HEADS * HEAD_WIDTH
        key_raw = mixed[:, :half].reshape(places, KEY_VALUE_HEADS, HEAD_WIDTH)
        values = mixed[:, half:].reshape(places, KEY_VALUE_HEADS, HEAD_WIDTH)
        angle_tables = rope_angles(jnp.where(key_pos < (1 << 30), key_pos, 0))
        key_rot = rotate(key_raw * inverse_root(key_raw) * gain_key, angle_tables, 1.0)
        return (
            embedded,
            normed,
            key_raw,
            angle_tables,
            key_rot.astype(bf16).transpose(1, 0, 2),
            values.astype(bf16).transpose(1, 0, 2),
        )

    query_pos = jnp.tile(slot_picked, group)

    def allowed_of(key_pos):
        return ((key_pos[None, :] <= query_pos[:, None]) & (key_pos[None, :] < my_length))[None]

    def scores_of(query_groups, key_rot, allowed):
        scores = (
            jnp.einsum("kqd,kjd->kqj", query_groups, key_rot, preferred_element_type=f32)
            * score_scale
        )
        return jnp.where(allowed, scores, masked_score)

    def attend(scores, allowed, values):
        part_max = jnp.max(scores, axis=-1, keepdims=True)
        weights = jnp.where(allowed, jnp.exp(scores - part_max), 0.0)
        out = jnp.einsum("kqj,kjd->kqd", weights.astype(bf16), values, preferred_element_type=f32)
        return (part_max, jnp.sum(weights, axis=-1, keepdims=True), out)

    keys = keys_of(arrived, key_pos)

    query_raw = mm(normed_slot, q_weight).reshape(slot_picks, heads_share, HEAD_WIDTH)
    query_tables = rope_angles(slot_picked)
    query_mine = rotate(query_raw * inverse_root(query_raw) * gain_query, query_tables, 1.0)
    (query_all,) = exchange("blk", "g", query_mine.astype(bf16).reshape(slot_picks, q_share))
    query_groups = (
        query_all.reshape(n_b, slot_picks, heads_share, HEAD_WIDTH)
        .transpose(0, 2, 1, 3)
        .reshape(KEY_VALUE_HEADS, group * slot_picks, HEAD_WIDTH)
    )
    allowed = allowed_of(key_pos)
    scores = scores_of(query_groups, keys[4], allowed)

    def attend_turn(state):
        turn, top, total, out = state
        tables, got = refetch(turn, 1)
        keys_now = keys_of(got, tables[2])
        allowed_now = allowed_of(tables[2])
        new = attend(scores_of(query_groups, keys_now[4], allowed_now), allowed_now, keys_now[5])
        both = jnp.maximum(top, new[0])
        old_factor, new_factor = jnp.exp(top - both), jnp.exp(new[0] - both)
        return (
            turn + 1,
            both,
            total * old_factor + new[1] * new_factor,
            out * old_factor + new[2] * new_factor,
        )

    _, part_max, part_sum, part_out = lax.while_loop(
        more, attend_turn, (jnp.int32(1),) + attend(scores, allowed, keys[5])
    )
    part_send = (
        part_out.astype(bf16)
        .reshape(QUERY_HEADS, slot_picks, HEAD_WIDTH)
        .transpose(1, 0, 2)
        .reshape(slot_picks, n_u, n_b, out_cut)
        .transpose(2, 0, 1, 3)
        .reshape(n_b, slot_picks, n_u * out_cut)
    )
    stats = jnp.stack([part_max[..., 0], part_sum[..., 0]]).reshape(2 * QUERY_HEADS, slot_picks)
    part_got, stats_all = exchange("blk", "sg", part_send, stats)
    stats_all = stats_all.reshape(n_b, 2, QUERY_HEADS, slot_picks)
    full_max = jnp.max(stats_all[:, 0], axis=0)
    shrink = jnp.exp(stats_all[:, 0] - full_max[None])
    full_sum = jnp.sum(stats_all[:, 1] * shrink, axis=0)
    log_total = full_max + jnp.log(full_sum)
    share_of = shrink / full_sum[None]
    heads_row = QUERY_HEADS // n_u
    cut_head = (b * out_cut) // HEAD_WIDTH
    my_share = lax.dynamic_index_in_dim(
        share_of.reshape(n_b, n_u, heads_row, slot_picks), cut_head, 2, keepdims=False
    )
    attended_wide = jnp.sum(
        part_got.astype(f32).reshape(n_b, slot_picks, n_u, out_cut)
        * my_share.transpose(0, 2, 1)[..., None],
        axis=0,
    )
    attended = attended_wide.astype(bf16).reshape(slot_picks, n_u * out_cut)

    after_attn = embedded_picks + sum_to_picks(mm(attended, out_weight))
    normed_mlp = to_slot((after_attn * inverse_root(after_attn) * gain_mlp).astype(bf16))
    gate_up = mm(normed_mlp, ff_weight)
    gate_part, up_part = gate_up[:, :ff_mine], gate_up[:, ff_mine:]
    sigmoid_gate = jax.nn.sigmoid(gate_part)
    activated = (gate_part * sigmoid_gate * up_part).astype(bf16)
    after_mlp = after_attn + sum_to_picks(mm(activated, contract_weight))
    final_rows = (after_mlp * inverse_root(after_mlp) * gain_final).astype(bf16)

    (final_all,) = exchange("ulysses", "g", to_slot(final_rows))
    final_all = final_all.reshape(all_picks, MODEL_WIDTH)
    table_low = embedding.astype(bf16)
    logits = mm_back(table_low, final_all)
    local_max = jnp.max(logits, axis=0)
    head_weights = jnp.exp(logits - local_max[None, :])
    local_sum = jnp.sum(head_weights, axis=0)
    head_rows = mm_outer(head_weights.astype(bf16), table_low).astype(bf16)
    head_stats = jnp.stack([local_max, local_sum], axis=1).reshape(n_u, slot_picks, 2)

    def merge_rows(rows, stats_in):
        top = jnp.max(stats_in[..., 0], axis=0)
        factor = jnp.exp(stats_in[..., 0] - top[None])
        total = jnp.sum(stats_in[..., 1] * factor, axis=0)
        return (jnp.sum(rows.astype(f32) * factor[..., None], axis=0), top, total)

    got_rows, got_stats = exchange(
        "ulysses",
        "ss",
        head_rows.reshape(n_u, slot_picks, MODEL_WIDTH),
        jnp.pad(head_stats, ((0, 0), (0, 0), (0, 126))),
    )
    slot_rows, slot_top, slot_total = merge_rows(got_rows, got_stats)
    slot_stats = jnp.stack([slot_top, slot_total], axis=1).reshape(n_b, picks, 2)
    got_rows, got_stats = exchange(
        "blk",
        "ss",
        slot_rows.astype(bf16).reshape(n_b, picks, MODEL_WIDTH),
        jnp.pad(slot_stats, ((0, 0), (0, 0), (0, 126))),
    )
    mean_rows, top, total = merge_rows(got_rows, got_stats)
    log_norm = top + jnp.log(total)
    target_logit = jnp.sum(final_rows.astype(f32) * target_rows, axis=1)
    loss_local = -jnp.sum(my_weight * (target_logit - log_norm))
    count_local = jnp.sum(my_valid.astype(f32))
    grad_final = my_weight[:, None] * (mean_rows / total[:, None] - target_rows)

    grad_after_mlp, grad_gain_final = norm_back(after_mlp, gain_final, grad_final)
    got_branch, norms_slot = exchange(
        "blk",
        "gg",
        grad_after_mlp.astype(bf16),
        jnp.broadcast_to(log_norm[:, None], (picks, 128)),
    )
    grad_branch = got_branch.reshape(slot_picks, MODEL_WIDTH)
    grad_contract = mm_outer(activated, grad_branch)
    grad_act = mm_back(grad_branch, contract_weight)
    grad_gate = grad_act * up_part * sigmoid_gate * (1.0 + gate_part * (1.0 - sigmoid_gate))
    grad_up = grad_act * gate_part * sigmoid_gate
    grad_gate_up = jnp.concatenate([grad_gate, grad_up], axis=1).astype(bf16)
    grad_expand = mm_outer(normed_mlp, grad_gate_up)
    grad_mid_part, grad_gain_mlp = norm_back(
        after_attn, gain_mlp, sum_to_picks(mm_back(grad_gate_up, ff_weight))
    )
    grad_after_attn = grad_after_mlp + grad_mid_part
    grad_attn_branch = to_slot(grad_after_attn.astype(bf16))
    grad_outflow = mm_outer(attended, grad_attn_branch)
    grad_layer = jnp.concatenate(
        [
            grad_expand.astype(bf16).reshape(n_u, wide_rows, MODEL_WIDTH),
            grad_outflow.astype(bf16).reshape(n_u, out_share, MODEL_WIDTH),
            grad_contract.astype(bf16).reshape(n_u, ff_share, MODEL_WIDTH),
        ],
        axis=1,
    )
    got_layer = lax.all_to_all(grad_layer, "ulysses", 0, 0, tiled=True)
    grad_attended = mm_back(grad_attn_branch, out_weight).astype(bf16)
    delta_part = jnp.sum(
        attended_wide * grad_attended.astype(f32).reshape(slot_picks, n_u, out_cut), axis=-1
    )
    got_attended, got_delta = exchange("blk", "gg", grad_attended, delta_part.T)
    grad_heads = (
        got_attended.reshape(n_b, slot_picks, n_u, out_cut)
        .transpose(1, 2, 0, 3)
        .reshape(slot_picks, QUERY_HEADS, HEAD_WIDTH)
        .transpose(1, 0, 2)
        .reshape(KEY_VALUE_HEADS, group * slot_picks, HEAD_WIDTH)
    )
    row_delta = jnp.sum(
        got_delta.transpose(1, 0, 2).reshape(QUERY_HEADS, HEAD_WIDTH // out_cut, slot_picks), axis=1
    ).reshape(KEY_VALUE_HEADS, group * slot_picks, 1)
    log_groups = log_total.reshape(KEY_VALUE_HEADS, group * slot_picks, 1)

    def score_grads(scores, allowed, values):
        probs = jnp.where(allowed, jnp.exp(scores - log_groups), 0.0)
        grad_probs = jnp.einsum("kqd,kjd->kqj", grad_heads, values, preferred_element_type=f32)
        return (probs, (probs * (grad_probs - row_delta) * score_scale).astype(bf16))

    def query_grads(grad_scores, key_rot):
        return jnp.einsum("kqj,kjd->kqd", grad_scores, key_rot, preferred_element_type=f32)

    def key_grads(probs, grad_scores, keys):
        grad_key = jnp.einsum(
            "kqj,kqd->kjd", grad_scores, query_groups, preferred_element_type=f32
        )
        grad_value = jnp.einsum(
            "kqj,kqd->kjd", probs.astype(bf16), grad_heads, preferred_element_type=f32
        )
        upstream = rotate(
            grad_key.astype(bf16).astype(f32).transpose(1, 0, 2), keys[3], -1.0
        )
        grad_raw, grad_gain = norm_back(keys[2], gain_key, upstream)
        grad_kv = jnp.concatenate(
            [
                grad_raw.reshape(places, -1).astype(bf16),
                grad_value.astype(bf16).transpose(1, 0, 2).reshape(places, -1),
            ],
            axis=1,
        )
        return (grad_kv, grad_gain)

    def row_grads(grad_kv, keys):
        return norm_back(keys[0], gain_attn, mm_back(grad_kv, kv_weight))

    def redo(turn, which):
        tables, got = refetch(turn, which)
        keys_now = keys_of(got, tables[2])
        allowed_now = allowed_of(tables[2])
        scores_now = scores_of(query_groups, keys_now[4], allowed_now)
        return (tables, keys_now) + score_grads(scores_now, allowed_now, keys_now[5])

    def query_turn(state):
        _, keys_now, _, grad_scores_now = redo(state[0], 2)
        return (state[0] + 1, state[1] + query_grads(grad_scores_now, keys_now[4]))

    probs, grad_scores = score_grads(scores, allowed, keys[5])
    _, grad_query_part = lax.while_loop(
        more, query_turn, (jnp.int32(1), query_grads(grad_scores, keys[4]))
    )
    (got_query,) = exchange(
        "blk",
        "s",
        grad_query_part.astype(bf16)
        .reshape(n_b, heads_share, slot_picks, HEAD_WIDTH)
        .transpose(0, 2, 1, 3)
        .reshape(n_b, slot_picks, q_share),
    )
    grad_query_rot = jnp.sum(got_query.astype(f32), axis=0).astype(bf16).astype(f32)
    grad_query_raw, grad_gain_query = norm_back(
        query_raw,
        gain_query,
        rotate(grad_query_rot.reshape(slot_picks, heads_share, HEAD_WIDTH), query_tables, -1.0),
    )
    grad_query_low = grad_query_raw.reshape(slot_picks, q_share).astype(bf16)
    grad_q_weight = mm_outer(normed_slot, grad_query_low)
    grad_normed_picks = sum_to_picks(mm_back(grad_query_low, q_weight))
    grad_pick_part, grad_gain_picks = norm_back(embedded_picks, gain_attn, grad_normed_picks)
    pick_back = to_slot((grad_after_attn + grad_pick_part).astype(bf16))

    grad_kv, grad_gain_key = key_grads(probs, grad_scores, keys)
    grad_kv_weight = mm_outer(keys[1], grad_kv)
    grad_rows, grad_gain_attn = row_grads(grad_kv, keys)

    def weight_turn(state):
        turn, weight_sum, key_sum, attn_sum = state
        _, keys_now, probs_now, grad_scores_now = redo(turn, 3)
        grad_kv_now, gain_key_now = key_grads(probs_now, grad_scores_now, keys_now)
        _, gain_attn_now = row_grads(grad_kv_now, keys_now)
        return (
            turn + 1,
            weight_sum + mm_outer(keys_now[1], grad_kv_now),
            key_sum + gain_key_now,
            attn_sum + gain_attn_now,
        )

    _, grad_kv_weight, grad_gain_key, grad_gain_attn = lax.while_loop(
        more, weight_turn, (jnp.int32(1), grad_kv_weight, grad_gain_key, grad_gain_attn)
    )
    grad_scales = jnp.concatenate(
        [
            grad_gain_attn + grad_gain_picks,
            grad_gain_mlp,
            grad_gain_final,
            grad_gain_query,
            grad_gain_key,
        ]
    )

    sum_layer = jnp.sum(got_layer.astype(f32), axis=0)
    sum_outflow = sum_layer[wide_rows : wide_rows + out_share]
    sum_contract = sum_layer[wide_rows + out_share :]
    got_ff = lax.all_to_all(
        sum_layer[:wide_rows].astype(bf16).reshape(n_b, in_rows, 2 * ff_mine),
        "blk",
        0,
        0,
        tiled=True,
    )
    sum_expand = (
        got_ff.astype(f32)
        .reshape(n_b, in_rows, 2, n_u, ff_share)
        .transpose(1, 2, 3, 0, 4)
        .reshape(in_rows, 2 * FF)
    )
    rows_low = (grad_rows + mm_outer(pick_hot, pick_back)).astype(bf16)
    sum_kv, rows_back, got_q, got_scales = settle_call(
        exchange,
        grad_kv_weight.astype(bf16).reshape(n_u, n_z, 2, in_rows, -1),
        rows_low.reshape(n_u, slots, MODEL_WIDTH),
        grad_q_weight.astype(bf16).reshape(n_u, n_b, in_rows, q_share),
        jnp.pad(
            grad_scales.reshape(n_all, scale_share), ((0, 0), (0, 128 - scale_share))
        ).reshape(n_all, 1, 128),
    )
    sum_q = got_q.astype(f32).transpose(1, 0, 2).reshape(in_rows, QUERY_WIDTH)
    sum_inflow = jnp.concatenate([sum_q, sum_kv], axis=1)
    sum_scales = jnp.sum(got_scales, axis=0)[0, :scale_share]

    def flat(array):
        return array.transpose(1, 0, 2).reshape(1, -1)

    (norms_all,) = exchange("ulysses", "g", norms_slot[:, :, 0].reshape(n_b, picks))
    table_grad, table_squares = table_grad_call(
        logits,
        final_all,
        norms_all.reshape(1, all_picks),
        flat(weights_all),
        flat(targets_all) - me * row_share,
        rows_back.reshape(places, MODEL_WIDTH),
        row_ids.reshape(1, places),
    )
    return_id = exchange.next_id()

    def return_turn(state):
        turn, so_far, _ = state
        tables, keys_now, probs_now, grad_scores_now = redo(turn, 4)
        grad_kv_now, _ = key_grads(probs_now, grad_scores_now, keys_now)
        rows_now, _ = row_grads(grad_kv_now, keys_now)
        rows_now = (rows_now + mm_outer(tables[3], pick_back)).astype(bf16)
        (back,) = exchange.many(
            (("ulysses", "s"),),
            rows_now.reshape(n_u, slots, MODEL_WIDTH),
            collective_id=return_id,
        )
        hot = (
            jnp.arange(row_share, dtype=jnp.int32)[:, None] == tables[0][None, :]
        ).astype(bf16)
        grown = so_far.astype(f32) + mm(hot, back.reshape(places, MODEL_WIDTH))
        return (turn + 1, grown.astype(bf16), jnp.sum(grown * grown, axis=0, keepdims=True))

    _, table_grad, table_squares = lax.while_loop(
        more, return_turn, (jnp.int32(1), table_grad, table_squares)
    )

    layer_grads = (sum_inflow, sum_outflow, sum_expand, sum_contract, sum_scales)
    squares = jnp.sum(table_squares)
    for grad_piece in layer_grads:
        squares = squares + jnp.sum(grad_piece * grad_piece)
    (totals,) = exchange(
        "all",
        "g",
        jnp.pad(jnp.stack([squares, count_local, loss_local]), (0, 125)).reshape(1, 128),
    )
    totals = jnp.sum(totals, axis=(0, 1))
    square_total, count_total, loss_total = totals[0], totals[1], totals[2]
    gradient_norm = jnp.sqrt(square_total) / count_total
    factor = jnp.minimum(1.0, clip_limit / gradient_norm) / count_total
    step_float = step_count[0].astype(f32)
    outputs = [loss_total / count_total, gradient_norm]
    outputs += adam_call(
        jnp.stack(
            [factor, 1.0 / (1.0 - beta_first**step_float), 1.0 / (1.0 - beta_second**step_float)]
        ),
        embedding,
        first_embedding,
        second_embedding,
        table_grad,
        learning_rates[0],
        weight_decays[0],
    )
    weights_now = (inflow, outflow, expand, contract, scales)
    firsts = (inflow_first_moment, first_outflow, first_expand, first_contract, first_scales)
    seconds = (inflow_second_moment, second_outflow, second_expand, second_contract, second_scales)
    for position in range(5):
        outputs += adam_update(
            weights_now[position],
            firsts[position],
            seconds[position],
            layer_grads[position] * factor,
            learning_rates[position + 1],
            weight_decays[position + 1],
            step_float,
        )
    return tuple(outputs)


def solution(mesh):
    rows = P(("ulysses", "blk"), None)
    flat_rows = P(("ulysses", "blk"))
    column = P(None, "blk")
    return jax.shard_map(
        local,
        mesh=mesh,
        in_specs=(column, P(), column, column, column, P()) + (rows,) * 15 + (flat_rows,) * 3,
        out_specs=(P(), P()) + (rows,) * 15 + (flat_rows,) * 3,
        check_vma=False,
    )
```

```python
import functools
import math

import jax
import jax.numpy as jnp
from jax import lax
from jax.experimental import pallas as pl
from jax.experimental.pallas import tpu as pltpu
from jax.sharding import PartitionSpec as P

MODEL_WIDTH = 1024
QUERY_HEADS = 16
KEY_VALUE_HEADS = 8
HEAD_WIDTH = 128
FF = 3072
QUERY_WIDTH = QUERY_HEADS * HEAD_WIDTH

norm_eps = 1e-06
rope_base = 1000000.0
clip_limit = 0.01
beta_first = 0.9
beta_second = 0.95
adam_eps = 1e-08
learning_rates = (0.01, 0.003, 0.07, 0.003, 0.002, 0.01)
weight_decays = (0.1, 0.1, 0.1, 0.1, 0.1, 0.0)
masked_score = -1e30

bf16 = jnp.bfloat16
f32 = jnp.float32
BOTH = ("ulysses", "blk")


def inverse_root(values):
    return lax.rsqrt(jnp.mean(values * values, axis=-1, keepdims=True) + norm_eps)


def norm_back(inputs, gain_vec, upstream):
    root_scale = inverse_root(inputs)
    unit_rows = inputs * root_scale
    weighted = upstream * gain_vec
    grad_inputs = root_scale * (
        weighted - unit_rows * jnp.mean(weighted * unit_rows, axis=-1, keepdims=True)
    )
    grad_gain = jnp.sum((upstream * unit_rows).reshape(-1, gain_vec.shape[-1]), axis=0)
    return (grad_inputs, grad_gain)


def rope_angles(positions):
    half_width = HEAD_WIDTH // 2
    frequency = rope_base ** (
        -(jnp.arange(half_width, dtype=jnp.int32).astype(f32) * 2.0 / HEAD_WIDTH)
    )
    angles = positions.astype(f32)[:, None] * frequency[None, :]
    return (jnp.cos(angles), jnp.sin(angles))


def rotate(values, tables, sign_value):
    half_width = values.shape[-1] // 2
    front_half = values[..., :half_width]
    back_half = values[..., half_width:]
    cosine_part = tables[0][:, None, :]
    sine_part = tables[1][:, None, :] * sign_value
    return jnp.concatenate(
        [
            front_half * cosine_part - back_half * sine_part,
            back_half * cosine_part + front_half * sine_part,
        ],
        axis=-1,
    )


def mm(left, right):
    return lax.dot_general(left, right, (((1,), (0,)), ((), ())), preferred_element_type=f32)


def mm_outer(left, right):
    return lax.dot_general(left, right, (((0,), (0,)), ((), ())), preferred_element_type=f32)


def mm_back(left, right):
    return lax.dot_general(left, right, (((1,), (1,)), ((), ())), preferred_element_type=f32)


def spread_rows(onehot, rows):
    return lax.dot_general(
        onehot.astype(f32),
        rows,
        (((0,), (0,)), ((), ())),
        precision=lax.Precision.HIGHEST,
        preferred_element_type=f32,
    )


def adam_update(weight_now, first_now, second_now, gradient, rate_value, decay_value, step_float):
    new_first = beta_first * first_now + (1.0 - beta_first) * gradient
    new_second = beta_second * second_now + (1.0 - beta_second) * gradient * gradient
    first_hat = new_first / (1.0 - beta_first**step_float)
    second_hat = new_second / (1.0 - beta_second**step_float)
    change = -rate_value * (
        first_hat / (jnp.sqrt(second_hat) + adam_eps) + decay_value * weight_now
    )
    return (change, new_first, new_second)


def place_of(axis, blk_count, peer):
    if axis == "all":
        return {"ulysses": peer // blk_count, "blk": lax.rem(peer, blk_count)}
    return {axis: peer}


def rank_of(axis, blk_count):
    row, column = lax.axis_index("ulysses"), lax.axis_index("blk")
    return {"ulysses": row, "blk": column, "all": row * blk_count + column}[axis]


def greet(axes, blk_count, counts):
    barrier = pltpu.get_barrier_semaphore()
    axes = ("all",) if "all" in axes else tuple(axes)
    total = 0
    for axis in axes:
        me, count = rank_of(axis, blk_count), counts[axis]

        def call(step, carry, axis=axis, me=me, count=count):
            pl.semaphore_signal(
                barrier,
                inc=1,
                device_id=place_of(axis, blk_count, lax.rem(me + step, count)),
                device_id_type=pl.DeviceIdType.MESH,
            )
            return carry

        lax.fori_loop(1, count, call, 0)
        total += count - 1
    pl.semaphore_wait(barrier, total)


def each(count, body, first=0):
    def step(k, carry):
        body(k)
        return carry

    lax.fori_loop(first, count, step, 0)


def remote(source, target, send_sem, recv_sem, device_id):
    return pltpu.make_async_remote_copy(
        src_ref=source,
        dst_ref=target,
        send_sem=send_sem,
        recv_sem=recv_sem,
        device_id=device_id,
        device_id_type=pl.DeviceIdType.MESH,
    )


class Part:
    def __init__(self, axis, kind, source, landing, send_sems, recv_sems, own_sem, blk_count):
        self.axis, self.kind, self.blk_count = axis, kind, blk_count
        self.source, self.landing = source, landing
        self.send_sems, self.recv_sems, self.own_sem = send_sems, recv_sems, own_sem
        self.me, self.count = rank_of(axis, blk_count), landing.shape[0]

    def copy(self, step):
        peer = lax.rem(self.me + step, self.count)
        return remote(
            self.source.at[peer] if self.kind == "s" else self.source,
            self.landing.at[self.me],
            self.send_sems.at[step],
            self.recv_sems.at[step],
            place_of(self.axis, self.blk_count, peer),
        )

    def own(self):
        return pltpu.make_async_copy(
            self.source.at[self.me] if self.kind == "s" else self.source,
            self.landing.at[self.me],
            self.own_sem,
        )

    def start(self):
        each(self.count, lambda step: self.copy(step).start(), 1)
        self.own().start()

    def finish(self):
        self.own().wait()
        each(self.count, lambda step: self.copy(step).wait(), 1)


def sems(count):
    return [
        pltpu.SemaphoreType.DMA((count,)),
        pltpu.SemaphoreType.DMA((count,)),
        pltpu.SemaphoreType.DMA,
    ]


def exchange_kernel(plan, blk_count, counts, *refs):
    parts = len(plan)
    entries = [
        Part(axis, kind, refs[k], refs[parts + k], *refs[2 * parts + 3 * k :][:3], blk_count)
        for k, (axis, kind) in enumerate(plan)
    ]
    greet({axis for axis, _ in plan}, blk_count, counts)
    for entry in entries:
        entry.start()
    for entry in entries:
        entry.finish()


def axis_counts():
    n_u, n_b = lax.axis_size("ulysses"), lax.axis_size("blk")
    return {"ulysses": n_u, "blk": n_b, "all": n_u * n_b}


VMEM = pl.BlockSpec(memory_space=pltpu.VMEM)


def remote_call(kernel, collective_id, shapes, scratch, arrays, name):
    return pl.pallas_call(
        kernel,
        out_shape=shapes,
        in_specs=[VMEM] * len(arrays),
        out_specs=[VMEM] * len(shapes),
        scratch_shapes=scratch,
        compiler_params=pltpu.CompilerParams(
            collective_id=collective_id,
            has_side_effects=True,
            vmem_limit_bytes=56 * 1024 * 1024,
        ),
        name=name,
    )(*arrays)


class Exchanger:
    def __init__(self):
        self.used = 0

    def next_id(self):
        self.used += 1
        return self.used - 1

    def many(self, plan, *arrays, collective_id=None):
        counts = axis_counts()
        shapes = [
            jax.ShapeDtypeStruct(
                array.shape if kind == "s" else (counts[axis],) + array.shape, array.dtype
            )
            for (axis, kind), array in zip(plan, arrays)
        ]
        scratch = []
        for axis, _ in plan:
            scratch += sems(counts[axis])
        if collective_id is None:
            collective_id = self.next_id()
        return remote_call(
            functools.partial(exchange_kernel, plan, counts["blk"], counts),
            collective_id,
            shapes,
            scratch,
            arrays,
            "exchange_" + str(collective_id),
        )

    def __call__(self, axis, kinds, *arrays):
        return self.many(tuple((axis, kind) for kind in kinds), *arrays)


def start_kernel(
    blk_count,
    counts,
    rows_in,
    kv_in,
    q_in,
    ff_in,
    rows_out,
    kv_out,
    q_out,
    ff_out,
    q_split,
    z_send,
    z_recv,
    own_sem,
    xy_send,
    xy_recv,
    core_send,
    core_recv,
    *part_sems,
):
    u, b = lax.axis_index("ulysses"), lax.axis_index("blk")
    n_u, n_z = kv_out.shape[0], kv_out.shape[1]
    z, c = b // 2, lax.rem(b, 2)
    greet({"ulysses", "blk"}, blk_count, counts)
    rows = Part("ulysses", "s", rows_in, rows_out, *part_sems[0:3], blk_count)
    first_q = Part("blk", "s", q_in, q_split, *part_sems[3:6], blk_count)
    then_q = Part("ulysses", "g", q_split, q_out, *part_sems[6:9], blk_count)
    split_ff = Part("blk", "s", ff_in, ff_out, *part_sems[9:12], blk_count)

    def along_z(step):
        mine = kv_out.at[u, z, c]
        return remote(
            kv_in,
            mine,
            z_send.at[step],
            z_recv.at[step],
            {"blk": lax.rem(z + step, n_z) * 2 + c},
        )

    def own_copy():
        return pltpu.make_async_copy(kv_in, kv_out.at[u, z, c], own_sem)

    def block(hop, step):
        return kv_out.at[lax.rem(u - hop + n_u, n_u), lax.rem(z - step + n_z, n_z), c]

    def across(hop, step):
        place = block(0, step)
        return remote(
            place,
            place,
            xy_send.at[hop, step],
            xy_recv.at[hop, step],
            {"ulysses": lax.rem(u + hop, n_u)},
        )

    def to_core(hop, step):
        place = block(hop, step)
        return remote(
            place,
            place,
            core_send.at[hop, step],
            core_recv.at[hop, step],
            {"blk": z * 2 + 1 - c},
        )

    own_copy().start()
    each(n_z, lambda step: along_z(step).start(), 1)
    first_q.start()
    rows.start()
    own_copy().wait()
    each(n_u, lambda hop: across(hop, 0).start(), 1)
    to_core(0, 0).start()
    split_ff.start()

    def pass_on(step):
        along_z(step).wait_recv()
        each(n_u, lambda hop: across(hop, step).start(), 1)
        to_core(0, step).start()

    each(n_z, pass_on, 1)
    first_q.finish()
    then_q.start()

    def share(step):
        def one(hop):
            across(hop, step).wait_recv()
            to_core(hop, step).start()

        each(n_u, one, 1)

    each(n_z, share)
    rows.finish()
    split_ff.finish()
    then_q.finish()
    each(n_z, lambda step: along_z(step).wait_send(), 1)
    each(n_z, lambda step: each(n_u, lambda hop: across(hop, step).wait_send(), 1))
    each(n_z, lambda step: each(n_u, lambda hop: to_core(hop, step).wait()))


def start_call(exchange, rows, kv_low, q_cols, ff_cols):
    counts = axis_counts()
    n_u, n_b = counts["ulysses"], counts["blk"]
    n_z = n_b // 2
    dma = pltpu.SemaphoreType.DMA
    return remote_call(
        functools.partial(start_kernel, n_b, counts),
        exchange.next_id(),
        [
            jax.ShapeDtypeStruct(rows.shape, bf16),
            jax.ShapeDtypeStruct((n_u, n_z, 2) + kv_low.shape, bf16),
            jax.ShapeDtypeStruct((n_u,) + q_cols.shape, bf16),
            jax.ShapeDtypeStruct(ff_cols.shape, bf16),
        ],
        [
            pltpu.VMEM(q_cols.shape, bf16),
            dma((n_z,)),
            dma((n_z,)),
            dma,
            dma((n_u, n_z)),
            dma((n_u, n_z)),
            dma((n_u, n_z)),
            dma((n_u, n_z)),
        ]
        + sems(n_u)
        + sems(n_b)
        + sems(n_u)
        + sems(n_b),
        (rows, kv_low, q_cols, ff_cols),
        "start",
    )


def settle_kernel(
    blk_count,
    counts,
    kv_in,
    rows_in,
    q_in,
    ff_in,
    gains_in,
    kv_out,
    rows_out,
    q_out,
    ff_out,
    gains_out,
    kv_core,
    kv_pair,
    kv_cross,
    kv_plane,
    kv_line,
    q_got,
    q_sum,
    core_send,
    core_recv,
    xy_send,
    xy_recv,
    z_send,
    z_recv,
    *part_sems,
):
    u, b = lax.axis_index("ulysses"), lax.axis_index("blk")
    n_u, n_z = kv_in.shape[0], kv_in.shape[1]
    z, c = b // 2, lax.rem(b, 2)
    greet({"all"}, blk_count, counts)
    rows = Part("ulysses", "s", rows_in, rows_out, *part_sems[0:3], blk_count)
    first_q = Part("ulysses", "s", q_in, q_got, *part_sems[3:6], blk_count)
    then_q = Part("blk", "s", q_sum, q_out, *part_sems[6:9], blk_count)
    gains = Part("all", "s", gains_in, gains_out, *part_sems[9:12], blk_count)
    split_ff = Part("blk", "s", ff_in, ff_out, *part_sems[12:15], blk_count)

    def place(hop, step):
        return (lax.rem(u + hop, n_u), lax.rem(z + step, n_z))

    def to_core(hop, step):
        row, line = place(hop, step)
        return remote(
            kv_in.at[row, line, 1 - c],
            kv_core.at[hop, step],
            core_send.at[hop, step],
            core_recv.at[hop, step],
            {"blk": z * 2 + 1 - c},
        )

    def across(hop, step):
        return remote(
            kv_pair.at[hop, step],
            kv_cross.at[hop, step],
            xy_send.at[hop, step],
            xy_recv.at[hop, step],
            {"ulysses": lax.rem(u + hop, n_u)},
        )

    def along_z(step):
        return remote(
            kv_plane.at[step],
            kv_line.at[step],
            z_send.at[step],
            z_recv.at[step],
            {"blk": lax.rem(z + step, n_z) * 2 + c},
        )

    each(n_z, lambda step: each(n_u, lambda hop: to_core(hop, step).start()))
    first_q.start()
    split_ff.start()

    def add_pair(step):
        def one(hop):
            row, line = place(hop, step)
            to_core(hop, step).wait_recv()
            kv_pair[hop, step] = (
                kv_in[row, line, c].astype(f32) + kv_core[hop, step].astype(f32)
            ).astype(bf16)

        def forward(hop):
            one(hop)
            across(hop, step).start()

        one(0)
        each(n_u, forward, 1)

    each(n_z, add_pair, 1)
    add_pair(0)
    rows.start()
    gains.start()
    first_q.finish()
    q_sum[...] = jnp.sum(q_got[...].astype(f32), axis=0).astype(bf16)
    then_q.start()

    def plane_sum(step):
        total = kv_pair[0, step].astype(f32)
        for hop in range(1, n_u):
            across(hop, step).wait_recv()
            total = total + kv_cross[hop, step].astype(f32)
        return total

    def add_plane(step):
        kv_plane[step] = plane_sum(step).astype(bf16)
        along_z(step).start()

    each(n_z, add_plane, 1)
    total = plane_sum(0)
    for step in range(1, n_z):
        along_z(step).wait_recv()
        total = total + kv_line[step].astype(f32)
    kv_out[...] = total
    then_q.finish()
    split_ff.finish()
    gains.finish()
    rows.finish()
    each(n_z, lambda step: each(n_u, lambda hop: to_core(hop, step).wait_send()))
    each(n_z, lambda step: each(n_u, lambda hop: across(hop, step).wait_send(), 1))
    each(n_z, lambda step: along_z(step).wait_send(), 1)


def settle_call(exchange, kv_grad, rows, q_grad, ff_grad, gains):
    counts = axis_counts()
    n_u, n_b = counts["ulysses"], counts["blk"]
    n_z = n_b // 2
    block = kv_grad.shape[3:]
    dma = pltpu.SemaphoreType.DMA
    return remote_call(
        functools.partial(settle_kernel, n_b, counts),
        exchange.next_id(),
        [
            jax.ShapeDtypeStruct(block, f32),
            jax.ShapeDtypeStruct(rows.shape, bf16),
            jax.ShapeDtypeStruct(q_grad.shape[1:], bf16),
            jax.ShapeDtypeStruct(ff_grad.shape, bf16),
            jax.ShapeDtypeStruct(gains.shape, f32),
        ],
        [
            pltpu.VMEM((n_u, n_z) + block, bf16),
            pltpu.VMEM((n_u, n_z) + block, bf16),
            pltpu.VMEM((n_u, n_z) + block, bf16),
            pltpu.VMEM((n_z,) + block, bf16),
            pltpu.VMEM((n_z,) + block, bf16),
            pltpu.VMEM(q_grad.shape, bf16),
            pltpu.VMEM(q_grad.shape[1:], bf16),
            dma((n_u, n_z)),
            dma((n_u, n_z)),
            dma((n_u, n_z)),
            dma((n_u, n_z)),
            dma((n_z,)),
            dma((n_z,)),
        ]
        + sems(n_u)
        + sems(n_u)
        + sems(n_b)
        + sems(n_u * n_b)
        + sems(n_b),
        (kv_grad, rows, q_grad, ff_grad, gains),
        "settle",
    )


def norm_back_rows(inputs, gain_vec, upstream):
    root_scale = inverse_root(inputs)
    unit_rows = inputs * root_scale
    weighted = upstream * gain_vec
    grad_inputs = root_scale * (
        weighted - unit_rows * jnp.mean(weighted * unit_rows, axis=-1, keepdims=True)
    )
    return (grad_inputs, jnp.sum(upstream * unit_rows, axis=0, keepdims=True))


class Links:
    def __init__(self, plan, blk_count, sem_refs):
        self.plan, self.blk_count, self.sem_refs = plan, blk_count, sem_refs

    def __call__(self, k, source, landing):
        axis, kind = self.plan[k]
        part = Part(axis, kind, source, landing, *self.sem_refs[3 * k : 3 * k + 3], self.blk_count)
        part.start()
        return part

    def now(self, k, source, landing):
        self(k, source, landing).finish()


def fused_call(exchange, body, plan, arrays, outs, scratch, name):
    counts = axis_counts()
    n_in, n_out, n_scratch = len(arrays), len(outs), len(scratch)
    sem_shapes = []
    for axis, _ in plan:
        sem_shapes += sems(counts[axis])

    def kernel(*refs):
        ins, refs = refs[:n_in], refs[n_in:]
        results, refs = refs[:n_out], refs[n_out:]
        kept, sem_refs = refs[:n_scratch], refs[n_scratch:]
        greet({axis for axis, _ in plan}, counts["blk"], counts)
        body(Links(plan, counts["blk"], sem_refs), ins, results, kept)

    return remote_call(
        kernel,
        exchange.next_id(),
        [jax.ShapeDtypeStruct(shape, dtype) for shape, dtype in outs],
        [pltpu.VMEM(shape, dtype) for shape, dtype in scratch] + sem_shapes,
        arrays,
        name,
    )


def sum_blocks(landing):
    total = landing[0].astype(f32)
    for k in range(1, landing.shape[0]):
        total = total + landing[k].astype(f32)
    return total


def flat_rows_of(ref):
    return ref[...].reshape(-1, ref.shape[-1])


def turned(values, cosines, sines):
    return values * cosines + pltpu.roll(values, HEAD_WIDTH // 2, 1) * sines


def lanes_of(columns, width, count):
    group = lax.broadcasted_iota(jnp.int32, (columns[0].shape[0], width * count), 1) // width
    spread = columns[0]
    for k in range(1, count):
        spread = jnp.where(group == k, columns[k], spread)
    return spread


def query_body(n_b, links, ins, outs, scratch):
    pick_part, gain_attn, gain_query, q_weight, cosines, sines, ff_rows, out_rows, down_rows = ins
    picks_out, normed_all, query_raw, query_all, ff_all, out_all, down_all = outs
    pick_got, normed_mine, query_mine = scratch
    first = links(0, pick_part, pick_got)
    behind = [
        links(3, ff_rows, ff_all),
        links(4, out_rows, out_all),
        links(5, down_rows, down_all),
    ]
    first.finish()
    rows = sum_blocks(pick_got)
    picks_out[...] = rows
    mine = rows[:, :MODEL_WIDTH]
    normed_mine[...] = (mine * inverse_root(mine) * gain_attn[...]).astype(bf16)
    links.now(1, normed_mine, normed_all)
    raw = mm(flat_rows_of(normed_all), q_weight[...])
    query_raw[...] = raw
    for k in range(raw.shape[1] // HEAD_WIDTH):
        head = raw[:, k * HEAD_WIDTH : (k + 1) * HEAD_WIDTH]
        query_mine[:, k * HEAD_WIDTH : (k + 1) * HEAD_WIDTH] = turned(
            head * inverse_root(head) * gain_query[...], cosines[...], sines[...]
        ).astype(bf16)
    links.now(2, query_mine, query_all)
    for part in behind:
        part.finish()


def forward_body(n_u, n_b, links, ins, outs, scratch):
    part_send, stats, mine, out_weight, ff_weight, down_weight, gain_mlp, gain_final = ins
    attended_out, log_out, after_out, normed_all, gate_up_out, top_out, final_mine, final_all = outs
    part_got, stats_all, shares, partial, partial_got, normed_mine, final_slot = scratch
    picks = after_out.shape[0]
    out_cut = attended_out.shape[1] // n_u
    heads_row = QUERY_HEADS // n_u
    cut_head = (lax.axis_index("blk") * out_cut) // HEAD_WIDTH
    sent = links(0, part_send, part_got)
    links.now(1, stats, stats_all)
    full_max = stats_all[0, :QUERY_HEADS]
    for k in range(1, n_b):
        full_max = jnp.maximum(full_max, stats_all[k, :QUERY_HEADS])
    full_sum = jnp.zeros_like(full_max)
    for k in range(n_b):
        full_sum += stats_all[k, QUERY_HEADS:] * jnp.exp(stats_all[k, :QUERY_HEADS] - full_max)
    log_total = full_max + jnp.log(full_sum)
    log_out[...] = log_total
    for row in range(n_u):
        head = row * heads_row + cut_head
        row_log = log_out[pl.ds(head, 1), :]
        for k in range(n_b):
            shares[pl.ds(k * n_u + row, 1), :] = jnp.exp(
                stats_all[k, pl.ds(head, 1), :] - row_log
            )
    columns = shares[...].T
    sent.finish()
    attended = jnp.zeros(attended_out.shape, f32)
    for k in range(n_b):
        attended += part_got[k].astype(f32) * lanes_of(
            [columns[:, k * n_u + row : k * n_u + row + 1] for row in range(n_u)], out_cut, n_u
        )
    attended_out[...] = attended

    def to_picks(which, rows):
        partial[...] = rows.astype(bf16).reshape(partial.shape)
        links.now(which, partial, partial_got.at[which // 4])
        return sum_blocks(partial_got.at[which // 4])

    after_attn = mine[:, :MODEL_WIDTH] + to_picks(2, mm(attended.astype(bf16), out_weight[...]))
    after_out[...] = after_attn
    normed_mine[...] = (after_attn * inverse_root(after_attn) * gain_mlp[...]).astype(bf16)
    links.now(3, normed_mine, normed_all)
    gate_up = mm(flat_rows_of(normed_all), ff_weight[...])
    gate_up_out[...] = gate_up
    half = gate_up.shape[1] // 2
    gate_part, up_part = gate_up[:, :half], gate_up[:, half:]
    activated = (gate_part * jax.nn.sigmoid(gate_part) * up_part).astype(bf16)
    after_mlp = after_attn + to_picks(4, mm(activated, down_weight[...]))
    top_out[...] = after_mlp
    final_mine[...] = (after_mlp * inverse_root(after_mlp) * gain_final[...]).astype(bf16)
    links.now(5, final_mine, final_slot)
    links.now(6, final_slot, final_all)


def backward_body(n_u, n_b, links, ins, outs, scratch):
    (
        head_rows,
        head_stats,
        final_mine,
        picks_in,
        weights,
        after_mlp,
        after_attn,
        gate_up_in,
        normed_all,
        attended,
        out_weight,
        ff_weight,
        down_weight,
        gain_mlp,
        gain_final,
    ) = ins
    (
        norms_all,
        terms,
        gain_mlp_out,
        gain_final_out,
        grad_ff,
        grad_out,
        grad_down,
        grad_after,
        branch_all,
        attended_all,
        delta_all,
    ) = outs
    (
        rows_got,
        stats_got,
        slot_stats,
        slot_got,
        factors,
        columns,
        norms_mine,
        partial,
        partial_got,
        mine_low,
        grad_all,
        attended_mine,
        deltas,
        delta_mine,
    ) = scratch
    picks = after_mlp.shape[0]
    slot_picks = n_b * picks
    b = lax.axis_index("blk")
    factors[...] = jnp.zeros_like(factors)
    first = links(0, head_rows, rows_got)
    links.now(1, head_stats, stats_got)
    tops = stats_got[0, 0:1, :]
    for k in range(1, n_u):
        tops = jnp.maximum(tops, stats_got[k, 0:1, :])
    total = jnp.zeros_like(tops)
    for k in range(n_u):
        factor = jnp.exp(stats_got[k, 0:1, :] - tops)
        factors[k : k + 1, :] = factor
        total += stats_got[k, 1:2, :] * factor
    slot_stats[...] = jnp.zeros_like(slot_stats)
    slot_stats[0:1, :] = tops
    slot_stats[1:2, :] = total
    slot_part = links(3, slot_stats, slot_got)
    by_row = factors[...].T
    first.finish()
    rows = rows_got[0].astype(f32) * by_row[:, 0:1]
    for k in range(1, n_u):
        rows += rows_got[k].astype(f32) * by_row[:, k : k + 1]
    partial[...] = rows.astype(bf16).reshape(partial.shape)
    back = links(2, partial, partial_got.at[0])
    slot_part.finish()
    tops = slot_got[0, 0:1, :]
    for k in range(1, n_b):
        tops = jnp.maximum(tops, slot_got[k, 0:1, :])
    total = jnp.zeros_like(tops)
    for k in range(n_b):
        factor = jnp.exp(slot_got[k, 0:1, :] - tops)
        factors[k : k + 1, :] = factor
        total += slot_got[k, 1:2, :] * factor
    log_norm = tops + jnp.log(total)
    for k in range(n_b):
        factors[k : k + 1, :] = factors[k : k + 1, :] / total
    factors[n_b : n_b + 1, :] = log_norm
    norms_mine[...] = jnp.broadcast_to(log_norm, norms_mine.shape)
    norms_part = links(4, norms_mine, norms_all)
    columns[...] = factors[...].T
    mine = columns[pl.ds(pl.multiple_of(b * picks, picks), picks), :]
    back.finish()
    target_rows = picks_in[:, MODEL_WIDTH:]
    grad_final = -target_rows
    for k in range(n_b):
        grad_final += partial_got[0, k].astype(f32) * mine[:, k : k + 1]
    grad_final = grad_final * weights[:, 0:1]
    target_logit = jnp.sum(
        final_mine[...].astype(f32) * target_rows, axis=-1, keepdims=True
    )
    terms[...] = weights[...] * (target_logit - mine[:, n_b : n_b + 1])
    grad_mlp, gain_rows = norm_back_rows(after_mlp[...], gain_final[...], grad_final)
    gain_final_out[...] = gain_rows
    mine_low[...] = grad_mlp.astype(bf16)
    links.now(5, mine_low, grad_all)
    branch = flat_rows_of(grad_all)
    gate_up = gate_up_in[...]
    half = gate_up.shape[1] // 2
    gate_part, up_part = gate_up[:, :half], gate_up[:, half:]
    sigmoid_gate = jax.nn.sigmoid(gate_part)
    grad_act = mm_back(branch, down_weight[...])
    grad_gate = grad_act * up_part * sigmoid_gate * (1.0 + gate_part * (1.0 - sigmoid_gate))
    grad_up = grad_act * gate_part * sigmoid_gate
    grad_gate_up = jnp.concatenate([grad_gate, grad_up], axis=1).astype(bf16)
    partial[...] = mm_back(grad_gate_up, ff_weight[...]).astype(bf16).reshape(partial.shape)
    back = links(6, partial, partial_got.at[1])
    activated = (gate_part * sigmoid_gate * up_part).astype(bf16)
    grad_down[...] = mm_outer(activated, branch).astype(bf16).reshape(grad_down.shape)
    back.finish()
    grad_mid, gain_rows = norm_back_rows(after_attn[...], gain_mlp[...], sum_blocks(partial_got.at[1]))
    gain_mlp_out[...] = gain_rows
    grad_attn = grad_mlp + grad_mid
    grad_after[...] = grad_attn
    mine_low[...] = grad_attn.astype(bf16)
    again = links(7, mine_low, branch_all)
    grad_ff[...] = (
        mm_outer(flat_rows_of(normed_all), grad_gate_up).astype(bf16).reshape(grad_ff.shape)
    )
    again.finish()
    branch = flat_rows_of(branch_all)
    grad_low = mm_back(branch, out_weight[...]).astype(bf16)
    attended_mine[...] = grad_low
    last = links(8, attended_mine, attended_all)
    out_cut = attended.shape[1] // n_u
    product = attended[...] * grad_low.astype(f32)
    group = lax.broadcasted_iota(jnp.int32, product.shape, 1) // out_cut
    lane = lax.broadcasted_iota(jnp.int32, deltas.shape, 1)
    sums = jnp.zeros(deltas.shape, f32)
    for row in range(n_u):
        one = jnp.sum(jnp.where(group == row, product, 0.0), axis=-1, keepdims=True)
        sums = jnp.where(lane == row, one, sums)
    deltas[...] = sums
    delta_mine[...] = deltas[...].T[:8, :]
    delta_part = links(9, delta_mine, delta_all)
    grad_out[...] = mm_outer(attended[...].astype(bf16), branch).astype(bf16).reshape(
        grad_out.shape
    )
    last.finish()
    delta_part.finish()
    norms_part.finish()


def query_back_body(links, ins, outs, scratch):
    (
        query_send,
        query_raw,
        cosines,
        sines,
        gain_query,
        q_weight,
        normed_all,
        picks_in,
        gain_attn,
        grad_after,
        grad_ff,
        grad_out,
        grad_down,
    ) = ins
    gain_query_out, gain_attn_out, grad_q, pick_back, ff_sum, out_sum, down_sum = outs
    query_got, grad_low, partial, partial_got, mine_low, ff_got, out_got, down_got = scratch
    first = links(0, query_send, query_got)
    behind = [
        links(3, grad_ff, ff_got),
        links(4, grad_out, out_got),
        links(5, grad_down, down_got),
    ]
    first.finish()
    upstream = sum_blocks(query_got).astype(bf16).astype(f32)
    gain_sum = jnp.zeros(gain_query_out.shape, f32)
    for k in range(upstream.shape[1] // HEAD_WIDTH):
        part = slice(k * HEAD_WIDTH, (k + 1) * HEAD_WIDTH)
        grad_head, gain_head = norm_back_rows(
            query_raw[:, part], gain_query[...], turned(upstream[:, part], cosines[...], -sines[...])
        )
        grad_low[:, part] = grad_head.astype(bf16)
        gain_sum += gain_head
    gain_query_out[...] = gain_sum
    partial[...] = mm_back(grad_low[...], q_weight[...]).astype(bf16).reshape(partial.shape)
    back = links(1, partial, partial_got)
    grad_q[...] = (
        mm_outer(flat_rows_of(normed_all), grad_low[...]).astype(bf16).reshape(grad_q.shape)
    )
    back.finish()
    grad_mine, gain_rows = norm_back_rows(
        picks_in[:, :MODEL_WIDTH], gain_attn[...], sum_blocks(partial_got)
    )
    gain_attn_out[...] = gain_rows
    mine_low[...] = (grad_after[...] + grad_mine).astype(bf16)
    links.now(2, mine_low, pick_back)
    for part in behind:
        part.finish()
    ff_sum[...] = sum_blocks(ff_got).astype(bf16)
    out_sum[...] = sum_blocks(out_got)
    down_sum[...] = sum_blocks(down_got)


class Named:
    pass


def named_call(exchange, body, plan, extra_sems, ins, outs, scratch, name):
    counts = axis_counts()
    sem_shapes = []
    for axis, _ in plan.values():
        sem_shapes += sems(counts[axis])
    order = {key: k for k, key in enumerate(plan)}
    extra = list(extra_sems)

    def kernel(*refs):
        r, s = Named(), Named()
        names = list(ins) + list(outs) + list(scratch)
        for key, ref in zip(names, refs):
            setattr(r, key, ref)
        sem_refs = refs[len(names) :]
        for key, ref in zip(extra, sem_refs[3 * len(plan) :]):
            setattr(s, key, ref)
        base = Links(list(plan.values()), counts["blk"], sem_refs)
        greet({axis for axis, _ in plan.values()}, counts["blk"], counts)
        body(r, lambda key, source, landing: base(order[key], source, landing), s)

    results = remote_call(
        kernel,
        exchange.next_id(),
        [jax.ShapeDtypeStruct(shape, dtype) for shape, dtype in outs.values()],
        [pltpu.VMEM(shape, dtype) for shape, dtype in scratch.values()]
        + sem_shapes
        + [pltpu.SemaphoreType.DMA(extra_sems[key]) for key in extra],
        list(ins.values()),
        name,
    )
    found = Named()
    for key, value in zip(outs, results):
        setattr(found, key, value)
    return found


def column_of(lane_row):
    count = lane_row.shape[1]
    down = lax.broadcasted_iota(jnp.int32, (count, count), 0)
    across = lax.broadcasted_iota(jnp.int32, (count, count), 1)
    return jnp.sum(jnp.where(down == across, lane_row, 0.0), axis=1, keepdims=True)


def begin_body(n_u, n_b, row_share, slots, r, links, s):
    u, b = lax.axis_index("ulysses"), lax.axis_index("blk")
    me = u * n_b + b
    block_len, picks = r.tokens.shape[1], r.picked.shape[1]
    places = n_u * slots
    gathers = [
        links("tokens", r.tokens, r.tokens_all),
        links("targets", r.targets, r.targets_all),
        links("picked", r.picked, r.picked_all),
        links("advantages", r.advantages, r.advantages_all),
    ]
    links("near", r.scales, r.near).finish()
    far = links("far", r.near, r.far)
    for part in gathers:
        part.finish()

    width = block_len + picks
    lane = lax.broadcasted_iota(jnp.int32, (1, width), 1)
    before = jnp.where(
        lax.broadcasted_iota(jnp.int32, (width, width), 0)
        < lax.broadcasted_iota(jnp.int32, (width, width), 1),
        1.0,
        0.0,
    ).astype(bf16)
    base = jnp.zeros((2 * n_u, 1), f32)
    found = [jnp.zeros((slots, width), f32) for _ in range(2 * n_u)]
    rank_of_slot = lax.broadcasted_iota(jnp.int32, (slots, width), 0).astype(f32)
    owner_first = lax.broadcasted_iota(jnp.int32, (n_u, 1), 0) * n_b + b
    most = jnp.zeros((n_u, 1), f32)
    counts = [jnp.zeros((n_u, width), f32) for _ in range(n_u * n_b)]
    for k in range(n_b):
        r.wants[:, :block_len] = r.tokens_all[k]
        r.wants[:, block_len:] = r.targets_all[k]
        wants = r.wants[...]
        local = wants - me * row_share
        sent = (local >= 0) & (local < row_share)
        own = r.wants[pl.ds(u, 1), :] - owner_first * row_share
        got = (own >= 0) & (own < row_share)
        r.masks[:n_u, :] = jnp.where(sent, 1.0, 0.0)
        r.masks[n_u:, :] = jnp.where(got, 1.0, 0.0)
        r.labels[:n_u, :] = (local + 1).astype(f32)
        r.labels[n_u:, :] = jnp.broadcast_to(k * width + lane + 1, (n_u, width)).astype(f32)
        masks = r.masks[...]
        ranks = mm(masks.astype(bf16), before) + base
        r.ranks[...] = jnp.where(masks > 0.0, ranks, -1.0)
        base += jnp.sum(masks, axis=1, keepdims=True)
        for row in range(2 * n_u):
            hit = r.ranks[row : row + 1, :] == rank_of_slot
            found[row] += jnp.where(hit, r.labels[row : row + 1, :], 0.0)
        for owner in range(n_u * n_b):
            far_row = wants - owner * row_share
            counts[owner] += jnp.where((far_row >= 0) & (far_row < row_share), 1.0, 0.0)
        r.slot_picked[:, k * picks : (k + 1) * picks] = r.picked_all[k, pl.ds(u, 1), :]
        valid = r.picked_all[k] < r.lengths[...]
        weights = jnp.where(valid, r.advantages_all[k], 0.0)
        for row in range(n_u):
            at = slice((row * n_b + k) * picks, (row * n_b + k + 1) * picks)
            r.weights[:, at] = weights[row : row + 1, :]
            r.target_ids[:, at] = r.targets_all[k, row : row + 1, :] - me * row_share
    for owner in range(n_u * n_b):
        most = jnp.maximum(most, jnp.sum(counts[owner], axis=1, keepdims=True))
    r.meta[...] = jnp.zeros_like(r.meta)
    r.meta[0:n_u, :] = jnp.broadcast_to(base[:n_u], (n_u, 128))
    r.meta[8 : 8 + n_u, :] = jnp.broadcast_to(most, (n_u, 128))
    mine_valid = r.picked[pl.ds(u, 1), :] < r.lengths[pl.ds(u, 1), :]
    mine_weight = jnp.where(mine_valid, r.advantages[pl.ds(u, 1), :], 0.0)
    r.meta[16:17, :] = jnp.broadcast_to(
        jnp.sum(jnp.where(mine_valid, 1.0, 0.0), axis=1, keepdims=True), (1, 128)
    )
    r.weight_wide[...] = jnp.broadcast_to(column_of(mine_weight), r.weight_wide.shape)
    my_length = r.lengths[pl.ds(u, 1), :]
    for row in range(n_u):
        here = slice(row * slots, (row + 1) * slots)
        r.row_ids[here, :] = jnp.sum(found[row], axis=1, keepdims=True).astype(jnp.int32) - 1
        entry = jnp.sum(found[n_u + row], axis=1, keepdims=True) - 1.0
        block = jnp.floor((entry + 0.5) * (1.0 / width))
        inside = entry - block * width
        token = (entry >= 0.0) & (inside < block_len)
        position = (block * block_len + inside).astype(jnp.int32)
        key_pos = jnp.where(token, position, 1 << 30)
        r.key_pos[here, :] = key_pos
        r.key_lim[here, :] = jnp.where(key_pos < my_length, key_pos, 1 << 30)
        r.positions[here, :] = jnp.where(token, position, 0)
        target = (block * picks + inside - block_len).astype(jnp.int32)
        r.target_of[here, :] = jnp.where((entry >= 0.0) & (inside >= block_len), target, -1)
    r.positions[places:, :] = column_of(r.slot_picked[...].astype(f32)).astype(jnp.int32)

    far.finish()
    share = r.scales.shape[1]
    for row in range(n_u):
        for k in range(n_b):
            at = (row * n_b + k) * share
            r.gains[:, at : at + share] = r.far[row, k].astype(bf16).astype(f32)
    r.gain_attn[...] = r.gains[:, :MODEL_WIDTH]
    r.gain_mlp[...] = r.gains[:, MODEL_WIDTH : 2 * MODEL_WIDTH]
    r.gain_final[...] = r.gains[:, 2 * MODEL_WIDTH : 3 * MODEL_WIDTH]
    r.gain_query[...] = r.gains[:, 3 * MODEL_WIDTH : 3 * MODEL_WIDTH + HEAD_WIDTH]
    r.gain_key[...] = r.gains[:, 3 * MODEL_WIDTH + HEAD_WIDTH :]


def totals_body(r, links, s):
    links("near", r.mine, r.near_all).finish()
    r.near[...] = sum_blocks(r.near_all)
    links("far", r.near, r.far_all).finish()
    r.total[...] = sum_blocks(r.far_all)


def head_of(ref, head):
    share = ref.shape[2] // HEAD_WIDTH
    at = head % share * HEAD_WIDTH
    return ref[head // share, :, at : at + HEAD_WIDTH]


def cuts_of(head, n_u, n_b):
    cut = QUERY_WIDTH // (n_u * n_b)
    heads_row, pieces = QUERY_HEADS // n_u, HEAD_WIDTH // cut
    row = head // heads_row
    return [
        (head % heads_row * pieces + t, slice(row * cut, (row + 1) * cut), slice(t * cut, (t + 1) * cut))
        for t in range(pieces)
    ]


def ff_cuts(n_u, n_b):
    cut = FF // (n_u * n_b)
    return [
        (
            k,
            slice((half * n_u + row) * cut, (half * n_u + row + 1) * cut),
            slice(half * FF + (row * n_b + k) * cut, half * FF + (row * n_b + k + 1) * cut),
        )
        for k in range(n_b)
        for half in range(2)
        for row in range(n_u)
    ]


def rise_body(n_u, n_b, r, links, s):
    u, b = lax.axis_index("ulysses"), lax.axis_index("blk")
    n_z = n_b // 2
    z, c = b // 2, lax.rem(b, 2)
    score_scale = HEAD_WIDTH ** (-0.5)

    def along_z(step):
        return remote(
            r.kv_in,
            r.kv_weight.at[u, z, c],
            s.z_send.at[step],
            s.z_recv.at[step],
            {"blk": lax.rem(z + step, n_z) * 2 + c},
        )

    def own_copy():
        return pltpu.make_async_copy(r.kv_in, r.kv_weight.at[u, z, c], s.own.at[0])

    def block(hop, step):
        return r.kv_weight.at[lax.rem(u - hop + n_u, n_u), lax.rem(z - step + n_z, n_z), c]

    def across(hop, step):
        place = block(0, step)
        return remote(
            place,
            place,
            s.xy_send.at[hop, step],
            s.xy_recv.at[hop, step],
            {"ulysses": lax.rem(u + hop, n_u)},
        )

    def to_core(hop, step):
        place = block(hop, step)
        return remote(
            place,
            place,
            s.core_send.at[hop, step],
            s.core_recv.at[hop, step],
            {"blk": z * 2 + 1 - c},
        )

    places = r.key_raw.shape[0]
    half = KEY_VALUE_HEADS * HEAD_WIDTH
    r.kv_in[...] = r.inflow[:, QUERY_WIDTH:].astype(bf16)
    own_copy().start()
    rows = links("rows", r.rows_in, r.arrived)
    each(n_z, lambda step: along_z(step).start(), 1)
    q_share = r.q_in.shape[2]
    for k in range(n_b):
        r.q_in[k] = r.inflow[:, k * q_share : (k + 1) * q_share].astype(bf16)
    q_split = links("q_split", r.q_in, r.q_part)
    own_copy().wait()
    each(n_u, lambda hop: across(hop, 0).start(), 1)
    to_core(0, 0).start()
    for k, there, here in ff_cuts(n_u, n_b):
        r.ff_in[k, :, there] = r.expand[:, here].astype(bf16)
    ff_split = links("ff_split", r.ff_in, r.ff_part)
    r.out_in[...] = r.outflow[...].astype(bf16)
    r.down_in[...] = r.contract[...].astype(bf16)
    rows.finish()

    arrived = flat_rows_of(r.arrived)
    pick_hot = jnp.where(r.key_pos[...] == r.slot_picked[...], 1.0, 0.0).astype(bf16)
    pick_lane = lax.broadcasted_iota(jnp.int32, pick_hot.shape, 1)
    target_hot = jnp.where(r.target_of[...] == pick_lane, 1.0, 0.0).astype(bf16)
    r.pick_send[:, :, :MODEL_WIDTH] = (
        mm_outer(pick_hot, arrived).astype(bf16).reshape(r.normed_slot.shape)
    )
    r.pick_send[:, :, MODEL_WIDTH:] = (
        mm_outer(target_hot, arrived).astype(bf16).reshape(r.normed_slot.shape)
    )
    picked = links("picks", r.pick_send, r.pick_got)

    def pass_on(step):
        along_z(step).wait_recv()
        each(n_u, lambda hop: across(hop, step).start(), 1)
        to_core(0, step).start()

    each(n_z, pass_on, 1)
    q_split.finish()
    q_all = links("q_all", r.q_part, r.q_weight)
    wide = arrived.astype(f32)
    r.normed_keys[...] = (wide * inverse_root(wide) * r.gain_attn[...]).astype(bf16)
    picked.finish()
    pick_rows = sum_blocks(r.pick_got)
    r.pick_rows[...] = pick_rows
    mine = pick_rows[:, :MODEL_WIDTH]
    r.normed_mine[...] = (mine * inverse_root(mine) * r.gain_attn[...]).astype(bf16)
    links("normed", r.normed_mine, r.normed_slot).finish()
    q_all.finish()
    raw = mm(flat_rows_of(r.normed_slot), r.q_weight[...].reshape(MODEL_WIDTH, -1))
    r.query_raw[...] = raw
    for k in range(raw.shape[1] // HEAD_WIDTH):
        part = slice(k * HEAD_WIDTH, (k + 1) * HEAD_WIDTH)
        head = raw[:, part]
        r.query_mine[:, part] = turned(
            head * inverse_root(head) * r.gain_query[...], r.rope_cos[places:], r.rope_sin[places:]
        ).astype(bf16)
    queries = links("queries", r.query_mine, r.query_all)

    def share(step):
        def one(hop):
            across(hop, step).wait_recv()
            to_core(hop, step).start()

        each(n_u, one, 1)

    each(n_z, share)
    out_all = links("out_all", r.out_in, r.out_weight)
    ff_split.finish()
    ff_all = links("ff_all", r.ff_part, r.ff_weight)
    down_all = links("down_all", r.down_in, r.down_weight)
    each(n_z, lambda step: each(n_u, lambda hop: to_core(hop, step).wait_recv()))

    wide_head = 2 * HEAD_WIDTH

    def project(k):
        for first in (0, half):
            at = pl.multiple_of(first + k * wide_head, wide_head)
            weight = r.kv_weight[:, :, :, :, pl.ds(at, wide_head)].reshape(MODEL_WIDTH, wide_head)
            got = mm(r.normed_keys[...], weight)
            here = pl.ds(pl.multiple_of(k * wide_head, wide_head), wide_head)
            if first:
                r.values[:, here] = got.astype(bf16)
            else:
                r.key_raw[:, here] = got
                turned_both = []
                for j in range(2):
                    head = got[:, j * HEAD_WIDTH : (j + 1) * HEAD_WIDTH]
                    turned_both.append(
                        turned(
                            head * inverse_root(head) * r.gain_key[...],
                            r.rope_cos[:places],
                            r.rope_sin[:places],
                        )
                    )
                r.key_rot[:, here] = jnp.concatenate(turned_both, axis=1).astype(bf16)

    each(KEY_VALUE_HEADS // 2, project)
    queries.finish()
    allowed = r.key_lim[...] <= r.slot_picked[...]
    for head in range(QUERY_HEADS):
        at = head // (QUERY_HEADS // KEY_VALUE_HEADS) * HEAD_WIDTH
        part = slice(at, at + HEAD_WIDTH)
        scores = mm_back(r.key_rot[:, part], head_of(r.query_all, head)) * score_scale
        scores = jnp.where(allowed, scores, masked_score)
        top = jnp.max(scores, axis=0, keepdims=True)
        weights = jnp.where(allowed, jnp.exp(scores - top), 0.0)
        r.stats[head : head + 1, :] = top
        r.stats[QUERY_HEADS + head : QUERY_HEADS + head + 1, :] = jnp.sum(
            weights, axis=0, keepdims=True
        )
        out = mm_outer(weights.astype(bf16), r.values[:, part]).astype(bf16)
        for target, there, here in cuts_of(head, n_u, n_b):
            r.part_send[target, :, there] = out[:, here]

    picks = r.after_attn.shape[0]
    out_cut = r.attended.shape[1] // n_u
    heads_row = QUERY_HEADS // n_u
    cut_head = (b * out_cut) // HEAD_WIDTH
    sent = links("parts", r.part_send, r.part_got)
    links("stats", r.stats, r.stats_all).finish()
    full_max = r.stats_all[0, :QUERY_HEADS]
    for k in range(1, n_b):
        full_max = jnp.maximum(full_max, r.stats_all[k, :QUERY_HEADS])
    full_sum = jnp.zeros_like(full_max)
    for k in range(n_b):
        full_sum += r.stats_all[k, QUERY_HEADS:] * jnp.exp(
            r.stats_all[k, :QUERY_HEADS] - full_max
        )
    r.log_total[...] = full_max + jnp.log(full_sum)
    for row in range(n_u):
        head = row * heads_row + cut_head
        row_log = r.log_total[pl.ds(head, 1), :]
        for k in range(n_b):
            r.shares[k * n_u + row : k * n_u + row + 1, :] = jnp.exp(
                r.stats_all[k, pl.ds(head, 1), :] - row_log
            )
    columns = r.shares[...].T
    sent.finish()
    attended = jnp.zeros(r.attended.shape, f32)
    for k in range(n_b):
        attended += r.part_got[k].astype(f32) * lanes_of(
            [columns[:, k * n_u + row : k * n_u + row + 1] for row in range(n_u)], out_cut, n_u
        )
    r.attended[...] = attended
    out_all.finish()

    def to_picks(key, rows):
        r.partial[...] = rows.astype(bf16).reshape(r.partial.shape)
        landing = r.partial_got.at[0 if key == "sum_out" else 1]
        links(key, r.partial, landing).finish()
        return sum_blocks(landing)

    after_attn = r.pick_rows[:, :MODEL_WIDTH] + to_picks(
        "sum_out", mm(attended.astype(bf16), flat_rows_of(r.out_weight))
    )
    r.after_attn[...] = after_attn
    r.normed_mine[...] = (after_attn * inverse_root(after_attn) * r.gain_mlp[...]).astype(bf16)
    links("normed_mlp", r.normed_mine, r.normed_mlp).finish()
    ff_all.finish()
    gate_up = mm(flat_rows_of(r.normed_mlp), r.ff_weight[...].reshape(MODEL_WIDTH, -1))
    r.gate_up[...] = gate_up
    half = gate_up.shape[1] // 2
    gate_part, up_part = gate_up[:, :half], gate_up[:, half:]
    activated = (gate_part * jax.nn.sigmoid(gate_part) * up_part).astype(bf16)
    down_all.finish()
    after_mlp = after_attn + to_picks("sum_mlp", mm(activated, flat_rows_of(r.down_weight)))
    r.after_mlp[...] = after_mlp
    r.final_mine[...] = (after_mlp * inverse_root(after_mlp) * r.gain_final[...]).astype(bf16)
    links("final", r.final_mine, r.final_slot).finish()
    links("final_all", r.final_slot, r.final_all).finish()
    each(n_z, lambda step: along_z(step).wait_send(), 1)
    each(n_z, lambda step: each(n_u, lambda hop: across(hop, step).wait_send(), 1))
    each(n_z, lambda step: each(n_u, lambda hop: to_core(hop, step).wait_send()))


def fall_body(n_u, n_b, r, links, s):
    u, b = lax.axis_index("ulysses"), lax.axis_index("blk")
    n_z = n_b // 2
    z, c = b // 2, lax.rem(b, 2)
    score_scale = HEAD_WIDTH ** (-0.5)
    picks = r.after_mlp.shape[0]
    places = r.key_raw.shape[0]
    r.factors[...] = jnp.zeros_like(r.factors)
    head_rows = links("head_rows", r.head_rows, r.rows_got)
    links("head_stats", r.head_stats, r.stats_got).finish()
    tops = r.stats_got[0, 0:1, :]
    for k in range(1, n_u):
        tops = jnp.maximum(tops, r.stats_got[k, 0:1, :])
    total = jnp.zeros_like(tops)
    for k in range(n_u):
        factor = jnp.exp(r.stats_got[k, 0:1, :] - tops)
        r.factors[k : k + 1, :] = factor
        total += r.stats_got[k, 1:2, :] * factor
    r.slot_stats[...] = jnp.zeros_like(r.slot_stats)
    r.slot_stats[0:1, :] = tops
    r.slot_stats[1:2, :] = total
    slot_part = links("slot_stats", r.slot_stats, r.slot_got)
    by_row = r.factors[...].T
    head_rows.finish()
    rows = r.rows_got[0].astype(f32) * by_row[:, 0:1]
    for k in range(1, n_u):
        rows += r.rows_got[k].astype(f32) * by_row[:, k : k + 1]
    r.partial[...] = rows.astype(bf16).reshape(r.partial.shape)
    back = links("slot_rows", r.partial, r.partial_got.at[0])
    slot_part.finish()
    tops = r.slot_got[0, 0:1, :]
    for k in range(1, n_b):
        tops = jnp.maximum(tops, r.slot_got[k, 0:1, :])
    total = jnp.zeros_like(tops)
    for k in range(n_b):
        factor = jnp.exp(r.slot_got[k, 0:1, :] - tops)
        r.factors[k : k + 1, :] = factor
        total += r.slot_got[k, 1:2, :] * factor
    log_norm = tops + jnp.log(total)
    for k in range(n_b):
        r.factors[k : k + 1, :] = r.factors[k : k + 1, :] / total
    r.factors[n_b : n_b + 1, :] = log_norm
    r.norms_mine[...] = jnp.broadcast_to(log_norm, r.norms_mine.shape)
    norms_part = links("norms", r.norms_mine, r.norms_all)
    r.columns[...] = r.factors[...].T
    mine = r.columns[pl.ds(pl.multiple_of(b * picks, picks), picks), :]
    back.finish()
    target_rows = r.pick_rows[:, MODEL_WIDTH:]
    grad_final = -target_rows
    for k in range(n_b):
        grad_final += r.partial_got[0, k].astype(f32) * mine[:, k : k + 1]
    grad_final = grad_final * r.weights[:, 0:1]
    target_logit = jnp.sum(
        r.final_mine[...].astype(f32) * target_rows, axis=-1, keepdims=True
    )
    r.terms[...] = r.weights[...] * (target_logit - mine[:, n_b : n_b + 1])
    grad_mlp, gain_final = norm_back_rows(r.after_mlp[...], r.gain_final[...], grad_final)
    r.mine_low[...] = grad_mlp.astype(bf16)
    links("branch", r.mine_low, r.grad_all).finish()
    branch = flat_rows_of(r.grad_all)
    gate_up = r.gate_up[...]
    half = gate_up.shape[1] // 2
    gate_part, up_part = gate_up[:, :half], gate_up[:, half:]
    sigmoid_gate = jax.nn.sigmoid(gate_part)
    grad_act = mm_back(branch, flat_rows_of(r.down_weight))
    grad_gate = grad_act * up_part * sigmoid_gate * (1.0 + gate_part * (1.0 - sigmoid_gate))
    grad_up = grad_act * gate_part * sigmoid_gate
    grad_gate_up = jnp.concatenate([grad_gate, grad_up], axis=1).astype(bf16)
    r.partial[...] = (
        mm_back(grad_gate_up, r.ff_weight[...].reshape(MODEL_WIDTH, -1))
        .astype(bf16)
        .reshape(r.partial.shape)
    )
    back = links("sum_ff", r.partial, r.partial_got.at[1])
    activated = (gate_part * sigmoid_gate * up_part).astype(bf16)
    r.grad_down[...] = mm_outer(activated, branch).astype(bf16).reshape(r.grad_down.shape)
    down_part = links("down", r.grad_down, r.down_got)
    r.grad_ff[...] = (
        mm_outer(flat_rows_of(r.normed_mlp), grad_gate_up).astype(bf16).reshape(r.grad_ff.shape)
    )
    ff_part = links("ff", r.grad_ff, r.ff_got)
    back.finish()
    grad_mid, gain_mlp = norm_back_rows(
        r.after_attn[...], r.gain_mlp[...], sum_blocks(r.partial_got.at[1])
    )
    grad_attn = grad_mlp + grad_mid
    r.mine_low[...] = grad_attn.astype(bf16)
    links("branch_attn", r.mine_low, r.branch_all).finish()
    branch = flat_rows_of(r.branch_all)
    grad_low = mm_back(branch, flat_rows_of(r.out_weight)).astype(bf16)
    r.attended_mine[...] = grad_low
    last = links("attended", r.attended_mine, r.attended_all)
    out_cut = r.attended.shape[1] // n_u
    product = r.attended[...] * grad_low.astype(f32)
    group = lax.broadcasted_iota(jnp.int32, product.shape, 1) // out_cut
    lane = lax.broadcasted_iota(jnp.int32, r.deltas.shape, 1)
    sums = jnp.zeros(r.deltas.shape, f32)
    for row in range(n_u):
        one = jnp.sum(jnp.where(group == row, product, 0.0), axis=-1, keepdims=True)
        sums = jnp.where(lane == row, one, sums)
    r.deltas[...] = sums
    r.delta_mine[...] = r.deltas[...].T[:8, :]
    delta_part = links("deltas", r.delta_mine, r.delta_all)
    r.grad_out[...] = (
        mm_outer(r.attended[...].astype(bf16), branch).astype(bf16).reshape(r.grad_out.shape)
    )
    out_part = links("out", r.grad_out, r.out_got)
    wide = flat_rows_of(r.arrived).astype(f32)
    r.normed_keys[...] = (wide * inverse_root(wide) * r.gain_attn[...]).astype(bf16)
    last.finish()
    delta_part.finish()

    allowed = r.key_lim[...] <= r.slot_picked[...]
    width = KEY_VALUE_HEADS * HEAD_WIDTH
    r.gain_key_row[...] = jnp.zeros((1, HEAD_WIDTH), f32)
    heads_each = QUERY_HEADS // KEY_VALUE_HEADS
    for kv_head in range(KEY_VALUE_HEADS):
        part = slice(kv_head * HEAD_WIDTH, (kv_head + 1) * HEAD_WIDTH)
        key, value = r.key_rot[:, part], r.values[:, part]
        grad_key = jnp.zeros(key.shape, f32)
        grad_value = jnp.zeros(key.shape, f32)
        for head in range(kv_head * heads_each, (kv_head + 1) * heads_each):
            query = head_of(r.query_all, head)
            cuts = cuts_of(head, n_u, n_b)
            upstream = jnp.concatenate([r.attended_all[at, :, there] for at, there, _ in cuts], 1)
            row = head // (QUERY_HEADS // n_u)
            delta = sum(r.delta_all[at, row : row + 1, :] for at, _, _ in cuts)
            scores = mm_back(key, query) * score_scale
            probs = jnp.where(allowed, jnp.exp(scores - r.log_total[head : head + 1, :]), 0.0)
            grad_probs = mm_back(value, upstream)
            grad_scores = (probs * (grad_probs - delta) * score_scale).astype(bf16)
            grad_query = mm_outer(grad_scores, key).astype(bf16)
            share = r.query_send.shape[2] // HEAD_WIDTH
            at = head % share * HEAD_WIDTH
            r.query_send[head // share, :, at : at + HEAD_WIDTH] = grad_query
            grad_key += mm(grad_scores, query)
            grad_value += mm(probs.astype(bf16), upstream)
        grad_head, gain_head = norm_back_rows(
            r.key_raw[:, part],
            r.gain_key[...],
            turned(grad_key.astype(bf16).astype(f32), r.rope_cos[:places], -r.rope_sin[:places]),
        )
        r.gain_key_row[...] += gain_head
        r.grad_kv[:, part] = grad_head.astype(bf16)
        r.grad_kv[:, width + kv_head * HEAD_WIDTH : width + (kv_head + 1) * HEAD_WIDTH] = (
            grad_value.astype(bf16)
        )
    query_part = links("grad_queries", r.query_send, r.query_got)

    def place(hop, step):
        return (lax.rem(u + hop, n_u), lax.rem(z + step, n_z))

    def to_core(hop, step):
        row, line = place(hop, step)
        return remote(
            r.kv_grad.at[row, line, 1 - c],
            r.kv_core.at[hop, step],
            s.core_send.at[hop, step],
            s.core_recv.at[hop, step],
            {"blk": z * 2 + 1 - c},
        )

    def across(hop, step):
        return remote(
            r.kv_core.at[hop, step],
            r.kv_cross.at[hop, step],
            s.xy_send.at[hop, step],
            s.xy_recv.at[hop, step],
            {"ulysses": lax.rem(u + hop, n_u)},
        )

    def along_z(step):
        return remote(
            r.kv_plane.at[step],
            r.kv_line.at[step],
            s.z_send.at[step],
            s.z_recv.at[step],
            {"blk": lax.rem(z + step, n_z) * 2 + c},
        )

    block_rows = MODEL_WIDTH // n_u

    def weight_grad(k):
        hop = lax.rem(k + 1, n_u)
        row = lax.rem(u + hop, n_u)
        columns = pl.ds(pl.multiple_of(row * block_rows, block_rows), block_rows)
        r.kv_grad[row] = (
            mm_outer(r.normed_keys[:, columns], r.grad_kv[...])
            .astype(bf16)
            .reshape(r.kv_grad.shape[1:])
        )
        each(n_z, lambda step: to_core(hop, step).start())

    each(n_u, weight_grad)
    query_part.finish()
    upstream = sum_blocks(r.query_got).astype(bf16).astype(f32)
    r.gain_query_row[...] = jnp.zeros((1, HEAD_WIDTH), f32)
    for k in range(upstream.shape[1] // HEAD_WIDTH):
        part = slice(k * HEAD_WIDTH, (k + 1) * HEAD_WIDTH)
        grad_head, gain_head = norm_back_rows(
            r.query_raw[:, part],
            r.gain_query[...],
            turned(upstream[:, part], r.rope_cos[places:], -r.rope_sin[places:]),
        )
        r.grad_low[:, part] = grad_head.astype(bf16)
        r.gain_query_row[...] += gain_head
    r.partial[...] = (
        mm_back(r.grad_low[...], r.q_weight[...].reshape(MODEL_WIDTH, -1))
        .astype(bf16)
        .reshape(r.partial.shape)
    )
    back = links("sum_query", r.partial, r.partial_got.at[2])

    def add_pair(hop):
        def one(step):
            row, line = place(hop, step)
            to_core(hop, step).wait_recv()
            r.kv_core[hop, step] = (
                r.kv_grad[row, line, c].astype(f32) + r.kv_core[hop, step].astype(f32)
            ).astype(bf16)

        return one

    def forward_hop(hop):
        def forward(step):
            add_pair(hop)(step)
            across(hop, step).start()

        each(n_z, forward)

    each(n_u, forward_hop, 1)
    each(n_z, add_pair(0))
    r.grad_q[...] = (
        mm_outer(flat_rows_of(r.normed_slot), r.grad_low[...]).astype(bf16).reshape(r.grad_q.shape)
    )
    q_part = links("q", r.grad_q, r.q_got)
    back.finish()
    grad_mine, gain_attn = norm_back_rows(
        r.pick_rows[:, :MODEL_WIDTH], r.gain_attn[...], sum_blocks(r.partial_got.at[2])
    )
    r.mine_low[...] = (grad_attn + grad_mine).astype(bf16)
    pick_part = links("pick_back", r.mine_low, r.pick_back)

    def row_grad(k):
        columns = pl.ds(pl.multiple_of(k * block_rows, block_rows), block_rows)
        r.grad_wide[:, columns] = mm_back(
            r.grad_kv[...], r.kv_weight[k].reshape(block_rows, -1)
        )

    each(n_u, row_grad)
    grad_rows, gain_keys = norm_back_rows(wide, r.gain_attn[...], r.grad_wide[...])
    pick_part.finish()
    pick_hot = jnp.where(r.key_pos[...] == r.slot_picked[...], 1.0, 0.0).astype(bf16)
    r.rows_send[...] = (
        (grad_rows + mm(pick_hot, flat_rows_of(r.pick_back)))
        .astype(bf16)
        .reshape(r.rows_send.shape)
    )
    rows_part = links("rows", r.rows_send, r.rows_back)

    r.gain_mlp_row[...] = gain_mlp
    r.gain_final_row[...] = gain_final
    r.gain_picks_row[...] = gain_attn
    r.gain_rows_row[...] = gain_keys
    r.gains_mine[...] = jnp.zeros_like(r.gains_mine)
    lines = MODEL_WIDTH // 128
    for j in range(lines):
        part = slice(j * 128, (j + 1) * 128)
        r.gains_mine[j : j + 1, :] = r.gain_picks_row[:, part] + r.gain_rows_row[:, part]
        r.gains_mine[lines + j : lines + j + 1, :] = r.gain_mlp_row[:, part]
        r.gains_mine[2 * lines + j : 2 * lines + j + 1, :] = r.gain_final_row[:, part]
    r.gains_mine[3 * lines : 3 * lines + 1, :] = r.gain_query_row[...]
    r.gains_mine[3 * lines + 1 : 3 * lines + 2, :] = r.gain_key_row[...]
    gains_part = links("gains_blk", r.gains_mine, r.gains_got)

    ff_part.finish()
    r.ff_sum[...] = sum_blocks(r.ff_got).astype(bf16)
    ff_last = links("ff_cols", r.ff_sum, r.ff_out)
    down_part.finish()
    r.down_out[...] = sum_blocks(r.down_got)
    out_part.finish()
    r.out_out[...] = sum_blocks(r.out_got)
    gains_part.finish()
    r.gains_slot[...] = sum_blocks(r.gains_got)
    gains_last = links("gains_ulysses", r.gains_slot, r.gains_all)
    q_part.finish()
    r.q_sum[...] = sum_blocks(r.q_got).astype(bf16)
    q_last = links("q_cols", r.q_sum, r.q_out)

    def plane_sum(step):
        total = r.kv_core[0, step].astype(f32)
        for hop in range(1, n_u):
            across(hop, step).wait_recv()
            total = total + r.kv_cross[hop, step].astype(f32)
        return total

    def add_plane(step):
        r.kv_plane[step] = plane_sum(step).astype(bf16)
        along_z(step).start()

    each(n_z, add_plane, 1)
    total = plane_sum(0)
    for step in range(1, n_z):
        along_z(step).wait_recv()
        total = total + r.kv_line[step].astype(f32)
    r.inflow_out[:, QUERY_WIDTH:] = total
    gains_last.finish()
    gains = sum_blocks(r.gains_all)
    r.gains_out[...] = gains
    for part in (norms_part, ff_last, q_last, rows_part):
        part.finish()
    q_share = r.q_out.shape[2]
    for k in range(n_b):
        r.inflow_out[:, k * q_share : (k + 1) * q_share] = r.q_out[k].astype(f32)
    for k, there, here in ff_cuts(n_u, n_b):
        r.expand_out[:, here] = r.ff_out[k, :, there].astype(f32)
    squares = jnp.sum(gains * gains) / (n_u * n_b)
    for ref in (r.inflow_out, r.expand_out, r.out_out, r.down_out):
        squares += jnp.sum(ref[...] * ref[...])
    r.squares[...] = jnp.full(r.squares.shape, squares, f32)
    each(n_z, lambda step: each(n_u, lambda hop: to_core(hop, step).wait_send()))
    each(n_z, lambda step: each(n_u, lambda hop: across(hop, step).wait_send(), 1))
    each(n_z, lambda step: along_z(step).wait_send(), 1)


def lookup_kernel(slots, fills_ref, ids_ref, table_ref, rows_ref, wide, sem):
    wide[...] = jnp.zeros_like(wide)

    def row_copy(place, row):
        return pltpu.make_async_copy(
            table_ref.at[pl.ds(row, 1), :], wide.at[pl.ds(place, 1), :], sem
        )

    def of_peer(peer, total):
        fill = fills_ref[peer]

        def fetch(k, carry):
            place = peer * slots + k
            row_copy(place, ids_ref[place]).start()
            return carry

        lax.fori_loop(0, fill, fetch, 0)
        return total + fill

    total = lax.fori_loop(0, fills_ref.shape[0], of_peer, 0)

    def drain(k, carry):
        row_copy(0, 0).wait()
        return carry

    lax.fori_loop(0, total, drain, 0)
    rows_ref[...] = wide[...].astype(rows_ref.dtype)


def lookup(fills, ids, table, slots):
    places = ids.shape[0]
    return pl.pallas_call(
        functools.partial(lookup_kernel, slots),
        out_shape=jax.ShapeDtypeStruct((places, table.shape[1]), bf16),
        in_specs=[
            pl.BlockSpec(memory_space=pltpu.SMEM),
            pl.BlockSpec(memory_space=pltpu.SMEM),
            pl.BlockSpec(memory_space=pl.ANY),
        ],
        out_specs=VMEM,
        scratch_shapes=[
            pltpu.VMEM((places, table.shape[1]), f32),
            pltpu.SemaphoreType.DMA,
        ],
        compiler_params=pltpu.CompilerParams(vmem_limit_bytes=40 * 1024 * 1024),
        name="lookup",
    )(fills, ids, table)


def table_tile(share):
    return -(-share // (9 * 16)) * 16


def table_grad_kernel(
    limit, logits, finals, norms, weights, targets, rows, row_ids, grad_out, squares
):
    tile = grad_out.shape[0]
    start = pl.program_id(0) * tile
    ids = start + lax.broadcasted_iota(jnp.int32, (tile, 1), 0)
    grad_logits = (
        weights[...]
        * (jnp.exp(logits[...] - norms[...]) - jnp.where(targets[...] == ids, 1.0, 0.0))
    ).astype(bf16)
    hot = jnp.where(row_ids[...] == ids, 1.0, 0.0).astype(bf16)
    grad = mm(grad_logits, finals[...]) + mm(hot, rows[...])
    grad_out[...] = grad.astype(bf16)

    @pl.when(pl.program_id(0) == 0)
    def _():
        squares[...] = jnp.zeros_like(squares)

    squares[...] += jnp.sum(jnp.where(ids < limit, grad * grad, 0.0), axis=0, keepdims=True)


def table_grad_call(logits, finals, norms, weights, targets, rows, row_ids):
    share, picks = logits.shape
    places, width = rows.shape
    tile = table_tile(share)
    whole = lambda *shape: pl.BlockSpec(shape, lambda i: (0, 0))
    return pl.pallas_call(
        functools.partial(table_grad_kernel, share),
        grid=(pl.cdiv(share, tile),),
        out_shape=[
            jax.ShapeDtypeStruct((share, width), bf16),
            jax.ShapeDtypeStruct((1, width), f32),
        ],
        in_specs=[
            pl.BlockSpec((tile, picks), lambda i: (i, 0)),
            whole(picks, width),
            whole(1, picks),
            whole(1, picks),
            whole(1, picks),
            whole(places, width),
            whole(1, places),
        ],
        out_specs=[
            pl.BlockSpec((tile, width), lambda i: (i, 0)),
            whole(1, width),
        ],
        compiler_params=pltpu.CompilerParams(vmem_limit_bytes=40 * 1024 * 1024),
        cost_estimate=pl.CostEstimate(
            flops=2 * share * width * (picks + places),
            bytes_accessed=share * (4 * picks + 2 * width),
            transcendentals=share * picks,
        ),
        name="table_grad",
    )(logits, finals, norms, weights, targets, rows, row_ids)


def adam_kernel(rate, decay, numbers, weight, first, second, grad, change, new_first, new_second):
    gradient = grad[...].astype(f32) * numbers[0]
    mean = beta_first * first[...] + (1.0 - beta_first) * gradient
    square = beta_second * second[...] + (1.0 - beta_second) * gradient * gradient
    new_first[...] = mean
    new_second[...] = square
    change[...] = -rate * (
        mean * numbers[1] / (jnp.sqrt(square * numbers[2]) + adam_eps) + decay * weight[...]
    )


def layer_adam_kernel(rates, decays, numbers, *refs):
    count = len(rates)
    for k in range(count):
        weight, first, second, grad = refs[4 * k : 4 * k + 4]
        adam_kernel(rates[k], decays[k], numbers, weight, first, second, grad, *refs[4 * count + 3 * k :][:3])


def layer_adam_call(numbers, groups, rates, decays):
    arrays = [array for group in groups for array in group]
    return pl.pallas_call(
        functools.partial(layer_adam_kernel, rates, decays),
        out_shape=[
            jax.ShapeDtypeStruct(group[0].shape, f32) for group in groups for _ in range(3)
        ],
        in_specs=[pl.BlockSpec(memory_space=pltpu.SMEM)] + [VMEM] * len(arrays),
        out_specs=[VMEM] * (3 * len(groups)),
        compiler_params=pltpu.CompilerParams(vmem_limit_bytes=32 * 1024 * 1024),
        name="layer_adam",
    )(numbers, *arrays)


def adam_call(numbers, weight, first, second, grad, rate, decay):
    share, width = weight.shape
    tile = table_tile(share)
    block = pl.BlockSpec((tile, width), lambda i: (i, 0))
    return pl.pallas_call(
        functools.partial(adam_kernel, rate, decay),
        grid=(pl.cdiv(share, tile),),
        out_shape=[jax.ShapeDtypeStruct((share, width), f32)] * 3,
        in_specs=[pl.BlockSpec(memory_space=pltpu.SMEM)] + [block] * 4,
        out_specs=[block] * 3,
        compiler_params=pltpu.CompilerParams(vmem_limit_bytes=48 * 1024 * 1024),
        name="adam",
    )(numbers, weight, first, second, grad)


def local(
    tokens,
    lengths,
    picked,
    targets,
    advantages,
    step_count,
    embedding,
    first_embedding,
    second_embedding,
    inflow,
    inflow_first_moment,
    inflow_second_moment,
    outflow,
    first_outflow,
    second_outflow,
    expand,
    first_expand,
    second_expand,
    contract,
    first_contract,
    second_contract,
    scales,
    first_scales,
    second_scales,
):
    exchange = Exchanger()
    n_u, n_b = lax.axis_size("ulysses"), lax.axis_size("blk")
    n_all = n_u * n_b
    n_z = n_b // 2
    u, b = lax.axis_index("ulysses"), lax.axis_index("blk")
    me = u * n_b + b
    slot_count, block_len = tokens.shape
    assert slot_count == n_u and n_b % 2 == 0
    picks = picked.shape[1]
    slot_picks = picks * n_b
    all_picks = slot_picks * n_u
    row_share = embedding.shape[0]
    group = QUERY_HEADS // KEY_VALUE_HEADS
    score_scale = HEAD_WIDTH ** (-0.5)
    in_rows, out_share, ff_share = inflow.shape[0], outflow.shape[0], contract.shape[0]
    q_share = QUERY_WIDTH // n_b
    heads_share = q_share // HEAD_WIDTH
    ff_mine = n_u * ff_share
    out_cut = QUERY_WIDTH // n_all
    scale_share = scales.shape[0]

    width = KEY_VALUE_HEADS * HEAD_WIDTH
    wants_mean = n_b * (block_len + picks) / n_all
    slots = -(-int(wants_mean + 5.2 * math.sqrt(wants_mean)) // 16) * 16
    places = n_u * slots
    blk_g = ("blk", "g")
    column = ((places, 1), jnp.int32)
    row_wide = ((1, MODEL_WIDTH), f32)
    head_wide = ((1, HEAD_WIDTH), f32)
    begin = named_call(
        exchange,
        functools.partial(begin_body, n_u, n_b, row_share, slots),
        {
            "tokens": blk_g,
            "targets": blk_g,
            "picked": blk_g,
            "advantages": blk_g,
            "near": blk_g,
            "far": ("ulysses", "g"),
        },
        {},
        {
            "tokens": tokens,
            "targets": targets,
            "picked": picked,
            "advantages": advantages,
            "lengths": lengths[:, None],
            "scales": scales[None, :],
        },
        {
            "tokens_all": ((n_b,) + tokens.shape, jnp.int32),
            "targets_all": ((n_b,) + targets.shape, jnp.int32),
            "slot_picked": ((1, slot_picks), jnp.int32),
            "weights": ((1, all_picks), f32),
            "target_ids": ((1, all_picks), jnp.int32),
            "weight_wide": ((picks, 128), f32),
            "row_ids": column,
            "key_pos": column,
            "key_lim": column,
            "target_of": column,
            "positions": ((places + slot_picks, 1), jnp.int32),
            "meta": ((24, 128), f32),
            "gain_attn": row_wide,
            "gain_mlp": row_wide,
            "gain_final": row_wide,
            "gain_query": head_wide,
            "gain_key": head_wide,
        },
        {
            "picked_all": ((n_b,) + picked.shape, jnp.int32),
            "advantages_all": ((n_b,) + advantages.shape, f32),
            "near": ((n_b, 1, scale_share), f32),
            "far": ((n_u, n_b, 1, scale_share), f32),
            "wants": ((n_u, block_len + picks), jnp.int32),
            "masks": ((2 * n_u, block_len + picks), f32),
            "labels": ((2 * n_u, block_len + picks), f32),
            "ranks": ((2 * n_u, block_len + picks), f32),
            "gains": ((1, n_all * scale_share), f32),
        },
        "begin",
    )
    gain_rows = [
        begin.gain_attn,
        begin.gain_mlp,
        begin.gain_final,
        begin.gain_query,
        begin.gain_key,
    ]
    gain_attn, gain_query, gain_key = begin.gain_attn[0], begin.gain_query[0], begin.gain_key[0]
    slot_picked = begin.slot_picked[0]
    rounds = (jnp.max(begin.meta[8 : 8 + n_u, 0]).astype(jnp.int32) + slots - 1) // slots
    count_local = begin.meta[16, 0]
    half = HEAD_WIDTH // 2
    lane = jnp.arange(HEAD_WIDTH, dtype=jnp.int32)
    frequency = rope_base ** (-((lane % half).astype(f32) * 2.0 / HEAD_WIDTH))
    angles = begin.positions.astype(f32) * frequency[None, :]
    rope_cos = jnp.cos(angles)
    rope_sin = jnp.sin(angles) * jnp.where(lane < half, -1.0, 1.0)[None, :]
    query_cos, query_sin = rope_cos[places:], rope_sin[places:]
    ff_width = 2 * ff_mine
    own_cut = n_u * out_cut
    rows_low = (picks, MODEL_WIDTH)
    slot_low = (n_b, picks, MODEL_WIDTH)
    stat_rows = (8, slot_picks)
    weight_wide = begin.weight_wide

    def fetch(fills, row_ids):
        rows = lookup(fills, jnp.maximum(row_ids, 0), embedding, slots)
        return rows.reshape(n_u, slots, MODEL_WIDTH)

    def widen_ff(array):
        return (
            array.astype(f32)
            .reshape(n_b, in_rows, 2, n_u, ff_share)
            .transpose(1, 2, 3, 0, 4)
            .reshape(in_rows, 2 * FF)
        )

    def head_of_table(final_all):
        table_low = embedding.astype(bf16)
        logits = mm_back(table_low, final_all)
        local_max = jnp.max(logits, axis=0)
        head_weights = jnp.exp(logits - local_max[None, :])
        local_sum = jnp.sum(head_weights, axis=0)
        head_rows = mm_outer(head_weights.astype(bf16), table_low).astype(bf16)
        head_stats = jnp.pad(
            jnp.stack([local_max, local_sum]).reshape(2, n_u, slot_picks).transpose(1, 0, 2),
            ((0, 0), (0, 6), (0, 0)),
        )
        return (logits, head_rows.reshape(n_u, slot_picks, MODEL_WIDTH), head_stats)

    def usual_way():
        fills = jnp.minimum(begin.meta[:n_u, 0].astype(jnp.int32), slots)
        lined = {
            "key_pos": begin.key_pos,
            "key_lim": begin.key_lim,
            "slot_picked": begin.slot_picked,
            "gain_attn": gain_rows[0],
            "gain_mlp": gain_rows[1],
            "gain_final": gain_rows[2],
            "gain_query": gain_rows[3],
            "gain_key": gain_rows[4],
            "rope_cos": rope_cos,
            "rope_sin": rope_sin,
        }
        kv_block = (in_rows, 2 * width)
        kv_shape = (n_u, n_z, 2) + kv_block
        q_shape = (n_u, n_b, in_rows, q_share)
        ff_shape = (n_u, n_b, in_rows, ff_width)
        out_shape = (n_u, out_share, MODEL_WIDTH)
        down_shape = (n_u, ff_share, MODEL_WIDTH)
        rows_shape = (n_u, slots, MODEL_WIDTH)
        blk_s, blk_g = ("blk", "s"), ("blk", "g")
        uly_s, uly_g = ("ulysses", "s"), ("ulysses", "g")
        rise = named_call(
            exchange,
            functools.partial(rise_body, n_u, n_b),
            {
                "rows": uly_s,
                "q_split": blk_s,
                "ff_split": blk_s,
                "picks": blk_s,
                "q_all": uly_g,
                "normed": blk_g,
                "queries": blk_g,
                "out_all": uly_g,
                "ff_all": uly_g,
                "down_all": uly_g,
                "parts": blk_s,
                "stats": blk_g,
                "sum_out": blk_s,
                "normed_mlp": blk_g,
                "sum_mlp": blk_s,
                "final": blk_g,
                "final_all": uly_g,
            },
            {
                "z_send": (n_z,),
                "z_recv": (n_z,),
                "own": (1,),
                "xy_send": (n_u, n_z),
                "xy_recv": (n_u, n_z),
                "core_send": (n_u, n_z),
                "core_recv": (n_u, n_z),
            },
            {
                "rows_in": fetch(fills, begin.row_ids.reshape(-1)),
                "inflow": inflow,
                "expand": expand,
                "outflow": outflow,
                "contract": contract,
                "target_of": begin.target_of,
                **lined,
            },
            {
                "arrived": (rows_shape, bf16),
                "kv_weight": (kv_shape, bf16),
                "q_weight": (q_shape, bf16),
                "ff_weight": (ff_shape, bf16),
                "out_weight": (out_shape, bf16),
                "down_weight": (down_shape, bf16),
                "pick_rows": ((picks, 2 * MODEL_WIDTH), f32),
                "normed_slot": (slot_low, bf16),
                "query_raw": ((slot_picks, q_share), f32),
                "query_all": ((n_b, slot_picks, q_share), bf16),
                "key_raw": ((places, width), f32),
                "key_rot": ((places, width), bf16),
                "values": ((places, width), bf16),
                "attended": ((slot_picks, own_cut), f32),
                "log_total": ((QUERY_HEADS, slot_picks), f32),
                "after_attn": (rows_low, f32),
                "normed_mlp": (slot_low, bf16),
                "gate_up": ((slot_picks, ff_width), f32),
                "after_mlp": (rows_low, f32),
                "final_mine": (rows_low, bf16),
                "final_all": ((n_u,) + slot_low, bf16),
            },
            {
                "kv_in": (kv_block, bf16),
                "q_in": (q_shape[1:], bf16),
                "ff_in": (ff_shape[1:], bf16),
                "out_in": (out_shape[1:], bf16),
                "down_in": (down_shape[1:], bf16),
                "q_part": (q_shape[1:], bf16),
                "ff_part": (ff_shape[1:], bf16),
                "pick_send": ((n_b, picks, 2 * MODEL_WIDTH), bf16),
                "pick_got": ((n_b, picks, 2 * MODEL_WIDTH), bf16),
                "normed_mine": (rows_low, bf16),
                "normed_keys": ((places, MODEL_WIDTH), bf16),
                "query_mine": ((slot_picks, q_share), bf16),
                "part_send": ((n_b, slot_picks, own_cut), bf16),
                "part_got": ((n_b, slot_picks, own_cut), bf16),
                "stats": ((2 * QUERY_HEADS, slot_picks), f32),
                "stats_all": ((n_b, 2 * QUERY_HEADS, slot_picks), f32),
                "shares": ((n_b * n_u, slot_picks), f32),
                "partial": (slot_low, bf16),
                "partial_got": ((2,) + slot_low, bf16),
                "final_slot": (slot_low, bf16),
            },
            "rise",
        )
        final_all = rise.final_all.reshape(all_picks, MODEL_WIDTH)
        logits, head_rows, head_stats = head_of_table(final_all)
        kept = (
            "arrived",
            "kv_weight",
            "q_weight",
            "ff_weight",
            "out_weight",
            "down_weight",
            "pick_rows",
            "normed_slot",
            "query_raw",
            "query_all",
            "key_raw",
            "key_rot",
            "values",
            "attended",
            "log_total",
            "after_attn",
            "normed_mlp",
            "gate_up",
            "after_mlp",
            "final_mine",
        )
        fall = named_call(
            exchange,
            functools.partial(fall_body, n_u, n_b),
            {
                "head_rows": uly_s,
                "head_stats": uly_s,
                "slot_stats": blk_g,
                "slot_rows": blk_s,
                "norms": uly_g,
                "branch": blk_g,
                "sum_ff": blk_s,
                "down": uly_s,
                "ff": uly_s,
                "branch_attn": blk_g,
                "attended": blk_g,
                "deltas": blk_g,
                "out": uly_s,
                "grad_queries": blk_s,
                "sum_query": blk_s,
                "q": uly_s,
                "pick_back": blk_g,
                "rows": uly_s,
                "gains_blk": blk_g,
                "gains_ulysses": uly_g,
                "ff_cols": blk_s,
                "q_cols": blk_s,
            },
            {
                "core_send": (n_u, n_z),
                "core_recv": (n_u, n_z),
                "xy_send": (n_u, n_z),
                "xy_recv": (n_u, n_z),
                "z_send": (n_z,),
                "z_recv": (n_z,),
            },
            {
                "head_rows": head_rows,
                "head_stats": head_stats,
                "weights": weight_wide,
                **{key: getattr(rise, key) for key in kept},
                **lined,
            },
            {
                "norms_all": ((n_u,) + stat_rows, f32),
                "terms": ((picks, 128), f32),
                "rows_back": (rows_shape, bf16),
                "inflow_out": (inflow.shape, f32),
                "expand_out": (expand.shape, f32),
                "out_out": (out_shape[1:], f32),
                "down_out": (down_shape[1:], f32),
                "gains_out": ((32, 128), f32),
                "squares": ((8, 128), f32),
            },
            {
                "rows_got": ((n_u, slot_picks, MODEL_WIDTH), bf16),
                "stats_got": ((n_u,) + stat_rows, f32),
                "slot_stats": (stat_rows, f32),
                "slot_got": ((n_b,) + stat_rows, f32),
                "factors": ((n_b + 8, slot_picks), f32),
                "columns": ((slot_picks, n_b + 8), f32),
                "norms_mine": (stat_rows, f32),
                "partial": (slot_low, bf16),
                "partial_got": ((3,) + slot_low, bf16),
                "mine_low": (rows_low, bf16),
                "grad_all": (slot_low, bf16),
                "branch_all": (slot_low, bf16),
                "grad_down": (down_shape, bf16),
                "down_got": (down_shape, bf16),
                "grad_ff": (ff_shape, bf16),
                "ff_got": (ff_shape, bf16),
                "grad_out": (out_shape, bf16),
                "out_got": (out_shape, bf16),
                "attended_mine": ((slot_picks, own_cut), bf16),
                "attended_all": ((n_b, slot_picks, own_cut), bf16),
                "deltas": ((slot_picks, 128), f32),
                "delta_mine": (stat_rows, f32),
                "delta_all": ((n_b,) + stat_rows, f32),
                "normed_keys": ((places, MODEL_WIDTH), bf16),
                "query_send": ((n_b, slot_picks, q_share), bf16),
                "query_got": ((n_b, slot_picks, q_share), bf16),
                "grad_kv": ((places, 2 * width), bf16),
                "kv_grad": (kv_shape, bf16),
                "kv_core": ((n_u, n_z) + kv_block, bf16),
                "kv_cross": ((n_u, n_z) + kv_block, bf16),
                "kv_plane": ((n_z,) + kv_block, bf16),
                "kv_line": ((n_z,) + kv_block, bf16),
                "grad_low": ((slot_picks, q_share), bf16),
                "grad_q": (q_shape, bf16),
                "q_got": (q_shape, bf16),
                "q_sum": (q_shape[1:], bf16),
                "pick_back": (slot_low, bf16),
                "grad_wide": ((places, MODEL_WIDTH), f32),
                "rows_send": (rows_shape, bf16),
                "gain_mlp_row": ((1, MODEL_WIDTH), f32),
                "gain_final_row": ((1, MODEL_WIDTH), f32),
                "gain_picks_row": ((1, MODEL_WIDTH), f32),
                "gain_rows_row": ((1, MODEL_WIDTH), f32),
                "gain_query_row": ((1, HEAD_WIDTH), f32),
                "gain_key_row": ((1, HEAD_WIDTH), f32),
                "gains_mine": ((32, 128), f32),
                "gains_got": ((n_b, 32, 128), f32),
                "gains_slot": ((32, 128), f32),
                "gains_all": ((n_u, 32, 128), f32),
                "ff_sum": (ff_shape[1:], bf16),
                "q_out": (q_shape[1:], bf16),
                "ff_out": (ff_shape[1:], bf16),
            },
            "fall",
        )
        table_grad, table_squares = table_grad_call(
            logits,
            final_all,
            fall.norms_all[:, 0].reshape(1, all_picks),
            begin.weights,
            begin.target_ids,
            fall.rows_back.reshape(places, MODEL_WIDTH),
            begin.row_ids.reshape(1, places),
        )
        return (
            -jnp.sum(fall.terms[:, 0]),
            fall.squares[0, 0] + jnp.sum(table_squares),
            table_grad,
            fall.inflow_out,
            fall.out_out,
            fall.expand_out,
            fall.down_out,
            lax.dynamic_slice_in_dim(fall.gains_out.reshape(-1), me * scale_share, scale_share),
        )

    def long_way():
        inflow_low = inflow.astype(bf16)
        q_cols = inflow_low[:, :QUERY_WIDTH].reshape(in_rows, n_b, q_share).transpose(1, 0, 2)
        ff_cols = (
            expand.astype(bf16)
            .reshape(in_rows, 2, n_u, n_b, ff_share)
            .transpose(3, 0, 1, 2, 4)
            .reshape(n_b, in_rows, 2 * ff_mine)
        )
        wants_block = block_len + picks
        wants_count = n_b * wants_block
        wants = (
            jnp.concatenate([begin.tokens_all, begin.targets_all], axis=2)
            .transpose(1, 0, 2)
            .reshape(n_u, wants_count)
        )
        my_length = lax.dynamic_index_in_dim(lengths, u, 0, keepdims=False)
        owners = wants // row_share
        own_owners = lax.dynamic_index_in_dim(owners, u, 0, keepdims=True)
        sent_mask = owners == me
        got_mask = own_owners == jnp.arange(n_u, dtype=jnp.int32)[:, None] * n_b + b
        masks = jnp.concatenate([sent_mask, got_mask], axis=0)
        totals_sent = jnp.sum(sent_mask.astype(f32), axis=1).astype(jnp.int32)
        lanes = math.gcd(wants_count, 128)
        blocks = masks.astype(bf16).reshape(2 * n_u, wants_count // lanes, lanes)
        before = (jnp.arange(lanes)[:, None] < jnp.arange(lanes)[None, :]).astype(bf16)
        block_sums = jnp.sum(blocks.astype(f32), axis=-1)
        chunk = jnp.arange(wants_count // lanes)
        block_base = mm(block_sums.astype(bf16), (chunk[:, None] < chunk[None, :]).astype(bf16))
        ranks = (
            mm(blocks.reshape(-1, lanes), before).reshape(blocks.shape) + block_base[:, :, None]
        ).reshape(2 * n_u, wants_count)
        ranks = jnp.where(masks, ranks.astype(jnp.int32), -1)
        labels = jnp.concatenate(
            [
                wants - me * row_share,
                jnp.broadcast_to(
                    jnp.arange(wants_count, dtype=jnp.int32)[None, :], (n_u, wants_count)
                ),
            ],
            axis=0,
        )

        def slot_tables(turn, hot):
            slot_rank = turn * slots + jnp.arange(slots, dtype=jnp.int32)
            hit = ranks[:, None, :] == slot_rank[None, :, None]
            found = jnp.sum(jnp.where(hit, labels[:, None, :] + 1, 0), axis=-1) - 1
            fills = jnp.clip(totals_sent - turn * slots, 0, slots)
            row_ids = found[:n_u].reshape(-1)
            entry = found[n_u:].reshape(-1)
            block, inside = entry // wants_block, entry % wants_block
            is_token = (entry >= 0) & (inside < block_len)
            key_pos = jnp.where(is_token, block * block_len + inside, 1 << 30)
            target_of = jnp.where(
                (entry >= 0) & (inside >= block_len), block * picks + inside - block_len, -1
            )
            if not hot:
                return (row_ids, fills, key_pos, None, target_of)
            pick_hot = (slot_picked[:, None] == key_pos[None, :]).astype(bf16)
            target_hot = (jnp.arange(slot_picks)[:, None] == target_of[None, :]).astype(bf16)
            return (row_ids, fills, key_pos, pick_hot, target_hot)

        row_ids, fills, key_pos, pick_hot, target_hot = slot_tables(jnp.int32(0), True)

        arrived, kv_weight, q_weight, ff_split = start_call(
            exchange, fetch(fills, row_ids), inflow_low[:, QUERY_WIDTH:], q_cols, ff_cols
        )
        arrived = arrived.reshape(places, MODEL_WIDTH)
        kv_weight = kv_weight.reshape(MODEL_WIDTH, -1)
        q_weight = q_weight.reshape(MODEL_WIDTH, q_share)
        def picked_rows(pick_hot, target_hot, arrived):
            return jnp.concatenate([mm(pick_hot, arrived), mm(target_hot, arrived)], axis=1)

        refetch_id = [exchange.next_id() for _ in range(5)]

        def refetch(turn, which):
            tables = slot_tables(turn, True)
            (got,) = exchange.many(
                (("ulysses", "s"),), fetch(tables[1], tables[0]), collective_id=refetch_id[which]
            )
            return (tables, got.reshape(places, MODEL_WIDTH))

        def more(state):
            return state[0] < rounds

        def picks_turn(state):
            tables, got = refetch(state[0], 0)
            return (state[0] + 1, state[1] + picked_rows(tables[3], tables[4], got))

        pick_part = picked_rows(pick_hot, target_hot, arrived)
        _, pick_part = lax.while_loop(more, picks_turn, (jnp.int32(1), pick_part))
        got_picks, normed_slot, query_raw, query_all, ff_all, out_all, down_all = fused_call(
            exchange,
            functools.partial(query_body, n_b),
            (("blk", "s"), ("blk", "g"), ("blk", "g")) + (("ulysses", "g"),) * 3,
            (
                pick_part.astype(bf16).reshape(n_b, picks, 2 * MODEL_WIDTH),
                gain_rows[0],
                gain_rows[3],
                q_weight,
                query_cos,
                query_sin,
                ff_split,
                outflow.astype(bf16),
                contract.astype(bf16),
            ),
            (
                ((picks, 2 * MODEL_WIDTH), f32),
                (slot_low, bf16),
                ((slot_picks, q_share), f32),
                ((n_b, slot_picks, q_share), bf16),
                ((n_u, n_b, in_rows, ff_width), bf16),
                ((n_u, out_share, MODEL_WIDTH), bf16),
                ((n_u, ff_share, MODEL_WIDTH), bf16),
            ),
            (
                ((n_b, picks, 2 * MODEL_WIDTH), bf16),
                (rows_low, bf16),
                ((slot_picks, q_share), bf16),
            ),
            "queries",
        )
        ff_weight = ff_all.reshape(MODEL_WIDTH, ff_width)
        out_weight = out_all.reshape(n_u * out_share, MODEL_WIDTH)
        down_weight = down_all.reshape(ff_mine, MODEL_WIDTH)

        def keys_of(arrived, key_pos):
            embedded = arrived.astype(f32)
            normed = (embedded * inverse_root(embedded) * gain_attn).astype(bf16)
            mixed = mm(normed, kv_weight)
            half = KEY_VALUE_HEADS * HEAD_WIDTH
            key_raw = mixed[:, :half].reshape(places, KEY_VALUE_HEADS, HEAD_WIDTH)
            values = mixed[:, half:].reshape(places, KEY_VALUE_HEADS, HEAD_WIDTH)
            angle_tables = rope_angles(jnp.where(key_pos < (1 << 30), key_pos, 0))
            key_rot = rotate(key_raw * inverse_root(key_raw) * gain_key, angle_tables, 1.0)
            return (
                embedded,
                normed,
                key_raw,
                angle_tables,
                key_rot.astype(bf16).transpose(1, 0, 2),
                values.astype(bf16).transpose(1, 0, 2),
            )

        query_pos = jnp.tile(slot_picked, group)

        def allowed_of(key_pos):
            return ((key_pos[None, :] <= query_pos[:, None]) & (key_pos[None, :] < my_length))[None]

        def scores_of(query_groups, key_rot, allowed):
            scores = (
                jnp.einsum("kqd,kjd->kqj", query_groups, key_rot, preferred_element_type=f32)
                * score_scale
            )
            return jnp.where(allowed, scores, masked_score)

        def attend(scores, allowed, values):
            part_max = jnp.max(scores, axis=-1, keepdims=True)
            weights = jnp.where(allowed, jnp.exp(scores - part_max), 0.0)
            out = jnp.einsum("kqj,kjd->kqd", weights.astype(bf16), values, preferred_element_type=f32)
            return (part_max, jnp.sum(weights, axis=-1, keepdims=True), out)

        keys = keys_of(arrived, key_pos)

        query_groups = (
            query_all.reshape(n_b, slot_picks, heads_share, HEAD_WIDTH)
            .transpose(0, 2, 1, 3)
            .reshape(KEY_VALUE_HEADS, group * slot_picks, HEAD_WIDTH)
        )
        allowed = allowed_of(key_pos)
        scores = scores_of(query_groups, keys[4], allowed)

        def attend_turn(state):
            turn, top, total, out = state
            tables, got = refetch(turn, 1)
            keys_now = keys_of(got, tables[2])
            allowed_now = allowed_of(tables[2])
            new = attend(scores_of(query_groups, keys_now[4], allowed_now), allowed_now, keys_now[5])
            both = jnp.maximum(top, new[0])
            old_factor, new_factor = jnp.exp(top - both), jnp.exp(new[0] - both)
            return (
                turn + 1,
                both,
                total * old_factor + new[1] * new_factor,
                out * old_factor + new[2] * new_factor,
            )

        _, part_max, part_sum, part_out = lax.while_loop(
            more, attend_turn, (jnp.int32(1),) + attend(scores, allowed, keys[5])
        )
        part_send = (
            part_out.astype(bf16)
            .reshape(QUERY_HEADS, slot_picks, HEAD_WIDTH)
            .transpose(1, 0, 2)
            .reshape(slot_picks, n_u, n_b, out_cut)
            .transpose(2, 0, 1, 3)
            .reshape(n_b, slot_picks, n_u * out_cut)
        )
        stats = jnp.stack([part_max[..., 0], part_sum[..., 0]]).reshape(2 * QUERY_HEADS, slot_picks)
        (
            attended,
            log_total,
            after_attn,
            normed_mlp,
            gate_up,
            after_mlp,
            final_mine,
            final_all,
        ) = fused_call(
            exchange,
            functools.partial(forward_body, n_u, n_b),
            (("blk", "s"), ("blk", "g"), ("blk", "s"), ("blk", "g"), ("blk", "s"), ("blk", "g"))
            + (("ulysses", "g"),),
            (
                part_send,
                stats,
                got_picks,
                out_weight,
                ff_weight,
                down_weight,
                gain_rows[1],
                gain_rows[2],
            ),
            (
                ((slot_picks, own_cut), f32),
                ((QUERY_HEADS, slot_picks), f32),
                (rows_low, f32),
                (slot_low, bf16),
                ((slot_picks, ff_width), f32),
                (rows_low, f32),
                (rows_low, bf16),
                ((n_u,) + slot_low, bf16),
            ),
            (
                ((n_b, slot_picks, own_cut), bf16),
                ((n_b, 2 * QUERY_HEADS, slot_picks), f32),
                ((n_b * n_u, slot_picks), f32),
                (slot_low, bf16),
                ((2,) + slot_low, bf16),
                (rows_low, bf16),
                (slot_low, bf16),
            ),
            "forward",
        )

        final_all = final_all.reshape(all_picks, MODEL_WIDTH)
        logits, head_rows, head_stats = head_of_table(final_all)
        (
            norms_all,
            terms,
            grad_gain_mlp,
            grad_gain_final,
            grad_ff,
            grad_out,
            grad_down,
            grad_after_attn,
            _,
            got_attended,
            got_delta,
        ) = fused_call(
            exchange,
            functools.partial(backward_body, n_u, n_b),
            (
                ("ulysses", "s"),
                ("ulysses", "s"),
                ("blk", "s"),
                ("blk", "g"),
                ("ulysses", "g"),
                ("blk", "g"),
                ("blk", "s"),
                ("blk", "g"),
                ("blk", "g"),
                ("blk", "g"),
            ),
            (
                head_rows,
                head_stats,
                final_mine,
                got_picks,
                weight_wide,
                after_mlp,
                after_attn,
                gate_up,
                normed_mlp,
                attended,
                out_weight,
                ff_weight,
                down_weight,
                gain_rows[1],
                gain_rows[2],
            ),
            (
                ((n_u,) + stat_rows, f32),
                ((picks, 128), f32),
                ((1, MODEL_WIDTH), f32),
                ((1, MODEL_WIDTH), f32),
                ((n_u, n_b, in_rows, ff_width), bf16),
                ((n_u, out_share, MODEL_WIDTH), bf16),
                ((n_u, ff_share, MODEL_WIDTH), bf16),
                (rows_low, f32),
                (slot_low, bf16),
                ((n_b, slot_picks, own_cut), bf16),
                ((n_b,) + stat_rows, f32),
            ),
            (
                ((n_u, slot_picks, MODEL_WIDTH), bf16),
                ((n_u,) + stat_rows, f32),
                (stat_rows, f32),
                ((n_b,) + stat_rows, f32),
                ((n_b + 8, slot_picks), f32),
                ((slot_picks, n_b + 8), f32),
                (stat_rows, f32),
                (slot_low, bf16),
                ((2,) + slot_low, bf16),
                (rows_low, bf16),
                (slot_low, bf16),
                ((slot_picks, own_cut), bf16),
                ((slot_picks, 128), f32),
                (stat_rows, f32),
            ),
            "backward",
        )
        loss_local = -jnp.sum(terms[:, 0])
        grad_heads = (
            got_attended.reshape(n_b, slot_picks, n_u, out_cut)
            .transpose(1, 2, 0, 3)
            .reshape(slot_picks, QUERY_HEADS, HEAD_WIDTH)
            .transpose(1, 0, 2)
            .reshape(KEY_VALUE_HEADS, group * slot_picks, HEAD_WIDTH)
        )
        row_delta = jnp.sum(
            got_delta[:, :n_u].transpose(1, 0, 2).reshape(QUERY_HEADS, HEAD_WIDTH // out_cut, slot_picks), axis=1
        ).reshape(KEY_VALUE_HEADS, group * slot_picks, 1)
        log_groups = log_total.reshape(KEY_VALUE_HEADS, group * slot_picks, 1)

        def score_grads(scores, allowed, values):
            probs = jnp.where(allowed, jnp.exp(scores - log_groups), 0.0)
            grad_probs = jnp.einsum("kqd,kjd->kqj", grad_heads, values, preferred_element_type=f32)
            return (probs, (probs * (grad_probs - row_delta) * score_scale).astype(bf16))

        def query_grads(grad_scores, key_rot):
            return jnp.einsum("kqj,kjd->kqd", grad_scores, key_rot, preferred_element_type=f32)

        def key_grads(probs, grad_scores, keys):
            grad_key = jnp.einsum(
                "kqj,kqd->kjd", grad_scores, query_groups, preferred_element_type=f32
            )
            grad_value = jnp.einsum(
                "kqj,kqd->kjd", probs.astype(bf16), grad_heads, preferred_element_type=f32
            )
            upstream = rotate(
                grad_key.astype(bf16).astype(f32).transpose(1, 0, 2), keys[3], -1.0
            )
            grad_raw, grad_gain = norm_back(keys[2], gain_key, upstream)
            grad_kv = jnp.concatenate(
                [
                    grad_raw.reshape(places, -1).astype(bf16),
                    grad_value.astype(bf16).transpose(1, 0, 2).reshape(places, -1),
                ],
                axis=1,
            )
            return (grad_kv, grad_gain)

        def row_grads(grad_kv, keys):
            return norm_back(keys[0], gain_attn, mm_back(grad_kv, kv_weight))

        def redo(turn, which):
            tables, got = refetch(turn, which)
            keys_now = keys_of(got, tables[2])
            allowed_now = allowed_of(tables[2])
            scores_now = scores_of(query_groups, keys_now[4], allowed_now)
            return (tables, keys_now) + score_grads(scores_now, allowed_now, keys_now[5])

        def query_turn(state):
            _, keys_now, _, grad_scores_now = redo(state[0], 2)
            return (state[0] + 1, state[1] + query_grads(grad_scores_now, keys_now[4]))

        probs, grad_scores = score_grads(scores, allowed, keys[5])
        _, grad_query_part = lax.while_loop(
            more, query_turn, (jnp.int32(1), query_grads(grad_scores, keys[4]))
        )
        query_send = (
            grad_query_part.astype(bf16)
            .reshape(n_b, heads_share, slot_picks, HEAD_WIDTH)
            .transpose(0, 2, 1, 3)
            .reshape(n_b, slot_picks, q_share)
        )
        (
            grad_gain_query,
            grad_gain_picks,
            grad_q,
            pick_back,
            sum_ff,
            sum_outflow,
            sum_contract,
        ) = fused_call(
            exchange,
            query_back_body,
            (("blk", "s"), ("blk", "s"), ("blk", "g")) + (("ulysses", "s"),) * 3,
            (
                query_send,
                query_raw,
                query_cos,
                query_sin,
                gain_rows[3],
                q_weight,
                normed_slot,
                got_picks,
                gain_rows[0],
                grad_after_attn,
                grad_ff,
                grad_out,
                grad_down,
            ),
            (
                ((1, HEAD_WIDTH), f32),
                ((1, MODEL_WIDTH), f32),
                ((n_u, n_b, in_rows, q_share), bf16),
                (slot_low, bf16),
                ((n_b, in_rows, ff_width), bf16),
                ((out_share, MODEL_WIDTH), f32),
                ((ff_share, MODEL_WIDTH), f32),
            ),
            (
                ((n_b, slot_picks, q_share), bf16),
                ((slot_picks, q_share), bf16),
                (slot_low, bf16),
                (slot_low, bf16),
                (rows_low, bf16),
                ((n_u, n_b, in_rows, ff_width), bf16),
                ((n_u, out_share, MODEL_WIDTH), bf16),
                ((n_u, ff_share, MODEL_WIDTH), bf16),
            ),
            "query_grads",
        )
        pick_back = pick_back.reshape(slot_picks, MODEL_WIDTH)

        grad_kv, grad_gain_key = key_grads(probs, grad_scores, keys)
        grad_kv_weight = mm_outer(keys[1], grad_kv)
        grad_rows, grad_gain_attn = row_grads(grad_kv, keys)

        def weight_turn(state):
            turn, weight_sum, key_sum, attn_sum = state
            _, keys_now, probs_now, grad_scores_now = redo(turn, 3)
            grad_kv_now, gain_key_now = key_grads(probs_now, grad_scores_now, keys_now)
            _, gain_attn_now = row_grads(grad_kv_now, keys_now)
            return (
                turn + 1,
                weight_sum + mm_outer(keys_now[1], grad_kv_now),
                key_sum + gain_key_now,
                attn_sum + gain_attn_now,
            )

        _, grad_kv_weight, grad_gain_key, grad_gain_attn = lax.while_loop(
            more, weight_turn, (jnp.int32(1), grad_kv_weight, grad_gain_key, grad_gain_attn)
        )
        grad_scales = jnp.concatenate(
            [
                grad_gain_attn + grad_gain_picks[0],
                grad_gain_mlp[0],
                grad_gain_final[0],
                grad_gain_query[0],
                grad_gain_key,
            ]
        )

        token_rows = (grad_rows + mm_outer(pick_hot, pick_back)).astype(bf16)
        sum_kv, rows_back, got_q, got_ff, got_scales = settle_call(
            exchange,
            grad_kv_weight.astype(bf16).reshape(n_u, n_z, 2, in_rows, -1),
            token_rows.reshape(n_u, slots, MODEL_WIDTH),
            grad_q,
            sum_ff,
            jnp.pad(
                grad_scales.reshape(n_all, scale_share), ((0, 0), (0, 128 - scale_share))
            ).reshape(n_all, 1, 128),
        )
        sum_q = got_q.astype(f32).transpose(1, 0, 2).reshape(in_rows, QUERY_WIDTH)
        sum_inflow = jnp.concatenate([sum_q, sum_kv], axis=1)
        sum_expand = widen_ff(got_ff)
        sum_scales = jnp.sum(got_scales, axis=0)[0, :scale_share]

        table_grad, table_squares = table_grad_call(
            logits,
            final_all,
            norms_all[:, 0].reshape(1, all_picks),
            begin.weights,
            begin.target_ids,
            rows_back.reshape(places, MODEL_WIDTH),
            row_ids.reshape(1, places),
        )
        return_id = exchange.next_id()

        def return_turn(state):
            turn, so_far, _ = state
            tables, keys_now, probs_now, grad_scores_now = redo(turn, 4)
            grad_kv_now, _ = key_grads(probs_now, grad_scores_now, keys_now)
            rows_now, _ = row_grads(grad_kv_now, keys_now)
            rows_now = (rows_now + mm_outer(tables[3], pick_back)).astype(bf16)
            (back,) = exchange.many(
                (("ulysses", "s"),),
                rows_now.reshape(n_u, slots, MODEL_WIDTH),
                collective_id=return_id,
            )
            hot = (
                jnp.arange(row_share, dtype=jnp.int32)[:, None] == tables[0][None, :]
            ).astype(bf16)
            grown = so_far.astype(f32) + mm(hot, back.reshape(places, MODEL_WIDTH))
            return (turn + 1, grown.astype(bf16), jnp.sum(grown * grown, axis=0, keepdims=True))

        _, table_grad, table_squares = lax.while_loop(
            more, return_turn, (jnp.int32(1), table_grad, table_squares)
        )
        squares = jnp.sum(table_squares)
        for grad_piece in (sum_inflow, sum_outflow, sum_expand, sum_contract, sum_scales):
            squares = squares + jnp.sum(grad_piece * grad_piece)
        return (
            loss_local,
            squares,
            table_grad,
            sum_inflow,
            sum_outflow,
            sum_expand,
            sum_contract,
            sum_scales,
        )

    step_float = step_count[0].astype(f32)
    first_scale = 1.0 / (1.0 - beta_first**step_float)
    second_scale = 1.0 / (1.0 - beta_second**step_float)

    def finish(loss_local, squares, table_grad, *layer_grads):
        totals = named_call(
            exchange,
            totals_body,
            {"near": ("blk", "g"), "far": ("ulysses", "g")},
            {},
            {"mine": jnp.pad(jnp.stack([squares, count_local, loss_local]), (0, 125)).reshape(1, 128)},
            {"total": ((1, 128), f32)},
            {
                "near_all": ((n_b, 1, 128), f32),
                "near": ((1, 128), f32),
                "far_all": ((n_u, 1, 128), f32),
            },
            "totals",
        ).total[0]
        square_total, count_total, loss_total = totals[0], totals[1], totals[2]
        gradient_norm = jnp.sqrt(square_total) / count_total
        factor = jnp.minimum(1.0, clip_limit / gradient_norm) / count_total
        outputs = [loss_total / count_total, gradient_norm]
        numbers = jnp.stack([factor, first_scale, second_scale])
        outputs += adam_call(
            numbers,
            embedding,
            first_embedding,
            second_embedding,
            table_grad,
            learning_rates[0],
            weight_decays[0],
        )
        outputs += layer_adam_call(
            numbers,
            (
                (inflow, inflow_first_moment, inflow_second_moment, layer_grads[0]),
                (outflow, first_outflow, second_outflow, layer_grads[1]),
                (expand, first_expand, second_expand, layer_grads[2]),
                (contract, first_contract, second_contract, layer_grads[3]),
            ),
            learning_rates[1:5],
            weight_decays[1:5],
        )
        outputs += adam_update(
            scales,
            first_scales,
            second_scales,
            layer_grads[4] * factor,
            learning_rates[5],
            weight_decays[5],
            step_float,
        )
        return tuple(outputs)

    _, outputs = lax.while_loop(
        lambda state: state[0],
        lambda state: (jnp.bool_(False), finish(*long_way())),
        (rounds > 1, finish(*usual_way())),
    )
    return outputs


def solution(mesh):
    rows = P(("ulysses", "blk"), None)
    flat_rows = P(("ulysses", "blk"))
    column = P(None, "blk")
    return jax.shard_map(
        local,
        mesh=mesh,
        in_specs=(column, P(), column, column, column, P()) + (rows,) * 15 + (flat_rows,) * 3,
        out_specs=(P(), P()) + (rows,) * 15 + (flat_rows,) * 3,
        check_vma=False,
    )
```

```python
import functools
import math

import jax
import jax.numpy as jnp
from jax import lax
from jax.experimental import pallas as pl
from jax.experimental.pallas import tpu as pltpu
from jax.sharding import PartitionSpec as P

MODEL_WIDTH = 1024
QUERY_HEADS = 16
KEY_VALUE_HEADS = 8
HEAD_WIDTH = 128
FF = 3072
QUERY_WIDTH = QUERY_HEADS * HEAD_WIDTH

norm_eps = 1e-06
rope_base = 1000000.0
clip_limit = 0.01
beta_first = 0.9
beta_second = 0.95
adam_eps = 1e-08
learning_rates = (0.01, 0.003, 0.07, 0.003, 0.002, 0.01)
weight_decays = (0.1, 0.1, 0.1, 0.1, 0.1, 0.0)
masked_score = -1e30

bf16 = jnp.bfloat16
f32 = jnp.float32
BLK, ULY, ALL = "blk", "ulysses", "all"
SPLIT, WHOLE = "s", "g"


def inverse_root(values):
    return lax.rsqrt(jnp.mean(values * values, axis=-1, keepdims=True) + norm_eps)


def norm_back(inputs, gain_vec, upstream):
    root_scale = inverse_root(inputs)
    unit_rows = inputs * root_scale
    weighted = upstream * gain_vec
    grad_inputs = root_scale * (
        weighted - unit_rows * jnp.mean(weighted * unit_rows, axis=-1, keepdims=True)
    )
    grad_gain = jnp.sum((upstream * unit_rows).reshape(-1, gain_vec.shape[-1]), axis=0)
    return (grad_inputs, grad_gain)


def rope_angles(positions):
    half_width = HEAD_WIDTH // 2
    frequency = rope_base ** (
        -(jnp.arange(half_width, dtype=jnp.int32).astype(f32) * 2.0 / HEAD_WIDTH)
    )
    angles = positions.astype(f32)[:, None] * frequency[None, :]
    return (jnp.cos(angles), jnp.sin(angles))


def rotate(values, tables, sign_value):
    half_width = values.shape[-1] // 2
    front_half = values[..., :half_width]
    back_half = values[..., half_width:]
    cosine_part = tables[0][:, None, :]
    sine_part = tables[1][:, None, :] * sign_value
    return jnp.concatenate(
        [
            front_half * cosine_part - back_half * sine_part,
            back_half * cosine_part + front_half * sine_part,
        ],
        axis=-1,
    )


def mm(left, right):
    return lax.dot_general(left, right, (((1,), (0,)), ((), ())), preferred_element_type=f32)


def mm_outer(left, right):
    return lax.dot_general(left, right, (((0,), (0,)), ((), ())), preferred_element_type=f32)


def mm_back(left, right):
    return lax.dot_general(left, right, (((1,), (1,)), ((), ())), preferred_element_type=f32)


def spread_rows(onehot, rows):
    return lax.dot_general(
        onehot.astype(f32),
        rows,
        (((0,), (0,)), ((), ())),
        precision=lax.Precision.HIGHEST,
        preferred_element_type=f32,
    )


def place_of(axis, blk_count, peer):
    if axis == ALL:
        return {ULY: peer // blk_count, BLK: lax.rem(peer, blk_count)}
    return {axis: peer}


def rank_of(axis, blk_count):
    row, column = lax.axis_index(ULY), lax.axis_index(BLK)
    return {ULY: row, BLK: column, ALL: row * blk_count + column}[axis]


def greet(axes, blk_count, counts):
    barrier = pltpu.get_barrier_semaphore()
    axes = (ALL,) if ALL in axes else tuple(axes)
    total = 0
    for axis in axes:
        me, count = rank_of(axis, blk_count), counts[axis]

        def call(step, carry, axis=axis, me=me, count=count):
            pl.semaphore_signal(
                barrier,
                inc=1,
                device_id=place_of(axis, blk_count, lax.rem(me + step, count)),
                device_id_type=pl.DeviceIdType.MESH,
            )
            return carry

        lax.fori_loop(1, count, call, 0)
        total += count - 1
    pl.semaphore_wait(barrier, total)


def each(count, body, first=0):
    def step(k, carry):
        body(k)
        return carry

    lax.fori_loop(first, count, step, 0)


def remote(source, target, send_sem, recv_sem, device_id):
    return pltpu.make_async_remote_copy(
        src_ref=source,
        dst_ref=target,
        send_sem=send_sem,
        recv_sem=recv_sem,
        device_id=device_id,
        device_id_type=pl.DeviceIdType.MESH,
    )


class Part:
    def __init__(self, axis, kind, source, landing, send_sems, recv_sems, own_sem, blk_count):
        self.axis, self.kind, self.blk_count = axis, kind, blk_count
        self.source, self.landing = source, landing
        self.send_sems, self.recv_sems, self.own_sem = send_sems, recv_sems, own_sem
        self.me, self.count = rank_of(axis, blk_count), landing.shape[0]

    def copy(self, step):
        peer = lax.rem(self.me + step, self.count)
        return remote(
            self.source.at[peer] if self.kind == SPLIT else self.source,
            self.landing.at[self.me],
            self.send_sems.at[step],
            self.recv_sems.at[step],
            place_of(self.axis, self.blk_count, peer),
        )

    def own(self):
        return pltpu.make_async_copy(
            self.source.at[self.me] if self.kind == SPLIT else self.source,
            self.landing.at[self.me],
            self.own_sem,
        )

    def start(self):
        each(self.count, lambda step: self.copy(step).start(), 1)
        self.own().start()

    def finish(self):
        self.own().wait()
        each(self.count, lambda step: self.copy(step).wait(), 1)


def sems(count):
    return [
        pltpu.SemaphoreType.DMA((count,)),
        pltpu.SemaphoreType.DMA((count,)),
        pltpu.SemaphoreType.DMA,
    ]


def exchange_kernel(plan, blk_count, counts, *refs):
    parts = len(plan)
    entries = [
        Part(axis, kind, refs[k], refs[parts + k], *refs[2 * parts + 3 * k :][:3], blk_count)
        for k, (axis, kind) in enumerate(plan)
    ]
    greet({axis for axis, _ in plan}, blk_count, counts)
    for entry in entries:
        entry.start()
    for entry in entries:
        entry.finish()


def axis_counts():
    n_u, n_b = lax.axis_size(ULY), lax.axis_size(BLK)
    return {ULY: n_u, BLK: n_b, ALL: n_u * n_b}


VMEM = pl.BlockSpec(memory_space=pltpu.VMEM)


def remote_call(kernel, collective_id, shapes, scratch, arrays, name):
    few = lax.axis_size(ULY) * lax.axis_size(BLK) <= 32
    return pl.pallas_call(
        kernel,
        out_shape=shapes,
        in_specs=[VMEM] * len(arrays),
        out_specs=[VMEM] * len(shapes),
        scratch_shapes=scratch,
        compiler_params=pltpu.CompilerParams(
            collective_id=collective_id,
            has_side_effects=True,
            vmem_limit_bytes=(40 if few else 57) * 1024 * 1024,
        ),
        name=name,
    )(*arrays)


class Exchanger:
    def __init__(self):
        self.used = 0

    def next_id(self):
        self.used += 1
        return self.used - 1

    def many(self, plan, *arrays, collective_id=None):
        counts = axis_counts()
        shapes = [
            jax.ShapeDtypeStruct(
                array.shape if kind == SPLIT else (counts[axis],) + array.shape, array.dtype
            )
            for (axis, kind), array in zip(plan, arrays)
        ]
        scratch = []
        for axis, _ in plan:
            scratch += sems(counts[axis])
        if collective_id is None:
            collective_id = self.next_id()
        return remote_call(
            functools.partial(exchange_kernel, plan, counts[BLK], counts),
            collective_id,
            shapes,
            scratch,
            arrays,
            "exchange_" + str(collective_id),
        )

    def __call__(self, axis, kinds, *arrays):
        return self.many(tuple((axis, kind) for kind in kinds), *arrays)


def start_kernel(
    blk_count,
    counts,
    rows_in,
    kv_in,
    q_in,
    ff_in,
    rows_out,
    kv_out,
    q_out,
    ff_out,
    q_split,
    z_send,
    z_recv,
    own_sem,
    xy_send,
    xy_recv,
    core_send,
    core_recv,
    *part_sems,
):
    u, b = lax.axis_index(ULY), lax.axis_index(BLK)
    n_u, n_z = kv_out.shape[0], kv_out.shape[1]
    z, c = b // 2, lax.rem(b, 2)
    greet({ULY, BLK}, blk_count, counts)
    rows = Part(ULY, SPLIT, rows_in, rows_out, *part_sems[0:3], blk_count)
    first_q = Part(BLK, SPLIT, q_in, q_split, *part_sems[3:6], blk_count)
    then_q = Part(ULY, WHOLE, q_split, q_out, *part_sems[6:9], blk_count)
    split_ff = Part(BLK, SPLIT, ff_in, ff_out, *part_sems[9:12], blk_count)

    def along_z(step):
        mine = kv_out.at[u, z, c]
        return remote(
            kv_in,
            mine,
            z_send.at[step],
            z_recv.at[step],
            {BLK: lax.rem(z + step, n_z) * 2 + c},
        )

    def own_copy():
        return pltpu.make_async_copy(kv_in, kv_out.at[u, z, c], own_sem)

    def block(hop, step):
        return kv_out.at[lax.rem(u - hop + n_u, n_u), lax.rem(z - step + n_z, n_z), c]

    def across(hop, step):
        place = block(0, step)
        return remote(
            place,
            place,
            xy_send.at[hop, step],
            xy_recv.at[hop, step],
            {ULY: lax.rem(u + hop, n_u)},
        )

    def to_core(hop, step):
        place = block(hop, step)
        return remote(
            place,
            place,
            core_send.at[hop, step],
            core_recv.at[hop, step],
            {BLK: z * 2 + 1 - c},
        )

    own_copy().start()
    each(n_z, lambda step: along_z(step).start(), 1)
    first_q.start()
    rows.start()
    own_copy().wait()
    each(n_u, lambda hop: across(hop, 0).start(), 1)
    to_core(0, 0).start()
    split_ff.start()

    def pass_on(step):
        along_z(step).wait_recv()
        each(n_u, lambda hop: across(hop, step).start(), 1)
        to_core(0, step).start()

    each(n_z, pass_on, 1)
    first_q.finish()
    then_q.start()

    def share(step):
        def one(hop):
            across(hop, step).wait_recv()
            to_core(hop, step).start()

        each(n_u, one, 1)

    each(n_z, share)
    rows.finish()
    split_ff.finish()
    then_q.finish()
    each(n_z, lambda step: along_z(step).wait_send(), 1)
    each(n_z, lambda step: each(n_u, lambda hop: across(hop, step).wait_send(), 1))
    each(n_z, lambda step: each(n_u, lambda hop: to_core(hop, step).wait()))


def start_call(exchange, rows, kv_low, q_cols, ff_cols):
    counts = axis_counts()
    n_u, n_b = counts[ULY], counts[BLK]
    n_z = n_b // 2
    dma = pltpu.SemaphoreType.DMA
    return remote_call(
        functools.partial(start_kernel, n_b, counts),
        exchange.next_id(),
        [
            jax.ShapeDtypeStruct(rows.shape, bf16),
            jax.ShapeDtypeStruct((n_u, n_z, 2) + kv_low.shape, bf16),
            jax.ShapeDtypeStruct((n_u,) + q_cols.shape, bf16),
            jax.ShapeDtypeStruct(ff_cols.shape, bf16),
        ],
        [
            pltpu.VMEM(q_cols.shape, bf16),
            dma((n_z,)),
            dma((n_z,)),
            dma,
            dma((n_u, n_z)),
            dma((n_u, n_z)),
            dma((n_u, n_z)),
            dma((n_u, n_z)),
        ]
        + sems(n_u)
        + sems(n_b)
        + sems(n_u)
        + sems(n_b),
        (rows, kv_low, q_cols, ff_cols),
        "start",
    )


def settle_kernel(
    blk_count,
    counts,
    kv_in,
    rows_in,
    q_in,
    ff_in,
    gains_in,
    kv_out,
    rows_out,
    q_out,
    ff_out,
    gains_out,
    kv_core,
    kv_pair,
    kv_cross,
    kv_plane,
    kv_line,
    q_got,
    q_sum,
    core_send,
    core_recv,
    xy_send,
    xy_recv,
    z_send,
    z_recv,
    *part_sems,
):
    u, b = lax.axis_index(ULY), lax.axis_index(BLK)
    n_u, n_z = kv_in.shape[0], kv_in.shape[1]
    z, c = b // 2, lax.rem(b, 2)
    greet({ALL}, blk_count, counts)
    rows = Part(ULY, SPLIT, rows_in, rows_out, *part_sems[0:3], blk_count)
    first_q = Part(ULY, SPLIT, q_in, q_got, *part_sems[3:6], blk_count)
    then_q = Part(BLK, SPLIT, q_sum, q_out, *part_sems[6:9], blk_count)
    gains = Part(ALL, SPLIT, gains_in, gains_out, *part_sems[9:12], blk_count)
    split_ff = Part(BLK, SPLIT, ff_in, ff_out, *part_sems[12:15], blk_count)

    def place(hop, step):
        return (lax.rem(u + hop, n_u), lax.rem(z + step, n_z))

    def to_core(hop, step):
        row, line = place(hop, step)
        return remote(
            kv_in.at[row, line, 1 - c],
            kv_core.at[hop, step],
            core_send.at[hop, step],
            core_recv.at[hop, step],
            {BLK: z * 2 + 1 - c},
        )

    def across(hop, step):
        return remote(
            kv_pair.at[hop, step],
            kv_cross.at[hop, step],
            xy_send.at[hop, step],
            xy_recv.at[hop, step],
            {ULY: lax.rem(u + hop, n_u)},
        )

    def along_z(step):
        return remote(
            kv_plane.at[step],
            kv_line.at[step],
            z_send.at[step],
            z_recv.at[step],
            {BLK: lax.rem(z + step, n_z) * 2 + c},
        )

    each(n_z, lambda step: each(n_u, lambda hop: to_core(hop, step).start()))
    first_q.start()
    split_ff.start()

    def add_pair(step):
        def one(hop):
            row, line = place(hop, step)
            to_core(hop, step).wait_recv()
            kv_pair[hop, step] = (
                kv_in[row, line, c].astype(f32) + kv_core[hop, step].astype(f32)
            ).astype(bf16)

        def forward(hop):
            one(hop)
            across(hop, step).start()

        one(0)
        each(n_u, forward, 1)

    each(n_z, add_pair, 1)
    add_pair(0)
    rows.start()
    gains.start()
    first_q.finish()
    q_sum[...] = jnp.sum(q_got[...].astype(f32), axis=0).astype(bf16)
    then_q.start()

    def plane_sum(step):
        total = kv_pair[0, step].astype(f32)
        for hop in range(1, n_u):
            across(hop, step).wait_recv()
            total = total + kv_cross[hop, step].astype(f32)
        return total

    def add_plane(step):
        kv_plane[step] = plane_sum(step).astype(bf16)
        along_z(step).start()

    each(n_z, add_plane, 1)
    total = plane_sum(0)
    for step in range(1, n_z):
        along_z(step).wait_recv()
        total = total + kv_line[step].astype(f32)
    kv_out[...] = total
    then_q.finish()
    split_ff.finish()
    gains.finish()
    rows.finish()
    each(n_z, lambda step: each(n_u, lambda hop: to_core(hop, step).wait_send()))
    each(n_z, lambda step: each(n_u, lambda hop: across(hop, step).wait_send(), 1))
    each(n_z, lambda step: along_z(step).wait_send(), 1)


def settle_call(exchange, kv_grad, rows, q_grad, ff_grad, gains):
    counts = axis_counts()
    n_u, n_b = counts[ULY], counts[BLK]
    n_z = n_b // 2
    block = kv_grad.shape[3:]
    dma = pltpu.SemaphoreType.DMA
    return remote_call(
        functools.partial(settle_kernel, n_b, counts),
        exchange.next_id(),
        [
            jax.ShapeDtypeStruct(block, f32),
            jax.ShapeDtypeStruct(rows.shape, bf16),
            jax.ShapeDtypeStruct(q_grad.shape[1:], bf16),
            jax.ShapeDtypeStruct(ff_grad.shape, bf16),
            jax.ShapeDtypeStruct(gains.shape, f32),
        ],
        [
            pltpu.VMEM((n_u, n_z) + block, bf16),
            pltpu.VMEM((n_u, n_z) + block, bf16),
            pltpu.VMEM((n_u, n_z) + block, bf16),
            pltpu.VMEM((n_z,) + block, bf16),
            pltpu.VMEM((n_z,) + block, bf16),
            pltpu.VMEM(q_grad.shape, bf16),
            pltpu.VMEM(q_grad.shape[1:], bf16),
            dma((n_u, n_z)),
            dma((n_u, n_z)),
            dma((n_u, n_z)),
            dma((n_u, n_z)),
            dma((n_z,)),
            dma((n_z,)),
        ]
        + sems(n_u)
        + sems(n_u)
        + sems(n_b)
        + sems(n_u * n_b)
        + sems(n_b),
        (kv_grad, rows, q_grad, ff_grad, gains),
        "settle",
    )


def norm_back_rows(inputs, gain_vec, upstream):
    root_scale = inverse_root(inputs)
    unit_rows = inputs * root_scale
    weighted = upstream * gain_vec
    grad_inputs = root_scale * (
        weighted - unit_rows * jnp.mean(weighted * unit_rows, axis=-1, keepdims=True)
    )
    return (grad_inputs, jnp.sum(upstream * unit_rows, axis=0, keepdims=True))


class Links:
    def __init__(self, plan, blk_count, sem_refs):
        self.plan, self.blk_count, self.sem_refs = plan, blk_count, sem_refs

    def __call__(self, k, source, landing):
        axis, kind = self.plan[k]
        part = Part(axis, kind, source, landing, *self.sem_refs[3 * k : 3 * k + 3], self.blk_count)
        part.start()
        return part

    def now(self, k, source, landing):
        self(k, source, landing).finish()


def fused_call(exchange, body, plan, arrays, outs, scratch, name):
    counts = axis_counts()
    n_in, n_out, n_scratch = len(arrays), len(outs), len(scratch)
    sem_shapes = []
    for axis, _ in plan:
        sem_shapes += sems(counts[axis])

    def kernel(*refs):
        ins, refs = refs[:n_in], refs[n_in:]
        results, refs = refs[:n_out], refs[n_out:]
        kept, sem_refs = refs[:n_scratch], refs[n_scratch:]
        greet({axis for axis, _ in plan}, counts[BLK], counts)
        body(Links(plan, counts[BLK], sem_refs), ins, results, kept)

    return remote_call(
        kernel,
        exchange.next_id(),
        [jax.ShapeDtypeStruct(shape, dtype) for shape, dtype in outs],
        [pltpu.VMEM(shape, dtype) for shape, dtype in scratch] + sem_shapes,
        arrays,
        name,
    )


def sum_blocks(landing):
    total = landing[0].astype(f32)
    for k in range(1, landing.shape[0]):
        total = total + landing[k].astype(f32)
    return total


def flat_rows_of(ref):
    return ref[...].reshape(-1, ref.shape[-1])


def turned(values, cosines, sines):
    return values * cosines + pltpu.roll(values, HEAD_WIDTH // 2, 1) * sines


def lanes_of(columns, width, count):
    group = lax.broadcasted_iota(jnp.int32, (columns[0].shape[0], width * count), 1) // width
    spread = columns[0]
    for k in range(1, count):
        spread = jnp.where(group == k, columns[k], spread)
    return spread


def query_body(n_b, links, ins, outs, scratch):
    pick_part, gain_attn, gain_query, q_weight, cosines, sines, ff_rows, out_rows, down_rows = ins
    picks_out, normed_all, query_raw, query_all, ff_all, out_all, down_all = outs
    pick_got, normed_mine, query_mine = scratch
    first = links(0, pick_part, pick_got)
    behind = [
        links(3, ff_rows, ff_all),
        links(4, out_rows, out_all),
        links(5, down_rows, down_all),
    ]
    first.finish()
    rows = sum_blocks(pick_got)
    picks_out[...] = rows
    mine = rows[:, :MODEL_WIDTH]
    normed_mine[...] = (mine * inverse_root(mine) * gain_attn[...]).astype(bf16)
    links.now(1, normed_mine, normed_all)
    raw = mm(flat_rows_of(normed_all), q_weight[...])
    query_raw[...] = raw
    for k in range(raw.shape[1] // HEAD_WIDTH):
        head = raw[:, k * HEAD_WIDTH : (k + 1) * HEAD_WIDTH]
        query_mine[:, k * HEAD_WIDTH : (k + 1) * HEAD_WIDTH] = turned(
            head * inverse_root(head) * gain_query[...], cosines[...], sines[...]
        ).astype(bf16)
    links.now(2, query_mine, query_all)
    for part in behind:
        part.finish()


def forward_body(n_u, n_b, links, ins, outs, scratch):
    part_send, stats, mine, out_weight, ff_weight, down_weight, gain_mlp, gain_final = ins
    attended_out, log_out, after_out, normed_all, gate_up_out, top_out, final_mine, final_all = outs
    part_got, stats_all, shares, partial, partial_got, normed_mine, final_slot = scratch
    picks = after_out.shape[0]
    out_cut = attended_out.shape[1] // n_u
    heads_row = QUERY_HEADS // n_u
    cut_head = (lax.axis_index(BLK) * out_cut) // HEAD_WIDTH
    sent = links(0, part_send, part_got)
    links.now(1, stats, stats_all)
    full_max = stats_all[0, :QUERY_HEADS]
    for k in range(1, n_b):
        full_max = jnp.maximum(full_max, stats_all[k, :QUERY_HEADS])
    full_sum = jnp.zeros_like(full_max)
    for k in range(n_b):
        full_sum += stats_all[k, QUERY_HEADS:] * jnp.exp(stats_all[k, :QUERY_HEADS] - full_max)
    log_total = full_max + jnp.log(full_sum)
    log_out[...] = log_total
    for row in range(n_u):
        head = row * heads_row + cut_head
        row_log = log_out[pl.ds(head, 1), :]
        for k in range(n_b):
            shares[pl.ds(k * n_u + row, 1), :] = jnp.exp(
                stats_all[k, pl.ds(head, 1), :] - row_log
            )
    columns = shares[...].T
    sent.finish()
    attended = jnp.zeros(attended_out.shape, f32)
    for k in range(n_b):
        attended += part_got[k].astype(f32) * lanes_of(
            [columns[:, k * n_u + row : k * n_u + row + 1] for row in range(n_u)], out_cut, n_u
        )
    attended_out[...] = attended

    def to_picks(which, rows):
        partial[...] = rows.astype(bf16).reshape(partial.shape)
        links.now(which, partial, partial_got.at[which // 4])
        return sum_blocks(partial_got.at[which // 4])

    after_attn = mine[:, :MODEL_WIDTH] + to_picks(2, mm(attended.astype(bf16), out_weight[...]))
    after_out[...] = after_attn
    normed_mine[...] = (after_attn * inverse_root(after_attn) * gain_mlp[...]).astype(bf16)
    links.now(3, normed_mine, normed_all)
    gate_up = mm(flat_rows_of(normed_all), ff_weight[...])
    gate_up_out[...] = gate_up
    half = gate_up.shape[1] // 2
    gate_part, up_part = gate_up[:, :half], gate_up[:, half:]
    activated = (gate_part * jax.nn.sigmoid(gate_part) * up_part).astype(bf16)
    after_mlp = after_attn + to_picks(4, mm(activated, down_weight[...]))
    top_out[...] = after_mlp
    final_mine[...] = (after_mlp * inverse_root(after_mlp) * gain_final[...]).astype(bf16)
    links.now(5, final_mine, final_slot)
    links.now(6, final_slot, final_all)


def backward_body(n_u, n_b, links, ins, outs, scratch):
    (
        head_rows,
        head_stats,
        final_mine,
        picks_in,
        weights,
        after_mlp,
        after_attn,
        gate_up_in,
        normed_all,
        attended,
        out_weight,
        ff_weight,
        down_weight,
        gain_mlp,
        gain_final,
    ) = ins
    (
        norms_all,
        terms,
        gain_mlp_out,
        gain_final_out,
        grad_ff,
        grad_out,
        grad_down,
        grad_after,
        branch_all,
        attended_all,
        delta_all,
    ) = outs
    (
        rows_got,
        stats_got,
        slot_stats,
        slot_got,
        factors,
        columns,
        norms_mine,
        partial,
        partial_got,
        mine_low,
        grad_all,
        attended_mine,
        deltas,
        delta_mine,
    ) = scratch
    picks = after_mlp.shape[0]
    slot_picks = n_b * picks
    b = lax.axis_index(BLK)
    factors[...] = jnp.zeros_like(factors)
    first = links(0, head_rows, rows_got)
    links.now(1, head_stats, stats_got)
    tops = stats_got[0, 0:1, :]
    for k in range(1, n_u):
        tops = jnp.maximum(tops, stats_got[k, 0:1, :])
    total = jnp.zeros_like(tops)
    for k in range(n_u):
        factor = jnp.exp(stats_got[k, 0:1, :] - tops)
        factors[k : k + 1, :] = factor
        total += stats_got[k, 1:2, :] * factor
    slot_stats[...] = jnp.zeros_like(slot_stats)
    slot_stats[0:1, :] = tops
    slot_stats[1:2, :] = total
    slot_part = links(3, slot_stats, slot_got)
    by_row = factors[...].T
    first.finish()
    rows = rows_got[0].astype(f32) * by_row[:, 0:1]
    for k in range(1, n_u):
        rows += rows_got[k].astype(f32) * by_row[:, k : k + 1]
    partial[...] = rows.astype(bf16).reshape(partial.shape)
    back = links(2, partial, partial_got.at[0])
    slot_part.finish()
    tops = slot_got[0, 0:1, :]
    for k in range(1, n_b):
        tops = jnp.maximum(tops, slot_got[k, 0:1, :])
    total = jnp.zeros_like(tops)
    for k in range(n_b):
        factor = jnp.exp(slot_got[k, 0:1, :] - tops)
        factors[k : k + 1, :] = factor
        total += slot_got[k, 1:2, :] * factor
    log_norm = tops + jnp.log(total)
    for k in range(n_b):
        factors[k : k + 1, :] = factors[k : k + 1, :] / total
    factors[n_b : n_b + 1, :] = log_norm
    norms_mine[...] = jnp.broadcast_to(log_norm, norms_mine.shape)
    norms_part = links(4, norms_mine, norms_all)
    columns[...] = factors[...].T
    mine = columns[pl.ds(pl.multiple_of(b * picks, picks), picks), :]
    back.finish()
    target_rows = picks_in[:, MODEL_WIDTH:]
    grad_final = -target_rows
    for k in range(n_b):
        grad_final += partial_got[0, k].astype(f32) * mine[:, k : k + 1]
    grad_final = grad_final * weights[:, 0:1]
    target_logit = jnp.sum(
        final_mine[...].astype(f32) * target_rows, axis=-1, keepdims=True
    )
    terms[...] = weights[...] * (target_logit - mine[:, n_b : n_b + 1])
    grad_mlp, gain_rows = norm_back_rows(after_mlp[...], gain_final[...], grad_final)
    gain_final_out[...] = gain_rows
    mine_low[...] = grad_mlp.astype(bf16)
    links.now(5, mine_low, grad_all)
    branch = flat_rows_of(grad_all)
    gate_up = gate_up_in[...]
    half = gate_up.shape[1] // 2
    gate_part, up_part = gate_up[:, :half], gate_up[:, half:]
    sigmoid_gate = jax.nn.sigmoid(gate_part)
    grad_act = mm_back(branch, down_weight[...])
    grad_gate = grad_act * up_part * sigmoid_gate * (1.0 + gate_part * (1.0 - sigmoid_gate))
    grad_up = grad_act * gate_part * sigmoid_gate
    grad_gate_up = jnp.concatenate([grad_gate, grad_up], axis=1).astype(bf16)
    partial[...] = mm_back(grad_gate_up, ff_weight[...]).astype(bf16).reshape(partial.shape)
    back = links(6, partial, partial_got.at[1])
    activated = (gate_part * sigmoid_gate * up_part).astype(bf16)
    grad_down[...] = mm_outer(activated, branch).astype(bf16).reshape(grad_down.shape)
    back.finish()
    grad_mid, gain_rows = norm_back_rows(after_attn[...], gain_mlp[...], sum_blocks(partial_got.at[1]))
    gain_mlp_out[...] = gain_rows
    grad_attn = grad_mlp + grad_mid
    grad_after[...] = grad_attn
    mine_low[...] = grad_attn.astype(bf16)
    again = links(7, mine_low, branch_all)
    grad_ff[...] = (
        mm_outer(flat_rows_of(normed_all), grad_gate_up).astype(bf16).reshape(grad_ff.shape)
    )
    again.finish()
    branch = flat_rows_of(branch_all)
    grad_low = mm_back(branch, out_weight[...]).astype(bf16)
    attended_mine[...] = grad_low
    last = links(8, attended_mine, attended_all)
    out_cut = attended.shape[1] // n_u
    product = attended[...] * grad_low.astype(f32)
    group = lax.broadcasted_iota(jnp.int32, product.shape, 1) // out_cut
    lane = lax.broadcasted_iota(jnp.int32, deltas.shape, 1)
    sums = jnp.zeros(deltas.shape, f32)
    for row in range(n_u):
        one = jnp.sum(jnp.where(group == row, product, 0.0), axis=-1, keepdims=True)
        sums = jnp.where(lane == row, one, sums)
    deltas[...] = sums
    delta_mine[...] = deltas[...].T[:8, :]
    delta_part = links(9, delta_mine, delta_all)
    grad_out[...] = mm_outer(attended[...].astype(bf16), branch).astype(bf16).reshape(
        grad_out.shape
    )
    last.finish()
    delta_part.finish()
    norms_part.finish()


def query_back_body(links, ins, outs, scratch):
    (
        query_send,
        query_raw,
        cosines,
        sines,
        gain_query,
        q_weight,
        normed_all,
        picks_in,
        gain_attn,
        grad_after,
        grad_ff,
        grad_out,
        grad_down,
    ) = ins
    gain_query_out, gain_attn_out, grad_q, pick_back, ff_sum, out_sum, down_sum = outs
    query_got, grad_low, partial, partial_got, mine_low, ff_got, out_got, down_got = scratch
    first = links(0, query_send, query_got)
    behind = [
        links(3, grad_ff, ff_got),
        links(4, grad_out, out_got),
        links(5, grad_down, down_got),
    ]
    first.finish()
    upstream = sum_blocks(query_got).astype(bf16).astype(f32)
    gain_sum = jnp.zeros(gain_query_out.shape, f32)
    for k in range(upstream.shape[1] // HEAD_WIDTH):
        part = slice(k * HEAD_WIDTH, (k + 1) * HEAD_WIDTH)
        grad_head, gain_head = norm_back_rows(
            query_raw[:, part], gain_query[...], turned(upstream[:, part], cosines[...], -sines[...])
        )
        grad_low[:, part] = grad_head.astype(bf16)
        gain_sum += gain_head
    gain_query_out[...] = gain_sum
    partial[...] = mm_back(grad_low[...], q_weight[...]).astype(bf16).reshape(partial.shape)
    back = links(1, partial, partial_got)
    grad_q[...] = (
        mm_outer(flat_rows_of(normed_all), grad_low[...]).astype(bf16).reshape(grad_q.shape)
    )
    back.finish()
    grad_mine, gain_rows = norm_back_rows(
        picks_in[:, :MODEL_WIDTH], gain_attn[...], sum_blocks(partial_got)
    )
    gain_attn_out[...] = gain_rows
    mine_low[...] = (grad_after[...] + grad_mine).astype(bf16)
    links.now(2, mine_low, pick_back)
    for part in behind:
        part.finish()
    ff_sum[...] = sum_blocks(ff_got).astype(bf16)
    out_sum[...] = sum_blocks(out_got)
    down_sum[...] = sum_blocks(down_got)


class Named:
    pass


def named_call(exchange, body, plan, extra_sems, ins, outs, scratch, name):
    counts = axis_counts()
    sem_shapes = []
    for axis, _ in plan.values():
        sem_shapes += sems(counts[axis])
    order = {key: k for k, key in enumerate(plan)}
    extra = list(extra_sems)

    def kernel(*refs):
        r, s = Named(), Named()
        names = list(ins) + list(outs) + list(scratch)
        for key, ref in zip(names, refs):
            setattr(r, key, ref)
        sem_refs = refs[len(names) :]
        for key, ref in zip(extra, sem_refs[3 * len(plan) :]):
            setattr(s, key, ref)
        base = Links(list(plan.values()), counts[BLK], sem_refs)
        links = Named()
        for key in plan:
            setattr(links, key, functools.partial(base, order[key]))
        greet({axis for axis, _ in plan.values()}, counts[BLK], counts)
        body(r, links, s)

    results = remote_call(
        kernel,
        exchange.next_id(),
        [jax.ShapeDtypeStruct(shape, dtype) for shape, dtype in outs.values()],
        [pltpu.VMEM(shape, dtype) for shape, dtype in scratch.values()]
        + sem_shapes
        + [pltpu.SemaphoreType.DMA(extra_sems[key]) for key in extra],
        list(ins.values()),
        name,
    )
    found = Named()
    for key, value in zip(outs, results):
        setattr(found, key, value)
    return found


def column_of(lane_row):
    count = lane_row.shape[1]
    down = lax.broadcasted_iota(jnp.int32, (count, count), 0)
    across = lax.broadcasted_iota(jnp.int32, (count, count), 1)
    return jnp.sum(jnp.where(down == across, lane_row, 0.0), axis=1, keepdims=True)


def begin_body(n_u, n_b, row_share, slots, r, links, s):
    u, b = lax.axis_index(ULY), lax.axis_index(BLK)
    me = u * n_b + b
    block_len, picks = r.tokens.shape[1], r.picked.shape[1]
    places = n_u * slots
    gathers = [
        links.tokens(r.tokens, r.tokens_all),
        links.targets(r.targets, r.targets_all),
        links.picked(r.picked, r.picked_all),
        links.advantages(r.advantages, r.advantages_all),
    ]
    links.near(r.scales, r.near).finish()
    far = links.far(r.near, r.far)
    for part in gathers:
        part.finish()

    width = block_len + picks
    lane = lax.broadcasted_iota(jnp.int32, (1, width), 1)
    before = jnp.where(
        lax.broadcasted_iota(jnp.int32, (width, width), 0)
        < lax.broadcasted_iota(jnp.int32, (width, width), 1),
        1.0,
        0.0,
    ).astype(bf16)
    base = jnp.zeros((2 * n_u, 1), f32)
    found = [jnp.zeros((slots, width), f32) for _ in range(2 * n_u)]
    rank_of_slot = lax.broadcasted_iota(jnp.int32, (slots, width), 0).astype(f32)
    owner_first = lax.broadcasted_iota(jnp.int32, (n_u, 1), 0) * n_b + b
    most = jnp.zeros((n_u, 1), f32)
    counts = [jnp.zeros((n_u, width), f32) for _ in range(n_u * n_b)]
    for k in range(n_b):
        r.wants[:, :block_len] = r.tokens_all[k]
        r.wants[:, block_len:] = r.targets_all[k]
        wants = r.wants[...]
        local = wants - me * row_share
        sent = (local >= 0) & (local < row_share)
        own = r.wants[pl.ds(u, 1), :] - owner_first * row_share
        got = (own >= 0) & (own < row_share)
        r.masks[:n_u, :] = jnp.where(sent, 1.0, 0.0)
        r.masks[n_u:, :] = jnp.where(got, 1.0, 0.0)
        r.labels[:n_u, :] = (local + 1).astype(f32)
        r.labels[n_u:, :] = jnp.broadcast_to(k * width + lane + 1, (n_u, width)).astype(f32)
        masks = r.masks[...]
        ranks = mm(masks.astype(bf16), before) + base
        r.ranks[...] = jnp.where(masks > 0.0, ranks, -1.0)
        base += jnp.sum(masks, axis=1, keepdims=True)
        for row in range(2 * n_u):
            hit = r.ranks[row : row + 1, :] == rank_of_slot
            found[row] += jnp.where(hit, r.labels[row : row + 1, :], 0.0)
        for owner in range(n_u * n_b):
            far_row = wants - owner * row_share
            counts[owner] += jnp.where((far_row >= 0) & (far_row < row_share), 1.0, 0.0)
        r.slot_picked[:, k * picks : (k + 1) * picks] = r.picked_all[k, pl.ds(u, 1), :]
        valid = r.picked_all[k] < r.lengths[...]
        weights = jnp.where(valid, r.advantages_all[k], 0.0)
        for row in range(n_u):
            at = slice((row * n_b + k) * picks, (row * n_b + k + 1) * picks)
            r.weights[:, at] = weights[row : row + 1, :]
            r.target_ids[:, at] = r.targets_all[k, row : row + 1, :] - me * row_share
    for owner in range(n_u * n_b):
        most = jnp.maximum(most, jnp.sum(counts[owner], axis=1, keepdims=True))
    r.meta[...] = jnp.zeros_like(r.meta)
    r.meta[0:n_u, :] = jnp.broadcast_to(base[:n_u], (n_u, 128))
    r.meta[8 : 8 + n_u, :] = jnp.broadcast_to(most, (n_u, 128))
    mine_valid = r.picked[pl.ds(u, 1), :] < r.lengths[pl.ds(u, 1), :]
    mine_weight = jnp.where(mine_valid, r.advantages[pl.ds(u, 1), :], 0.0)
    r.meta[16:17, :] = jnp.broadcast_to(
        jnp.sum(jnp.where(mine_valid, 1.0, 0.0), axis=1, keepdims=True), (1, 128)
    )
    r.weight_wide[...] = jnp.broadcast_to(column_of(mine_weight), r.weight_wide.shape)
    my_length = r.lengths[pl.ds(u, 1), :]
    for row in range(n_u):
        here = slice(row * slots, (row + 1) * slots)
        r.row_ids[here, :] = jnp.sum(found[row], axis=1, keepdims=True).astype(jnp.int32) - 1
        entry = jnp.sum(found[n_u + row], axis=1, keepdims=True) - 1.0
        block = jnp.floor((entry + 0.5) * (1.0 / width))
        inside = entry - block * width
        token = (entry >= 0.0) & (inside < block_len)
        position = (block * block_len + inside).astype(jnp.int32)
        key_pos = jnp.where(token, position, 1 << 30)
        r.key_pos[here, :] = key_pos
        r.key_lim[here, :] = jnp.where(key_pos < my_length, key_pos, 1 << 30)
        r.positions[here, :] = jnp.where(token, position, 0)
        target = (block * picks + inside - block_len).astype(jnp.int32)
        r.target_of[here, :] = jnp.where((entry >= 0.0) & (inside >= block_len), target, -1)
    r.positions[places:, :] = column_of(r.slot_picked[...].astype(f32)).astype(jnp.int32)

    far.finish()
    share = r.scales.shape[1]
    for row in range(n_u):
        for k in range(n_b):
            at = (row * n_b + k) * share
            r.gains[:, at : at + share] = r.far[row, k].astype(bf16).astype(f32)
    r.gain_attn[...] = r.gains[:, :MODEL_WIDTH]
    r.gain_mlp[...] = r.gains[:, MODEL_WIDTH : 2 * MODEL_WIDTH]
    r.gain_final[...] = r.gains[:, 2 * MODEL_WIDTH : 3 * MODEL_WIDTH]
    r.gain_query[...] = r.gains[:, 3 * MODEL_WIDTH : 3 * MODEL_WIDTH + HEAD_WIDTH]
    r.gain_key[...] = r.gains[:, 3 * MODEL_WIDTH + HEAD_WIDTH :]


def totals_body(r, links, s):
    lane = lax.broadcasted_iota(jnp.int32, (1, 128), 1)
    squares = r.tails[0:1, 0:1] + jnp.sum(r.table_squares[...], axis=1, keepdims=True)
    row = jnp.where(lane == 0, squares, 0.0)
    row = jnp.where(lane == 1, r.counts[0:1, :], row)
    r.mine[...] = jnp.where(lane == 2, r.tails[1:2, 0:1], row)
    links.near(r.mine, r.all).finish()
    total = sum_blocks(r.all)
    count = total[:, 1:2]
    norm = jnp.sqrt(total[:, 0:1]) / count
    factor = jnp.minimum(1.0, clip_limit / norm) / count
    row = jnp.where(lane == 0, factor, r.steps[...])
    row = jnp.where(lane == 3, total[:, 2:3] / count, row)
    r.numbers[...] = jnp.where(lane == 4, norm, row)


def head_of(ref, head):
    share = ref.shape[2] // HEAD_WIDTH
    at = head % share * HEAD_WIDTH
    return ref[head // share, :, at : at + HEAD_WIDTH]


def cuts_of(head, n_u, n_b):
    cut = QUERY_WIDTH // (n_u * n_b)
    heads_row, pieces = QUERY_HEADS // n_u, HEAD_WIDTH // cut
    row = head // heads_row
    return [
        (head % heads_row * pieces + t, slice(row * cut, (row + 1) * cut), slice(t * cut, (t + 1) * cut))
        for t in range(pieces)
    ]


def ff_cuts(n_u, n_b):
    cut = FF // (n_u * n_b)
    return [
        (
            k,
            slice((half * n_u + row) * cut, (half * n_u + row + 1) * cut),
            slice(half * FF + (row * n_b + k) * cut, half * FF + (row * n_b + k + 1) * cut),
        )
        for k in range(n_b)
        for half in range(2)
        for row in range(n_u)
    ]


def rise_body(n_u, n_b, r, links, s):
    u, b = lax.axis_index(ULY), lax.axis_index(BLK)
    n_z = n_b // 2
    z, c = b // 2, lax.rem(b, 2)
    score_scale = HEAD_WIDTH ** (-0.5)

    def along_z(step):
        return remote(
            r.kv_in,
            r.kv_weight.at[u, z, c],
            s.z_send.at[step],
            s.z_recv.at[step],
            {BLK: lax.rem(z + step, n_z) * 2 + c},
        )

    def own_copy():
        return pltpu.make_async_copy(r.kv_in, r.kv_weight.at[u, z, c], s.own.at[0])

    def block(hop, step):
        return r.kv_weight.at[lax.rem(u - hop + n_u, n_u), lax.rem(z - step + n_z, n_z), c]

    def across(hop, step):
        place = block(0, step)
        return remote(
            place,
            place,
            s.xy_send.at[hop, step],
            s.xy_recv.at[hop, step],
            {ULY: lax.rem(u + hop, n_u)},
        )

    def to_core(hop, step):
        place = block(hop, step)
        return remote(
            place,
            place,
            s.core_send.at[hop, step],
            s.core_recv.at[hop, step],
            {BLK: z * 2 + 1 - c},
        )

    places = r.key_raw.shape[0]
    half = KEY_VALUE_HEADS * HEAD_WIDTH
    r.kv_in[...] = r.inflow[:, QUERY_WIDTH:].astype(bf16)
    own_copy().start()
    rows = links.rows(r.rows_in, r.arrived)
    each(n_z, lambda step: along_z(step).start(), 1)
    q_share = r.q_in.shape[2]
    for k in range(n_b):
        r.q_in[k] = r.inflow[:, k * q_share : (k + 1) * q_share].astype(bf16)
    q_split = links.q_split(r.q_in, r.q_part)
    own_copy().wait()
    each(n_u, lambda hop: across(hop, 0).start(), 1)
    to_core(0, 0).start()
    for k, there, here in ff_cuts(n_u, n_b):
        r.ff_in[k, :, there] = r.expand[:, here].astype(bf16)
    ff_split = links.ff_split(r.ff_in, r.ff_part)
    r.out_in[...] = r.outflow[...].astype(bf16)
    r.down_in[...] = r.contract[...].astype(bf16)
    rows.finish()

    arrived = flat_rows_of(r.arrived)
    pick_hot = jnp.where(r.key_pos[...] == r.slot_picked[...], 1.0, 0.0).astype(bf16)
    pick_lane = lax.broadcasted_iota(jnp.int32, pick_hot.shape, 1)
    target_hot = jnp.where(r.target_of[...] == pick_lane, 1.0, 0.0).astype(bf16)
    r.pick_send[:, :, :MODEL_WIDTH] = (
        mm_outer(pick_hot, arrived).astype(bf16).reshape(r.normed_slot.shape)
    )
    r.pick_send[:, :, MODEL_WIDTH:] = (
        mm_outer(target_hot, arrived).astype(bf16).reshape(r.normed_slot.shape)
    )
    picked = links.picks(r.pick_send, r.pick_got)

    def pass_on(step):
        along_z(step).wait_recv()
        each(n_u, lambda hop: across(hop, step).start(), 1)
        to_core(0, step).start()

    each(n_z, pass_on, 1)
    q_split.finish()
    q_all = links.q_all(r.q_part, r.q_weight)
    wide = arrived.astype(f32)
    r.normed_keys[...] = (wide * inverse_root(wide) * r.gain_attn[...]).astype(bf16)
    picked.finish()
    pick_rows = sum_blocks(r.pick_got)
    r.pick_rows[...] = pick_rows
    mine = pick_rows[:, :MODEL_WIDTH]
    r.normed_mine[...] = (mine * inverse_root(mine) * r.gain_attn[...]).astype(bf16)
    links.normed(r.normed_mine, r.normed_slot).finish()
    q_all.finish()
    raw = mm(flat_rows_of(r.normed_slot), r.q_weight[...].reshape(MODEL_WIDTH, -1))
    r.query_raw[...] = raw
    for k in range(raw.shape[1] // HEAD_WIDTH):
        part = slice(k * HEAD_WIDTH, (k + 1) * HEAD_WIDTH)
        head = raw[:, part]
        r.query_mine[:, part] = turned(
            head * inverse_root(head) * r.gain_query[...], r.rope_cos[places:], r.rope_sin[places:]
        ).astype(bf16)
    queries = links.queries(r.query_mine, r.query_all)

    def share(step):
        def one(hop):
            across(hop, step).wait_recv()
            to_core(hop, step).start()

        each(n_u, one, 1)

    each(n_z, share)
    out_all = links.out_all(r.out_in, r.out_weight)
    ff_split.finish()
    ff_all = links.ff_all(r.ff_part, r.ff_weight)
    down_all = links.down_all(r.down_in, r.down_weight)
    each(n_z, lambda step: each(n_u, lambda hop: to_core(hop, step).wait_recv()))

    wide_head = 2 * HEAD_WIDTH

    def project(k):
        for first in (0, half):
            at = pl.multiple_of(first + k * wide_head, wide_head)
            weight = r.kv_weight[:, :, :, :, pl.ds(at, wide_head)].reshape(MODEL_WIDTH, wide_head)
            got = mm(r.normed_keys[...], weight)
            here = pl.ds(pl.multiple_of(k * wide_head, wide_head), wide_head)
            if first:
                r.values[:, here] = got.astype(bf16)
            else:
                r.key_raw[:, here] = got
                turned_both = []
                for j in range(2):
                    head = got[:, j * HEAD_WIDTH : (j + 1) * HEAD_WIDTH]
                    turned_both.append(
                        turned(
                            head * inverse_root(head) * r.gain_key[...],
                            r.rope_cos[:places],
                            r.rope_sin[:places],
                        )
                    )
                r.key_rot[:, here] = jnp.concatenate(turned_both, axis=1).astype(bf16)

    each(KEY_VALUE_HEADS // 2, project)
    queries.finish()
    allowed = r.key_lim[...] <= r.slot_picked[...]
    for head in range(QUERY_HEADS):
        at = head // (QUERY_HEADS // KEY_VALUE_HEADS) * HEAD_WIDTH
        part = slice(at, at + HEAD_WIDTH)
        scores = mm_back(r.key_rot[:, part], head_of(r.query_all, head)) * score_scale
        scores = jnp.where(allowed, scores, masked_score)
        top = jnp.max(scores, axis=0, keepdims=True)
        weights = jnp.where(allowed, jnp.exp(scores - top), 0.0)
        r.stats[head : head + 1, :] = top
        r.stats[QUERY_HEADS + head : QUERY_HEADS + head + 1, :] = jnp.sum(
            weights, axis=0, keepdims=True
        )
        out = mm_outer(weights.astype(bf16), r.values[:, part]).astype(bf16)
        for target, there, here in cuts_of(head, n_u, n_b):
            r.part_send[target, :, there] = out[:, here]

    picks = r.after_attn.shape[0]
    out_cut = r.attended.shape[1] // n_u
    heads_row = QUERY_HEADS // n_u
    cut_head = (b * out_cut) // HEAD_WIDTH
    sent = links.parts(r.part_send, r.part_got)
    links.stats(r.stats, r.stats_all).finish()
    full_max = r.stats_all[0, :QUERY_HEADS]
    for k in range(1, n_b):
        full_max = jnp.maximum(full_max, r.stats_all[k, :QUERY_HEADS])
    full_sum = jnp.zeros_like(full_max)
    for k in range(n_b):
        full_sum += r.stats_all[k, QUERY_HEADS:] * jnp.exp(
            r.stats_all[k, :QUERY_HEADS] - full_max
        )
    r.log_total[...] = full_max + jnp.log(full_sum)
    for row in range(n_u):
        head = row * heads_row + cut_head
        row_log = r.log_total[pl.ds(head, 1), :]
        for k in range(n_b):
            r.shares[k * n_u + row : k * n_u + row + 1, :] = jnp.exp(
                r.stats_all[k, pl.ds(head, 1), :] - row_log
            )
    columns = r.shares[...].T
    sent.finish()
    attended = jnp.zeros(r.attended.shape, f32)
    for k in range(n_b):
        attended += r.part_got[k].astype(f32) * lanes_of(
            [columns[:, k * n_u + row : k * n_u + row + 1] for row in range(n_u)], out_cut, n_u
        )
    r.attended[...] = attended
    out_all.finish()

    def to_picks(which, send, rows):
        r.partial[...] = rows.astype(bf16).reshape(r.partial.shape)
        landing = r.partial_got.at[which]
        send(r.partial, landing).finish()
        return sum_blocks(landing)

    after_attn = r.pick_rows[:, :MODEL_WIDTH] + to_picks(
        0, links.sum_out, mm(attended.astype(bf16), flat_rows_of(r.out_weight))
    )
    r.after_attn[...] = after_attn
    r.normed_mine[...] = (after_attn * inverse_root(after_attn) * r.gain_mlp[...]).astype(bf16)
    links.normed_mlp(r.normed_mine, r.normed_mlp).finish()
    ff_all.finish()
    gate_up = mm(flat_rows_of(r.normed_mlp), r.ff_weight[...].reshape(MODEL_WIDTH, -1))
    r.gate_up[...] = gate_up
    half = gate_up.shape[1] // 2
    gate_part, up_part = gate_up[:, :half], gate_up[:, half:]
    activated = (gate_part * jax.nn.sigmoid(gate_part) * up_part).astype(bf16)
    down_all.finish()
    after_mlp = after_attn + to_picks(1, links.sum_mlp, mm(activated, flat_rows_of(r.down_weight)))
    r.after_mlp[...] = after_mlp
    r.final_mine[...] = (after_mlp * inverse_root(after_mlp) * r.gain_final[...]).astype(bf16)
    links.final(r.final_mine, r.final_slot).finish()
    links.final_all(r.final_slot, r.final_all).finish()
    each(n_z, lambda step: along_z(step).wait_send(), 1)
    each(n_z, lambda step: each(n_u, lambda hop: across(hop, step).wait_send(), 1))
    each(n_z, lambda step: each(n_u, lambda hop: to_core(hop, step).wait_send()))


def fall_body(n_u, n_b, r, links, s):
    u, b = lax.axis_index(ULY), lax.axis_index(BLK)
    n_z = n_b // 2
    z, c = b // 2, lax.rem(b, 2)
    score_scale = HEAD_WIDTH ** (-0.5)
    picks = r.after_mlp.shape[0]
    places = r.key_raw.shape[0]
    r.factors[...] = jnp.zeros_like(r.factors)
    head_rows = links.head_rows(r.head_rows, r.rows_got)
    links.head_stats(r.head_stats, r.stats_got).finish()
    tops = r.stats_got[0, 0:1, :]
    for k in range(1, n_u):
        tops = jnp.maximum(tops, r.stats_got[k, 0:1, :])
    total = jnp.zeros_like(tops)
    for k in range(n_u):
        factor = jnp.exp(r.stats_got[k, 0:1, :] - tops)
        r.factors[k : k + 1, :] = factor
        total += r.stats_got[k, 1:2, :] * factor
    r.slot_stats[...] = jnp.zeros_like(r.slot_stats)
    r.slot_stats[0:1, :] = tops
    r.slot_stats[1:2, :] = total
    slot_part = links.slot_stats(r.slot_stats, r.slot_got)
    by_row = r.factors[...].T
    head_rows.finish()
    rows = r.rows_got[0].astype(f32) * by_row[:, 0:1]
    for k in range(1, n_u):
        rows += r.rows_got[k].astype(f32) * by_row[:, k : k + 1]
    r.partial[...] = rows.astype(bf16).reshape(r.partial.shape)
    back = links.slot_rows(r.partial, r.partial_got.at[0])
    slot_part.finish()
    tops = r.slot_got[0, 0:1, :]
    for k in range(1, n_b):
        tops = jnp.maximum(tops, r.slot_got[k, 0:1, :])
    total = jnp.zeros_like(tops)
    for k in range(n_b):
        factor = jnp.exp(r.slot_got[k, 0:1, :] - tops)
        r.factors[k : k + 1, :] = factor
        total += r.slot_got[k, 1:2, :] * factor
    log_norm = tops + jnp.log(total)
    for k in range(n_b):
        r.factors[k : k + 1, :] = r.factors[k : k + 1, :] / total
    r.factors[n_b : n_b + 1, :] = log_norm
    r.norms_mine[...] = jnp.broadcast_to(log_norm, r.norms_mine.shape)
    norms_part = links.norms(r.norms_mine, r.norms_all)
    r.columns[...] = r.factors[...].T
    mine = r.columns[pl.ds(pl.multiple_of(b * picks, picks), picks), :]
    back.finish()
    target_rows = r.pick_rows[:, MODEL_WIDTH:]
    grad_final = -target_rows
    for k in range(n_b):
        grad_final += r.partial_got[0, k].astype(f32) * mine[:, k : k + 1]
    grad_final = grad_final * r.weights[:, 0:1]
    target_logit = jnp.sum(
        r.final_mine[...].astype(f32) * target_rows, axis=-1, keepdims=True
    )
    r.terms[...] = r.weights[...] * (target_logit - mine[:, n_b : n_b + 1])
    grad_mlp, gain_final = norm_back_rows(r.after_mlp[...], r.gain_final[...], grad_final)
    r.mine_low[...] = grad_mlp.astype(bf16)
    links.branch(r.mine_low, r.grad_all).finish()
    branch = flat_rows_of(r.grad_all)
    gate_up = r.gate_up[...]
    half = gate_up.shape[1] // 2
    gate_part, up_part = gate_up[:, :half], gate_up[:, half:]
    sigmoid_gate = jax.nn.sigmoid(gate_part)
    grad_act = mm_back(branch, flat_rows_of(r.down_weight))
    grad_gate = grad_act * up_part * sigmoid_gate * (1.0 + gate_part * (1.0 - sigmoid_gate))
    grad_up = grad_act * gate_part * sigmoid_gate
    grad_gate_up = jnp.concatenate([grad_gate, grad_up], axis=1).astype(bf16)
    r.partial[...] = (
        mm_back(grad_gate_up, r.ff_weight[...].reshape(MODEL_WIDTH, -1))
        .astype(bf16)
        .reshape(r.partial.shape)
    )
    back = links.sum_ff(r.partial, r.partial_got.at[1])
    activated = (gate_part * sigmoid_gate * up_part).astype(bf16)
    r.grad_down[...] = mm_outer(activated, branch).astype(bf16).reshape(r.grad_down.shape)
    down_part = links.down(r.grad_down, r.down_got)
    r.grad_ff[...] = (
        mm_outer(flat_rows_of(r.normed_mlp), grad_gate_up).astype(bf16).reshape(r.grad_ff.shape)
    )
    ff_part = links.ff(r.grad_ff, r.ff_got)
    back.finish()
    grad_mid, gain_mlp = norm_back_rows(
        r.after_attn[...], r.gain_mlp[...], sum_blocks(r.partial_got.at[1])
    )
    grad_attn = grad_mlp + grad_mid
    r.mine_low[...] = grad_attn.astype(bf16)
    links.branch_attn(r.mine_low, r.branch_all).finish()
    branch = flat_rows_of(r.branch_all)
    grad_low = mm_back(branch, flat_rows_of(r.out_weight)).astype(bf16)
    r.attended_mine[...] = grad_low
    last = links.attended(r.attended_mine, r.attended_all)
    out_cut = r.attended.shape[1] // n_u
    product = r.attended[...] * grad_low.astype(f32)
    group = lax.broadcasted_iota(jnp.int32, product.shape, 1) // out_cut
    lane = lax.broadcasted_iota(jnp.int32, r.deltas.shape, 1)
    sums = jnp.zeros(r.deltas.shape, f32)
    for row in range(n_u):
        one = jnp.sum(jnp.where(group == row, product, 0.0), axis=-1, keepdims=True)
        sums = jnp.where(lane == row, one, sums)
    r.deltas[...] = sums
    r.delta_mine[...] = r.deltas[...].T[:8, :]
    delta_part = links.deltas(r.delta_mine, r.delta_all)
    r.grad_out[...] = (
        mm_outer(r.attended[...].astype(bf16), branch).astype(bf16).reshape(r.grad_out.shape)
    )
    out_part = links.out(r.grad_out, r.out_got)
    wide = flat_rows_of(r.arrived).astype(f32)
    r.normed_keys[...] = (wide * inverse_root(wide) * r.gain_attn[...]).astype(bf16)
    last.finish()
    delta_part.finish()

    allowed = r.key_lim[...] <= r.slot_picked[...]
    width = KEY_VALUE_HEADS * HEAD_WIDTH
    r.gain_key_row[...] = jnp.zeros((1, HEAD_WIDTH), f32)
    heads_each = QUERY_HEADS // KEY_VALUE_HEADS
    for kv_head in range(KEY_VALUE_HEADS):
        part = slice(kv_head * HEAD_WIDTH, (kv_head + 1) * HEAD_WIDTH)
        key, value = r.key_rot[:, part], r.values[:, part]
        grad_key = jnp.zeros(key.shape, f32)
        grad_value = jnp.zeros(key.shape, f32)
        for head in range(kv_head * heads_each, (kv_head + 1) * heads_each):
            query = head_of(r.query_all, head)
            cuts = cuts_of(head, n_u, n_b)
            upstream = jnp.concatenate([r.attended_all[at, :, there] for at, there, _ in cuts], 1)
            row = head // (QUERY_HEADS // n_u)
            delta = sum(r.delta_all[at, row : row + 1, :] for at, _, _ in cuts)
            scores = mm_back(key, query) * score_scale
            probs = jnp.where(allowed, jnp.exp(scores - r.log_total[head : head + 1, :]), 0.0)
            grad_probs = mm_back(value, upstream)
            grad_scores = (probs * (grad_probs - delta) * score_scale).astype(bf16)
            grad_query = mm_outer(grad_scores, key).astype(bf16)
            share = r.query_send.shape[2] // HEAD_WIDTH
            at = head % share * HEAD_WIDTH
            r.query_send[head // share, :, at : at + HEAD_WIDTH] = grad_query
            grad_key += mm(grad_scores, query)
            grad_value += mm(probs.astype(bf16), upstream)
        grad_head, gain_head = norm_back_rows(
            r.key_raw[:, part],
            r.gain_key[...],
            turned(grad_key.astype(bf16).astype(f32), r.rope_cos[:places], -r.rope_sin[:places]),
        )
        r.gain_key_row[...] += gain_head
        r.grad_kv[:, part] = grad_head.astype(bf16)
        r.grad_kv[:, width + kv_head * HEAD_WIDTH : width + (kv_head + 1) * HEAD_WIDTH] = (
            grad_value.astype(bf16)
        )
    query_part = links.grad_queries(r.query_send, r.query_got)

    def place(hop, step):
        return (lax.rem(u + hop, n_u), lax.rem(z + step, n_z))

    def to_core(hop, step):
        row, line = place(hop, step)
        return remote(
            r.kv_grad.at[row, line, 1 - c],
            r.kv_core.at[hop, step],
            s.core_send.at[hop, step],
            s.core_recv.at[hop, step],
            {BLK: z * 2 + 1 - c},
        )

    def across(hop, step):
        return remote(
            r.kv_core.at[hop, step],
            r.kv_cross.at[hop, step],
            s.xy_send.at[hop, step],
            s.xy_recv.at[hop, step],
            {ULY: lax.rem(u + hop, n_u)},
        )

    def along_z(step):
        return remote(
            r.kv_plane.at[step],
            r.kv_line.at[step],
            s.z_send.at[step],
            s.z_recv.at[step],
            {BLK: lax.rem(z + step, n_z) * 2 + c},
        )

    block_rows = MODEL_WIDTH // n_u

    def weight_grad(k):
        hop = lax.rem(k + 1, n_u)
        row = lax.rem(u + hop, n_u)
        columns = pl.ds(pl.multiple_of(row * block_rows, block_rows), block_rows)
        r.kv_grad[row] = (
            mm_outer(r.normed_keys[:, columns], r.grad_kv[...])
            .astype(bf16)
            .reshape(r.kv_grad.shape[1:])
        )
        each(n_z, lambda step: to_core(hop, step).start())

    each(n_u, weight_grad)
    query_part.finish()
    upstream = sum_blocks(r.query_got).astype(bf16).astype(f32)
    r.gain_query_row[...] = jnp.zeros((1, HEAD_WIDTH), f32)
    for k in range(upstream.shape[1] // HEAD_WIDTH):
        part = slice(k * HEAD_WIDTH, (k + 1) * HEAD_WIDTH)
        grad_head, gain_head = norm_back_rows(
            r.query_raw[:, part],
            r.gain_query[...],
            turned(upstream[:, part], r.rope_cos[places:], -r.rope_sin[places:]),
        )
        r.grad_low[:, part] = grad_head.astype(bf16)
        r.gain_query_row[...] += gain_head
    r.partial[...] = (
        mm_back(r.grad_low[...], r.q_weight[...].reshape(MODEL_WIDTH, -1))
        .astype(bf16)
        .reshape(r.partial.shape)
    )
    back = links.sum_query(r.partial, r.partial_got.at[2])

    def add_pair(hop):
        def one(step):
            row, line = place(hop, step)
            to_core(hop, step).wait_recv()
            r.kv_core[hop, step] = (
                r.kv_grad[row, line, c].astype(f32) + r.kv_core[hop, step].astype(f32)
            ).astype(bf16)

        return one

    def forward_hop(hop):
        def forward(step):
            add_pair(hop)(step)
            across(hop, step).start()

        each(n_z, forward)

    each(n_u, forward_hop, 1)
    each(n_z, add_pair(0))
    r.grad_q[...] = (
        mm_outer(flat_rows_of(r.normed_slot), r.grad_low[...]).astype(bf16).reshape(r.grad_q.shape)
    )
    q_part = links.q(r.grad_q, r.q_got)
    back.finish()
    grad_mine, gain_attn = norm_back_rows(
        r.pick_rows[:, :MODEL_WIDTH], r.gain_attn[...], sum_blocks(r.partial_got.at[2])
    )
    r.mine_low[...] = (grad_attn + grad_mine).astype(bf16)
    pick_part = links.pick_back(r.mine_low, r.pick_back)

    def row_grad(k):
        columns = pl.ds(pl.multiple_of(k * block_rows, block_rows), block_rows)
        r.grad_wide[:, columns] = mm_back(
            r.grad_kv[...], r.kv_weight[k].reshape(block_rows, -1)
        )

    each(n_u, row_grad)
    grad_rows, gain_keys = norm_back_rows(wide, r.gain_attn[...], r.grad_wide[...])
    pick_part.finish()
    pick_hot = jnp.where(r.key_pos[...] == r.slot_picked[...], 1.0, 0.0).astype(bf16)
    r.rows_send[...] = (
        (grad_rows + mm(pick_hot, flat_rows_of(r.pick_back)))
        .astype(bf16)
        .reshape(r.rows_send.shape)
    )
    rows_part = links.rows(r.rows_send, r.rows_back)

    r.gain_mlp_row[...] = gain_mlp
    r.gain_final_row[...] = gain_final
    r.gain_picks_row[...] = gain_attn
    r.gain_rows_row[...] = gain_keys
    r.gains_mine[...] = jnp.zeros_like(r.gains_mine)
    lines = MODEL_WIDTH // 128
    for j in range(lines):
        part = slice(j * 128, (j + 1) * 128)
        r.gains_mine[j : j + 1, :] = r.gain_picks_row[:, part] + r.gain_rows_row[:, part]
        r.gains_mine[lines + j : lines + j + 1, :] = r.gain_mlp_row[:, part]
        r.gains_mine[2 * lines + j : 2 * lines + j + 1, :] = r.gain_final_row[:, part]
    r.gains_mine[3 * lines : 3 * lines + 1, :] = r.gain_query_row[...]
    r.gains_mine[3 * lines + 1 : 3 * lines + 2, :] = r.gain_key_row[...]
    gains_part = links.gains_blk(r.gains_mine, r.gains_got)

    ff_part.finish()
    r.ff_sum[...] = sum_blocks(r.ff_got).astype(bf16)
    ff_last = links.ff_cols(r.ff_sum, r.ff_out)
    down_part.finish()
    r.down_out[...] = sum_blocks(r.down_got)
    out_part.finish()
    r.out_out[...] = sum_blocks(r.out_got)
    gains_part.finish()
    r.gains_slot[...] = sum_blocks(r.gains_got)
    gains_last = links.gains_ulysses(r.gains_slot, r.gains_all)
    q_part.finish()
    r.q_sum[...] = sum_blocks(r.q_got).astype(bf16)
    q_last = links.q_cols(r.q_sum, r.q_out)

    def plane_sum(step):
        total = r.kv_core[0, step].astype(f32)
        for hop in range(1, n_u):
            across(hop, step).wait_recv()
            total = total + r.kv_cross[hop, step].astype(f32)
        return total

    def add_plane(step):
        r.kv_plane[step] = plane_sum(step).astype(bf16)
        along_z(step).start()

    each(n_z, add_plane, 1)
    total = plane_sum(0)
    for step in range(1, n_z):
        along_z(step).wait_recv()
        total = total + r.kv_line[step].astype(f32)
    r.inflow_out[:, QUERY_WIDTH:] = total
    gains_last.finish()
    gains = sum_blocks(r.gains_all)
    for part in (norms_part, ff_last, q_last, rows_part):
        part.finish()
    q_share = r.q_out.shape[2]
    for k in range(n_b):
        r.inflow_out[:, k * q_share : (k + 1) * q_share] = r.q_out[k].astype(f32)
    for k, there, here in ff_cuts(n_u, n_b):
        r.expand_out[:, here] = r.ff_out[k, :, there].astype(f32)
    squares = jnp.sum(gains * gains) / (n_u * n_b)
    for ref in (r.inflow_out, r.expand_out, r.out_out, r.down_out):
        squares += jnp.sum(ref[...] * ref[...])
    r.tails[...] = jnp.zeros_like(r.tails)
    r.tails[0:1, :] = jnp.full((1, 128), squares, f32)
    r.tails[1:2, :] = jnp.full((1, 128), -jnp.sum(r.terms[:, 0:1]), f32)
    for row in range(n_u):
        at = slice(row * n_b * picks, (row + 1) * n_b * picks)
        r.norms_row[:, at] = r.norms_all[row, 0:1, :]
    for k in range(gains.shape[0] - 6):
        r.gains_line[:, k * 128 : (k + 1) * 128] = gains[k : k + 1, :]
    share = r.gains_out.shape[1]
    me = u * n_b + b
    own = jnp.zeros((1, share), f32)
    for k in range(n_u * n_b):
        own = jnp.where(me == k, r.gains_line[:, k * share : (k + 1) * share], own)
    r.gains_out[...] = own
    each(n_z, lambda step: each(n_u, lambda hop: to_core(hop, step).wait_send()))
    each(n_z, lambda step: each(n_u, lambda hop: across(hop, step).wait_send(), 1))
    each(n_z, lambda step: along_z(step).wait_send(), 1)


def lookup_kernel(slots, fills_ref, ids_ref, table_ref, rows_ref, wide, sem):
    wide[...] = jnp.zeros_like(wide)

    def row_copy(place, row):
        return pltpu.make_async_copy(
            table_ref.at[pl.ds(row, 1), :], wide.at[pl.ds(place, 1), :], sem
        )

    def of_peer(peer, total):
        fill = fills_ref[peer]

        def fetch(k, carry):
            place = peer * slots + k
            row_copy(place, ids_ref[place]).start()
            return carry

        lax.fori_loop(0, fill, fetch, 0)
        return total + fill

    total = lax.fori_loop(0, fills_ref.shape[0], of_peer, 0)

    def drain(k, carry):
        row_copy(0, 0).wait()
        return carry

    lax.fori_loop(0, total, drain, 0)
    rows_ref[...] = wide[...].astype(rows_ref.dtype)


def lookup(fills, ids, table, slots):
    places = ids.shape[0]
    return pl.pallas_call(
        functools.partial(lookup_kernel, slots),
        out_shape=jax.ShapeDtypeStruct((places, table.shape[1]), bf16),
        in_specs=[
            pl.BlockSpec(memory_space=pltpu.SMEM),
            pl.BlockSpec(memory_space=pltpu.SMEM),
            pl.BlockSpec(memory_space=pl.ANY),
        ],
        out_specs=VMEM,
        scratch_shapes=[
            pltpu.VMEM((places, table.shape[1]), f32),
            pltpu.SemaphoreType.DMA,
        ],
        compiler_params=pltpu.CompilerParams(vmem_limit_bytes=40 * 1024 * 1024),
        name="lookup",
    )(fills, ids, table)


def table_tile(share, count=9):
    return -(-share // (count * 16)) * 16


def head_kernel(share, finals, table, logits, rows, stats, mixed, top, total):
    tile = table.shape[0]
    step = pl.program_id(0)
    known = step * tile + lax.broadcasted_iota(jnp.int32, (tile, 1), 0) < share
    low = jnp.where(known, table[...], 0.0).astype(bf16)
    scores = mm_back(low, finals[...])
    logits[...] = scores
    scores = jnp.where(known, scores, masked_score)

    @pl.when(step == 0)
    def _():
        top[...] = jnp.full(top.shape, masked_score, f32)
        total[...] = jnp.zeros_like(total)
        mixed[...] = jnp.zeros_like(mixed)

    new_top = jnp.maximum(top[...], jnp.max(scores, axis=0, keepdims=True))
    shrink = jnp.exp(top[...] - new_top)
    weights = jnp.exp(scores - new_top)
    top[...] = new_top
    total[...] = total[...] * shrink + jnp.sum(weights, axis=0, keepdims=True)
    mixed[...] = mixed[...] * shrink + mm_outer(low, weights.astype(bf16))

    @pl.when(step == pl.num_programs(0) - 1)
    def _():
        rows[...] = mixed[...].T.astype(bf16)
        stats[...] = jnp.zeros_like(stats)
        width = stats.shape[2]
        for k in range(stats.shape[0]):
            at = slice(k * width, (k + 1) * width)
            stats[k, 0:1, :] = top[:, at]
            stats[k, 1:2, :] = total[:, at]


def head_call(finals, table, n_u):
    share, width = table.shape
    picks = finals.shape[0]
    tile = table_tile(share, 6)
    stats = (n_u, 8, picks // n_u)
    return pl.pallas_call(
        functools.partial(head_kernel, share),
        grid=(pl.cdiv(share, tile),),
        out_shape=[
            jax.ShapeDtypeStruct((share, picks), f32),
            jax.ShapeDtypeStruct((picks, width), bf16),
            jax.ShapeDtypeStruct(stats, f32),
        ],
        in_specs=[
            pl.BlockSpec((picks, width), lambda i: (0, 0)),
            pl.BlockSpec((tile, width), lambda i: (i, 0)),
        ],
        out_specs=[
            pl.BlockSpec((tile, picks), lambda i: (i, 0)),
            pl.BlockSpec((picks, width), lambda i: (0, 0)),
            pl.BlockSpec(stats, lambda i: (0, 0, 0)),
        ],
        scratch_shapes=[
            pltpu.VMEM((width, picks), f32),
            pltpu.VMEM((1, picks), f32),
            pltpu.VMEM((1, picks), f32),
        ],
        compiler_params=pltpu.CompilerParams(vmem_limit_bytes=44 * 1024 * 1024),
        name="head",
    )(finals, table)


def table_grad_kernel(
    limit, logits, finals, norms, weights, targets, rows, row_ids, grad_out, squares
):
    tile = grad_out.shape[0]
    start = pl.program_id(0) * tile
    ids = start + lax.broadcasted_iota(jnp.int32, (tile, 1), 0)
    grad_logits = (
        weights[...]
        * (jnp.exp(logits[...] - norms[...]) - jnp.where(targets[...] == ids, 1.0, 0.0))
    ).astype(bf16)
    hot = jnp.where(row_ids[...] == ids, 1.0, 0.0).astype(bf16)
    grad = mm(grad_logits, finals[...]) + mm(hot, rows[...])
    grad_out[...] = grad.astype(bf16)

    @pl.when(pl.program_id(0) == 0)
    def _():
        squares[...] = jnp.zeros_like(squares)

    squares[...] += jnp.sum(jnp.where(ids < limit, grad * grad, 0.0), axis=0, keepdims=True)


def table_grad_call(logits, finals, norms, weights, targets, rows, row_ids):
    share, picks = logits.shape
    places, width = rows.shape
    tile = table_tile(share)
    whole = lambda *shape: pl.BlockSpec(shape, lambda i: (0, 0))
    return pl.pallas_call(
        functools.partial(table_grad_kernel, share),
        grid=(pl.cdiv(share, tile),),
        out_shape=[
            jax.ShapeDtypeStruct((share, width), bf16),
            jax.ShapeDtypeStruct((1, width), f32),
        ],
        in_specs=[
            pl.BlockSpec((tile, picks), lambda i: (i, 0)),
            whole(picks, width),
            whole(1, picks),
            whole(1, picks),
            whole(1, picks),
            whole(places, width),
            whole(1, places),
        ],
        out_specs=[
            pl.BlockSpec((tile, width), lambda i: (i, 0)),
            whole(1, width),
        ],
        compiler_params=pltpu.CompilerParams(vmem_limit_bytes=60 * 1024 * 1024),
        cost_estimate=pl.CostEstimate(
            flops=2 * share * width * (picks + places),
            bytes_accessed=share * (4 * picks + 2 * width),
            transcendentals=share * picks,
        ),
        name="table_grad",
    )(logits, finals, norms, weights, targets, rows, row_ids)


def adam_kernel(rate, decay, numbers, weight, first, second, grad, change, new_first, new_second):
    gradient = grad[...].astype(f32) * numbers[:, 0:1]
    mean = beta_first * first[...] + (1.0 - beta_first) * gradient
    square = beta_second * second[...] + (1.0 - beta_second) * gradient * gradient
    new_first[...] = mean
    new_second[...] = square
    change[...] = -rate * (
        mean * numbers[:, 1:2] / (jnp.sqrt(square * numbers[:, 2:3]) + adam_eps)
        + decay * weight[...]
    )


def layer_adam_kernel(rates, decays, numbers, *refs):
    count = len(rates)
    for k in range(count):
        weight, first, second, grad = refs[4 * k : 4 * k + 4]
        adam_kernel(rates[k], decays[k], numbers, weight, first, second, grad, *refs[4 * count + 3 * k :][:3])


def layer_adam_call(numbers, groups, rates, decays):
    arrays = [array for group in groups for array in group]
    return pl.pallas_call(
        functools.partial(layer_adam_kernel, rates, decays),
        out_shape=[
            jax.ShapeDtypeStruct(group[0].shape, f32) for group in groups for _ in range(3)
        ],
        in_specs=[VMEM] * (1 + len(arrays)),
        out_specs=[VMEM] * (3 * len(groups)),
        compiler_params=pltpu.CompilerParams(vmem_limit_bytes=32 * 1024 * 1024),
        name="layer_adam",
    )(numbers, *arrays)


def adam_call(numbers, weight, first, second, grad, rate, decay):
    share, width = weight.shape
    tile = table_tile(share)
    block = pl.BlockSpec((tile, width), lambda i: (i, 0))
    return pl.pallas_call(
        functools.partial(adam_kernel, rate, decay),
        grid=(pl.cdiv(share, tile),),
        out_shape=[jax.ShapeDtypeStruct((share, width), f32)] * 3,
        in_specs=[pl.BlockSpec((1, 128), lambda i: (0, 0))] + [block] * 4,
        out_specs=[block] * 3,
        compiler_params=pltpu.CompilerParams(vmem_limit_bytes=60 * 1024 * 1024),
        name="adam",
    )(numbers, weight, first, second, grad)


def local(
    tokens,
    lengths,
    picked,
    targets,
    advantages,
    step_count,
    embedding,
    first_embedding,
    second_embedding,
    inflow,
    inflow_first_moment,
    inflow_second_moment,
    outflow,
    first_outflow,
    second_outflow,
    expand,
    first_expand,
    second_expand,
    contract,
    first_contract,
    second_contract,
    scales,
    first_scales,
    second_scales,
):
    exchange = Exchanger()
    n_u, n_b = lax.axis_size(ULY), lax.axis_size(BLK)
    n_all = n_u * n_b
    n_z = n_b // 2
    u, b = lax.axis_index(ULY), lax.axis_index(BLK)
    me = u * n_b + b
    slot_count, block_len = tokens.shape
    assert slot_count == n_u and n_b % 2 == 0
    picks = picked.shape[1]
    slot_picks = picks * n_b
    all_picks = slot_picks * n_u
    row_share = embedding.shape[0]
    group = QUERY_HEADS // KEY_VALUE_HEADS
    score_scale = HEAD_WIDTH ** (-0.5)
    in_rows, out_share, ff_share = inflow.shape[0], outflow.shape[0], contract.shape[0]
    q_share = QUERY_WIDTH // n_b
    heads_share = q_share // HEAD_WIDTH
    ff_mine = n_u * ff_share
    out_cut = QUERY_WIDTH // n_all
    scale_share = scales.shape[0]

    width = KEY_VALUE_HEADS * HEAD_WIDTH
    wants_mean = n_b * (block_len + picks) / n_all
    slots = -(-int(wants_mean + 5.2 * math.sqrt(wants_mean)) // 16) * 16
    places = n_u * slots
    blk_g = (BLK, WHOLE)
    column = ((places, 1), jnp.int32)
    row_wide = ((1, MODEL_WIDTH), f32)
    head_wide = ((1, HEAD_WIDTH), f32)
    def begin_call():
        return named_call(
            exchange,
            functools.partial(begin_body, n_u, n_b, row_share, slots),
            dict(
                tokens=blk_g,
                targets=blk_g,
                picked=blk_g,
                advantages=blk_g,
                near=blk_g,
                far=(ULY, WHOLE),
            ),
            {},
            dict(
                tokens=tokens,
                targets=targets,
                picked=picked,
                advantages=advantages,
                lengths=lengths[:, None],
                scales=scales[None, :],
            ),
            dict(
                tokens_all=((n_b,) + tokens.shape, jnp.int32),
                targets_all=((n_b,) + targets.shape, jnp.int32),
                slot_picked=((1, slot_picks), jnp.int32),
                weights=((1, all_picks), f32),
                target_ids=((1, all_picks), jnp.int32),
                weight_wide=((picks, 128), f32),
                row_ids=column,
                key_pos=column,
                key_lim=column,
                target_of=column,
                positions=((places + slot_picks, 1), jnp.int32),
                meta=((24, 128), f32),
                gain_attn=row_wide,
                gain_mlp=row_wide,
                gain_final=row_wide,
                gain_query=head_wide,
                gain_key=head_wide,
            ),
            dict(
                picked_all=((n_b,) + picked.shape, jnp.int32),
                advantages_all=((n_b,) + advantages.shape, f32),
                near=((n_b, 1, scale_share), f32),
                far=((n_u, n_b, 1, scale_share), f32),
                wants=((n_u, block_len + picks), jnp.int32),
                masks=((2 * n_u, block_len + picks), f32),
                labels=((2 * n_u, block_len + picks), f32),
                ranks=((2 * n_u, block_len + picks), f32),
                gains=((1, n_all * scale_share), f32),
            ),
            "begin",
        )

    begin = begin_call()
    gain_rows = [
        begin.gain_attn,
        begin.gain_mlp,
        begin.gain_final,
        begin.gain_query,
        begin.gain_key,
    ]
    gain_attn, gain_query, gain_key = begin.gain_attn[0], begin.gain_query[0], begin.gain_key[0]
    slot_picked = begin.slot_picked[0]
    rounds = (jnp.max(begin.meta[8 : 8 + n_u, 0]).astype(jnp.int32) + slots - 1) // slots
    count_local = begin.meta[16, 0]
    half = HEAD_WIDTH // 2
    lane = jnp.arange(HEAD_WIDTH, dtype=jnp.int32)
    frequency = rope_base ** (-((lane % half).astype(f32) * 2.0 / HEAD_WIDTH))
    angles = begin.positions.astype(f32) * frequency[None, :]
    rope_cos = jnp.cos(angles)
    rope_sin = jnp.sin(angles) * jnp.where(lane < half, -1.0, 1.0)[None, :]
    query_cos, query_sin = rope_cos[places:], rope_sin[places:]
    ff_width = 2 * ff_mine
    own_cut = n_u * out_cut
    rows_low = (picks, MODEL_WIDTH)
    slot_low = (n_b, picks, MODEL_WIDTH)
    stat_rows = (8, slot_picks)
    weight_wide = begin.weight_wide

    def fetch(fills, row_ids):
        rows = lookup(fills, jnp.maximum(row_ids, 0), embedding, slots)
        return rows.reshape(n_u, slots, MODEL_WIDTH)

    def widen_ff(array):
        return (
            array.astype(f32)
            .reshape(n_b, in_rows, 2, n_u, ff_share)
            .transpose(1, 2, 3, 0, 4)
            .reshape(in_rows, 2 * FF)
        )

    def head_of_table(final_all):
        logits, head_rows, head_stats = head_call(final_all, embedding, n_u)
        return (logits, head_rows.reshape(n_u, slot_picks, MODEL_WIDTH), head_stats)

    def usual_way():
        fills = jnp.minimum(begin.meta[:n_u, 0].astype(jnp.int32), slots)
        lined = dict(
            key_pos=begin.key_pos,
            key_lim=begin.key_lim,
            slot_picked=begin.slot_picked,
            gain_attn=gain_rows[0],
            gain_mlp=gain_rows[1],
            gain_final=gain_rows[2],
            gain_query=gain_rows[3],
            gain_key=gain_rows[4],
            rope_cos=rope_cos,
            rope_sin=rope_sin,
        )
        kv_block = (in_rows, 2 * width)
        kv_shape = (n_u, n_z, 2) + kv_block
        q_shape = (n_u, n_b, in_rows, q_share)
        ff_shape = (n_u, n_b, in_rows, ff_width)
        out_shape = (n_u, out_share, MODEL_WIDTH)
        down_shape = (n_u, ff_share, MODEL_WIDTH)
        rows_shape = (n_u, slots, MODEL_WIDTH)
        blk_s, blk_g = (BLK, SPLIT), (BLK, WHOLE)
        uly_s, uly_g = (ULY, SPLIT), (ULY, WHOLE)
        rise = named_call(
            exchange,
            functools.partial(rise_body, n_u, n_b),
            dict(
                rows=uly_s,
                q_split=blk_s,
                ff_split=blk_s,
                picks=blk_s,
                q_all=uly_g,
                normed=blk_g,
                queries=blk_g,
                out_all=uly_g,
                ff_all=uly_g,
                down_all=uly_g,
                parts=blk_s,
                stats=blk_g,
                sum_out=blk_s,
                normed_mlp=blk_g,
                sum_mlp=blk_s,
                final=blk_g,
                final_all=uly_g,
            ),
            dict(
                z_send=(n_z,),
                z_recv=(n_z,),
                own=(1,),
                xy_send=(n_u, n_z),
                xy_recv=(n_u, n_z),
                core_send=(n_u, n_z),
                core_recv=(n_u, n_z),
            ),
            dict(
                rows_in=fetch(fills, begin.row_ids.reshape(-1)),
                inflow=inflow,
                expand=expand,
                outflow=outflow,
                contract=contract,
                target_of=begin.target_of,
                **lined,
            ),
            dict(
                arrived=(rows_shape, bf16),
                kv_weight=(kv_shape, bf16),
                q_weight=(q_shape, bf16),
                ff_weight=(ff_shape, bf16),
                out_weight=(out_shape, bf16),
                down_weight=(down_shape, bf16),
                pick_rows=((picks, 2 * MODEL_WIDTH), f32),
                normed_slot=(slot_low, bf16),
                query_raw=((slot_picks, q_share), f32),
                query_all=((n_b, slot_picks, q_share), bf16),
                key_raw=((places, width), f32),
                key_rot=((places, width), bf16),
                values=((places, width), bf16),
                attended=((slot_picks, own_cut), f32),
                log_total=((QUERY_HEADS, slot_picks), f32),
                after_attn=(rows_low, f32),
                normed_mlp=(slot_low, bf16),
                gate_up=((slot_picks, ff_width), f32),
                after_mlp=(rows_low, f32),
                final_mine=(rows_low, bf16),
                final_all=((n_u,) + slot_low, bf16),
            ),
            dict(
                kv_in=(kv_block, bf16),
                q_in=(q_shape[1:], bf16),
                ff_in=(ff_shape[1:], bf16),
                out_in=(out_shape[1:], bf16),
                down_in=(down_shape[1:], bf16),
                q_part=(q_shape[1:], bf16),
                ff_part=(ff_shape[1:], bf16),
                pick_send=((n_b, picks, 2 * MODEL_WIDTH), bf16),
                pick_got=((n_b, picks, 2 * MODEL_WIDTH), bf16),
                normed_mine=(rows_low, bf16),
                normed_keys=((places, MODEL_WIDTH), bf16),
                query_mine=((slot_picks, q_share), bf16),
                part_send=((n_b, slot_picks, own_cut), bf16),
                part_got=((n_b, slot_picks, own_cut), bf16),
                stats=((2 * QUERY_HEADS, slot_picks), f32),
                stats_all=((n_b, 2 * QUERY_HEADS, slot_picks), f32),
                shares=((n_b * n_u, slot_picks), f32),
                partial=(slot_low, bf16),
                partial_got=((2,) + slot_low, bf16),
                final_slot=(slot_low, bf16),
            ),
            "rise",
        )
        final_all = rise.final_all.reshape(all_picks, MODEL_WIDTH)
        logits, head_rows, head_stats = head_of_table(final_all)
        fall = named_call(
            exchange,
            functools.partial(fall_body, n_u, n_b),
            dict(
                head_rows=uly_s,
                head_stats=uly_s,
                slot_stats=blk_g,
                slot_rows=blk_s,
                norms=uly_g,
                branch=blk_g,
                sum_ff=blk_s,
                down=uly_s,
                ff=uly_s,
                branch_attn=blk_g,
                attended=blk_g,
                deltas=blk_g,
                out=uly_s,
                grad_queries=blk_s,
                sum_query=blk_s,
                q=uly_s,
                pick_back=blk_g,
                rows=uly_s,
                gains_blk=blk_g,
                gains_ulysses=uly_g,
                ff_cols=blk_s,
                q_cols=blk_s,
            ),
            dict(
                core_send=(n_u, n_z),
                core_recv=(n_u, n_z),
                xy_send=(n_u, n_z),
                xy_recv=(n_u, n_z),
                z_send=(n_z,),
                z_recv=(n_z,),
            ),
            dict(
                head_rows=head_rows,
                head_stats=head_stats,
                weights=weight_wide,
                arrived=rise.arrived,
                kv_weight=rise.kv_weight,
                q_weight=rise.q_weight,
                ff_weight=rise.ff_weight,
                out_weight=rise.out_weight,
                down_weight=rise.down_weight,
                pick_rows=rise.pick_rows,
                normed_slot=rise.normed_slot,
                query_raw=rise.query_raw,
                query_all=rise.query_all,
                key_raw=rise.key_raw,
                key_rot=rise.key_rot,
                values=rise.values,
                attended=rise.attended,
                log_total=rise.log_total,
                after_attn=rise.after_attn,
                normed_mlp=rise.normed_mlp,
                gate_up=rise.gate_up,
                after_mlp=rise.after_mlp,
                final_mine=rise.final_mine,
                **lined,
            ),
            dict(
                rows_back=(rows_shape, bf16),
                inflow_out=(inflow.shape, f32),
                expand_out=(expand.shape, f32),
                out_out=(out_shape[1:], f32),
                down_out=(down_shape[1:], f32),
                gains_out=((1, scale_share), f32),
                tails=((8, 128), f32),
                norms_row=((1, all_picks), f32),
            ),
            dict(
                rows_got=((n_u, slot_picks, MODEL_WIDTH), bf16),
                stats_got=((n_u,) + stat_rows, f32),
                slot_stats=(stat_rows, f32),
                slot_got=((n_b,) + stat_rows, f32),
                factors=((n_b + 8, slot_picks), f32),
                columns=((slot_picks, n_b + 8), f32),
                norms_mine=(stat_rows, f32),
                partial=(slot_low, bf16),
                partial_got=((3,) + slot_low, bf16),
                mine_low=(rows_low, bf16),
                grad_all=(slot_low, bf16),
                branch_all=(slot_low, bf16),
                grad_down=(down_shape, bf16),
                down_got=(down_shape, bf16),
                grad_ff=(ff_shape, bf16),
                ff_got=(ff_shape, bf16),
                grad_out=(out_shape, bf16),
                out_got=(out_shape, bf16),
                attended_mine=((slot_picks, own_cut), bf16),
                attended_all=((n_b, slot_picks, own_cut), bf16),
                deltas=((slot_picks, 128), f32),
                delta_mine=(stat_rows, f32),
                delta_all=((n_b,) + stat_rows, f32),
                normed_keys=((places, MODEL_WIDTH), bf16),
                query_send=((n_b, slot_picks, q_share), bf16),
                query_got=((n_b, slot_picks, q_share), bf16),
                grad_kv=((places, 2 * width), bf16),
                kv_grad=(kv_shape, bf16),
                kv_core=((n_u, n_z) + kv_block, bf16),
                kv_cross=((n_u, n_z) + kv_block, bf16),
                kv_plane=((n_z,) + kv_block, bf16),
                kv_line=((n_z,) + kv_block, bf16),
                grad_low=((slot_picks, q_share), bf16),
                grad_q=(q_shape, bf16),
                q_got=(q_shape, bf16),
                q_sum=(q_shape[1:], bf16),
                pick_back=(slot_low, bf16),
                grad_wide=((places, MODEL_WIDTH), f32),
                rows_send=(rows_shape, bf16),
                gain_mlp_row=((1, MODEL_WIDTH), f32),
                gain_final_row=((1, MODEL_WIDTH), f32),
                gain_picks_row=((1, MODEL_WIDTH), f32),
                gain_rows_row=((1, MODEL_WIDTH), f32),
                gain_query_row=((1, HEAD_WIDTH), f32),
                gain_key_row=((1, HEAD_WIDTH), f32),
                norms_all=((n_u,) + stat_rows, f32),
                terms=((picks, 128), f32),
                gains_line=((1, n_all * scale_share), f32),
                gains_mine=((32, 128), f32),
                gains_got=((n_b, 32, 128), f32),
                gains_slot=((32, 128), f32),
                gains_all=((n_u, 32, 128), f32),
                ff_sum=(ff_shape[1:], bf16),
                q_out=(q_shape[1:], bf16),
                ff_out=(ff_shape[1:], bf16),
            ),
            "fall",
        )
        table_grad, table_squares = table_grad_call(
            logits,
            final_all,
            fall.norms_row,
            begin.weights,
            begin.target_ids,
            fall.rows_back.reshape(places, MODEL_WIDTH),
            begin.row_ids.reshape(1, places),
        )
        return (
            fall.tails,
            table_squares,
            table_grad,
            fall.inflow_out,
            fall.out_out,
            fall.expand_out,
            fall.down_out,
            fall.gains_out,
        )

    def long_way():
        inflow_low = inflow.astype(bf16)
        q_cols = inflow_low[:, :QUERY_WIDTH].reshape(in_rows, n_b, q_share).transpose(1, 0, 2)
        ff_cols = (
            expand.astype(bf16)
            .reshape(in_rows, 2, n_u, n_b, ff_share)
            .transpose(3, 0, 1, 2, 4)
            .reshape(n_b, in_rows, 2 * ff_mine)
        )
        wants_block = block_len + picks
        wants_count = n_b * wants_block
        wants = (
            jnp.concatenate([begin.tokens_all, begin.targets_all], axis=2)
            .transpose(1, 0, 2)
            .reshape(n_u, wants_count)
        )
        my_length = lax.dynamic_index_in_dim(lengths, u, 0, keepdims=False)
        owners = wants // row_share
        own_owners = lax.dynamic_index_in_dim(owners, u, 0, keepdims=True)
        sent_mask = owners == me
        got_mask = own_owners == jnp.arange(n_u, dtype=jnp.int32)[:, None] * n_b + b
        masks = jnp.concatenate([sent_mask, got_mask], axis=0)
        totals_sent = jnp.sum(sent_mask.astype(f32), axis=1).astype(jnp.int32)
        lanes = math.gcd(wants_count, 128)
        blocks = masks.astype(bf16).reshape(2 * n_u, wants_count // lanes, lanes)
        before = (jnp.arange(lanes)[:, None] < jnp.arange(lanes)[None, :]).astype(bf16)
        block_sums = jnp.sum(blocks.astype(f32), axis=-1)
        chunk = jnp.arange(wants_count // lanes)
        block_base = mm(block_sums.astype(bf16), (chunk[:, None] < chunk[None, :]).astype(bf16))
        ranks = (
            mm(blocks.reshape(-1, lanes), before).reshape(blocks.shape) + block_base[:, :, None]
        ).reshape(2 * n_u, wants_count)
        ranks = jnp.where(masks, ranks.astype(jnp.int32), -1)
        labels = jnp.concatenate(
            [
                wants - me * row_share,
                jnp.broadcast_to(
                    jnp.arange(wants_count, dtype=jnp.int32)[None, :], (n_u, wants_count)
                ),
            ],
            axis=0,
        )

        def slot_tables(turn, hot):
            slot_rank = turn * slots + jnp.arange(slots, dtype=jnp.int32)
            hit = ranks[:, None, :] == slot_rank[None, :, None]
            found = jnp.sum(jnp.where(hit, labels[:, None, :] + 1, 0), axis=-1) - 1
            fills = jnp.clip(totals_sent - turn * slots, 0, slots)
            row_ids = found[:n_u].reshape(-1)
            entry = found[n_u:].reshape(-1)
            block, inside = entry // wants_block, entry % wants_block
            is_token = (entry >= 0) & (inside < block_len)
            key_pos = jnp.where(is_token, block * block_len + inside, 1 << 30)
            target_of = jnp.where(
                (entry >= 0) & (inside >= block_len), block * picks + inside - block_len, -1
            )
            if not hot:
                return (row_ids, fills, key_pos, None, target_of)
            pick_hot = (slot_picked[:, None] == key_pos[None, :]).astype(bf16)
            target_hot = (jnp.arange(slot_picks)[:, None] == target_of[None, :]).astype(bf16)
            return (row_ids, fills, key_pos, pick_hot, target_hot)

        row_ids, fills, key_pos, pick_hot, target_hot = slot_tables(jnp.int32(0), True)

        arrived, kv_weight, q_weight, ff_split = start_call(
            exchange, fetch(fills, row_ids), inflow_low[:, QUERY_WIDTH:], q_cols, ff_cols
        )
        arrived = arrived.reshape(places, MODEL_WIDTH)
        kv_weight = kv_weight.reshape(MODEL_WIDTH, -1)
        q_weight = q_weight.reshape(MODEL_WIDTH, q_share)
        def picked_rows(pick_hot, target_hot, arrived):
            return jnp.concatenate([mm(pick_hot, arrived), mm(target_hot, arrived)], axis=1)

        refetch_id = [exchange.next_id() for _ in range(5)]

        def refetch(turn, which):
            tables = slot_tables(turn, True)
            (got,) = exchange.many(
                ((ULY, SPLIT),), fetch(tables[1], tables[0]), collective_id=refetch_id[which]
            )
            return (tables, got.reshape(places, MODEL_WIDTH))

        def more(state):
            return state[0] < rounds

        def picks_turn(state):
            tables, got = refetch(state[0], 0)
            return (state[0] + 1, state[1] + picked_rows(tables[3], tables[4], got))

        pick_part = picked_rows(pick_hot, target_hot, arrived)
        _, pick_part = lax.while_loop(more, picks_turn, (jnp.int32(1), pick_part))
        got_picks, normed_slot, query_raw, query_all, ff_all, out_all, down_all = fused_call(
            exchange,
            functools.partial(query_body, n_b),
            ((BLK, SPLIT), (BLK, WHOLE), (BLK, WHOLE)) + ((ULY, WHOLE),) * 3,
            (
                pick_part.astype(bf16).reshape(n_b, picks, 2 * MODEL_WIDTH),
                gain_rows[0],
                gain_rows[3],
                q_weight,
                query_cos,
                query_sin,
                ff_split,
                outflow.astype(bf16),
                contract.astype(bf16),
            ),
            (
                ((picks, 2 * MODEL_WIDTH), f32),
                (slot_low, bf16),
                ((slot_picks, q_share), f32),
                ((n_b, slot_picks, q_share), bf16),
                ((n_u, n_b, in_rows, ff_width), bf16),
                ((n_u, out_share, MODEL_WIDTH), bf16),
                ((n_u, ff_share, MODEL_WIDTH), bf16),
            ),
            (
                ((n_b, picks, 2 * MODEL_WIDTH), bf16),
                (rows_low, bf16),
                ((slot_picks, q_share), bf16),
            ),
            "queries",
        )
        ff_weight = ff_all.reshape(MODEL_WIDTH, ff_width)
        out_weight = out_all.reshape(n_u * out_share, MODEL_WIDTH)
        down_weight = down_all.reshape(ff_mine, MODEL_WIDTH)

        def keys_of(arrived, key_pos):
            embedded = arrived.astype(f32)
            normed = (embedded * inverse_root(embedded) * gain_attn).astype(bf16)
            mixed = mm(normed, kv_weight)
            half = KEY_VALUE_HEADS * HEAD_WIDTH
            key_raw = mixed[:, :half].reshape(places, KEY_VALUE_HEADS, HEAD_WIDTH)
            values = mixed[:, half:].reshape(places, KEY_VALUE_HEADS, HEAD_WIDTH)
            angle_tables = rope_angles(jnp.where(key_pos < (1 << 30), key_pos, 0))
            key_rot = rotate(key_raw * inverse_root(key_raw) * gain_key, angle_tables, 1.0)
            return (
                embedded,
                normed,
                key_raw,
                angle_tables,
                key_rot.astype(bf16).transpose(1, 0, 2),
                values.astype(bf16).transpose(1, 0, 2),
            )

        query_pos = jnp.tile(slot_picked, group)

        def allowed_of(key_pos):
            return ((key_pos[None, :] <= query_pos[:, None]) & (key_pos[None, :] < my_length))[None]

        def scores_of(query_groups, key_rot, allowed):
            scores = (
                jnp.einsum("kqd,kjd->kqj", query_groups, key_rot, preferred_element_type=f32)
                * score_scale
            )
            return jnp.where(allowed, scores, masked_score)

        def attend(scores, allowed, values):
            part_max = jnp.max(scores, axis=-1, keepdims=True)
            weights = jnp.where(allowed, jnp.exp(scores - part_max), 0.0)
            out = jnp.einsum("kqj,kjd->kqd", weights.astype(bf16), values, preferred_element_type=f32)
            return (part_max, jnp.sum(weights, axis=-1, keepdims=True), out)

        keys = keys_of(arrived, key_pos)

        query_groups = (
            query_all.reshape(n_b, slot_picks, heads_share, HEAD_WIDTH)
            .transpose(0, 2, 1, 3)
            .reshape(KEY_VALUE_HEADS, group * slot_picks, HEAD_WIDTH)
        )
        allowed = allowed_of(key_pos)
        scores = scores_of(query_groups, keys[4], allowed)

        def attend_turn(state):
            turn, top, total, out = state
            tables, got = refetch(turn, 1)
            keys_now = keys_of(got, tables[2])
            allowed_now = allowed_of(tables[2])
            new = attend(scores_of(query_groups, keys_now[4], allowed_now), allowed_now, keys_now[5])
            both = jnp.maximum(top, new[0])
            old_factor, new_factor = jnp.exp(top - both), jnp.exp(new[0] - both)
            return (
                turn + 1,
                both,
                total * old_factor + new[1] * new_factor,
                out * old_factor + new[2] * new_factor,
            )

        _, part_max, part_sum, part_out = lax.while_loop(
            more, attend_turn, (jnp.int32(1),) + attend(scores, allowed, keys[5])
        )
        part_send = (
            part_out.astype(bf16)
            .reshape(QUERY_HEADS, slot_picks, HEAD_WIDTH)
            .transpose(1, 0, 2)
            .reshape(slot_picks, n_u, n_b, out_cut)
            .transpose(2, 0, 1, 3)
            .reshape(n_b, slot_picks, n_u * out_cut)
        )
        stats = jnp.stack([part_max[..., 0], part_sum[..., 0]]).reshape(2 * QUERY_HEADS, slot_picks)
        (
            attended,
            log_total,
            after_attn,
            normed_mlp,
            gate_up,
            after_mlp,
            final_mine,
            final_all,
        ) = fused_call(
            exchange,
            functools.partial(forward_body, n_u, n_b),
            ((BLK, SPLIT), (BLK, WHOLE), (BLK, SPLIT), (BLK, WHOLE), (BLK, SPLIT), (BLK, WHOLE))
            + ((ULY, WHOLE),),
            (
                part_send,
                stats,
                got_picks,
                out_weight,
                ff_weight,
                down_weight,
                gain_rows[1],
                gain_rows[2],
            ),
            (
                ((slot_picks, own_cut), f32),
                ((QUERY_HEADS, slot_picks), f32),
                (rows_low, f32),
                (slot_low, bf16),
                ((slot_picks, ff_width), f32),
                (rows_low, f32),
                (rows_low, bf16),
                ((n_u,) + slot_low, bf16),
            ),
            (
                ((n_b, slot_picks, own_cut), bf16),
                ((n_b, 2 * QUERY_HEADS, slot_picks), f32),
                ((n_b * n_u, slot_picks), f32),
                (slot_low, bf16),
                ((2,) + slot_low, bf16),
                (rows_low, bf16),
                (slot_low, bf16),
            ),
            "forward",
        )

        final_all = final_all.reshape(all_picks, MODEL_WIDTH)
        logits, head_rows, head_stats = head_of_table(final_all)
        (
            norms_all,
            terms,
            grad_gain_mlp,
            grad_gain_final,
            grad_ff,
            grad_out,
            grad_down,
            grad_after_attn,
            _,
            got_attended,
            got_delta,
        ) = fused_call(
            exchange,
            functools.partial(backward_body, n_u, n_b),
            (
                (ULY, SPLIT),
                (ULY, SPLIT),
                (BLK, SPLIT),
                (BLK, WHOLE),
                (ULY, WHOLE),
                (BLK, WHOLE),
                (BLK, SPLIT),
                (BLK, WHOLE),
                (BLK, WHOLE),
                (BLK, WHOLE),
            ),
            (
                head_rows,
                head_stats,
                final_mine,
                got_picks,
                weight_wide,
                after_mlp,
                after_attn,
                gate_up,
                normed_mlp,
                attended,
                out_weight,
                ff_weight,
                down_weight,
                gain_rows[1],
                gain_rows[2],
            ),
            (
                ((n_u,) + stat_rows, f32),
                ((picks, 128), f32),
                ((1, MODEL_WIDTH), f32),
                ((1, MODEL_WIDTH), f32),
                ((n_u, n_b, in_rows, ff_width), bf16),
                ((n_u, out_share, MODEL_WIDTH), bf16),
                ((n_u, ff_share, MODEL_WIDTH), bf16),
                (rows_low, f32),
                (slot_low, bf16),
                ((n_b, slot_picks, own_cut), bf16),
                ((n_b,) + stat_rows, f32),
            ),
            (
                ((n_u, slot_picks, MODEL_WIDTH), bf16),
                ((n_u,) + stat_rows, f32),
                (stat_rows, f32),
                ((n_b,) + stat_rows, f32),
                ((n_b + 8, slot_picks), f32),
                ((slot_picks, n_b + 8), f32),
                (stat_rows, f32),
                (slot_low, bf16),
                ((2,) + slot_low, bf16),
                (rows_low, bf16),
                (slot_low, bf16),
                ((slot_picks, own_cut), bf16),
                ((slot_picks, 128), f32),
                (stat_rows, f32),
            ),
            "backward",
        )
        loss_local = -jnp.sum(terms[:, 0])
        grad_heads = (
            got_attended.reshape(n_b, slot_picks, n_u, out_cut)
            .transpose(1, 2, 0, 3)
            .reshape(slot_picks, QUERY_HEADS, HEAD_WIDTH)
            .transpose(1, 0, 2)
            .reshape(KEY_VALUE_HEADS, group * slot_picks, HEAD_WIDTH)
        )
        row_delta = jnp.sum(
            got_delta[:, :n_u].transpose(1, 0, 2).reshape(QUERY_HEADS, HEAD_WIDTH // out_cut, slot_picks), axis=1
        ).reshape(KEY_VALUE_HEADS, group * slot_picks, 1)
        log_groups = log_total.reshape(KEY_VALUE_HEADS, group * slot_picks, 1)

        def score_grads(scores, allowed, values):
            probs = jnp.where(allowed, jnp.exp(scores - log_groups), 0.0)
            grad_probs = jnp.einsum("kqd,kjd->kqj", grad_heads, values, preferred_element_type=f32)
            return (probs, (probs * (grad_probs - row_delta) * score_scale).astype(bf16))

        def query_grads(grad_scores, key_rot):
            return jnp.einsum("kqj,kjd->kqd", grad_scores, key_rot, preferred_element_type=f32)

        def key_grads(probs, grad_scores, keys):
            grad_key = jnp.einsum(
                "kqj,kqd->kjd", grad_scores, query_groups, preferred_element_type=f32
            )
            grad_value = jnp.einsum(
                "kqj,kqd->kjd", probs.astype(bf16), grad_heads, preferred_element_type=f32
            )
            upstream = rotate(
                grad_key.astype(bf16).astype(f32).transpose(1, 0, 2), keys[3], -1.0
            )
            grad_raw, grad_gain = norm_back(keys[2], gain_key, upstream)
            grad_kv = jnp.concatenate(
                [
                    grad_raw.reshape(places, -1).astype(bf16),
                    grad_value.astype(bf16).transpose(1, 0, 2).reshape(places, -1),
                ],
                axis=1,
            )
            return (grad_kv, grad_gain)

        def row_grads(grad_kv, keys):
            return norm_back(keys[0], gain_attn, mm_back(grad_kv, kv_weight))

        def redo(turn, which):
            tables, got = refetch(turn, which)
            keys_now = keys_of(got, tables[2])
            allowed_now = allowed_of(tables[2])
            scores_now = scores_of(query_groups, keys_now[4], allowed_now)
            return (tables, keys_now) + score_grads(scores_now, allowed_now, keys_now[5])

        def query_turn(state):
            _, keys_now, _, grad_scores_now = redo(state[0], 2)
            return (state[0] + 1, state[1] + query_grads(grad_scores_now, keys_now[4]))

        probs, grad_scores = score_grads(scores, allowed, keys[5])
        _, grad_query_part = lax.while_loop(
            more, query_turn, (jnp.int32(1), query_grads(grad_scores, keys[4]))
        )
        query_send = (
            grad_query_part.astype(bf16)
            .reshape(n_b, heads_share, slot_picks, HEAD_WIDTH)
            .transpose(0, 2, 1, 3)
            .reshape(n_b, slot_picks, q_share)
        )
        (
            grad_gain_query,
            grad_gain_picks,
            grad_q,
            pick_back,
            sum_ff,
            sum_outflow,
            sum_contract,
        ) = fused_call(
            exchange,
            query_back_body,
            ((BLK, SPLIT), (BLK, SPLIT), (BLK, WHOLE)) + ((ULY, SPLIT),) * 3,
            (
                query_send,
                query_raw,
                query_cos,
                query_sin,
                gain_rows[3],
                q_weight,
                normed_slot,
                got_picks,
                gain_rows[0],
                grad_after_attn,
                grad_ff,
                grad_out,
                grad_down,
            ),
            (
                ((1, HEAD_WIDTH), f32),
                ((1, MODEL_WIDTH), f32),
                ((n_u, n_b, in_rows, q_share), bf16),
                (slot_low, bf16),
                ((n_b, in_rows, ff_width), bf16),
                ((out_share, MODEL_WIDTH), f32),
                ((ff_share, MODEL_WIDTH), f32),
            ),
            (
                ((n_b, slot_picks, q_share), bf16),
                ((slot_picks, q_share), bf16),
                (slot_low, bf16),
                (slot_low, bf16),
                (rows_low, bf16),
                ((n_u, n_b, in_rows, ff_width), bf16),
                ((n_u, out_share, MODEL_WIDTH), bf16),
                ((n_u, ff_share, MODEL_WIDTH), bf16),
            ),
            "query_grads",
        )
        pick_back = pick_back.reshape(slot_picks, MODEL_WIDTH)

        grad_kv, grad_gain_key = key_grads(probs, grad_scores, keys)
        grad_kv_weight = mm_outer(keys[1], grad_kv)
        grad_rows, grad_gain_attn = row_grads(grad_kv, keys)

        def weight_turn(state):
            turn, weight_sum, key_sum, attn_sum = state
            _, keys_now, probs_now, grad_scores_now = redo(turn, 3)
            grad_kv_now, gain_key_now = key_grads(probs_now, grad_scores_now, keys_now)
            _, gain_attn_now = row_grads(grad_kv_now, keys_now)
            return (
                turn + 1,
                weight_sum + mm_outer(keys_now[1], grad_kv_now),
                key_sum + gain_key_now,
                attn_sum + gain_attn_now,
            )

        _, grad_kv_weight, grad_gain_key, grad_gain_attn = lax.while_loop(
            more, weight_turn, (jnp.int32(1), grad_kv_weight, grad_gain_key, grad_gain_attn)
        )
        grad_scales = jnp.concatenate(
            [
                grad_gain_attn + grad_gain_picks[0],
                grad_gain_mlp[0],
                grad_gain_final[0],
                grad_gain_query[0],
                grad_gain_key,
            ]
        )

        token_rows = (grad_rows + mm_outer(pick_hot, pick_back)).astype(bf16)
        sum_kv, rows_back, got_q, got_ff, got_scales = settle_call(
            exchange,
            grad_kv_weight.astype(bf16).reshape(n_u, n_z, 2, in_rows, -1),
            token_rows.reshape(n_u, slots, MODEL_WIDTH),
            grad_q,
            sum_ff,
            jnp.pad(
                grad_scales.reshape(n_all, scale_share), ((0, 0), (0, 128 - scale_share))
            ).reshape(n_all, 1, 128),
        )
        sum_q = got_q.astype(f32).transpose(1, 0, 2).reshape(in_rows, QUERY_WIDTH)
        sum_inflow = jnp.concatenate([sum_q, sum_kv], axis=1)
        sum_expand = widen_ff(got_ff)
        sum_scales = jnp.sum(got_scales, axis=0)[0, :scale_share]

        table_grad, table_squares = table_grad_call(
            logits,
            final_all,
            norms_all[:, 0].reshape(1, all_picks),
            begin.weights,
            begin.target_ids,
            rows_back.reshape(places, MODEL_WIDTH),
            row_ids.reshape(1, places),
        )
        return_id = exchange.next_id()

        def return_turn(state):
            turn, so_far, _ = state
            tables, keys_now, probs_now, grad_scores_now = redo(turn, 4)
            grad_kv_now, _ = key_grads(probs_now, grad_scores_now, keys_now)
            rows_now, _ = row_grads(grad_kv_now, keys_now)
            rows_now = (rows_now + mm_outer(tables[3], pick_back)).astype(bf16)
            (back,) = exchange.many(
                ((ULY, SPLIT),),
                rows_now.reshape(n_u, slots, MODEL_WIDTH),
                collective_id=return_id,
            )
            hot = (
                jnp.arange(row_share, dtype=jnp.int32)[:, None] == tables[0][None, :]
            ).astype(bf16)
            grown = so_far.astype(f32) + mm(hot, back.reshape(places, MODEL_WIDTH))
            return (turn + 1, grown.astype(bf16), jnp.sum(grown * grown, axis=0, keepdims=True))

        _, table_grad, table_squares = lax.while_loop(
            more, return_turn, (jnp.int32(1), table_grad, table_squares)
        )
        squares = jnp.zeros((), f32)
        for grad_piece in (sum_inflow, sum_outflow, sum_expand, sum_contract, sum_scales):
            squares = squares + jnp.sum(grad_piece * grad_piece)
        tails = jnp.pad(jnp.stack([squares, loss_local]), (0, 6))
        return (
            jnp.broadcast_to(tails[:, None], (8, 128)),
            table_squares,
            table_grad,
            sum_inflow,
            sum_outflow,
            sum_expand,
            sum_contract,
            sum_scales[None, :],
        )

    step_float = step_count[0].astype(f32)
    first_scale = 1.0 / (1.0 - beta_first**step_float)
    second_scale = 1.0 / (1.0 - beta_second**step_float)

    steps = jnp.pad(jnp.stack([first_scale, second_scale]), (1, 125)).reshape(1, 128)

    def finish(tails, table_squares, table_grad, *layer_grads):
        numbers = named_call(
            exchange,
            totals_body,
            dict(near=(ALL, WHOLE)),
            {},
            dict(
                tails=tails,
                table_squares=table_squares,
                counts=begin.meta[16:],
                steps=steps,
            ),
            dict(numbers=((1, 128), f32)),
            dict(mine=((1, 128), f32), all=((n_all, 1, 128), f32)),
            "totals",
        ).numbers
        outputs = [numbers[0, 3], numbers[0, 4]]
        outputs += adam_call(
            numbers,
            embedding,
            first_embedding,
            second_embedding,
            table_grad,
            learning_rates[0],
            weight_decays[0],
        )
        outputs += layer_adam_call(
            numbers,
            (
                (inflow, inflow_first_moment, inflow_second_moment, layer_grads[0]),
                (outflow, first_outflow, second_outflow, layer_grads[1]),
                (expand, first_expand, second_expand, layer_grads[2]),
                (contract, first_contract, second_contract, layer_grads[3]),
                (scales[None, :], first_scales[None, :], second_scales[None, :], layer_grads[4]),
            ),
            learning_rates[1:],
            weight_decays[1:],
        )
        outputs[-3:] = [array[0] for array in outputs[-3:]]
        return tuple(outputs)

    _, outputs = lax.while_loop(
        lambda state: state[0],
        lambda state: (jnp.bool_(False), finish(*long_way())),
        (rounds > 1, finish(*usual_way())),
    )
    return outputs


def solution(mesh):
    rows = P((ULY, BLK), None)
    flat_rows = P((ULY, BLK))
    column = P(None, BLK)
    return jax.shard_map(
        local,
        mesh=mesh,
        in_specs=(column, P(), column, column, column, P()) + (rows,) * 15 + (flat_rows,) * 3,
        out_specs=(P(), P()) + (rows,) * 15 + (flat_rows,) * 3,
        check_vma=False,
    )
```

```python
import functools
import math

import jax
import jax.numpy as jnp
from jax import lax
from jax.experimental import pallas as pl
from jax.experimental.pallas import tpu as pltpu
from jax.sharding import PartitionSpec as P

MODEL_WIDTH = 1024
QUERY_HEADS = 16
KEY_VALUE_HEADS = 8
HEAD_WIDTH = 128
FF = 3072
QUERY_WIDTH = QUERY_HEADS * HEAD_WIDTH

norm_eps = 1e-06
rope_base = 1000000.0
clip_limit = 0.01
beta_first = 0.9
beta_second = 0.95
adam_eps = 1e-08
learning_rates = (0.01, 0.003, 0.07, 0.003, 0.002, 0.01)
weight_decays = (0.1, 0.1, 0.1, 0.1, 0.1, 0.0)
masked_score = -1e30

bf16 = jnp.bfloat16
f32 = jnp.float32
BLK, ULY, ALL = "blk", "ulysses", "all"
SPLIT, WHOLE = "s", "g"


def inverse_root(values):
    return lax.rsqrt(jnp.mean(values * values, axis=-1, keepdims=True) + norm_eps)


def norm_back(inputs, gain_vec, upstream):
    root_scale = inverse_root(inputs)
    unit_rows = inputs * root_scale
    weighted = upstream * gain_vec
    grad_inputs = root_scale * (
        weighted - unit_rows * jnp.mean(weighted * unit_rows, axis=-1, keepdims=True)
    )
    grad_gain = jnp.sum((upstream * unit_rows).reshape(-1, gain_vec.shape[-1]), axis=0)
    return (grad_inputs, grad_gain)


def rope_angles(positions):
    half_width = HEAD_WIDTH // 2
    frequency = rope_base ** (
        -(jnp.arange(half_width, dtype=jnp.int32).astype(f32) * 2.0 / HEAD_WIDTH)
    )
    angles = positions.astype(f32)[:, None] * frequency[None, :]
    return (jnp.cos(angles), jnp.sin(angles))


def rotate(values, tables, sign_value):
    half_width = values.shape[-1] // 2
    front_half = values[..., :half_width]
    back_half = values[..., half_width:]
    cosine_part = tables[0][:, None, :]
    sine_part = tables[1][:, None, :] * sign_value
    return jnp.concatenate(
        [
            front_half * cosine_part - back_half * sine_part,
            back_half * cosine_part + front_half * sine_part,
        ],
        axis=-1,
    )


def mm(left, right):
    return lax.dot_general(left, right, (((1,), (0,)), ((), ())), preferred_element_type=f32)


def mm_outer(left, right):
    return lax.dot_general(left, right, (((0,), (0,)), ((), ())), preferred_element_type=f32)


def mm_back(left, right):
    return lax.dot_general(left, right, (((1,), (1,)), ((), ())), preferred_element_type=f32)


def spread_rows(onehot, rows):
    return lax.dot_general(
        onehot.astype(f32),
        rows,
        (((0,), (0,)), ((), ())),
        precision=lax.Precision.HIGHEST,
        preferred_element_type=f32,
    )


def place_of(axis, blk_count, peer):
    if axis == ALL:
        return {ULY: peer // blk_count, BLK: lax.rem(peer, blk_count)}
    return {axis: peer}


def rank_of(axis, blk_count):
    row, column = lax.axis_index(ULY), lax.axis_index(BLK)
    return {ULY: row, BLK: column, ALL: row * blk_count + column}[axis]


def greet(axes, blk_count, counts):
    barrier = pltpu.get_barrier_semaphore()
    axes = (ALL,) if ALL in axes else tuple(axes)
    total = 0
    for axis in axes:
        me, count = rank_of(axis, blk_count), counts[axis]

        def call(step, carry, axis=axis, me=me, count=count):
            pl.semaphore_signal(
                barrier,
                inc=1,
                device_id=place_of(axis, blk_count, lax.rem(me + step, count)),
                device_id_type=pl.DeviceIdType.MESH,
            )
            return carry

        lax.fori_loop(1, count, call, 0)
        total += count - 1
    pl.semaphore_wait(barrier, total)


def each(count, body, first=0):
    def step(k, carry):
        body(k)
        return carry

    lax.fori_loop(first, count, step, 0)


def remote(source, target, send_sem, recv_sem, device_id):
    return pltpu.make_async_remote_copy(
        src_ref=source,
        dst_ref=target,
        send_sem=send_sem,
        recv_sem=recv_sem,
        device_id=device_id,
        device_id_type=pl.DeviceIdType.MESH,
    )


class Part:
    def __init__(self, axis, kind, source, landing, send_sems, recv_sems, own_sem, blk_count):
        self.axis, self.kind, self.blk_count = axis, kind, blk_count
        self.source, self.landing = source, landing
        self.send_sems, self.recv_sems, self.own_sem = send_sems, recv_sems, own_sem
        self.me, self.count = rank_of(axis, blk_count), landing.shape[0]

    def copy(self, step):
        peer = lax.rem(self.me + step, self.count)
        return remote(
            self.source.at[peer] if self.kind == SPLIT else self.source,
            self.landing.at[self.me],
            self.send_sems.at[step],
            self.recv_sems.at[step],
            place_of(self.axis, self.blk_count, peer),
        )

    def own(self):
        return pltpu.make_async_copy(
            self.source.at[self.me] if self.kind == SPLIT else self.source,
            self.landing.at[self.me],
            self.own_sem,
        )

    def start(self):
        each(self.count, lambda step: self.copy(step).start(), 1)
        self.own().start()

    def finish(self):
        self.own().wait()
        each(self.count, lambda step: self.copy(step).wait(), 1)


def sems(count):
    return [
        pltpu.SemaphoreType.DMA((count,)),
        pltpu.SemaphoreType.DMA((count,)),
        pltpu.SemaphoreType.DMA,
    ]


def exchange_kernel(plan, blk_count, counts, *refs):
    parts = len(plan)
    entries = [
        Part(axis, kind, refs[k], refs[parts + k], *refs[2 * parts + 3 * k :][:3], blk_count)
        for k, (axis, kind) in enumerate(plan)
    ]
    greet({axis for axis, _ in plan}, blk_count, counts)
    for entry in entries:
        entry.start()
    for entry in entries:
        entry.finish()


def axis_counts():
    n_u, n_b = lax.axis_size(ULY), lax.axis_size(BLK)
    return {ULY: n_u, BLK: n_b, ALL: n_u * n_b}


VMEM = pl.BlockSpec(memory_space=pltpu.VMEM)


def remote_call(kernel, collective_id, shapes, scratch, arrays, name, grant=40):
    few = lax.axis_size(ULY) * lax.axis_size(BLK) <= 32
    return pl.pallas_call(
        kernel,
        out_shape=shapes,
        in_specs=[VMEM] * len(arrays),
        out_specs=[VMEM] * len(shapes),
        scratch_shapes=scratch,
        compiler_params=pltpu.CompilerParams(
            collective_id=collective_id,
            has_side_effects=True,
            vmem_limit_bytes=(grant if few or grant < 40 else 57) * 1024 * 1024,
        ),
        name=name,
    )(*arrays)


class Exchanger:
    def __init__(self):
        self.used = 0

    def next_id(self):
        self.used += 1
        return self.used - 1

    def many(self, plan, *arrays, collective_id=None):
        counts = axis_counts()
        shapes = [
            jax.ShapeDtypeStruct(
                array.shape if kind == SPLIT else (counts[axis],) + array.shape, array.dtype
            )
            for (axis, kind), array in zip(plan, arrays)
        ]
        scratch = []
        for axis, _ in plan:
            scratch += sems(counts[axis])
        if collective_id is None:
            collective_id = self.next_id()
        return remote_call(
            functools.partial(exchange_kernel, plan, counts[BLK], counts),
            collective_id,
            shapes,
            scratch,
            arrays,
            "exchange_" + str(collective_id),
        )

    def __call__(self, axis, kinds, *arrays):
        return self.many(tuple((axis, kind) for kind in kinds), *arrays)


def start_kernel(
    blk_count,
    counts,
    rows_in,
    kv_in,
    q_in,
    ff_in,
    rows_out,
    kv_out,
    q_out,
    ff_out,
    q_split,
    z_send,
    z_recv,
    own_sem,
    xy_send,
    xy_recv,
    core_send,
    core_recv,
    *part_sems,
):
    u, b = lax.axis_index(ULY), lax.axis_index(BLK)
    n_u, n_z = kv_out.shape[0], kv_out.shape[1]
    z, c = b // 2, lax.rem(b, 2)
    greet({ULY, BLK}, blk_count, counts)
    rows = Part(ULY, SPLIT, rows_in, rows_out, *part_sems[0:3], blk_count)
    first_q = Part(BLK, SPLIT, q_in, q_split, *part_sems[3:6], blk_count)
    then_q = Part(ULY, WHOLE, q_split, q_out, *part_sems[6:9], blk_count)
    split_ff = Part(BLK, SPLIT, ff_in, ff_out, *part_sems[9:12], blk_count)

    def along_z(step):
        mine = kv_out.at[u, z, c]
        return remote(
            kv_in,
            mine,
            z_send.at[step],
            z_recv.at[step],
            {BLK: lax.rem(z + step, n_z) * 2 + c},
        )

    def own_copy():
        return pltpu.make_async_copy(kv_in, kv_out.at[u, z, c], own_sem)

    def block(hop, step):
        return kv_out.at[lax.rem(u - hop + n_u, n_u), lax.rem(z - step + n_z, n_z), c]

    def across(hop, step):
        place = block(0, step)
        return remote(
            place,
            place,
            xy_send.at[hop, step],
            xy_recv.at[hop, step],
            {ULY: lax.rem(u + hop, n_u)},
        )

    def to_core(hop, step):
        place = block(hop, step)
        return remote(
            place,
            place,
            core_send.at[hop, step],
            core_recv.at[hop, step],
            {BLK: z * 2 + 1 - c},
        )

    own_copy().start()
    each(n_z, lambda step: along_z(step).start(), 1)
    first_q.start()
    rows.start()
    own_copy().wait()
    each(n_u, lambda hop: across(hop, 0).start(), 1)
    to_core(0, 0).start()
    split_ff.start()

    def pass_on(step):
        along_z(step).wait_recv()
        each(n_u, lambda hop: across(hop, step).start(), 1)
        to_core(0, step).start()

    each(n_z, pass_on, 1)
    first_q.finish()
    then_q.start()

    def share(step):
        def one(hop):
            across(hop, step).wait_recv()
            to_core(hop, step).start()

        each(n_u, one, 1)

    each(n_z, share)
    rows.finish()
    split_ff.finish()
    then_q.finish()
    each(n_z, lambda step: along_z(step).wait_send(), 1)
    each(n_z, lambda step: each(n_u, lambda hop: across(hop, step).wait_send(), 1))
    each(n_z, lambda step: each(n_u, lambda hop: to_core(hop, step).wait()))


def start_call(exchange, rows, kv_low, q_cols, ff_cols):
    counts = axis_counts()
    n_u, n_b = counts[ULY], counts[BLK]
    n_z = n_b // 2
    dma = pltpu.SemaphoreType.DMA
    return remote_call(
        functools.partial(start_kernel, n_b, counts),
        exchange.next_id(),
        [
            jax.ShapeDtypeStruct(rows.shape, bf16),
            jax.ShapeDtypeStruct((n_u, n_z, 2) + kv_low.shape, bf16),
            jax.ShapeDtypeStruct((n_u,) + q_cols.shape, bf16),
            jax.ShapeDtypeStruct(ff_cols.shape, bf16),
        ],
        [
            pltpu.VMEM(q_cols.shape, bf16),
            dma((n_z,)),
            dma((n_z,)),
            dma,
            dma((n_u, n_z)),
            dma((n_u, n_z)),
            dma((n_u, n_z)),
            dma((n_u, n_z)),
        ]
        + sems(n_u)
        + sems(n_b)
        + sems(n_u)
        + sems(n_b),
        (rows, kv_low, q_cols, ff_cols),
        "start",
    )


def settle_kernel(
    blk_count,
    counts,
    kv_in,
    rows_in,
    q_in,
    ff_in,
    gains_in,
    kv_out,
    rows_out,
    q_out,
    ff_out,
    gains_out,
    kv_core,
    kv_pair,
    kv_cross,
    kv_plane,
    kv_line,
    q_got,
    q_sum,
    core_send,
    core_recv,
    xy_send,
    xy_recv,
    z_send,
    z_recv,
    *part_sems,
):
    u, b = lax.axis_index(ULY), lax.axis_index(BLK)
    n_u, n_z = kv_in.shape[0], kv_in.shape[1]
    z, c = b // 2, lax.rem(b, 2)
    greet({ALL}, blk_count, counts)
    rows = Part(ULY, SPLIT, rows_in, rows_out, *part_sems[0:3], blk_count)
    first_q = Part(ULY, SPLIT, q_in, q_got, *part_sems[3:6], blk_count)
    then_q = Part(BLK, SPLIT, q_sum, q_out, *part_sems[6:9], blk_count)
    gains = Part(ALL, SPLIT, gains_in, gains_out, *part_sems[9:12], blk_count)
    split_ff = Part(BLK, SPLIT, ff_in, ff_out, *part_sems[12:15], blk_count)

    def place(hop, step):
        return (lax.rem(u + hop, n_u), lax.rem(z + step, n_z))

    def to_core(hop, step):
        row, line = place(hop, step)
        return remote(
            kv_in.at[row, line, 1 - c],
            kv_core.at[hop, step],
            core_send.at[hop, step],
            core_recv.at[hop, step],
            {BLK: z * 2 + 1 - c},
        )

    def across(hop, step):
        return remote(
            kv_pair.at[hop, step],
            kv_cross.at[hop, step],
            xy_send.at[hop, step],
            xy_recv.at[hop, step],
            {ULY: lax.rem(u + hop, n_u)},
        )

    def along_z(step):
        return remote(
            kv_plane.at[step],
            kv_line.at[step],
            z_send.at[step],
            z_recv.at[step],
            {BLK: lax.rem(z + step, n_z) * 2 + c},
        )

    each(n_z, lambda step: each(n_u, lambda hop: to_core(hop, step).start()))
    first_q.start()
    split_ff.start()

    def add_pair(step):
        def one(hop):
            row, line = place(hop, step)
            to_core(hop, step).wait_recv()
            kv_pair[hop, step] = (
                kv_in[row, line, c].astype(f32) + kv_core[hop, step].astype(f32)
            ).astype(bf16)

        def forward(hop):
            one(hop)
            across(hop, step).start()

        one(0)
        each(n_u, forward, 1)

    each(n_z, add_pair, 1)
    add_pair(0)
    rows.start()
    gains.start()
    first_q.finish()
    q_sum[...] = jnp.sum(q_got[...].astype(f32), axis=0).astype(bf16)
    then_q.start()

    def plane_sum(step):
        total = kv_pair[0, step].astype(f32)
        for hop in range(1, n_u):
            across(hop, step).wait_recv()
            total = total + kv_cross[hop, step].astype(f32)
        return total

    def add_plane(step):
        kv_plane[step] = plane_sum(step).astype(bf16)
        along_z(step).start()

    each(n_z, add_plane, 1)
    total = plane_sum(0)
    for step in range(1, n_z):
        along_z(step).wait_recv()
        total = total + kv_line[step].astype(f32)
    kv_out[...] = total
    then_q.finish()
    split_ff.finish()
    gains.finish()
    rows.finish()
    each(n_z, lambda step: each(n_u, lambda hop: to_core(hop, step).wait_send()))
    each(n_z, lambda step: each(n_u, lambda hop: across(hop, step).wait_send(), 1))
    each(n_z, lambda step: along_z(step).wait_send(), 1)


def settle_call(exchange, kv_grad, rows, q_grad, ff_grad, gains):
    counts = axis_counts()
    n_u, n_b = counts[ULY], counts[BLK]
    n_z = n_b // 2
    block = kv_grad.shape[3:]
    dma = pltpu.SemaphoreType.DMA
    return remote_call(
        functools.partial(settle_kernel, n_b, counts),
        exchange.next_id(),
        [
            jax.ShapeDtypeStruct(block, f32),
            jax.ShapeDtypeStruct(rows.shape, bf16),
            jax.ShapeDtypeStruct(q_grad.shape[1:], bf16),
            jax.ShapeDtypeStruct(ff_grad.shape, bf16),
            jax.ShapeDtypeStruct(gains.shape, f32),
        ],
        [
            pltpu.VMEM((n_u, n_z) + block, bf16),
            pltpu.VMEM((n_u, n_z) + block, bf16),
            pltpu.VMEM((n_u, n_z) + block, bf16),
            pltpu.VMEM((n_z,) + block, bf16),
            pltpu.VMEM((n_z,) + block, bf16),
            pltpu.VMEM(q_grad.shape, bf16),
            pltpu.VMEM(q_grad.shape[1:], bf16),
            dma((n_u, n_z)),
            dma((n_u, n_z)),
            dma((n_u, n_z)),
            dma((n_u, n_z)),
            dma((n_z,)),
            dma((n_z,)),
        ]
        + sems(n_u)
        + sems(n_u)
        + sems(n_b)
        + sems(n_u * n_b)
        + sems(n_b),
        (kv_grad, rows, q_grad, ff_grad, gains),
        "settle",
    )


def norm_back_rows(inputs, gain_vec, upstream):
    root_scale = inverse_root(inputs)
    unit_rows = inputs * root_scale
    weighted = upstream * gain_vec
    grad_inputs = root_scale * (
        weighted - unit_rows * jnp.mean(weighted * unit_rows, axis=-1, keepdims=True)
    )
    return (grad_inputs, jnp.sum(upstream * unit_rows, axis=0, keepdims=True))


class Links:
    def __init__(self, plan, blk_count, sem_refs):
        self.plan, self.blk_count, self.sem_refs = plan, blk_count, sem_refs

    def __call__(self, k, source, landing):
        axis, kind = self.plan[k]
        part = Part(axis, kind, source, landing, *self.sem_refs[3 * k : 3 * k + 3], self.blk_count)
        part.start()
        return part

    def now(self, k, source, landing):
        self(k, source, landing).finish()


def fused_call(exchange, body, plan, arrays, outs, scratch, name):
    counts = axis_counts()
    n_in, n_out, n_scratch = len(arrays), len(outs), len(scratch)
    sem_shapes = []
    for axis, _ in plan:
        sem_shapes += sems(counts[axis])

    def kernel(*refs):
        ins, refs = refs[:n_in], refs[n_in:]
        results, refs = refs[:n_out], refs[n_out:]
        kept, sem_refs = refs[:n_scratch], refs[n_scratch:]
        greet({axis for axis, _ in plan}, counts[BLK], counts)
        body(Links(plan, counts[BLK], sem_refs), ins, results, kept)

    return remote_call(
        kernel,
        exchange.next_id(),
        [jax.ShapeDtypeStruct(shape, dtype) for shape, dtype in outs],
        [pltpu.VMEM(shape, dtype) for shape, dtype in scratch] + sem_shapes,
        arrays,
        name,
    )


def sum_blocks(landing):
    total = landing[0].astype(f32)
    for k in range(1, landing.shape[0]):
        total = total + landing[k].astype(f32)
    return total


def flat_rows_of(ref):
    return ref[...].reshape(-1, ref.shape[-1])


def turned(values, cosines, sines):
    return values * cosines + pltpu.roll(values, HEAD_WIDTH // 2, 1) * sines


def lanes_of(columns, width, count):
    group = lax.broadcasted_iota(jnp.int32, (columns[0].shape[0], width * count), 1) // width
    spread = columns[0]
    for k in range(1, count):
        spread = jnp.where(group == k, columns[k], spread)
    return spread


def query_body(n_b, links, ins, outs, scratch):
    pick_part, gain_attn, gain_query, q_weight, cosines, sines, ff_rows, out_rows, down_rows = ins
    picks_out, normed_all, query_raw, query_all, ff_all, out_all, down_all = outs
    pick_got, normed_mine, query_mine = scratch
    first = links(0, pick_part, pick_got)
    behind = [
        links(3, ff_rows, ff_all),
        links(4, out_rows, out_all),
        links(5, down_rows, down_all),
    ]
    first.finish()
    rows = sum_blocks(pick_got)
    picks_out[...] = rows
    mine = rows[:, :MODEL_WIDTH]
    normed_mine[...] = (mine * inverse_root(mine) * gain_attn[...]).astype(bf16)
    links.now(1, normed_mine, normed_all)
    raw = mm(flat_rows_of(normed_all), q_weight[...])
    query_raw[...] = raw
    for k in range(raw.shape[1] // HEAD_WIDTH):
        head = raw[:, k * HEAD_WIDTH : (k + 1) * HEAD_WIDTH]
        query_mine[:, k * HEAD_WIDTH : (k + 1) * HEAD_WIDTH] = turned(
            head * inverse_root(head) * gain_query[...], cosines[...], sines[...]
        ).astype(bf16)
    links.now(2, query_mine, query_all)
    for part in behind:
        part.finish()


def forward_body(n_u, n_b, links, ins, outs, scratch):
    part_send, stats, mine, out_weight, ff_weight, down_weight, gain_mlp, gain_final = ins
    attended_out, log_out, after_out, normed_all, gate_up_out, top_out, final_mine, final_all = outs
    part_got, stats_all, shares, partial, partial_got, normed_mine, final_slot = scratch
    picks = after_out.shape[0]
    out_cut = attended_out.shape[1] // n_u
    heads_row = QUERY_HEADS // n_u
    cut_head = (lax.axis_index(BLK) * out_cut) // HEAD_WIDTH
    sent = links(0, part_send, part_got)
    links.now(1, stats, stats_all)
    full_max = stats_all[0, :QUERY_HEADS]
    for k in range(1, n_b):
        full_max = jnp.maximum(full_max, stats_all[k, :QUERY_HEADS])
    full_sum = jnp.zeros_like(full_max)
    for k in range(n_b):
        full_sum += stats_all[k, QUERY_HEADS:] * jnp.exp(stats_all[k, :QUERY_HEADS] - full_max)
    log_total = full_max + jnp.log(full_sum)
    log_out[...] = log_total
    for row in range(n_u):
        head = row * heads_row + cut_head
        row_log = log_out[pl.ds(head, 1), :]
        for k in range(n_b):
            shares[pl.ds(k * n_u + row, 1), :] = jnp.exp(
                stats_all[k, pl.ds(head, 1), :] - row_log
            )
    columns = shares[...].T
    sent.finish()
    attended = jnp.zeros(attended_out.shape, f32)
    for k in range(n_b):
        attended += part_got[k].astype(f32) * lanes_of(
            [columns[:, k * n_u + row : k * n_u + row + 1] for row in range(n_u)], out_cut, n_u
        )
    attended_out[...] = attended

    def to_picks(which, rows):
        partial[...] = rows.astype(bf16).reshape(partial.shape)
        links.now(which, partial, partial_got.at[which // 4])
        return sum_blocks(partial_got.at[which // 4])

    after_attn = mine[:, :MODEL_WIDTH] + to_picks(2, mm(attended.astype(bf16), out_weight[...]))
    after_out[...] = after_attn
    normed_mine[...] = (after_attn * inverse_root(after_attn) * gain_mlp[...]).astype(bf16)
    links.now(3, normed_mine, normed_all)
    gate_up = mm(flat_rows_of(normed_all), ff_weight[...])
    gate_up_out[...] = gate_up
    half = gate_up.shape[1] // 2
    gate_part, up_part = gate_up[:, :half], gate_up[:, half:]
    activated = (gate_part * jax.nn.sigmoid(gate_part) * up_part).astype(bf16)
    after_mlp = after_attn + to_picks(4, mm(activated, down_weight[...]))
    top_out[...] = after_mlp
    final_mine[...] = (after_mlp * inverse_root(after_mlp) * gain_final[...]).astype(bf16)
    links.now(5, final_mine, final_slot)
    links.now(6, final_slot, final_all)


def backward_body(n_u, n_b, links, ins, outs, scratch):
    (
        head_rows,
        head_stats,
        final_mine,
        picks_in,
        weights,
        after_mlp,
        after_attn,
        gate_up_in,
        normed_all,
        attended,
        out_weight,
        ff_weight,
        down_weight,
        gain_mlp,
        gain_final,
    ) = ins
    (
        norms_all,
        terms,
        gain_mlp_out,
        gain_final_out,
        grad_ff,
        grad_out,
        grad_down,
        grad_after,
        branch_all,
        attended_all,
        delta_all,
    ) = outs
    (
        rows_got,
        stats_got,
        slot_stats,
        slot_got,
        factors,
        columns,
        norms_mine,
        partial,
        partial_got,
        mine_low,
        grad_all,
        attended_mine,
        deltas,
        delta_mine,
    ) = scratch
    picks = after_mlp.shape[0]
    slot_picks = n_b * picks
    b = lax.axis_index(BLK)
    factors[...] = jnp.zeros_like(factors)
    first = links(0, head_rows, rows_got)
    links.now(1, head_stats, stats_got)
    tops = stats_got[0, 0:1, :]
    for k in range(1, n_u):
        tops = jnp.maximum(tops, stats_got[k, 0:1, :])
    total = jnp.zeros_like(tops)
    for k in range(n_u):
        factor = jnp.exp(stats_got[k, 0:1, :] - tops)
        factors[k : k + 1, :] = factor
        total += stats_got[k, 1:2, :] * factor
    slot_stats[...] = jnp.zeros_like(slot_stats)
    slot_stats[0:1, :] = tops
    slot_stats[1:2, :] = total
    slot_part = links(3, slot_stats, slot_got)
    by_row = factors[...].T
    first.finish()
    rows = rows_got[0].astype(f32) * by_row[:, 0:1]
    for k in range(1, n_u):
        rows += rows_got[k].astype(f32) * by_row[:, k : k + 1]
    partial[...] = rows.astype(bf16).reshape(partial.shape)
    back = links(2, partial, partial_got.at[0])
    slot_part.finish()
    tops = slot_got[0, 0:1, :]
    for k in range(1, n_b):
        tops = jnp.maximum(tops, slot_got[k, 0:1, :])
    total = jnp.zeros_like(tops)
    for k in range(n_b):
        factor = jnp.exp(slot_got[k, 0:1, :] - tops)
        factors[k : k + 1, :] = factor
        total += slot_got[k, 1:2, :] * factor
    log_norm = tops + jnp.log(total)
    for k in range(n_b):
        factors[k : k + 1, :] = factors[k : k + 1, :] / total
    factors[n_b : n_b + 1, :] = log_norm
    norms_mine[...] = jnp.broadcast_to(log_norm, norms_mine.shape)
    norms_part = links(4, norms_mine, norms_all)
    columns[...] = factors[...].T
    mine = columns[pl.ds(pl.multiple_of(b * picks, picks), picks), :]
    back.finish()
    target_rows = picks_in[:, MODEL_WIDTH:]
    grad_final = -target_rows
    for k in range(n_b):
        grad_final += partial_got[0, k].astype(f32) * mine[:, k : k + 1]
    grad_final = grad_final * weights[:, 0:1]
    target_logit = jnp.sum(
        final_mine[...].astype(f32) * target_rows, axis=-1, keepdims=True
    )
    terms[...] = weights[...] * (target_logit - mine[:, n_b : n_b + 1])
    grad_mlp, gain_rows = norm_back_rows(after_mlp[...], gain_final[...], grad_final)
    gain_final_out[...] = gain_rows
    mine_low[...] = grad_mlp.astype(bf16)
    links.now(5, mine_low, grad_all)
    branch = flat_rows_of(grad_all)
    gate_up = gate_up_in[...]
    half = gate_up.shape[1] // 2
    gate_part, up_part = gate_up[:, :half], gate_up[:, half:]
    sigmoid_gate = jax.nn.sigmoid(gate_part)
    grad_act = mm_back(branch, down_weight[...])
    grad_gate = grad_act * up_part * sigmoid_gate * (1.0 + gate_part * (1.0 - sigmoid_gate))
    grad_up = grad_act * gate_part * sigmoid_gate
    grad_gate_up = jnp.concatenate([grad_gate, grad_up], axis=1).astype(bf16)
    partial[...] = mm_back(grad_gate_up, ff_weight[...]).astype(bf16).reshape(partial.shape)
    back = links(6, partial, partial_got.at[1])
    activated = (gate_part * sigmoid_gate * up_part).astype(bf16)
    grad_down[...] = mm_outer(activated, branch).astype(bf16).reshape(grad_down.shape)
    back.finish()
    grad_mid, gain_rows = norm_back_rows(after_attn[...], gain_mlp[...], sum_blocks(partial_got.at[1]))
    gain_mlp_out[...] = gain_rows
    grad_attn = grad_mlp + grad_mid
    grad_after[...] = grad_attn
    mine_low[...] = grad_attn.astype(bf16)
    again = links(7, mine_low, branch_all)
    grad_ff[...] = (
        mm_outer(flat_rows_of(normed_all), grad_gate_up).astype(bf16).reshape(grad_ff.shape)
    )
    again.finish()
    branch = flat_rows_of(branch_all)
    grad_low = mm_back(branch, out_weight[...]).astype(bf16)
    attended_mine[...] = grad_low
    last = links(8, attended_mine, attended_all)
    out_cut = attended.shape[1] // n_u
    product = attended[...] * grad_low.astype(f32)
    group = lax.broadcasted_iota(jnp.int32, product.shape, 1) // out_cut
    lane = lax.broadcasted_iota(jnp.int32, deltas.shape, 1)
    sums = jnp.zeros(deltas.shape, f32)
    for row in range(n_u):
        one = jnp.sum(jnp.where(group == row, product, 0.0), axis=-1, keepdims=True)
        sums = jnp.where(lane == row, one, sums)
    deltas[...] = sums
    delta_mine[...] = deltas[...].T[:8, :]
    delta_part = links(9, delta_mine, delta_all)
    grad_out[...] = mm_outer(attended[...].astype(bf16), branch).astype(bf16).reshape(
        grad_out.shape
    )
    last.finish()
    delta_part.finish()
    norms_part.finish()


def query_back_body(links, ins, outs, scratch):
    (
        query_send,
        query_raw,
        cosines,
        sines,
        gain_query,
        q_weight,
        normed_all,
        picks_in,
        gain_attn,
        grad_after,
        grad_ff,
        grad_out,
        grad_down,
    ) = ins
    gain_query_out, gain_attn_out, grad_q, pick_back, ff_sum, out_sum, down_sum = outs
    query_got, grad_low, partial, partial_got, mine_low, ff_got, out_got, down_got = scratch
    first = links(0, query_send, query_got)
    behind = [
        links(3, grad_ff, ff_got),
        links(4, grad_out, out_got),
        links(5, grad_down, down_got),
    ]
    first.finish()
    upstream = sum_blocks(query_got).astype(bf16).astype(f32)
    gain_sum = jnp.zeros(gain_query_out.shape, f32)
    for k in range(upstream.shape[1] // HEAD_WIDTH):
        part = slice(k * HEAD_WIDTH, (k + 1) * HEAD_WIDTH)
        grad_head, gain_head = norm_back_rows(
            query_raw[:, part], gain_query[...], turned(upstream[:, part], cosines[...], -sines[...])
        )
        grad_low[:, part] = grad_head.astype(bf16)
        gain_sum += gain_head
    gain_query_out[...] = gain_sum
    partial[...] = mm_back(grad_low[...], q_weight[...]).astype(bf16).reshape(partial.shape)
    back = links(1, partial, partial_got)
    grad_q[...] = (
        mm_outer(flat_rows_of(normed_all), grad_low[...]).astype(bf16).reshape(grad_q.shape)
    )
    back.finish()
    grad_mine, gain_rows = norm_back_rows(
        picks_in[:, :MODEL_WIDTH], gain_attn[...], sum_blocks(partial_got)
    )
    gain_attn_out[...] = gain_rows
    mine_low[...] = (grad_after[...] + grad_mine).astype(bf16)
    links.now(2, mine_low, pick_back)
    for part in behind:
        part.finish()
    ff_sum[...] = sum_blocks(ff_got).astype(bf16)
    out_sum[...] = sum_blocks(out_got)
    down_sum[...] = sum_blocks(down_got)


class Named:
    pass


def named_call(exchange, body, plan, extra_sems, ins, outs, scratch, name, grant=40):
    counts = axis_counts()
    sem_shapes = []
    for axis, _ in plan.values():
        sem_shapes += sems(counts[axis])
    order = {key: k for k, key in enumerate(plan)}
    extra = list(extra_sems)

    def kernel(*refs):
        r, s = Named(), Named()
        names = list(ins) + list(outs) + list(scratch)
        for key, ref in zip(names, refs):
            setattr(r, key, ref)
        sem_refs = refs[len(names) :]
        for key, ref in zip(extra, sem_refs[3 * len(plan) :]):
            setattr(s, key, ref)
        base = Links(list(plan.values()), counts[BLK], sem_refs)
        links = Named()
        for key in plan:
            setattr(links, key, functools.partial(base, order[key]))
        greet({axis for axis, _ in plan.values()}, counts[BLK], counts)
        body(r, links, s)

    results = remote_call(
        kernel,
        exchange.next_id(),
        [jax.ShapeDtypeStruct(shape, dtype) for shape, dtype in outs.values()],
        [pltpu.VMEM(shape, dtype) for shape, dtype in scratch.values()]
        + sem_shapes
        + [pltpu.SemaphoreType.DMA(extra_sems[key]) for key in extra],
        list(ins.values()),
        name,
        grant,
    )
    found = Named()
    for key, value in zip(outs, results):
        setattr(found, key, value)
    return found


def column_of(lane_row):
    count = lane_row.shape[1]
    down = lax.broadcasted_iota(jnp.int32, (count, count), 0)
    across = lax.broadcasted_iota(jnp.int32, (count, count), 1)
    return jnp.sum(jnp.where(down == across, lane_row, 0.0), axis=1, keepdims=True)


def begin_body(n_u, n_b, row_share, slots, r, links, s):
    u, b = lax.axis_index(ULY), lax.axis_index(BLK)
    me = u * n_b + b
    block_len, picks = r.tokens.shape[1], r.picked.shape[1]
    places = n_u * slots
    gathers = [
        links.tokens(r.tokens, r.tokens_all),
        links.targets(r.targets, r.targets_all),
        links.picked(r.picked, r.picked_all),
        links.advantages(r.advantages, r.advantages_all),
    ]
    links.near(r.scales, r.near).finish()
    far = links.far(r.near, r.far)
    for part in gathers:
        part.finish()

    width = block_len + picks
    lane = lax.broadcasted_iota(jnp.int32, (1, width), 1)
    before = jnp.where(
        lax.broadcasted_iota(jnp.int32, (width, width), 0)
        < lax.broadcasted_iota(jnp.int32, (width, width), 1),
        1.0,
        0.0,
    ).astype(bf16)
    base = jnp.zeros((2 * n_u, 1), f32)
    found = [jnp.zeros((slots, width), f32) for _ in range(2 * n_u)]
    rank_of_slot = lax.broadcasted_iota(jnp.int32, (slots, width), 0).astype(f32)
    owner_first = lax.broadcasted_iota(jnp.int32, (n_u, 1), 0) * n_b + b
    most = jnp.zeros((n_u, 1), f32)
    counts = [jnp.zeros((n_u, width), f32) for _ in range(n_u * n_b)]
    for k in range(n_b):
        r.wants[:, :block_len] = r.tokens_all[k]
        r.wants[:, block_len:] = r.targets_all[k]
        wants = r.wants[...]
        local = wants - me * row_share
        sent = (local >= 0) & (local < row_share)
        own = r.wants[pl.ds(u, 1), :] - owner_first * row_share
        got = (own >= 0) & (own < row_share)
        r.masks[:n_u, :] = jnp.where(sent, 1.0, 0.0)
        r.masks[n_u:, :] = jnp.where(got, 1.0, 0.0)
        r.labels[:n_u, :] = (local + 1).astype(f32)
        r.labels[n_u:, :] = jnp.broadcast_to(k * width + lane + 1, (n_u, width)).astype(f32)
        masks = r.masks[...]
        ranks = mm(masks.astype(bf16), before) + base
        r.ranks[...] = jnp.where(masks > 0.0, ranks, -1.0)
        base += jnp.sum(masks, axis=1, keepdims=True)
        for row in range(2 * n_u):
            hit = r.ranks[row : row + 1, :] == rank_of_slot
            found[row] += jnp.where(hit, r.labels[row : row + 1, :], 0.0)
        for owner in range(n_u * n_b):
            far_row = wants - owner * row_share
            counts[owner] += jnp.where((far_row >= 0) & (far_row < row_share), 1.0, 0.0)
        r.slot_picked[:, k * picks : (k + 1) * picks] = r.picked_all[k, pl.ds(u, 1), :]
        valid = r.picked_all[k] < r.lengths[...]
        weights = jnp.where(valid, r.advantages_all[k], 0.0)
        for row in range(n_u):
            at = slice((row * n_b + k) * picks, (row * n_b + k + 1) * picks)
            r.weights[:, at] = weights[row : row + 1, :]
            r.target_ids[:, at] = r.targets_all[k, row : row + 1, :] - me * row_share
    for owner in range(n_u * n_b):
        most = jnp.maximum(most, jnp.sum(counts[owner], axis=1, keepdims=True))
    r.meta[...] = jnp.zeros_like(r.meta)
    r.meta[0:n_u, :] = jnp.broadcast_to(base[:n_u], (n_u, 128))
    r.meta[8 : 8 + n_u, :] = jnp.broadcast_to(most, (n_u, 128))
    mine_valid = r.picked[pl.ds(u, 1), :] < r.lengths[pl.ds(u, 1), :]
    mine_weight = jnp.where(mine_valid, r.advantages[pl.ds(u, 1), :], 0.0)
    r.meta[16:17, :] = jnp.broadcast_to(
        jnp.sum(jnp.where(mine_valid, 1.0, 0.0), axis=1, keepdims=True), (1, 128)
    )
    r.weight_wide[...] = jnp.broadcast_to(column_of(mine_weight), r.weight_wide.shape)
    my_length = r.lengths[pl.ds(u, 1), :]
    for row in range(n_u):
        here = slice(row * slots, (row + 1) * slots)
        r.row_ids[here, :] = jnp.sum(found[row], axis=1, keepdims=True).astype(jnp.int32) - 1
        entry = jnp.sum(found[n_u + row], axis=1, keepdims=True) - 1.0
        block = jnp.floor((entry + 0.5) * (1.0 / width))
        inside = entry - block * width
        token = (entry >= 0.0) & (inside < block_len)
        position = (block * block_len + inside).astype(jnp.int32)
        key_pos = jnp.where(token, position, 1 << 30)
        r.key_pos[here, :] = key_pos
        r.key_lim[here, :] = jnp.where(key_pos < my_length, key_pos, 1 << 30)
        r.positions[here, :] = jnp.where(token, position, 0)
        target = (block * picks + inside - block_len).astype(jnp.int32)
        r.target_of[here, :] = jnp.where((entry >= 0.0) & (inside >= block_len), target, -1)
    r.positions[places:, :] = column_of(r.slot_picked[...].astype(f32)).astype(jnp.int32)

    far.finish()
    share = r.scales.shape[1]
    for row in range(n_u):
        for k in range(n_b):
            at = (row * n_b + k) * share
            r.gains[:, at : at + share] = r.far[row, k].astype(bf16).astype(f32)
    r.gain_attn[...] = r.gains[:, :MODEL_WIDTH]
    r.gain_mlp[...] = r.gains[:, MODEL_WIDTH : 2 * MODEL_WIDTH]
    r.gain_final[...] = r.gains[:, 2 * MODEL_WIDTH : 3 * MODEL_WIDTH]
    r.gain_query[...] = r.gains[:, 3 * MODEL_WIDTH : 3 * MODEL_WIDTH + HEAD_WIDTH]
    r.gain_key[...] = r.gains[:, 3 * MODEL_WIDTH + HEAD_WIDTH :]


def totals_body(r, links, s):
    lane = lax.broadcasted_iota(jnp.int32, (1, 128), 1)
    squares = r.tails[0:1, 0:1] + jnp.sum(r.table_squares[...], axis=1, keepdims=True)
    row = jnp.where(lane == 0, squares, 0.0)
    row = jnp.where(lane == 1, r.counts[0:1, :], row)
    r.mine[...] = jnp.where(lane == 2, r.tails[1:2, 0:1], row)
    links.near(r.mine, r.all).finish()
    total = sum_blocks(r.all)
    count = total[:, 1:2]
    norm = jnp.sqrt(total[:, 0:1]) / count
    factor = jnp.minimum(1.0, clip_limit / norm) / count
    row = jnp.where(lane == 0, factor, r.steps[...])
    row = jnp.where(lane == 3, total[:, 2:3] / count, row)
    r.numbers[...] = jnp.where(lane == 4, norm, row)


def head_of(ref, head):
    share = ref.shape[2] // HEAD_WIDTH
    at = head % share * HEAD_WIDTH
    return ref[head // share, :, at : at + HEAD_WIDTH]


def cuts_of(head, n_u, n_b):
    cut = QUERY_WIDTH // (n_u * n_b)
    heads_row, pieces = QUERY_HEADS // n_u, HEAD_WIDTH // cut
    row = head // heads_row
    return [
        (head % heads_row * pieces + t, slice(row * cut, (row + 1) * cut), slice(t * cut, (t + 1) * cut))
        for t in range(pieces)
    ]


def ff_cuts(n_u, n_b):
    cut = FF // (n_u * n_b)
    return [
        (
            k,
            slice((half * n_u + row) * cut, (half * n_u + row + 1) * cut),
            slice(half * FF + (row * n_b + k) * cut, half * FF + (row * n_b + k + 1) * cut),
        )
        for k in range(n_b)
        for half in range(2)
        for row in range(n_u)
    ]


def rise_body(n_u, n_b, r, links, s):
    u, b = lax.axis_index(ULY), lax.axis_index(BLK)
    n_z = n_b // 2
    z, c = b // 2, lax.rem(b, 2)
    score_scale = HEAD_WIDTH ** (-0.5)

    def along_z(step):
        return remote(
            r.kv_in,
            r.kv_weight.at[u, z, c],
            s.z_send.at[step],
            s.z_recv.at[step],
            {BLK: lax.rem(z + step, n_z) * 2 + c},
        )

    def own_copy():
        return pltpu.make_async_copy(r.kv_in, r.kv_weight.at[u, z, c], s.own.at[0])

    def block(hop, step):
        return r.kv_weight.at[lax.rem(u - hop + n_u, n_u), lax.rem(z - step + n_z, n_z), c]

    def across(hop, step):
        place = block(0, step)
        return remote(
            place,
            place,
            s.xy_send.at[hop, step],
            s.xy_recv.at[hop, step],
            {ULY: lax.rem(u + hop, n_u)},
        )

    def to_core(hop, step):
        place = block(hop, step)
        return remote(
            place,
            place,
            s.core_send.at[hop, step],
            s.core_recv.at[hop, step],
            {BLK: z * 2 + 1 - c},
        )

    places = r.key_raw.shape[0]
    half = KEY_VALUE_HEADS * HEAD_WIDTH
    r.kv_in[...] = r.inflow[:, QUERY_WIDTH:].astype(bf16)
    own_copy().start()
    rows = links.rows(r.rows_in, r.arrived)
    each(n_z, lambda step: along_z(step).start(), 1)
    q_share = r.q_in.shape[2]
    for k in range(n_b):
        r.q_in[k] = r.inflow[:, k * q_share : (k + 1) * q_share].astype(bf16)
    q_split = links.q_split(r.q_in, r.q_part)
    own_copy().wait()
    each(n_u, lambda hop: across(hop, 0).start(), 1)
    to_core(0, 0).start()
    for k, there, here in ff_cuts(n_u, n_b):
        r.ff_in[k, :, there] = r.expand[:, here].astype(bf16)
    ff_split = links.ff_split(r.ff_in, r.ff_part)
    r.out_in[...] = r.outflow[...].astype(bf16)
    r.down_in[...] = r.contract[...].astype(bf16)
    rows.finish()

    arrived = flat_rows_of(r.arrived)
    pick_hot = jnp.where(r.key_pos[...] == r.slot_picked[...], 1.0, 0.0).astype(bf16)
    pick_lane = lax.broadcasted_iota(jnp.int32, pick_hot.shape, 1)
    target_hot = jnp.where(r.target_of[...] == pick_lane, 1.0, 0.0).astype(bf16)
    r.pick_send[...] = mm_outer(pick_hot, arrived).astype(bf16).reshape(r.pick_send.shape)
    picked = links.picks(r.pick_send, r.pick_got)
    r.aim_send[...] = mm_outer(target_hot, arrived).astype(bf16).reshape(r.aim_send.shape)

    def pass_on(step):
        along_z(step).wait_recv()
        each(n_u, lambda hop: across(hop, step).start(), 1)
        to_core(0, step).start()

    each(n_z, pass_on, 1)
    q_split.finish()
    q_all = links.q_all(r.q_part, r.q_weight)
    wide = arrived.astype(f32)
    r.normed_keys[...] = (wide * inverse_root(wide) * r.gain_attn[...]).astype(bf16)
    picked.finish()
    mine = sum_blocks(r.pick_got)
    r.pick_rows[:, :MODEL_WIDTH] = mine
    r.normed_mine[...] = (mine * inverse_root(mine) * r.gain_attn[...]).astype(bf16)
    links.normed(r.normed_mine, r.normed_slot).finish()
    q_all.finish()
    raw = mm(flat_rows_of(r.normed_slot), r.q_weight[...].reshape(MODEL_WIDTH, -1))
    r.query_raw[...] = raw
    for k in range(raw.shape[1] // HEAD_WIDTH):
        part = slice(k * HEAD_WIDTH, (k + 1) * HEAD_WIDTH)
        head = raw[:, part]
        r.query_mine[:, part] = turned(
            head * inverse_root(head) * r.gain_query[...], r.rope_cos[places:], r.rope_sin[places:]
        ).astype(bf16)
    queries = links.queries(r.query_mine, r.query_all)

    def share(step):
        def one(hop):
            across(hop, step).wait_recv()
            to_core(hop, step).start()

        each(n_u, one, 1)

    each(n_z, share)
    out_all = links.out_all(r.out_in, r.out_weight)
    ff_split.finish()
    ff_all = links.ff_all(r.ff_part, r.ff_weight)
    down_all = links.down_all(r.down_in, r.down_weight)
    each(n_z, lambda step: each(n_u, lambda hop: to_core(hop, step).wait_recv()))

    wide_head = 2 * HEAD_WIDTH

    def project(k):
        for first in (0, half):
            at = pl.multiple_of(first + k * wide_head, wide_head)
            weight = r.kv_weight[:, :, :, :, pl.ds(at, wide_head)].reshape(MODEL_WIDTH, wide_head)
            got = mm(r.normed_keys[...], weight)
            here = pl.ds(pl.multiple_of(k * wide_head, wide_head), wide_head)
            if first:
                r.values[:, here] = got.astype(bf16)
            else:
                r.key_raw[:, here] = got
                turned_both = []
                for j in range(2):
                    head = got[:, j * HEAD_WIDTH : (j + 1) * HEAD_WIDTH]
                    turned_both.append(
                        turned(
                            head * inverse_root(head) * r.gain_key[...],
                            r.rope_cos[:places],
                            r.rope_sin[:places],
                        )
                    )
                r.key_rot[:, here] = jnp.concatenate(turned_both, axis=1).astype(bf16)

    each(KEY_VALUE_HEADS // 2, project)
    queries.finish()
    allowed = r.key_lim[...] <= r.slot_picked[...]
    for head in range(QUERY_HEADS):
        at = head // (QUERY_HEADS // KEY_VALUE_HEADS) * HEAD_WIDTH
        part = slice(at, at + HEAD_WIDTH)
        scores = mm_back(r.key_rot[:, part], head_of(r.query_all, head)) * score_scale
        scores = jnp.where(allowed, scores, masked_score)
        top = jnp.max(scores, axis=0, keepdims=True)
        weights = jnp.where(allowed, jnp.exp(scores - top), 0.0)
        r.stats[head : head + 1, :] = top
        r.stats[QUERY_HEADS + head : QUERY_HEADS + head + 1, :] = jnp.sum(
            weights, axis=0, keepdims=True
        )
        out = mm_outer(weights.astype(bf16), r.values[:, part]).astype(bf16)
        for target, there, here in cuts_of(head, n_u, n_b):
            r.part_send[target, :, there] = out[:, here]

    picks = r.after_attn.shape[0]
    out_cut = r.attended.shape[1] // n_u
    heads_row = QUERY_HEADS // n_u
    cut_head = (b * out_cut) // HEAD_WIDTH
    sent = links.parts(r.part_send, r.part_got)
    links.stats(r.stats, r.stats_all).finish()
    full_max = r.stats_all[0, :QUERY_HEADS]
    for k in range(1, n_b):
        full_max = jnp.maximum(full_max, r.stats_all[k, :QUERY_HEADS])
    full_sum = jnp.zeros_like(full_max)
    for k in range(n_b):
        full_sum += r.stats_all[k, QUERY_HEADS:] * jnp.exp(
            r.stats_all[k, :QUERY_HEADS] - full_max
        )
    r.log_total[...] = full_max + jnp.log(full_sum)
    for row in range(n_u):
        head = row * heads_row + cut_head
        row_log = r.log_total[pl.ds(head, 1), :]
        for k in range(n_b):
            r.shares[k * n_u + row : k * n_u + row + 1, :] = jnp.exp(
                r.stats_all[k, pl.ds(head, 1), :] - row_log
            )
    columns = r.shares[...].T
    sent.finish()
    attended = jnp.zeros(r.attended.shape, f32)
    for k in range(n_b):
        attended += r.part_got[k].astype(f32) * lanes_of(
            [columns[:, k * n_u + row : k * n_u + row + 1] for row in range(n_u)], out_cut, n_u
        )
    r.attended[...] = attended
    out_all.finish()

    def to_picks(which, send, rows):
        r.partial[...] = rows.astype(bf16).reshape(r.partial.shape)
        landing = r.partial_got.at[which]
        send(r.partial, landing).finish()
        return sum_blocks(landing)

    after_attn = r.pick_rows[:, :MODEL_WIDTH] + to_picks(
        0, links.sum_out, mm(attended.astype(bf16), flat_rows_of(r.out_weight))
    )
    r.after_attn[...] = after_attn
    r.normed_mine[...] = (after_attn * inverse_root(after_attn) * r.gain_mlp[...]).astype(bf16)
    links.normed_mlp(r.normed_mine, r.normed_mlp).finish()
    ff_all.finish()
    gate_up = mm(flat_rows_of(r.normed_mlp), r.ff_weight[...].reshape(MODEL_WIDTH, -1))
    r.gate_up[...] = gate_up
    half = gate_up.shape[1] // 2
    gate_part, up_part = gate_up[:, :half], gate_up[:, half:]
    activated = (gate_part * jax.nn.sigmoid(gate_part) * up_part).astype(bf16)
    down_all.finish()
    after_mlp = after_attn + to_picks(1, links.sum_mlp, mm(activated, flat_rows_of(r.down_weight)))
    r.after_mlp[...] = after_mlp
    r.final_mine[...] = (after_mlp * inverse_root(after_mlp) * r.gain_final[...]).astype(bf16)
    links.final(r.final_mine, r.final_slot).finish()
    final_all = links.final_all(r.final_slot, r.final_all)
    aims = links.aims(r.aim_send, r.aim_got)
    aims.finish()
    r.pick_rows[:, MODEL_WIDTH:] = sum_blocks(r.aim_got)
    final_all.finish()
    each(n_z, lambda step: along_z(step).wait_send(), 1)
    each(n_z, lambda step: each(n_u, lambda hop: across(hop, step).wait_send(), 1))
    each(n_z, lambda step: each(n_u, lambda hop: to_core(hop, step).wait_send()))


def fall_body(n_u, n_b, r, links, s):
    u, b = lax.axis_index(ULY), lax.axis_index(BLK)
    n_z = n_b // 2
    z, c = b // 2, lax.rem(b, 2)
    score_scale = HEAD_WIDTH ** (-0.5)
    picks = r.after_mlp.shape[0]
    places = r.key_raw.shape[0]
    r.factors[...] = jnp.zeros_like(r.factors)
    head_rows = links.head_rows(r.head_rows, r.rows_got)
    links.head_stats(r.head_stats, r.stats_got).finish()
    tops = r.stats_got[0, 0:1, :]
    for k in range(1, n_u):
        tops = jnp.maximum(tops, r.stats_got[k, 0:1, :])
    total = jnp.zeros_like(tops)
    for k in range(n_u):
        factor = jnp.exp(r.stats_got[k, 0:1, :] - tops)
        r.factors[k : k + 1, :] = factor
        total += r.stats_got[k, 1:2, :] * factor
    r.slot_stats[...] = jnp.zeros_like(r.slot_stats)
    r.slot_stats[0:1, :] = tops
    r.slot_stats[1:2, :] = total
    slot_part = links.slot_stats(r.slot_stats, r.slot_got)
    by_row = r.factors[...].T
    head_rows.finish()
    rows = r.rows_got[0].astype(f32) * by_row[:, 0:1]
    for k in range(1, n_u):
        rows += r.rows_got[k].astype(f32) * by_row[:, k : k + 1]
    r.partial[...] = rows.astype(bf16).reshape(r.partial.shape)
    back = links.slot_rows(r.partial, r.partial_got.at[0])
    slot_part.finish()
    tops = r.slot_got[0, 0:1, :]
    for k in range(1, n_b):
        tops = jnp.maximum(tops, r.slot_got[k, 0:1, :])
    total = jnp.zeros_like(tops)
    for k in range(n_b):
        factor = jnp.exp(r.slot_got[k, 0:1, :] - tops)
        r.factors[k : k + 1, :] = factor
        total += r.slot_got[k, 1:2, :] * factor
    log_norm = tops + jnp.log(total)
    for k in range(n_b):
        r.factors[k : k + 1, :] = r.factors[k : k + 1, :] / total
    r.factors[n_b : n_b + 1, :] = log_norm
    r.norms_mine[...] = jnp.broadcast_to(log_norm, r.norms_mine.shape)
    norms_part = links.norms(r.norms_mine, r.norms_all)
    r.columns[...] = r.factors[...].T
    mine = r.columns[pl.ds(pl.multiple_of(b * picks, picks), picks), :]
    back.finish()
    target_rows = r.pick_rows[:, MODEL_WIDTH:]
    grad_final = -target_rows
    for k in range(n_b):
        grad_final += r.partial_got[0, k].astype(f32) * mine[:, k : k + 1]
    grad_final = grad_final * r.weights[:, 0:1]
    target_logit = jnp.sum(
        r.final_mine[...].astype(f32) * target_rows, axis=-1, keepdims=True
    )
    r.terms[...] = r.weights[...] * (target_logit - mine[:, n_b : n_b + 1])
    grad_mlp, gain_final = norm_back_rows(r.after_mlp[...], r.gain_final[...], grad_final)
    r.mine_low[...] = grad_mlp.astype(bf16)
    links.branch(r.mine_low, r.grad_all).finish()
    branch = flat_rows_of(r.grad_all)
    gate_up = r.gate_up[...]
    half = gate_up.shape[1] // 2
    gate_part, up_part = gate_up[:, :half], gate_up[:, half:]
    sigmoid_gate = jax.nn.sigmoid(gate_part)
    grad_act = mm_back(branch, flat_rows_of(r.down_weight))
    grad_gate = grad_act * up_part * sigmoid_gate * (1.0 + gate_part * (1.0 - sigmoid_gate))
    grad_up = grad_act * gate_part * sigmoid_gate
    grad_gate_up = jnp.concatenate([grad_gate, grad_up], axis=1).astype(bf16)
    r.partial[...] = (
        mm_back(grad_gate_up, r.ff_weight[...].reshape(MODEL_WIDTH, -1))
        .astype(bf16)
        .reshape(r.partial.shape)
    )
    back = links.sum_ff(r.partial, r.partial_got.at[1])
    activated = (gate_part * sigmoid_gate * up_part).astype(bf16)
    r.grad_down[...] = mm_outer(activated, branch).astype(bf16).reshape(r.grad_down.shape)
    down_part = links.down(r.grad_down, r.down_got)
    r.grad_ff[...] = (
        mm_outer(flat_rows_of(r.normed_mlp), grad_gate_up).astype(bf16).reshape(r.grad_ff.shape)
    )
    ff_part = links.ff(r.grad_ff, r.ff_got)
    back.finish()
    grad_mid, gain_mlp = norm_back_rows(
        r.after_attn[...], r.gain_mlp[...], sum_blocks(r.partial_got.at[1])
    )
    grad_attn = grad_mlp + grad_mid
    r.mine_low[...] = grad_attn.astype(bf16)
    links.branch_attn(r.mine_low, r.branch_all).finish()
    branch = flat_rows_of(r.branch_all)
    grad_low = mm_back(branch, flat_rows_of(r.out_weight)).astype(bf16)
    r.attended_mine[...] = grad_low
    last = links.attended(r.attended_mine, r.attended_all)
    out_cut = r.attended.shape[1] // n_u
    product = r.attended[...] * grad_low.astype(f32)
    group = lax.broadcasted_iota(jnp.int32, product.shape, 1) // out_cut
    lane = lax.broadcasted_iota(jnp.int32, r.deltas.shape, 1)
    sums = jnp.zeros(r.deltas.shape, f32)
    for row in range(n_u):
        one = jnp.sum(jnp.where(group == row, product, 0.0), axis=-1, keepdims=True)
        sums = jnp.where(lane == row, one, sums)
    r.deltas[...] = sums
    r.delta_mine[...] = r.deltas[...].T[:8, :]
    delta_part = links.deltas(r.delta_mine, r.delta_all)
    r.grad_out[...] = (
        mm_outer(r.attended[...].astype(bf16), branch).astype(bf16).reshape(r.grad_out.shape)
    )
    out_part = links.out(r.grad_out, r.out_got)
    wide = flat_rows_of(r.arrived).astype(f32)
    r.normed_keys[...] = (wide * inverse_root(wide) * r.gain_attn[...]).astype(bf16)
    last.finish()
    delta_part.finish()

    ff_part.finish()
    r.ff_sum[...] = sum_blocks(r.ff_got).astype(bf16)
    ff_last = links.ff_cols(r.ff_sum, r.ff_out)

    allowed = r.key_lim[...] <= r.slot_picked[...]
    width = KEY_VALUE_HEADS * HEAD_WIDTH
    r.gain_key_row[...] = jnp.zeros((1, HEAD_WIDTH), f32)
    heads_each = QUERY_HEADS // KEY_VALUE_HEADS
    for kv_head in range(KEY_VALUE_HEADS):
        part = slice(kv_head * HEAD_WIDTH, (kv_head + 1) * HEAD_WIDTH)
        key, value = r.key_rot[:, part], r.values[:, part]
        grad_key = jnp.zeros(key.shape, f32)
        grad_value = jnp.zeros(key.shape, f32)
        for head in range(kv_head * heads_each, (kv_head + 1) * heads_each):
            query = head_of(r.query_all, head)
            cuts = cuts_of(head, n_u, n_b)
            upstream = jnp.concatenate([r.attended_all[at, :, there] for at, there, _ in cuts], 1)
            row = head // (QUERY_HEADS // n_u)
            delta = sum(r.delta_all[at, row : row + 1, :] for at, _, _ in cuts)
            scores = mm_back(key, query) * score_scale
            probs = jnp.where(allowed, jnp.exp(scores - r.log_total[head : head + 1, :]), 0.0)
            grad_probs = mm_back(value, upstream)
            grad_scores = (probs * (grad_probs - delta) * score_scale).astype(bf16)
            grad_query = mm_outer(grad_scores, key).astype(bf16)
            share = r.query_send.shape[2] // HEAD_WIDTH
            at = head % share * HEAD_WIDTH
            r.query_send[head // share, :, at : at + HEAD_WIDTH] = grad_query
            grad_key += mm(grad_scores, query)
            grad_value += mm(probs.astype(bf16), upstream)
        grad_head, gain_head = norm_back_rows(
            r.key_raw[:, part],
            r.gain_key[...],
            turned(grad_key.astype(bf16).astype(f32), r.rope_cos[:places], -r.rope_sin[:places]),
        )
        r.gain_key_row[...] += gain_head
        r.grad_kv[:, part] = grad_head.astype(bf16)
        r.grad_kv[:, width + kv_head * HEAD_WIDTH : width + (kv_head + 1) * HEAD_WIDTH] = (
            grad_value.astype(bf16)
        )
    query_part = links.grad_queries(r.query_send, r.query_got)

    def place(hop, step):
        return (lax.rem(u + hop, n_u), lax.rem(z + step, n_z))

    def to_core(hop, step):
        row, line = place(hop, step)
        return remote(
            r.kv_grad.at[row, line, 1 - c],
            r.kv_core.at[hop, step],
            s.core_send.at[hop, step],
            s.core_recv.at[hop, step],
            {BLK: z * 2 + 1 - c},
        )

    def across(hop, step):
        return remote(
            r.kv_core.at[hop, step],
            r.kv_cross.at[hop, step],
            s.xy_send.at[hop, step],
            s.xy_recv.at[hop, step],
            {ULY: lax.rem(u + hop, n_u)},
        )

    def along_z(step):
        return remote(
            r.kv_plane.at[step],
            r.kv_line.at[step],
            s.z_send.at[step],
            s.z_recv.at[step],
            {BLK: lax.rem(z + step, n_z) * 2 + c},
        )

    block_rows = MODEL_WIDTH // n_u

    def weight_grad(k):
        hop = lax.rem(k + 1, n_u)
        row = lax.rem(u + hop, n_u)
        columns = pl.ds(pl.multiple_of(row * block_rows, block_rows), block_rows)
        r.kv_grad[row] = (
            mm_outer(r.normed_keys[:, columns], r.grad_kv[...])
            .astype(bf16)
            .reshape(r.kv_grad.shape[1:])
        )
        each(n_z, lambda step: to_core(hop, step).start())

    each(n_u, weight_grad)
    def add_pair(hop, step):
        row, line = place(hop, step)
        to_core(hop, step).wait_recv()
        r.kv_core[hop, step] = (
            r.kv_grad[row, line, c].astype(f32) + r.kv_core[hop, step].astype(f32)
        ).astype(bf16)

    def send_pairs(k):
        step = lax.rem(k + 1, n_z)

        def one(hop):
            add_pair(hop, step)
            across(hop, step).start()

        each(n_u, one, 1)
        add_pair(0, step)

    each(n_z, send_pairs)
    down_part.finish()
    r.down_out[...] = sum_blocks(r.down_got)
    out_part.finish()
    r.out_out[...] = sum_blocks(r.out_got)
    query_part.finish()
    upstream = sum_blocks(r.query_got).astype(bf16).astype(f32)
    r.gain_query_row[...] = jnp.zeros((1, HEAD_WIDTH), f32)
    for k in range(upstream.shape[1] // HEAD_WIDTH):
        part = slice(k * HEAD_WIDTH, (k + 1) * HEAD_WIDTH)
        grad_head, gain_head = norm_back_rows(
            r.query_raw[:, part],
            r.gain_query[...],
            turned(upstream[:, part], r.rope_cos[places:], -r.rope_sin[places:]),
        )
        r.grad_low[:, part] = grad_head.astype(bf16)
        r.gain_query_row[...] += gain_head
    r.partial[...] = (
        mm_back(r.grad_low[...], r.q_weight[...].reshape(MODEL_WIDTH, -1))
        .astype(bf16)
        .reshape(r.partial.shape)
    )
    back = links.sum_query(r.partial, r.partial_got.at[2])

    r.grad_q[...] = (
        mm_outer(flat_rows_of(r.normed_slot), r.grad_low[...]).astype(bf16).reshape(r.grad_q.shape)
    )
    q_part = links.q(r.grad_q, r.q_got)
    back.finish()
    grad_mine, gain_attn = norm_back_rows(
        r.pick_rows[:, :MODEL_WIDTH], r.gain_attn[...], sum_blocks(r.partial_got.at[2])
    )
    r.mine_low[...] = (grad_attn + grad_mine).astype(bf16)
    pick_part = links.pick_back(r.mine_low, r.pick_back)

    def row_grad(k):
        columns = pl.ds(pl.multiple_of(k * block_rows, block_rows), block_rows)
        r.grad_wide[:, columns] = mm_back(
            r.grad_kv[...], r.kv_weight[k].reshape(block_rows, -1)
        )

    each(n_u, row_grad)
    grad_rows, gain_keys = norm_back_rows(wide, r.gain_attn[...], r.grad_wide[...])
    def plane_sum(step):
        total = r.kv_core[0, step].astype(f32)
        for hop in range(1, n_u):
            across(hop, step).wait_recv()
            total = total + r.kv_cross[hop, step].astype(f32)
        return total

    def add_plane(step):
        r.kv_plane[step] = plane_sum(step).astype(bf16)
        along_z(step).start()

    each(n_z, add_plane, 1)
    pick_part.finish()
    pick_hot = jnp.where(r.key_pos[...] == r.slot_picked[...], 1.0, 0.0).astype(bf16)
    r.rows_send[...] = (
        (grad_rows + mm(pick_hot, flat_rows_of(r.pick_back)))
        .astype(bf16)
        .reshape(r.rows_send.shape)
    )
    rows_part = links.rows(r.rows_send, r.rows_back)

    r.gain_mlp_row[...] = gain_mlp
    r.gain_final_row[...] = gain_final
    r.gain_picks_row[...] = gain_attn
    r.gain_rows_row[...] = gain_keys
    r.gains_mine[...] = jnp.zeros_like(r.gains_mine)
    lines = MODEL_WIDTH // 128
    for j in range(lines):
        part = slice(j * 128, (j + 1) * 128)
        r.gains_mine[j : j + 1, :] = r.gain_picks_row[:, part] + r.gain_rows_row[:, part]
        r.gains_mine[lines + j : lines + j + 1, :] = r.gain_mlp_row[:, part]
        r.gains_mine[2 * lines + j : 2 * lines + j + 1, :] = r.gain_final_row[:, part]
    r.gains_mine[3 * lines : 3 * lines + 1, :] = r.gain_query_row[...]
    r.gains_mine[3 * lines + 1 : 3 * lines + 2, :] = r.gain_key_row[...]
    gains_part = links.gains_blk(r.gains_mine, r.gains_got)

    gains_part.finish()
    r.gains_slot[...] = sum_blocks(r.gains_got)
    gains_last = links.gains_ulysses(r.gains_slot, r.gains_all)
    q_part.finish()
    r.q_sum[...] = sum_blocks(r.q_got).astype(bf16)
    q_last = links.q_cols(r.q_sum, r.q_out)

    total = plane_sum(0)
    for step in range(1, n_z):
        along_z(step).wait_recv()
        total = total + r.kv_line[step].astype(f32)
    r.inflow_out[:, QUERY_WIDTH:] = total
    gains_last.finish()
    gains = sum_blocks(r.gains_all)
    for part in (norms_part, ff_last, q_last, rows_part):
        part.finish()
    q_share = r.q_out.shape[2]
    for k in range(n_b):
        r.inflow_out[:, k * q_share : (k + 1) * q_share] = r.q_out[k].astype(f32)
    for k, there, here in ff_cuts(n_u, n_b):
        r.expand_out[:, here] = r.ff_out[k, :, there].astype(f32)
    squares = jnp.sum(gains * gains) / (n_u * n_b)
    for ref in (r.inflow_out, r.expand_out, r.out_out, r.down_out):
        squares += jnp.sum(ref[...] * ref[...])
    r.tails[...] = jnp.zeros_like(r.tails)
    r.tails[0:1, :] = jnp.full((1, 128), squares, f32)
    r.tails[1:2, :] = jnp.full((1, 128), -jnp.sum(r.terms[:, 0:1]), f32)
    for row in range(n_u):
        at = slice(row * n_b * picks, (row + 1) * n_b * picks)
        r.norms_row[:, at] = r.norms_all[row, 0:1, :]
    for k in range(gains.shape[0] - 6):
        r.gains_line[:, k * 128 : (k + 1) * 128] = gains[k : k + 1, :]
    share = r.gains_out.shape[1]
    me = u * n_b + b
    own = jnp.zeros((1, share), f32)
    for k in range(n_u * n_b):
        own = jnp.where(me == k, r.gains_line[:, k * share : (k + 1) * share], own)
    r.gains_out[...] = own
    each(n_z, lambda step: each(n_u, lambda hop: to_core(hop, step).wait_send()))
    each(n_z, lambda step: each(n_u, lambda hop: across(hop, step).wait_send(), 1))
    each(n_z, lambda step: along_z(step).wait_send(), 1)


def lookup_kernel(slots, fills_ref, ids_ref, table_ref, rows_ref, wide, sem):
    wide[...] = jnp.zeros_like(wide)

    def row_copy(place, row):
        return pltpu.make_async_copy(
            table_ref.at[pl.ds(row, 1), :], wide.at[pl.ds(place, 1), :], sem
        )

    def of_peer(peer, total):
        fill = fills_ref[peer]

        def fetch(k, carry):
            place = peer * slots + k
            row_copy(place, ids_ref[place]).start()
            return carry

        lax.fori_loop(0, fill, fetch, 0)
        return total + fill

    total = lax.fori_loop(0, fills_ref.shape[0], of_peer, 0)

    def drain(k, carry):
        row_copy(0, 0).wait()
        return carry

    lax.fori_loop(0, total, drain, 0)
    rows_ref[...] = wide[...].astype(rows_ref.dtype)


def lookup(fills, ids, table, slots):
    places = ids.shape[0]
    return pl.pallas_call(
        functools.partial(lookup_kernel, slots),
        out_shape=jax.ShapeDtypeStruct((places, table.shape[1]), bf16),
        in_specs=[
            pl.BlockSpec(memory_space=pltpu.SMEM),
            pl.BlockSpec(memory_space=pltpu.SMEM),
            pl.BlockSpec(memory_space=pl.ANY),
        ],
        out_specs=VMEM,
        scratch_shapes=[
            pltpu.VMEM((places, table.shape[1]), f32),
            pltpu.SemaphoreType.DMA,
        ],
        compiler_params=pltpu.CompilerParams(vmem_limit_bytes=40 * 1024 * 1024),
        name="lookup",
    )(fills, ids, table)


def table_tile(share, count=9):
    return -(-share // (count * 16)) * 16


def head_kernel(share, finals, table, logits, rows, stats, mixed, top, total):
    tile = table.shape[0]
    step = pl.program_id(0)
    known = step * tile + lax.broadcasted_iota(jnp.int32, (tile, 1), 0) < share
    low = jnp.where(known, table[...], 0.0).astype(bf16)
    scores = mm_back(low, finals[...])
    logits[...] = scores
    scores = jnp.where(known, scores, masked_score)

    @pl.when(step == 0)
    def _():
        top[...] = jnp.full(top.shape, masked_score, f32)
        total[...] = jnp.zeros_like(total)
        mixed[...] = jnp.zeros_like(mixed)

    new_top = jnp.maximum(top[...], jnp.max(scores, axis=0, keepdims=True))
    shrink = jnp.exp(top[...] - new_top)
    weights = jnp.exp(scores - new_top)
    top[...] = new_top
    total[...] = total[...] * shrink + jnp.sum(weights, axis=0, keepdims=True)
    mixed[...] = mixed[...] * shrink + mm_outer(low, weights.astype(bf16))

    @pl.when(step == pl.num_programs(0) - 1)
    def _():
        rows[...] = mixed[...].T.astype(bf16)
        stats[...] = jnp.zeros_like(stats)
        width = stats.shape[2]
        for k in range(stats.shape[0]):
            at = slice(k * width, (k + 1) * width)
            stats[k, 0:1, :] = top[:, at]
            stats[k, 1:2, :] = total[:, at]


def head_call(finals, table, n_u):
    share, width = table.shape
    picks = finals.shape[0]
    tile = table_tile(share, 6)
    stats = (n_u, 8, picks // n_u)
    return pl.pallas_call(
        functools.partial(head_kernel, share),
        grid=(pl.cdiv(share, tile),),
        out_shape=[
            jax.ShapeDtypeStruct((share, picks), f32),
            jax.ShapeDtypeStruct((picks, width), bf16),
            jax.ShapeDtypeStruct(stats, f32),
        ],
        in_specs=[
            pl.BlockSpec((picks, width), lambda i: (0, 0)),
            pl.BlockSpec((tile, width), lambda i: (i, 0)),
        ],
        out_specs=[
            pl.BlockSpec((tile, picks), lambda i: (i, 0)),
            pl.BlockSpec((picks, width), lambda i: (0, 0)),
            pl.BlockSpec(stats, lambda i: (0, 0, 0)),
        ],
        scratch_shapes=[
            pltpu.VMEM((width, picks), f32),
            pltpu.VMEM((1, picks), f32),
            pltpu.VMEM((1, picks), f32),
        ],
        compiler_params=pltpu.CompilerParams(vmem_limit_bytes=44 * 1024 * 1024),
        name="head",
    )(finals, table)


def table_grad_kernel(
    limit, logits, finals, norms, weights, targets, rows, row_ids, grad_out, squares
):
    tile = grad_out.shape[0]
    start = pl.program_id(0) * tile
    ids = start + lax.broadcasted_iota(jnp.int32, (tile, 1), 0)
    grad_logits = (
        weights[...]
        * (jnp.exp(logits[...] - norms[...]) - jnp.where(targets[...] == ids, 1.0, 0.0))
    ).astype(bf16)
    hot = jnp.where(row_ids[...] == ids, 1.0, 0.0).astype(bf16)
    grad = mm(grad_logits, finals[...]) + mm(hot, rows[...])
    grad_out[...] = grad.astype(bf16)

    @pl.when(pl.program_id(0) == 0)
    def _():
        squares[...] = jnp.zeros_like(squares)

    squares[...] += jnp.sum(jnp.where(ids < limit, grad * grad, 0.0), axis=0, keepdims=True)


def table_grad_call(logits, finals, norms, weights, targets, rows, row_ids):
    share, picks = logits.shape
    places, width = rows.shape
    tile = table_tile(share)
    whole = lambda *shape: pl.BlockSpec(shape, lambda i: (0, 0))
    return pl.pallas_call(
        functools.partial(table_grad_kernel, share),
        grid=(pl.cdiv(share, tile),),
        out_shape=[
            jax.ShapeDtypeStruct((share, width), bf16),
            jax.ShapeDtypeStruct((1, width), f32),
        ],
        in_specs=[
            pl.BlockSpec((tile, picks), lambda i: (i, 0)),
            whole(picks, width),
            whole(1, picks),
            whole(1, picks),
            whole(1, picks),
            whole(places, width),
            whole(1, places),
        ],
        out_specs=[
            pl.BlockSpec((tile, width), lambda i: (i, 0)),
            whole(1, width),
        ],
        compiler_params=pltpu.CompilerParams(vmem_limit_bytes=32 * 1024 * 1024),
        cost_estimate=pl.CostEstimate(
            flops=2 * share * width * (picks + places),
            bytes_accessed=share * (4 * picks + 2 * width),
            transcendentals=share * picks,
        ),
        name="table_grad",
    )(logits, finals, norms, weights, targets, rows, row_ids)


def adam_kernel(rate, decay, numbers, weight, first, second, grad, change, new_first, new_second):
    gradient = grad[...].astype(f32) * numbers[:, 0:1]
    mean = beta_first * first[...] + (1.0 - beta_first) * gradient
    square = beta_second * second[...] + (1.0 - beta_second) * gradient * gradient
    new_first[...] = mean
    new_second[...] = square
    change[...] = -rate * (
        mean * numbers[:, 1:2] / (jnp.sqrt(square * numbers[:, 2:3]) + adam_eps)
        + decay * weight[...]
    )


def layer_adam_kernel(rates, decays, numbers, *refs):
    count = len(rates)
    for k in range(count):
        weight, first, second, grad = refs[4 * k : 4 * k + 4]
        adam_kernel(rates[k], decays[k], numbers, weight, first, second, grad, *refs[4 * count + 3 * k :][:3])


def layer_adam_call(numbers, groups, rates, decays):
    arrays = [array for group in groups for array in group]
    return pl.pallas_call(
        functools.partial(layer_adam_kernel, rates, decays),
        out_shape=[
            jax.ShapeDtypeStruct(group[0].shape, f32) for group in groups for _ in range(3)
        ],
        in_specs=[VMEM] * (1 + len(arrays)),
        out_specs=[VMEM] * (3 * len(groups)),
        compiler_params=pltpu.CompilerParams(vmem_limit_bytes=32 * 1024 * 1024),
        name="layer_adam",
    )(numbers, *arrays)


def adam_call(numbers, weight, first, second, grad, rate, decay):
    share, width = weight.shape
    tile = table_tile(share)
    block = pl.BlockSpec((tile, width), lambda i: (i, 0))
    return pl.pallas_call(
        functools.partial(adam_kernel, rate, decay),
        grid=(pl.cdiv(share, tile),),
        out_shape=[jax.ShapeDtypeStruct((share, width), f32)] * 3,
        in_specs=[pl.BlockSpec((1, 128), lambda i: (0, 0))] + [block] * 4,
        out_specs=[block] * 3,
        compiler_params=pltpu.CompilerParams(vmem_limit_bytes=40 * 1024 * 1024),
        name="adam",
    )(numbers, weight, first, second, grad)


def local(
    tokens,
    lengths,
    picked,
    targets,
    advantages,
    step_count,
    embedding,
    first_embedding,
    second_embedding,
    inflow,
    inflow_first_moment,
    inflow_second_moment,
    outflow,
    first_outflow,
    second_outflow,
    expand,
    first_expand,
    second_expand,
    contract,
    first_contract,
    second_contract,
    scales,
    first_scales,
    second_scales,
):
    exchange = Exchanger()
    n_u, n_b = lax.axis_size(ULY), lax.axis_size(BLK)
    n_all = n_u * n_b
    n_z = n_b // 2
    u, b = lax.axis_index(ULY), lax.axis_index(BLK)
    me = u * n_b + b
    slot_count, block_len = tokens.shape
    assert slot_count == n_u and n_b % 2 == 0
    picks = picked.shape[1]
    slot_picks = picks * n_b
    all_picks = slot_picks * n_u
    row_share = embedding.shape[0]
    group = QUERY_HEADS // KEY_VALUE_HEADS
    score_scale = HEAD_WIDTH ** (-0.5)
    in_rows, out_share, ff_share = inflow.shape[0], outflow.shape[0], contract.shape[0]
    q_share = QUERY_WIDTH // n_b
    heads_share = q_share // HEAD_WIDTH
    ff_mine = n_u * ff_share
    out_cut = QUERY_WIDTH // n_all
    scale_share = scales.shape[0]

    width = KEY_VALUE_HEADS * HEAD_WIDTH
    wants_mean = n_b * (block_len + picks) / n_all
    slots = -(-int(wants_mean + 5.2 * math.sqrt(wants_mean)) // 16) * 16
    places = n_u * slots
    blk_g = (BLK, WHOLE)
    column = ((places, 1), jnp.int32)
    row_wide = ((1, MODEL_WIDTH), f32)
    head_wide = ((1, HEAD_WIDTH), f32)
    def begin_call():
        return named_call(
            exchange,
            functools.partial(begin_body, n_u, n_b, row_share, slots),
            dict(
                tokens=blk_g,
                targets=blk_g,
                picked=blk_g,
                advantages=blk_g,
                near=blk_g,
                far=(ULY, WHOLE),
            ),
            {},
            dict(
                tokens=tokens,
                targets=targets,
                picked=picked,
                advantages=advantages,
                lengths=lengths[:, None],
                scales=scales[None, :],
            ),
            dict(
                tokens_all=((n_b,) + tokens.shape, jnp.int32),
                targets_all=((n_b,) + targets.shape, jnp.int32),
                slot_picked=((1, slot_picks), jnp.int32),
                weights=((1, all_picks), f32),
                target_ids=((1, all_picks), jnp.int32),
                weight_wide=((picks, 128), f32),
                row_ids=column,
                key_pos=column,
                key_lim=column,
                target_of=column,
                positions=((places + slot_picks, 1), jnp.int32),
                meta=((24, 128), f32),
                gain_attn=row_wide,
                gain_mlp=row_wide,
                gain_final=row_wide,
                gain_query=head_wide,
                gain_key=head_wide,
            ),
            dict(
                picked_all=((n_b,) + picked.shape, jnp.int32),
                advantages_all=((n_b,) + advantages.shape, f32),
                near=((n_b, 1, scale_share), f32),
                far=((n_u, n_b, 1, scale_share), f32),
                wants=((n_u, block_len + picks), jnp.int32),
                masks=((2 * n_u, block_len + picks), f32),
                labels=((2 * n_u, block_len + picks), f32),
                ranks=((2 * n_u, block_len + picks), f32),
                gains=((1, n_all * scale_share), f32),
            ),
            "begin",
        )

    begin = begin_call()
    gain_rows = [
        begin.gain_attn,
        begin.gain_mlp,
        begin.gain_final,
        begin.gain_query,
        begin.gain_key,
    ]
    gain_attn, gain_query, gain_key = begin.gain_attn[0], begin.gain_query[0], begin.gain_key[0]
    slot_picked = begin.slot_picked[0]
    rounds = (jnp.max(begin.meta[8 : 8 + n_u, 0]).astype(jnp.int32) + slots - 1) // slots
    count_local = begin.meta[16, 0]
    half = HEAD_WIDTH // 2
    lane = jnp.arange(HEAD_WIDTH, dtype=jnp.int32)
    frequency = rope_base ** (-((lane % half).astype(f32) * 2.0 / HEAD_WIDTH))
    angles = begin.positions.astype(f32) * frequency[None, :]
    rope_cos = jnp.cos(angles)
    rope_sin = jnp.sin(angles) * jnp.where(lane < half, -1.0, 1.0)[None, :]
    query_cos, query_sin = rope_cos[places:], rope_sin[places:]
    ff_width = 2 * ff_mine
    own_cut = n_u * out_cut
    rows_low = (picks, MODEL_WIDTH)
    slot_low = (n_b, picks, MODEL_WIDTH)
    stat_rows = (8, slot_picks)
    weight_wide = begin.weight_wide

    def fetch(fills, row_ids):
        rows = lookup(fills, jnp.maximum(row_ids, 0), embedding, slots)
        return rows.reshape(n_u, slots, MODEL_WIDTH)

    def widen_ff(array):
        return (
            array.astype(f32)
            .reshape(n_b, in_rows, 2, n_u, ff_share)
            .transpose(1, 2, 3, 0, 4)
            .reshape(in_rows, 2 * FF)
        )

    def head_of_table(final_all):
        logits, head_rows, head_stats = head_call(final_all, embedding, n_u)
        return (logits, head_rows.reshape(n_u, slot_picks, MODEL_WIDTH), head_stats)

    def usual_way():
        fills = jnp.minimum(begin.meta[:n_u, 0].astype(jnp.int32), slots)
        lined = dict(
            key_pos=begin.key_pos,
            key_lim=begin.key_lim,
            slot_picked=begin.slot_picked,
            gain_attn=gain_rows[0],
            gain_mlp=gain_rows[1],
            gain_final=gain_rows[2],
            gain_query=gain_rows[3],
            gain_key=gain_rows[4],
            rope_cos=rope_cos,
            rope_sin=rope_sin,
        )
        kv_block = (in_rows, 2 * width)
        kv_shape = (n_u, n_z, 2) + kv_block
        q_shape = (n_u, n_b, in_rows, q_share)
        ff_shape = (n_u, n_b, in_rows, ff_width)
        out_shape = (n_u, out_share, MODEL_WIDTH)
        down_shape = (n_u, ff_share, MODEL_WIDTH)
        rows_shape = (n_u, slots, MODEL_WIDTH)
        blk_s, blk_g = (BLK, SPLIT), (BLK, WHOLE)
        uly_s, uly_g = (ULY, SPLIT), (ULY, WHOLE)
        rise = named_call(
            exchange,
            functools.partial(rise_body, n_u, n_b),
            dict(
                rows=uly_s,
                q_split=blk_s,
                ff_split=blk_s,
                picks=blk_s,
                aims=blk_s,
                q_all=uly_g,
                normed=blk_g,
                queries=blk_g,
                out_all=uly_g,
                ff_all=uly_g,
                down_all=uly_g,
                parts=blk_s,
                stats=blk_g,
                sum_out=blk_s,
                normed_mlp=blk_g,
                sum_mlp=blk_s,
                final=blk_g,
                final_all=uly_g,
            ),
            dict(
                z_send=(n_z,),
                z_recv=(n_z,),
                own=(1,),
                xy_send=(n_u, n_z),
                xy_recv=(n_u, n_z),
                core_send=(n_u, n_z),
                core_recv=(n_u, n_z),
            ),
            dict(
                rows_in=fetch(fills, begin.row_ids.reshape(-1)),
                inflow=inflow,
                expand=expand,
                outflow=outflow,
                contract=contract,
                target_of=begin.target_of,
                **lined,
            ),
            dict(
                arrived=(rows_shape, bf16),
                kv_weight=(kv_shape, bf16),
                q_weight=(q_shape, bf16),
                ff_weight=(ff_shape, bf16),
                out_weight=(out_shape, bf16),
                down_weight=(down_shape, bf16),
                pick_rows=((picks, 2 * MODEL_WIDTH), f32),
                normed_slot=(slot_low, bf16),
                query_raw=((slot_picks, q_share), f32),
                query_all=((n_b, slot_picks, q_share), bf16),
                key_raw=((places, width), f32),
                key_rot=((places, width), bf16),
                values=((places, width), bf16),
                attended=((slot_picks, own_cut), f32),
                log_total=((QUERY_HEADS, slot_picks), f32),
                after_attn=(rows_low, f32),
                normed_mlp=(slot_low, bf16),
                gate_up=((slot_picks, ff_width), f32),
                after_mlp=(rows_low, f32),
                final_mine=(rows_low, bf16),
                final_all=((n_u,) + slot_low, bf16),
            ),
            dict(
                kv_in=(kv_block, bf16),
                q_in=(q_shape[1:], bf16),
                ff_in=(ff_shape[1:], bf16),
                out_in=(out_shape[1:], bf16),
                down_in=(down_shape[1:], bf16),
                q_part=(q_shape[1:], bf16),
                ff_part=(ff_shape[1:], bf16),
                pick_send=(slot_low, bf16),
                pick_got=(slot_low, bf16),
                aim_send=(slot_low, bf16),
                aim_got=(slot_low, bf16),
                normed_mine=(rows_low, bf16),
                normed_keys=((places, MODEL_WIDTH), bf16),
                query_mine=((slot_picks, q_share), bf16),
                part_send=((n_b, slot_picks, own_cut), bf16),
                part_got=((n_b, slot_picks, own_cut), bf16),
                stats=((2 * QUERY_HEADS, slot_picks), f32),
                stats_all=((n_b, 2 * QUERY_HEADS, slot_picks), f32),
                shares=((n_b * n_u, slot_picks), f32),
                partial=(slot_low, bf16),
                partial_got=((2,) + slot_low, bf16),
                final_slot=(slot_low, bf16),
            ),
            "rise",
        )
        final_all = rise.final_all.reshape(all_picks, MODEL_WIDTH)
        logits, head_rows, head_stats = head_of_table(final_all)
        fall = named_call(
            exchange,
            functools.partial(fall_body, n_u, n_b),
            dict(
                head_rows=uly_s,
                head_stats=uly_s,
                slot_stats=blk_g,
                slot_rows=blk_s,
                norms=uly_g,
                branch=blk_g,
                sum_ff=blk_s,
                down=uly_s,
                ff=uly_s,
                branch_attn=blk_g,
                attended=blk_g,
                deltas=blk_g,
                out=uly_s,
                grad_queries=blk_s,
                sum_query=blk_s,
                q=uly_s,
                pick_back=blk_g,
                rows=uly_s,
                gains_blk=blk_g,
                gains_ulysses=uly_g,
                ff_cols=blk_s,
                q_cols=blk_s,
            ),
            dict(
                core_send=(n_u, n_z),
                core_recv=(n_u, n_z),
                xy_send=(n_u, n_z),
                xy_recv=(n_u, n_z),
                z_send=(n_z,),
                z_recv=(n_z,),
            ),
            dict(
                head_rows=head_rows,
                head_stats=head_stats,
                weights=weight_wide,
                arrived=rise.arrived,
                kv_weight=rise.kv_weight,
                q_weight=rise.q_weight,
                ff_weight=rise.ff_weight,
                out_weight=rise.out_weight,
                down_weight=rise.down_weight,
                pick_rows=rise.pick_rows,
                normed_slot=rise.normed_slot,
                query_raw=rise.query_raw,
                query_all=rise.query_all,
                key_raw=rise.key_raw,
                key_rot=rise.key_rot,
                values=rise.values,
                attended=rise.attended,
                log_total=rise.log_total,
                after_attn=rise.after_attn,
                normed_mlp=rise.normed_mlp,
                gate_up=rise.gate_up,
                after_mlp=rise.after_mlp,
                final_mine=rise.final_mine,
                **lined,
            ),
            dict(
                rows_back=(rows_shape, bf16),
                inflow_out=(inflow.shape, f32),
                expand_out=(expand.shape, f32),
                out_out=(out_shape[1:], f32),
                down_out=(down_shape[1:], f32),
                gains_out=((1, scale_share), f32),
                tails=((8, 128), f32),
                norms_row=((1, all_picks), f32),
            ),
            dict(
                rows_got=((n_u, slot_picks, MODEL_WIDTH), bf16),
                stats_got=((n_u,) + stat_rows, f32),
                slot_stats=(stat_rows, f32),
                slot_got=((n_b,) + stat_rows, f32),
                factors=((n_b + 8, slot_picks), f32),
                columns=((slot_picks, n_b + 8), f32),
                norms_mine=(stat_rows, f32),
                partial=(slot_low, bf16),
                partial_got=((3,) + slot_low, bf16),
                mine_low=(rows_low, bf16),
                grad_all=(slot_low, bf16),
                branch_all=(slot_low, bf16),
                grad_down=(down_shape, bf16),
                down_got=(down_shape, bf16),
                grad_ff=(ff_shape, bf16),
                ff_got=(ff_shape, bf16),
                grad_out=(out_shape, bf16),
                out_got=(out_shape, bf16),
                attended_mine=((slot_picks, own_cut), bf16),
                attended_all=((n_b, slot_picks, own_cut), bf16),
                deltas=((slot_picks, 128), f32),
                delta_mine=(stat_rows, f32),
                delta_all=((n_b,) + stat_rows, f32),
                normed_keys=((places, MODEL_WIDTH), bf16),
                query_send=((n_b, slot_picks, q_share), bf16),
                query_got=((n_b, slot_picks, q_share), bf16),
                grad_kv=((places, 2 * width), bf16),
                kv_grad=(kv_shape, bf16),
                kv_core=((n_u, n_z) + kv_block, bf16),
                kv_cross=((n_u, n_z) + kv_block, bf16),
                kv_plane=((n_z,) + kv_block, bf16),
                kv_line=((n_z,) + kv_block, bf16),
                grad_low=((slot_picks, q_share), bf16),
                grad_q=(q_shape, bf16),
                q_got=(q_shape, bf16),
                q_sum=(q_shape[1:], bf16),
                pick_back=(slot_low, bf16),
                grad_wide=((places, MODEL_WIDTH), f32),
                rows_send=(rows_shape, bf16),
                gain_mlp_row=((1, MODEL_WIDTH), f32),
                gain_final_row=((1, MODEL_WIDTH), f32),
                gain_picks_row=((1, MODEL_WIDTH), f32),
                gain_rows_row=((1, MODEL_WIDTH), f32),
                gain_query_row=((1, HEAD_WIDTH), f32),
                gain_key_row=((1, HEAD_WIDTH), f32),
                norms_all=((n_u,) + stat_rows, f32),
                terms=((picks, 128), f32),
                gains_line=((1, n_all * scale_share), f32),
                gains_mine=((32, 128), f32),
                gains_got=((n_b, 32, 128), f32),
                gains_slot=((32, 128), f32),
                gains_all=((n_u, 32, 128), f32),
                ff_sum=(ff_shape[1:], bf16),
                q_out=(q_shape[1:], bf16),
                ff_out=(ff_shape[1:], bf16),
            ),
            "fall",
        )
        table_grad, table_squares = table_grad_call(
            logits,
            final_all,
            fall.norms_row,
            begin.weights,
            begin.target_ids,
            fall.rows_back.reshape(places, MODEL_WIDTH),
            begin.row_ids.reshape(1, places),
        )
        return (
            fall.tails,
            table_squares,
            table_grad,
            fall.inflow_out,
            fall.out_out,
            fall.expand_out,
            fall.down_out,
            fall.gains_out,
        )

    def long_way():
        inflow_low = inflow.astype(bf16)
        q_cols = inflow_low[:, :QUERY_WIDTH].reshape(in_rows, n_b, q_share).transpose(1, 0, 2)
        ff_cols = (
            expand.astype(bf16)
            .reshape(in_rows, 2, n_u, n_b, ff_share)
            .transpose(3, 0, 1, 2, 4)
            .reshape(n_b, in_rows, 2 * ff_mine)
        )
        wants_block = block_len + picks
        wants_count = n_b * wants_block
        wants = (
            jnp.concatenate([begin.tokens_all, begin.targets_all], axis=2)
            .transpose(1, 0, 2)
            .reshape(n_u, wants_count)
        )
        my_length = lax.dynamic_index_in_dim(lengths, u, 0, keepdims=False)
        owners = wants // row_share
        own_owners = lax.dynamic_index_in_dim(owners, u, 0, keepdims=True)
        sent_mask = owners == me
        got_mask = own_owners == jnp.arange(n_u, dtype=jnp.int32)[:, None] * n_b + b
        masks = jnp.concatenate([sent_mask, got_mask], axis=0)
        totals_sent = jnp.sum(sent_mask.astype(f32), axis=1).astype(jnp.int32)
        lanes = math.gcd(wants_count, 128)
        blocks = masks.astype(bf16).reshape(2 * n_u, wants_count // lanes, lanes)
        before = (jnp.arange(lanes)[:, None] < jnp.arange(lanes)[None, :]).astype(bf16)
        block_sums = jnp.sum(blocks.astype(f32), axis=-1)
        chunk = jnp.arange(wants_count // lanes)
        block_base = mm(block_sums.astype(bf16), (chunk[:, None] < chunk[None, :]).astype(bf16))
        ranks = (
            mm(blocks.reshape(-1, lanes), before).reshape(blocks.shape) + block_base[:, :, None]
        ).reshape(2 * n_u, wants_count)
        ranks = jnp.where(masks, ranks.astype(jnp.int32), -1)
        labels = jnp.concatenate(
            [
                wants - me * row_share,
                jnp.broadcast_to(
                    jnp.arange(wants_count, dtype=jnp.int32)[None, :], (n_u, wants_count)
                ),
            ],
            axis=0,
        )

        def slot_tables(turn, hot):
            slot_rank = turn * slots + jnp.arange(slots, dtype=jnp.int32)
            hit = ranks[:, None, :] == slot_rank[None, :, None]
            found = jnp.sum(jnp.where(hit, labels[:, None, :] + 1, 0), axis=-1) - 1
            fills = jnp.clip(totals_sent - turn * slots, 0, slots)
            row_ids = found[:n_u].reshape(-1)
            entry = found[n_u:].reshape(-1)
            block, inside = entry // wants_block, entry % wants_block
            is_token = (entry >= 0) & (inside < block_len)
            key_pos = jnp.where(is_token, block * block_len + inside, 1 << 30)
            target_of = jnp.where(
                (entry >= 0) & (inside >= block_len), block * picks + inside - block_len, -1
            )
            if not hot:
                return (row_ids, fills, key_pos, None, target_of)
            pick_hot = (slot_picked[:, None] == key_pos[None, :]).astype(bf16)
            target_hot = (jnp.arange(slot_picks)[:, None] == target_of[None, :]).astype(bf16)
            return (row_ids, fills, key_pos, pick_hot, target_hot)

        row_ids, fills, key_pos, pick_hot, target_hot = slot_tables(jnp.int32(0), True)

        arrived, kv_weight, q_weight, ff_split = start_call(
            exchange, fetch(fills, row_ids), inflow_low[:, QUERY_WIDTH:], q_cols, ff_cols
        )
        arrived = arrived.reshape(places, MODEL_WIDTH)
        kv_weight = kv_weight.reshape(MODEL_WIDTH, -1)
        q_weight = q_weight.reshape(MODEL_WIDTH, q_share)
        def picked_rows(pick_hot, target_hot, arrived):
            return jnp.concatenate([mm(pick_hot, arrived), mm(target_hot, arrived)], axis=1)

        refetch_id = [exchange.next_id() for _ in range(5)]

        def refetch(turn, which):
            tables = slot_tables(turn, True)
            (got,) = exchange.many(
                ((ULY, SPLIT),), fetch(tables[1], tables[0]), collective_id=refetch_id[which]
            )
            return (tables, got.reshape(places, MODEL_WIDTH))

        def more(state):
            return state[0] < rounds

        def picks_turn(state):
            tables, got = refetch(state[0], 0)
            return (state[0] + 1, state[1] + picked_rows(tables[3], tables[4], got))

        pick_part = picked_rows(pick_hot, target_hot, arrived)
        _, pick_part = lax.while_loop(more, picks_turn, (jnp.int32(1), pick_part))
        got_picks, normed_slot, query_raw, query_all, ff_all, out_all, down_all = fused_call(
            exchange,
            functools.partial(query_body, n_b),
            ((BLK, SPLIT), (BLK, WHOLE), (BLK, WHOLE)) + ((ULY, WHOLE),) * 3,
            (
                pick_part.astype(bf16).reshape(n_b, picks, 2 * MODEL_WIDTH),
                gain_rows[0],
                gain_rows[3],
                q_weight,
                query_cos,
                query_sin,
                ff_split,
                outflow.astype(bf16),
                contract.astype(bf16),
            ),
            (
                ((picks, 2 * MODEL_WIDTH), f32),
                (slot_low, bf16),
                ((slot_picks, q_share), f32),
                ((n_b, slot_picks, q_share), bf16),
                ((n_u, n_b, in_rows, ff_width), bf16),
                ((n_u, out_share, MODEL_WIDTH), bf16),
                ((n_u, ff_share, MODEL_WIDTH), bf16),
            ),
            (
                ((n_b, picks, 2 * MODEL_WIDTH), bf16),
                (rows_low, bf16),
                ((slot_picks, q_share), bf16),
            ),
            "queries",
        )
        ff_weight = ff_all.reshape(MODEL_WIDTH, ff_width)
        out_weight = out_all.reshape(n_u * out_share, MODEL_WIDTH)
        down_weight = down_all.reshape(ff_mine, MODEL_WIDTH)

        def keys_of(arrived, key_pos):
            embedded = arrived.astype(f32)
            normed = (embedded * inverse_root(embedded) * gain_attn).astype(bf16)
            mixed = mm(normed, kv_weight)
            half = KEY_VALUE_HEADS * HEAD_WIDTH
            key_raw = mixed[:, :half].reshape(places, KEY_VALUE_HEADS, HEAD_WIDTH)
            values = mixed[:, half:].reshape(places, KEY_VALUE_HEADS, HEAD_WIDTH)
            angle_tables = rope_angles(jnp.where(key_pos < (1 << 30), key_pos, 0))
            key_rot = rotate(key_raw * inverse_root(key_raw) * gain_key, angle_tables, 1.0)
            return (
                embedded,
                normed,
                key_raw,
                angle_tables,
                key_rot.astype(bf16).transpose(1, 0, 2),
                values.astype(bf16).transpose(1, 0, 2),
            )

        query_pos = jnp.tile(slot_picked, group)

        def allowed_of(key_pos):
            return ((key_pos[None, :] <= query_pos[:, None]) & (key_pos[None, :] < my_length))[None]

        def scores_of(query_groups, key_rot, allowed):
            scores = (
                jnp.einsum("kqd,kjd->kqj", query_groups, key_rot, preferred_element_type=f32)
                * score_scale
            )
            return jnp.where(allowed, scores, masked_score)

        def attend(scores, allowed, values):
            part_max = jnp.max(scores, axis=-1, keepdims=True)
            weights = jnp.where(allowed, jnp.exp(scores - part_max), 0.0)
            out = jnp.einsum("kqj,kjd->kqd", weights.astype(bf16), values, preferred_element_type=f32)
            return (part_max, jnp.sum(weights, axis=-1, keepdims=True), out)

        keys = keys_of(arrived, key_pos)

        query_groups = (
            query_all.reshape(n_b, slot_picks, heads_share, HEAD_WIDTH)
            .transpose(0, 2, 1, 3)
            .reshape(KEY_VALUE_HEADS, group * slot_picks, HEAD_WIDTH)
        )
        allowed = allowed_of(key_pos)
        scores = scores_of(query_groups, keys[4], allowed)

        def attend_turn(state):
            turn, top, total, out = state
            tables, got = refetch(turn, 1)
            keys_now = keys_of(got, tables[2])
            allowed_now = allowed_of(tables[2])
            new = attend(scores_of(query_groups, keys_now[4], allowed_now), allowed_now, keys_now[5])
            both = jnp.maximum(top, new[0])
            old_factor, new_factor = jnp.exp(top - both), jnp.exp(new[0] - both)
            return (
                turn + 1,
                both,
                total * old_factor + new[1] * new_factor,
                out * old_factor + new[2] * new_factor,
            )

        _, part_max, part_sum, part_out = lax.while_loop(
            more, attend_turn, (jnp.int32(1),) + attend(scores, allowed, keys[5])
        )
        part_send = (
            part_out.astype(bf16)
            .reshape(QUERY_HEADS, slot_picks, HEAD_WIDTH)
            .transpose(1, 0, 2)
            .reshape(slot_picks, n_u, n_b, out_cut)
            .transpose(2, 0, 1, 3)
            .reshape(n_b, slot_picks, n_u * out_cut)
        )
        stats = jnp.stack([part_max[..., 0], part_sum[..., 0]]).reshape(2 * QUERY_HEADS, slot_picks)
        (
            attended,
            log_total,
            after_attn,
            normed_mlp,
            gate_up,
            after_mlp,
            final_mine,
            final_all,
        ) = fused_call(
            exchange,
            functools.partial(forward_body, n_u, n_b),
            ((BLK, SPLIT), (BLK, WHOLE), (BLK, SPLIT), (BLK, WHOLE), (BLK, SPLIT), (BLK, WHOLE))
            + ((ULY, WHOLE),),
            (
                part_send,
                stats,
                got_picks,
                out_weight,
                ff_weight,
                down_weight,
                gain_rows[1],
                gain_rows[2],
            ),
            (
                ((slot_picks, own_cut), f32),
                ((QUERY_HEADS, slot_picks), f32),
                (rows_low, f32),
                (slot_low, bf16),
                ((slot_picks, ff_width), f32),
                (rows_low, f32),
                (rows_low, bf16),
                ((n_u,) + slot_low, bf16),
            ),
            (
                ((n_b, slot_picks, own_cut), bf16),
                ((n_b, 2 * QUERY_HEADS, slot_picks), f32),
                ((n_b * n_u, slot_picks), f32),
                (slot_low, bf16),
                ((2,) + slot_low, bf16),
                (rows_low, bf16),
                (slot_low, bf16),
            ),
            "forward",
        )

        final_all = final_all.reshape(all_picks, MODEL_WIDTH)
        logits, head_rows, head_stats = head_of_table(final_all)
        (
            norms_all,
            terms,
            grad_gain_mlp,
            grad_gain_final,
            grad_ff,
            grad_out,
            grad_down,
            grad_after_attn,
            _,
            got_attended,
            got_delta,
        ) = fused_call(
            exchange,
            functools.partial(backward_body, n_u, n_b),
            (
                (ULY, SPLIT),
                (ULY, SPLIT),
                (BLK, SPLIT),
                (BLK, WHOLE),
                (ULY, WHOLE),
                (BLK, WHOLE),
                (BLK, SPLIT),
                (BLK, WHOLE),
                (BLK, WHOLE),
                (BLK, WHOLE),
            ),
            (
                head_rows,
                head_stats,
                final_mine,
                got_picks,
                weight_wide,
                after_mlp,
                after_attn,
                gate_up,
                normed_mlp,
                attended,
                out_weight,
                ff_weight,
                down_weight,
                gain_rows[1],
                gain_rows[2],
            ),
            (
                ((n_u,) + stat_rows, f32),
                ((picks, 128), f32),
                ((1, MODEL_WIDTH), f32),
                ((1, MODEL_WIDTH), f32),
                ((n_u, n_b, in_rows, ff_width), bf16),
                ((n_u, out_share, MODEL_WIDTH), bf16),
                ((n_u, ff_share, MODEL_WIDTH), bf16),
                (rows_low, f32),
                (slot_low, bf16),
                ((n_b, slot_picks, own_cut), bf16),
                ((n_b,) + stat_rows, f32),
            ),
            (
                ((n_u, slot_picks, MODEL_WIDTH), bf16),
                ((n_u,) + stat_rows, f32),
                (stat_rows, f32),
                ((n_b,) + stat_rows, f32),
                ((n_b + 8, slot_picks), f32),
                ((slot_picks, n_b + 8), f32),
                (stat_rows, f32),
                (slot_low, bf16),
                ((2,) + slot_low, bf16),
                (rows_low, bf16),
                (slot_low, bf16),
                ((slot_picks, own_cut), bf16),
                ((slot_picks, 128), f32),
                (stat_rows, f32),
            ),
            "backward",
        )
        loss_local = -jnp.sum(terms[:, 0])
        grad_heads = (
            got_attended.reshape(n_b, slot_picks, n_u, out_cut)
            .transpose(1, 2, 0, 3)
            .reshape(slot_picks, QUERY_HEADS, HEAD_WIDTH)
            .transpose(1, 0, 2)
            .reshape(KEY_VALUE_HEADS, group * slot_picks, HEAD_WIDTH)
        )
        row_delta = jnp.sum(
            got_delta[:, :n_u].transpose(1, 0, 2).reshape(QUERY_HEADS, HEAD_WIDTH // out_cut, slot_picks), axis=1
        ).reshape(KEY_VALUE_HEADS, group * slot_picks, 1)
        log_groups = log_total.reshape(KEY_VALUE_HEADS, group * slot_picks, 1)

        def score_grads(scores, allowed, values):
            probs = jnp.where(allowed, jnp.exp(scores - log_groups), 0.0)
            grad_probs = jnp.einsum("kqd,kjd->kqj", grad_heads, values, preferred_element_type=f32)
            return (probs, (probs * (grad_probs - row_delta) * score_scale).astype(bf16))

        def query_grads(grad_scores, key_rot):
            return jnp.einsum("kqj,kjd->kqd", grad_scores, key_rot, preferred_element_type=f32)

        def key_grads(probs, grad_scores, keys):
            grad_key = jnp.einsum(
                "kqj,kqd->kjd", grad_scores, query_groups, preferred_element_type=f32
            )
            grad_value = jnp.einsum(
                "kqj,kqd->kjd", probs.astype(bf16), grad_heads, preferred_element_type=f32
            )
            upstream = rotate(
                grad_key.astype(bf16).astype(f32).transpose(1, 0, 2), keys[3], -1.0
            )
            grad_raw, grad_gain = norm_back(keys[2], gain_key, upstream)
            grad_kv = jnp.concatenate(
                [
                    grad_raw.reshape(places, -1).astype(bf16),
                    grad_value.astype(bf16).transpose(1, 0, 2).reshape(places, -1),
                ],
                axis=1,
            )
            return (grad_kv, grad_gain)

        def row_grads(grad_kv, keys):
            return norm_back(keys[0], gain_attn, mm_back(grad_kv, kv_weight))

        def redo(turn, which):
            tables, got = refetch(turn, which)
            keys_now = keys_of(got, tables[2])
            allowed_now = allowed_of(tables[2])
            scores_now = scores_of(query_groups, keys_now[4], allowed_now)
            return (tables, keys_now) + score_grads(scores_now, allowed_now, keys_now[5])

        def query_turn(state):
            _, keys_now, _, grad_scores_now = redo(state[0], 2)
            return (state[0] + 1, state[1] + query_grads(grad_scores_now, keys_now[4]))

        probs, grad_scores = score_grads(scores, allowed, keys[5])
        _, grad_query_part = lax.while_loop(
            more, query_turn, (jnp.int32(1), query_grads(grad_scores, keys[4]))
        )
        query_send = (
            grad_query_part.astype(bf16)
            .reshape(n_b, heads_share, slot_picks, HEAD_WIDTH)
            .transpose(0, 2, 1, 3)
            .reshape(n_b, slot_picks, q_share)
        )
        (
            grad_gain_query,
            grad_gain_picks,
            grad_q,
            pick_back,
            sum_ff,
            sum_outflow,
            sum_contract,
        ) = fused_call(
            exchange,
            query_back_body,
            ((BLK, SPLIT), (BLK, SPLIT), (BLK, WHOLE)) + ((ULY, SPLIT),) * 3,
            (
                query_send,
                query_raw,
                query_cos,
                query_sin,
                gain_rows[3],
                q_weight,
                normed_slot,
                got_picks,
                gain_rows[0],
                grad_after_attn,
                grad_ff,
                grad_out,
                grad_down,
            ),
            (
                ((1, HEAD_WIDTH), f32),
                ((1, MODEL_WIDTH), f32),
                ((n_u, n_b, in_rows, q_share), bf16),
                (slot_low, bf16),
                ((n_b, in_rows, ff_width), bf16),
                ((out_share, MODEL_WIDTH), f32),
                ((ff_share, MODEL_WIDTH), f32),
            ),
            (
                ((n_b, slot_picks, q_share), bf16),
                ((slot_picks, q_share), bf16),
                (slot_low, bf16),
                (slot_low, bf16),
                (rows_low, bf16),
                ((n_u, n_b, in_rows, ff_width), bf16),
                ((n_u, out_share, MODEL_WIDTH), bf16),
                ((n_u, ff_share, MODEL_WIDTH), bf16),
            ),
            "query_grads",
        )
        pick_back = pick_back.reshape(slot_picks, MODEL_WIDTH)

        grad_kv, grad_gain_key = key_grads(probs, grad_scores, keys)
        grad_kv_weight = mm_outer(keys[1], grad_kv)
        grad_rows, grad_gain_attn = row_grads(grad_kv, keys)

        def weight_turn(state):
            turn, weight_sum, key_sum, attn_sum = state
            _, keys_now, probs_now, grad_scores_now = redo(turn, 3)
            grad_kv_now, gain_key_now = key_grads(probs_now, grad_scores_now, keys_now)
            _, gain_attn_now = row_grads(grad_kv_now, keys_now)
            return (
                turn + 1,
                weight_sum + mm_outer(keys_now[1], grad_kv_now),
                key_sum + gain_key_now,
                attn_sum + gain_attn_now,
            )

        _, grad_kv_weight, grad_gain_key, grad_gain_attn = lax.while_loop(
            more, weight_turn, (jnp.int32(1), grad_kv_weight, grad_gain_key, grad_gain_attn)
        )
        grad_scales = jnp.concatenate(
            [
                grad_gain_attn + grad_gain_picks[0],
                grad_gain_mlp[0],
                grad_gain_final[0],
                grad_gain_query[0],
                grad_gain_key,
            ]
        )

        token_rows = (grad_rows + mm_outer(pick_hot, pick_back)).astype(bf16)
        sum_kv, rows_back, got_q, got_ff, got_scales = settle_call(
            exchange,
            grad_kv_weight.astype(bf16).reshape(n_u, n_z, 2, in_rows, -1),
            token_rows.reshape(n_u, slots, MODEL_WIDTH),
            grad_q,
            sum_ff,
            jnp.pad(
                grad_scales.reshape(n_all, scale_share), ((0, 0), (0, 128 - scale_share))
            ).reshape(n_all, 1, 128),
        )
        sum_q = got_q.astype(f32).transpose(1, 0, 2).reshape(in_rows, QUERY_WIDTH)
        sum_inflow = jnp.concatenate([sum_q, sum_kv], axis=1)
        sum_expand = widen_ff(got_ff)
        sum_scales = jnp.sum(got_scales, axis=0)[0, :scale_share]

        table_grad, table_squares = table_grad_call(
            logits,
            final_all,
            norms_all[:, 0].reshape(1, all_picks),
            begin.weights,
            begin.target_ids,
            rows_back.reshape(places, MODEL_WIDTH),
            row_ids.reshape(1, places),
        )
        return_id = exchange.next_id()

        def return_turn(state):
            turn, so_far, _ = state
            tables, keys_now, probs_now, grad_scores_now = redo(turn, 4)
            grad_kv_now, _ = key_grads(probs_now, grad_scores_now, keys_now)
            rows_now, _ = row_grads(grad_kv_now, keys_now)
            rows_now = (rows_now + mm_outer(tables[3], pick_back)).astype(bf16)
            (back,) = exchange.many(
                ((ULY, SPLIT),),
                rows_now.reshape(n_u, slots, MODEL_WIDTH),
                collective_id=return_id,
            )
            hot = (
                jnp.arange(row_share, dtype=jnp.int32)[:, None] == tables[0][None, :]
            ).astype(bf16)
            grown = so_far.astype(f32) + mm(hot, back.reshape(places, MODEL_WIDTH))
            return (turn + 1, grown.astype(bf16), jnp.sum(grown * grown, axis=0, keepdims=True))

        _, table_grad, table_squares = lax.while_loop(
            more, return_turn, (jnp.int32(1), table_grad, table_squares)
        )
        squares = jnp.zeros((), f32)
        for grad_piece in (sum_inflow, sum_outflow, sum_expand, sum_contract, sum_scales):
            squares = squares + jnp.sum(grad_piece * grad_piece)
        tails = jnp.pad(jnp.stack([squares, loss_local]), (0, 6))
        return (
            jnp.broadcast_to(tails[:, None], (8, 128)),
            table_squares,
            table_grad,
            sum_inflow,
            sum_outflow,
            sum_expand,
            sum_contract,
            sum_scales[None, :],
        )

    step_float = step_count[0].astype(f32)
    first_scale = 1.0 / (1.0 - beta_first**step_float)
    second_scale = 1.0 / (1.0 - beta_second**step_float)

    steps = jnp.pad(jnp.stack([first_scale, second_scale]), (1, 125)).reshape(1, 128)

    def finish(tails, table_squares, table_grad, *layer_grads):
        numbers = named_call(
            exchange,
            totals_body,
            dict(near=(ALL, WHOLE)),
            {},
            dict(
                tails=tails,
                table_squares=table_squares,
                counts=begin.meta[16:],
                steps=steps,
            ),
            dict(numbers=((1, 128), f32)),
            dict(mine=((1, 128), f32), all=((n_all, 1, 128), f32)),
            "totals",
            8,
        ).numbers
        outputs = [numbers[0, 3], numbers[0, 4]]
        outputs += adam_call(
            numbers,
            embedding,
            first_embedding,
            second_embedding,
            table_grad,
            learning_rates[0],
            weight_decays[0],
        )
        outputs += layer_adam_call(
            numbers,
            (
                (inflow, inflow_first_moment, inflow_second_moment, layer_grads[0]),
                (outflow, first_outflow, second_outflow, layer_grads[1]),
                (expand, first_expand, second_expand, layer_grads[2]),
                (contract, first_contract, second_contract, layer_grads[3]),
                (scales[None, :], first_scales[None, :], second_scales[None, :], layer_grads[4]),
            ),
            learning_rates[1:],
            weight_decays[1:],
        )
        outputs[-3:] = [array[0] for array in outputs[-3:]]
        return tuple(outputs)

    _, outputs = lax.while_loop(
        lambda state: state[0],
        lambda state: (jnp.bool_(False), finish(*long_way())),
        (rounds > 1, finish(*usual_way())),
    )
    return outputs


def solution(mesh):
    rows = P((ULY, BLK), None)
    flat_rows = P((ULY, BLK))
    column = P(None, BLK)
    return jax.shard_map(
        local,
        mesh=mesh,
        in_specs=(column, P(), column, column, column, P()) + (rows,) * 15 + (flat_rows,) * 3,
        out_specs=(P(), P()) + (rows,) * 15 + (flat_rows,) * 3,
        check_vma=False,
    )
```

```python
import functools
import math

import jax
import jax.numpy as jnp
from jax import lax
from jax.experimental import pallas as pl
from jax.experimental.pallas import tpu as pltpu
from jax.sharding import PartitionSpec as P

MODEL_WIDTH = 1024
QUERY_HEADS = 16
KEY_VALUE_HEADS = 8
HEAD_WIDTH = 128
FF = 3072
QUERY_WIDTH = QUERY_HEADS * HEAD_WIDTH

norm_eps = 1e-06
rope_base = 1000000.0
clip_limit = 0.01
beta_first = 0.9
beta_second = 0.95
adam_eps = 1e-08
learning_rates = (0.01, 0.003, 0.07, 0.003, 0.002, 0.01)
weight_decays = (0.1, 0.1, 0.1, 0.1, 0.1, 0.0)
masked_score = -1e30

bf16 = jnp.bfloat16
f32 = jnp.float32
BLK, ULY, ALL = "blk", "ulysses", "all"
SPLIT, WHOLE = "s", "g"


def inverse_root(values):
    return lax.rsqrt(jnp.mean(values * values, axis=-1, keepdims=True) + norm_eps)


def norm_back(inputs, gain_vec, upstream):
    root_scale = inverse_root(inputs)
    unit_rows = inputs * root_scale
    weighted = upstream * gain_vec
    grad_inputs = root_scale * (
        weighted - unit_rows * jnp.mean(weighted * unit_rows, axis=-1, keepdims=True)
    )
    grad_gain = jnp.sum((upstream * unit_rows).reshape(-1, gain_vec.shape[-1]), axis=0)
    return (grad_inputs, grad_gain)


def rope_angles(positions):
    half_width = HEAD_WIDTH // 2
    frequency = rope_base ** (
        -(jnp.arange(half_width, dtype=jnp.int32).astype(f32) * 2.0 / HEAD_WIDTH)
    )
    angles = positions.astype(f32)[:, None] * frequency[None, :]
    return (jnp.cos(angles), jnp.sin(angles))


def rotate(values, tables, sign_value):
    half_width = values.shape[-1] // 2
    front_half = values[..., :half_width]
    back_half = values[..., half_width:]
    cosine_part = tables[0][:, None, :]
    sine_part = tables[1][:, None, :] * sign_value
    return jnp.concatenate(
        [
            front_half * cosine_part - back_half * sine_part,
            back_half * cosine_part + front_half * sine_part,
        ],
        axis=-1,
    )


def mm(left, right):
    return lax.dot_general(left, right, (((1,), (0,)), ((), ())), preferred_element_type=f32)


def mm_outer(left, right):
    return lax.dot_general(left, right, (((0,), (0,)), ((), ())), preferred_element_type=f32)


def mm_back(left, right):
    return lax.dot_general(left, right, (((1,), (1,)), ((), ())), preferred_element_type=f32)


def spread_rows(onehot, rows):
    return lax.dot_general(
        onehot.astype(f32),
        rows,
        (((0,), (0,)), ((), ())),
        precision=lax.Precision.HIGHEST,
        preferred_element_type=f32,
    )


def place_of(axis, blk_count, peer):
    if axis == ALL:
        return {ULY: peer // blk_count, BLK: lax.rem(peer, blk_count)}
    return {axis: peer}


def rank_of(axis, blk_count):
    row, column = lax.axis_index(ULY), lax.axis_index(BLK)
    return {ULY: row, BLK: column, ALL: row * blk_count + column}[axis]


def greet(axes, blk_count, counts):
    barrier = pltpu.get_barrier_semaphore()
    axes = (ALL,) if ALL in axes else tuple(axes)
    total = 0
    for axis in axes:
        me, count = rank_of(axis, blk_count), counts[axis]

        def call(step, carry, axis=axis, me=me, count=count):
            pl.semaphore_signal(
                barrier,
                inc=1,
                device_id=place_of(axis, blk_count, lax.rem(me + step, count)),
                device_id_type=pl.DeviceIdType.MESH,
            )
            return carry

        lax.fori_loop(1, count, call, 0)
        total += count - 1
    pl.semaphore_wait(barrier, total)


def each(count, body, first=0):
    def step(k, carry):
        body(k)
        return carry

    lax.fori_loop(first, count, step, 0)


def remote(source, target, send_sem, recv_sem, device_id):
    return pltpu.make_async_remote_copy(
        src_ref=source,
        dst_ref=target,
        send_sem=send_sem,
        recv_sem=recv_sem,
        device_id=device_id,
        device_id_type=pl.DeviceIdType.MESH,
    )


class Part:
    def __init__(self, axis, kind, source, landing, send_sems, recv_sems, own_sem, blk_count):
        self.axis, self.kind, self.blk_count = axis, kind, blk_count
        self.source, self.landing = source, landing
        self.send_sems, self.recv_sems, self.own_sem = send_sems, recv_sems, own_sem
        self.me, self.count = rank_of(axis, blk_count), landing.shape[0]

    def copy(self, step):
        peer = lax.rem(self.me + step, self.count)
        return remote(
            self.source.at[peer] if self.kind == SPLIT else self.source,
            self.landing.at[self.me],
            self.send_sems.at[step],
            self.recv_sems.at[step],
            place_of(self.axis, self.blk_count, peer),
        )

    def own(self):
        return pltpu.make_async_copy(
            self.source.at[self.me] if self.kind == SPLIT else self.source,
            self.landing.at[self.me],
            self.own_sem,
        )

    def start(self):
        each(self.count, lambda step: self.copy(step).start(), 1)
        self.own().start()

    def finish(self):
        self.own().wait()
        each(self.count, lambda step: self.copy(step).wait(), 1)


def sems(count):
    return [
        pltpu.SemaphoreType.DMA((count,)),
        pltpu.SemaphoreType.DMA((count,)),
        pltpu.SemaphoreType.DMA,
    ]


def exchange_kernel(plan, blk_count, counts, *refs):
    parts = len(plan)
    entries = [
        Part(axis, kind, refs[k], refs[parts + k], *refs[2 * parts + 3 * k :][:3], blk_count)
        for k, (axis, kind) in enumerate(plan)
    ]
    greet({axis for axis, _ in plan}, blk_count, counts)
    for entry in entries:
        entry.start()
    for entry in entries:
        entry.finish()


def axis_counts():
    n_u, n_b = lax.axis_size(ULY), lax.axis_size(BLK)
    return {ULY: n_u, BLK: n_b, ALL: n_u * n_b}


VMEM = pl.BlockSpec(memory_space=pltpu.VMEM)


def remote_call(kernel, collective_id, shapes, scratch, arrays, name, grant=40):
    few = lax.axis_size(ULY) * lax.axis_size(BLK) <= 32
    return pl.pallas_call(
        kernel,
        out_shape=shapes,
        in_specs=[VMEM] * len(arrays),
        out_specs=[VMEM] * len(shapes),
        scratch_shapes=scratch,
        compiler_params=pltpu.CompilerParams(
            collective_id=collective_id,
            has_side_effects=True,
            vmem_limit_bytes=(grant if few or grant < 40 else 57) * 1024 * 1024,
        ),
        name=name,
    )(*arrays)


class Exchanger:
    def __init__(self):
        self.used = 0

    def next_id(self):
        self.used += 1
        return self.used - 1

    def many(self, plan, *arrays, collective_id=None):
        counts = axis_counts()
        shapes = [
            jax.ShapeDtypeStruct(
                array.shape if kind == SPLIT else (counts[axis],) + array.shape, array.dtype
            )
            for (axis, kind), array in zip(plan, arrays)
        ]
        scratch = []
        for axis, _ in plan:
            scratch += sems(counts[axis])
        if collective_id is None:
            collective_id = self.next_id()
        return remote_call(
            functools.partial(exchange_kernel, plan, counts[BLK], counts),
            collective_id,
            shapes,
            scratch,
            arrays,
            "exchange_" + str(collective_id),
        )

    def __call__(self, axis, kinds, *arrays):
        return self.many(tuple((axis, kind) for kind in kinds), *arrays)


def start_kernel(
    blk_count,
    counts,
    rows_in,
    kv_in,
    q_in,
    ff_in,
    rows_out,
    kv_out,
    q_out,
    ff_out,
    q_split,
    z_send,
    z_recv,
    own_sem,
    xy_send,
    xy_recv,
    core_send,
    core_recv,
    *part_sems,
):
    u, b = lax.axis_index(ULY), lax.axis_index(BLK)
    n_u, n_z = kv_out.shape[0], kv_out.shape[1]
    z, c = b // 2, lax.rem(b, 2)
    greet({ULY, BLK}, blk_count, counts)
    rows = Part(ULY, SPLIT, rows_in, rows_out, *part_sems[0:3], blk_count)
    first_q = Part(BLK, SPLIT, q_in, q_split, *part_sems[3:6], blk_count)
    then_q = Part(ULY, WHOLE, q_split, q_out, *part_sems[6:9], blk_count)
    split_ff = Part(BLK, SPLIT, ff_in, ff_out, *part_sems[9:12], blk_count)

    def along_z(step):
        mine = kv_out.at[u, z, c]
        return remote(
            kv_in,
            mine,
            z_send.at[step],
            z_recv.at[step],
            {BLK: lax.rem(z + step, n_z) * 2 + c},
        )

    def own_copy():
        return pltpu.make_async_copy(kv_in, kv_out.at[u, z, c], own_sem)

    def block(hop, step):
        return kv_out.at[lax.rem(u - hop + n_u, n_u), lax.rem(z - step + n_z, n_z), c]

    def across(hop, step):
        place = block(0, step)
        return remote(
            place,
            place,
            xy_send.at[hop, step],
            xy_recv.at[hop, step],
            {ULY: lax.rem(u + hop, n_u)},
        )

    def to_core(hop, step):
        place = block(hop, step)
        return remote(
            place,
            place,
            core_send.at[hop, step],
            core_recv.at[hop, step],
            {BLK: z * 2 + 1 - c},
        )

    own_copy().start()
    each(n_z, lambda step: along_z(step).start(), 1)
    first_q.start()
    rows.start()
    own_copy().wait()
    each(n_u, lambda hop: across(hop, 0).start(), 1)
    to_core(0, 0).start()
    split_ff.start()

    def pass_on(step):
        along_z(step).wait_recv()
        each(n_u, lambda hop: across(hop, step).start(), 1)
        to_core(0, step).start()

    each(n_z, pass_on, 1)
    first_q.finish()
    then_q.start()

    def share(step):
        def one(hop):
            across(hop, step).wait_recv()
            to_core(hop, step).start()

        each(n_u, one, 1)

    each(n_z, share)
    rows.finish()
    split_ff.finish()
    then_q.finish()
    each(n_z, lambda step: along_z(step).wait_send(), 1)
    each(n_z, lambda step: each(n_u, lambda hop: across(hop, step).wait_send(), 1))
    each(n_z, lambda step: each(n_u, lambda hop: to_core(hop, step).wait()))


def start_call(exchange, rows, kv_low, q_cols, ff_cols):
    counts = axis_counts()
    n_u, n_b = counts[ULY], counts[BLK]
    n_z = n_b // 2
    dma = pltpu.SemaphoreType.DMA
    return remote_call(
        functools.partial(start_kernel, n_b, counts),
        exchange.next_id(),
        [
            jax.ShapeDtypeStruct(rows.shape, bf16),
            jax.ShapeDtypeStruct((n_u, n_z, 2) + kv_low.shape, bf16),
            jax.ShapeDtypeStruct((n_u,) + q_cols.shape, bf16),
            jax.ShapeDtypeStruct(ff_cols.shape, bf16),
        ],
        [
            pltpu.VMEM(q_cols.shape, bf16),
            dma((n_z,)),
            dma((n_z,)),
            dma,
            dma((n_u, n_z)),
            dma((n_u, n_z)),
            dma((n_u, n_z)),
            dma((n_u, n_z)),
        ]
        + sems(n_u)
        + sems(n_b)
        + sems(n_u)
        + sems(n_b),
        (rows, kv_low, q_cols, ff_cols),
        "start",
    )


def settle_kernel(
    blk_count,
    counts,
    kv_in,
    rows_in,
    q_in,
    ff_in,
    gains_in,
    kv_out,
    rows_out,
    q_out,
    ff_out,
    gains_out,
    kv_core,
    kv_pair,
    kv_cross,
    kv_plane,
    kv_line,
    q_got,
    q_sum,
    core_send,
    core_recv,
    xy_send,
    xy_recv,
    z_send,
    z_recv,
    *part_sems,
):
    u, b = lax.axis_index(ULY), lax.axis_index(BLK)
    n_u, n_z = kv_in.shape[0], kv_in.shape[1]
    z, c = b // 2, lax.rem(b, 2)
    greet({ALL}, blk_count, counts)
    rows = Part(ULY, SPLIT, rows_in, rows_out, *part_sems[0:3], blk_count)
    first_q = Part(ULY, SPLIT, q_in, q_got, *part_sems[3:6], blk_count)
    then_q = Part(BLK, SPLIT, q_sum, q_out, *part_sems[6:9], blk_count)
    gains = Part(ALL, SPLIT, gains_in, gains_out, *part_sems[9:12], blk_count)
    split_ff = Part(BLK, SPLIT, ff_in, ff_out, *part_sems[12:15], blk_count)

    def place(hop, step):
        return (lax.rem(u + hop, n_u), lax.rem(z + step, n_z))

    def to_core(hop, step):
        row, line = place(hop, step)
        return remote(
            kv_in.at[row, line, 1 - c],
            kv_core.at[hop, step],
            core_send.at[hop, step],
            core_recv.at[hop, step],
            {BLK: z * 2 + 1 - c},
        )

    def across(hop, step):
        return remote(
            kv_pair.at[hop, step],
            kv_cross.at[hop, step],
            xy_send.at[hop, step],
            xy_recv.at[hop, step],
            {ULY: lax.rem(u + hop, n_u)},
        )

    def along_z(step):
        return remote(
            kv_plane.at[step],
            kv_line.at[step],
            z_send.at[step],
            z_recv.at[step],
            {BLK: lax.rem(z + step, n_z) * 2 + c},
        )

    each(n_z, lambda step: each(n_u, lambda hop: to_core(hop, step).start()))
    first_q.start()
    split_ff.start()

    def add_pair(step):
        def one(hop):
            row, line = place(hop, step)
            to_core(hop, step).wait_recv()
            kv_pair[hop, step] = (
                kv_in[row, line, c].astype(f32) + kv_core[hop, step].astype(f32)
            ).astype(bf16)

        def forward(hop):
            one(hop)
            across(hop, step).start()

        one(0)
        each(n_u, forward, 1)

    each(n_z, add_pair, 1)
    add_pair(0)
    rows.start()
    gains.start()
    first_q.finish()
    q_sum[...] = jnp.sum(q_got[...].astype(f32), axis=0).astype(bf16)
    then_q.start()

    def plane_sum(step):
        total = kv_pair[0, step].astype(f32)
        for hop in range(1, n_u):
            across(hop, step).wait_recv()
            total = total + kv_cross[hop, step].astype(f32)
        return total

    def add_plane(step):
        kv_plane[step] = plane_sum(step).astype(bf16)
        along_z(step).start()

    each(n_z, add_plane, 1)
    total = plane_sum(0)
    for step in range(1, n_z):
        along_z(step).wait_recv()
        total = total + kv_line[step].astype(f32)
    kv_out[...] = total
    then_q.finish()
    split_ff.finish()
    gains.finish()
    rows.finish()
    each(n_z, lambda step: each(n_u, lambda hop: to_core(hop, step).wait_send()))
    each(n_z, lambda step: each(n_u, lambda hop: across(hop, step).wait_send(), 1))
    each(n_z, lambda step: along_z(step).wait_send(), 1)


def settle_call(exchange, kv_grad, rows, q_grad, ff_grad, gains):
    counts = axis_counts()
    n_u, n_b = counts[ULY], counts[BLK]
    n_z = n_b // 2
    block = kv_grad.shape[3:]
    dma = pltpu.SemaphoreType.DMA
    return remote_call(
        functools.partial(settle_kernel, n_b, counts),
        exchange.next_id(),
        [
            jax.ShapeDtypeStruct(block, f32),
            jax.ShapeDtypeStruct(rows.shape, bf16),
            jax.ShapeDtypeStruct(q_grad.shape[1:], bf16),
            jax.ShapeDtypeStruct(ff_grad.shape, bf16),
            jax.ShapeDtypeStruct(gains.shape, f32),
        ],
        [
            pltpu.VMEM((n_u, n_z) + block, bf16),
            pltpu.VMEM((n_u, n_z) + block, bf16),
            pltpu.VMEM((n_u, n_z) + block, bf16),
            pltpu.VMEM((n_z,) + block, bf16),
            pltpu.VMEM((n_z,) + block, bf16),
            pltpu.VMEM(q_grad.shape, bf16),
            pltpu.VMEM(q_grad.shape[1:], bf16),
            dma((n_u, n_z)),
            dma((n_u, n_z)),
            dma((n_u, n_z)),
            dma((n_u, n_z)),
            dma((n_z,)),
            dma((n_z,)),
        ]
        + sems(n_u)
        + sems(n_u)
        + sems(n_b)
        + sems(n_u * n_b)
        + sems(n_b),
        (kv_grad, rows, q_grad, ff_grad, gains),
        "settle",
    )


def norm_back_rows(inputs, gain_vec, upstream):
    root_scale = inverse_root(inputs)
    unit_rows = inputs * root_scale
    weighted = upstream * gain_vec
    grad_inputs = root_scale * (
        weighted - unit_rows * jnp.mean(weighted * unit_rows, axis=-1, keepdims=True)
    )
    return (grad_inputs, jnp.sum(upstream * unit_rows, axis=0, keepdims=True))


class Links:
    def __init__(self, plan, blk_count, sem_refs):
        self.plan, self.blk_count, self.sem_refs = plan, blk_count, sem_refs

    def __call__(self, k, source, landing):
        axis, kind = self.plan[k]
        part = Part(axis, kind, source, landing, *self.sem_refs[3 * k : 3 * k + 3], self.blk_count)
        part.start()
        return part

    def now(self, k, source, landing):
        self(k, source, landing).finish()


def fused_call(exchange, body, plan, arrays, outs, scratch, name):
    counts = axis_counts()
    n_in, n_out, n_scratch = len(arrays), len(outs), len(scratch)
    sem_shapes = []
    for axis, _ in plan:
        sem_shapes += sems(counts[axis])

    def kernel(*refs):
        ins, refs = refs[:n_in], refs[n_in:]
        results, refs = refs[:n_out], refs[n_out:]
        kept, sem_refs = refs[:n_scratch], refs[n_scratch:]
        greet({axis for axis, _ in plan}, counts[BLK], counts)
        body(Links(plan, counts[BLK], sem_refs), ins, results, kept)

    return remote_call(
        kernel,
        exchange.next_id(),
        [jax.ShapeDtypeStruct(shape, dtype) for shape, dtype in outs],
        [pltpu.VMEM(shape, dtype) for shape, dtype in scratch] + sem_shapes,
        arrays,
        name,
    )


def sum_blocks(landing):
    total = landing[0].astype(f32)
    for k in range(1, landing.shape[0]):
        total = total + landing[k].astype(f32)
    return total


def flat_rows_of(ref):
    return ref[...].reshape(-1, ref.shape[-1])


def turned(values, cosines, sines):
    return values * cosines + pltpu.roll(values, HEAD_WIDTH // 2, 1) * sines


def lanes_of(columns, width, count):
    group = lax.broadcasted_iota(jnp.int32, (columns[0].shape[0], width * count), 1) // width
    spread = columns[0]
    for k in range(1, count):
        spread = jnp.where(group == k, columns[k], spread)
    return spread


def query_body(n_b, links, ins, outs, scratch):
    pick_part, gain_attn, gain_query, q_weight, cosines, sines, ff_rows, out_rows, down_rows = ins
    picks_out, normed_all, query_raw, query_all, ff_all, out_all, down_all = outs
    pick_got, normed_mine, query_mine = scratch
    first = links(0, pick_part, pick_got)
    behind = [
        links(3, ff_rows, ff_all),
        links(4, out_rows, out_all),
        links(5, down_rows, down_all),
    ]
    first.finish()
    rows = sum_blocks(pick_got)
    picks_out[...] = rows
    mine = rows[:, :MODEL_WIDTH]
    normed_mine[...] = (mine * inverse_root(mine) * gain_attn[...]).astype(bf16)
    links.now(1, normed_mine, normed_all)
    raw = mm(flat_rows_of(normed_all), q_weight[...])
    query_raw[...] = raw
    for k in range(raw.shape[1] // HEAD_WIDTH):
        head = raw[:, k * HEAD_WIDTH : (k + 1) * HEAD_WIDTH]
        query_mine[:, k * HEAD_WIDTH : (k + 1) * HEAD_WIDTH] = turned(
            head * inverse_root(head) * gain_query[...], cosines[...], sines[...]
        ).astype(bf16)
    links.now(2, query_mine, query_all)
    for part in behind:
        part.finish()


def forward_body(n_u, n_b, links, ins, outs, scratch):
    part_send, stats, mine, out_weight, ff_weight, down_weight, gain_mlp, gain_final = ins
    attended_out, log_out, after_out, normed_all, gate_up_out, top_out, final_mine, final_all = outs
    part_got, stats_all, shares, partial, partial_got, normed_mine, final_slot = scratch
    picks = after_out.shape[0]
    out_cut = attended_out.shape[1] // n_u
    heads_row = QUERY_HEADS // n_u
    cut_head = (lax.axis_index(BLK) * out_cut) // HEAD_WIDTH
    sent = links(0, part_send, part_got)
    links.now(1, stats, stats_all)
    full_max = stats_all[0, :QUERY_HEADS]
    for k in range(1, n_b):
        full_max = jnp.maximum(full_max, stats_all[k, :QUERY_HEADS])
    full_sum = jnp.zeros_like(full_max)
    for k in range(n_b):
        full_sum += stats_all[k, QUERY_HEADS:] * jnp.exp(stats_all[k, :QUERY_HEADS] - full_max)
    log_total = full_max + jnp.log(full_sum)
    log_out[...] = log_total
    for row in range(n_u):
        head = row * heads_row + cut_head
        row_log = log_out[pl.ds(head, 1), :]
        for k in range(n_b):
            shares[pl.ds(k * n_u + row, 1), :] = jnp.exp(
                stats_all[k, pl.ds(head, 1), :] - row_log
            )
    columns = shares[...].T
    sent.finish()
    attended = jnp.zeros(attended_out.shape, f32)
    for k in range(n_b):
        attended += part_got[k].astype(f32) * lanes_of(
            [columns[:, k * n_u + row : k * n_u + row + 1] for row in range(n_u)], out_cut, n_u
        )
    attended_out[...] = attended

    def to_picks(which, rows):
        partial[...] = rows.astype(bf16).reshape(partial.shape)
        links.now(which, partial, partial_got.at[which // 4])
        return sum_blocks(partial_got.at[which // 4])

    after_attn = mine[:, :MODEL_WIDTH] + to_picks(2, mm(attended.astype(bf16), out_weight[...]))
    after_out[...] = after_attn
    normed_mine[...] = (after_attn * inverse_root(after_attn) * gain_mlp[...]).astype(bf16)
    links.now(3, normed_mine, normed_all)
    gate_up = mm(flat_rows_of(normed_all), ff_weight[...])
    gate_up_out[...] = gate_up
    half = gate_up.shape[1] // 2
    gate_part, up_part = gate_up[:, :half], gate_up[:, half:]
    activated = (gate_part * jax.nn.sigmoid(gate_part) * up_part).astype(bf16)
    after_mlp = after_attn + to_picks(4, mm(activated, down_weight[...]))
    top_out[...] = after_mlp
    final_mine[...] = (after_mlp * inverse_root(after_mlp) * gain_final[...]).astype(bf16)
    links.now(5, final_mine, final_slot)
    links.now(6, final_slot, final_all)


def backward_body(n_u, n_b, links, ins, outs, scratch):
    (
        head_rows,
        head_stats,
        final_mine,
        picks_in,
        weights,
        after_mlp,
        after_attn,
        gate_up_in,
        normed_all,
        attended,
        out_weight,
        ff_weight,
        down_weight,
        gain_mlp,
        gain_final,
    ) = ins
    (
        norms_all,
        terms,
        gain_mlp_out,
        gain_final_out,
        grad_ff,
        grad_out,
        grad_down,
        grad_after,
        branch_all,
        attended_all,
        delta_all,
    ) = outs
    (
        rows_got,
        stats_got,
        slot_stats,
        slot_got,
        factors,
        columns,
        norms_mine,
        partial,
        partial_got,
        mine_low,
        grad_all,
        attended_mine,
        deltas,
        delta_mine,
    ) = scratch
    picks = after_mlp.shape[0]
    slot_picks = n_b * picks
    b = lax.axis_index(BLK)
    factors[...] = jnp.zeros_like(factors)
    first = links(0, head_rows, rows_got)
    links.now(1, head_stats, stats_got)
    tops = stats_got[0, 0:1, :]
    for k in range(1, n_u):
        tops = jnp.maximum(tops, stats_got[k, 0:1, :])
    total = jnp.zeros_like(tops)
    for k in range(n_u):
        factor = jnp.exp(stats_got[k, 0:1, :] - tops)
        factors[k : k + 1, :] = factor
        total += stats_got[k, 1:2, :] * factor
    slot_stats[...] = jnp.zeros_like(slot_stats)
    slot_stats[0:1, :] = tops
    slot_stats[1:2, :] = total
    slot_part = links(3, slot_stats, slot_got)
    by_row = factors[...].T
    first.finish()
    rows = rows_got[0].astype(f32) * by_row[:, 0:1]
    for k in range(1, n_u):
        rows += rows_got[k].astype(f32) * by_row[:, k : k + 1]
    partial[...] = rows.astype(bf16).reshape(partial.shape)
    back = links(2, partial, partial_got.at[0])
    slot_part.finish()
    tops = slot_got[0, 0:1, :]
    for k in range(1, n_b):
        tops = jnp.maximum(tops, slot_got[k, 0:1, :])
    total = jnp.zeros_like(tops)
    for k in range(n_b):
        factor = jnp.exp(slot_got[k, 0:1, :] - tops)
        factors[k : k + 1, :] = factor
        total += slot_got[k, 1:2, :] * factor
    log_norm = tops + jnp.log(total)
    for k in range(n_b):
        factors[k : k + 1, :] = factors[k : k + 1, :] / total
    factors[n_b : n_b + 1, :] = log_norm
    norms_mine[...] = jnp.broadcast_to(log_norm, norms_mine.shape)
    norms_part = links(4, norms_mine, norms_all)
    columns[...] = factors[...].T
    mine = columns[pl.ds(pl.multiple_of(b * picks, picks), picks), :]
    back.finish()
    target_rows = picks_in[:, MODEL_WIDTH:]
    grad_final = -target_rows
    for k in range(n_b):
        grad_final += partial_got[0, k].astype(f32) * mine[:, k : k + 1]
    grad_final = grad_final * weights[:, 0:1]
    target_logit = jnp.sum(
        final_mine[...].astype(f32) * target_rows, axis=-1, keepdims=True
    )
    terms[...] = weights[...] * (target_logit - mine[:, n_b : n_b + 1])
    grad_mlp, gain_rows = norm_back_rows(after_mlp[...], gain_final[...], grad_final)
    gain_final_out[...] = gain_rows
    mine_low[...] = grad_mlp.astype(bf16)
    links.now(5, mine_low, grad_all)
    branch = flat_rows_of(grad_all)
    gate_up = gate_up_in[...]
    half = gate_up.shape[1] // 2
    gate_part, up_part = gate_up[:, :half], gate_up[:, half:]
    sigmoid_gate = jax.nn.sigmoid(gate_part)
    grad_act = mm_back(branch, down_weight[...])
    grad_gate = grad_act * up_part * sigmoid_gate * (1.0 + gate_part * (1.0 - sigmoid_gate))
    grad_up = grad_act * gate_part * sigmoid_gate
    grad_gate_up = jnp.concatenate([grad_gate, grad_up], axis=1).astype(bf16)
    partial[...] = mm_back(grad_gate_up, ff_weight[...]).astype(bf16).reshape(partial.shape)
    back = links(6, partial, partial_got.at[1])
    activated = (gate_part * sigmoid_gate * up_part).astype(bf16)
    grad_down[...] = mm_outer(activated, branch).astype(bf16).reshape(grad_down.shape)
    back.finish()
    grad_mid, gain_rows = norm_back_rows(after_attn[...], gain_mlp[...], sum_blocks(partial_got.at[1]))
    gain_mlp_out[...] = gain_rows
    grad_attn = grad_mlp + grad_mid
    grad_after[...] = grad_attn
    mine_low[...] = grad_attn.astype(bf16)
    again = links(7, mine_low, branch_all)
    grad_ff[...] = (
        mm_outer(flat_rows_of(normed_all), grad_gate_up).astype(bf16).reshape(grad_ff.shape)
    )
    again.finish()
    branch = flat_rows_of(branch_all)
    grad_low = mm_back(branch, out_weight[...]).astype(bf16)
    attended_mine[...] = grad_low
    last = links(8, attended_mine, attended_all)
    out_cut = attended.shape[1] // n_u
    product = attended[...] * grad_low.astype(f32)
    group = lax.broadcasted_iota(jnp.int32, product.shape, 1) // out_cut
    lane = lax.broadcasted_iota(jnp.int32, deltas.shape, 1)
    sums = jnp.zeros(deltas.shape, f32)
    for row in range(n_u):
        one = jnp.sum(jnp.where(group == row, product, 0.0), axis=-1, keepdims=True)
        sums = jnp.where(lane == row, one, sums)
    deltas[...] = sums
    delta_mine[...] = deltas[...].T[:8, :]
    delta_part = links(9, delta_mine, delta_all)
    grad_out[...] = mm_outer(attended[...].astype(bf16), branch).astype(bf16).reshape(
        grad_out.shape
    )
    last.finish()
    delta_part.finish()
    norms_part.finish()


def query_back_body(links, ins, outs, scratch):
    (
        query_send,
        query_raw,
        cosines,
        sines,
        gain_query,
        q_weight,
        normed_all,
        picks_in,
        gain_attn,
        grad_after,
        grad_ff,
        grad_out,
        grad_down,
    ) = ins
    gain_query_out, gain_attn_out, grad_q, pick_back, ff_sum, out_sum, down_sum = outs
    query_got, grad_low, partial, partial_got, mine_low, ff_got, out_got, down_got = scratch
    first = links(0, query_send, query_got)
    behind = [
        links(3, grad_ff, ff_got),
        links(4, grad_out, out_got),
        links(5, grad_down, down_got),
    ]
    first.finish()
    upstream = sum_blocks(query_got).astype(bf16).astype(f32)
    gain_sum = jnp.zeros(gain_query_out.shape, f32)
    for k in range(upstream.shape[1] // HEAD_WIDTH):
        part = slice(k * HEAD_WIDTH, (k + 1) * HEAD_WIDTH)
        grad_head, gain_head = norm_back_rows(
            query_raw[:, part], gain_query[...], turned(upstream[:, part], cosines[...], -sines[...])
        )
        grad_low[:, part] = grad_head.astype(bf16)
        gain_sum += gain_head
    gain_query_out[...] = gain_sum
    partial[...] = mm_back(grad_low[...], q_weight[...]).astype(bf16).reshape(partial.shape)
    back = links(1, partial, partial_got)
    grad_q[...] = (
        mm_outer(flat_rows_of(normed_all), grad_low[...]).astype(bf16).reshape(grad_q.shape)
    )
    back.finish()
    grad_mine, gain_rows = norm_back_rows(
        picks_in[:, :MODEL_WIDTH], gain_attn[...], sum_blocks(partial_got)
    )
    gain_attn_out[...] = gain_rows
    mine_low[...] = (grad_after[...] + grad_mine).astype(bf16)
    links.now(2, mine_low, pick_back)
    for part in behind:
        part.finish()
    ff_sum[...] = sum_blocks(ff_got).astype(bf16)
    out_sum[...] = sum_blocks(out_got)
    down_sum[...] = sum_blocks(down_got)


class Named:
    pass


def named_call(exchange, body, plan, extra_sems, ins, outs, scratch, name, grant=40):
    counts = axis_counts()
    sem_shapes = []
    for axis, _ in plan.values():
        sem_shapes += sems(counts[axis])
    order = {key: k for k, key in enumerate(plan)}
    extra = list(extra_sems)

    def kernel(*refs):
        r, s = Named(), Named()
        names = list(ins) + list(outs) + list(scratch)
        for key, ref in zip(names, refs):
            setattr(r, key, ref)
        sem_refs = refs[len(names) :]
        for key, ref in zip(extra, sem_refs[3 * len(plan) :]):
            setattr(s, key, ref)
        base = Links(list(plan.values()), counts[BLK], sem_refs)
        links = Named()
        for key in plan:
            setattr(links, key, functools.partial(base, order[key]))
        greet({axis for axis, _ in plan.values()}, counts[BLK], counts)
        body(r, links, s)

    results = remote_call(
        kernel,
        exchange.next_id(),
        [jax.ShapeDtypeStruct(shape, dtype) for shape, dtype in outs.values()],
        [pltpu.VMEM(shape, dtype) for shape, dtype in scratch.values()]
        + sem_shapes
        + [pltpu.SemaphoreType.DMA(extra_sems[key]) for key in extra],
        list(ins.values()),
        name,
        grant,
    )
    found = Named()
    for key, value in zip(outs, results):
        setattr(found, key, value)
    return found


def column_of(lane_row):
    count = lane_row.shape[1]
    down = lax.broadcasted_iota(jnp.int32, (count, count), 0)
    across = lax.broadcasted_iota(jnp.int32, (count, count), 1)
    return jnp.sum(jnp.where(down == across, lane_row, 0.0), axis=1, keepdims=True)


def begin_body(n_u, n_b, row_share, slots, r, links, s):
    u, b = lax.axis_index(ULY), lax.axis_index(BLK)
    me = u * n_b + b
    block_len, picks = r.tokens.shape[1], r.picked.shape[1]
    places = n_u * slots
    gathers = [
        links.tokens(r.tokens, r.tokens_all),
        links.targets(r.targets, r.targets_all),
        links.picked(r.picked, r.picked_all),
        links.advantages(r.advantages, r.advantages_all),
    ]
    links.near(r.scales, r.near).finish()
    far = links.far(r.near, r.far)
    for part in gathers:
        part.finish()

    width = block_len + picks
    lane = lax.broadcasted_iota(jnp.int32, (1, width), 1)
    before = jnp.where(
        lax.broadcasted_iota(jnp.int32, (width, width), 0)
        < lax.broadcasted_iota(jnp.int32, (width, width), 1),
        1.0,
        0.0,
    ).astype(bf16)
    base = jnp.zeros((2 * n_u, 1), f32)
    found = [jnp.zeros((slots, width), f32) for _ in range(2 * n_u)]
    rank_of_slot = lax.broadcasted_iota(jnp.int32, (slots, width), 0).astype(f32)
    owner_first = lax.broadcasted_iota(jnp.int32, (n_u, 1), 0) * n_b + b
    most = jnp.zeros((n_u, 1), f32)
    counts = [jnp.zeros((n_u, width), f32) for _ in range(n_u * n_b)]
    for k in range(n_b):
        r.wants[:, :block_len] = r.tokens_all[k]
        r.wants[:, block_len:] = r.targets_all[k]
        wants = r.wants[...]
        local = wants - me * row_share
        sent = (local >= 0) & (local < row_share)
        own = r.wants[pl.ds(u, 1), :] - owner_first * row_share
        got = (own >= 0) & (own < row_share)
        r.masks[:n_u, :] = jnp.where(sent, 1.0, 0.0)
        r.masks[n_u:, :] = jnp.where(got, 1.0, 0.0)
        r.labels[:n_u, :] = (local + 1).astype(f32)
        r.labels[n_u:, :] = jnp.broadcast_to(k * width + lane + 1, (n_u, width)).astype(f32)
        masks = r.masks[...]
        ranks = mm(masks.astype(bf16), before) + base
        r.ranks[...] = jnp.where(masks > 0.0, ranks, -1.0)
        base += jnp.sum(masks, axis=1, keepdims=True)
        for row in range(2 * n_u):
            hit = r.ranks[row : row + 1, :] == rank_of_slot
            found[row] += jnp.where(hit, r.labels[row : row + 1, :], 0.0)
        for owner in range(n_u * n_b):
            far_row = wants - owner * row_share
            counts[owner] += jnp.where((far_row >= 0) & (far_row < row_share), 1.0, 0.0)
        r.slot_picked[:, k * picks : (k + 1) * picks] = r.picked_all[k, pl.ds(u, 1), :]
        valid = r.picked_all[k] < r.lengths[...]
        weights = jnp.where(valid, r.advantages_all[k], 0.0)
        for row in range(n_u):
            at = slice((row * n_b + k) * picks, (row * n_b + k + 1) * picks)
            r.weights[:, at] = weights[row : row + 1, :]
            r.target_ids[:, at] = r.targets_all[k, row : row + 1, :] - me * row_share
    for owner in range(n_u * n_b):
        most = jnp.maximum(most, jnp.sum(counts[owner], axis=1, keepdims=True))
    r.meta[...] = jnp.zeros_like(r.meta)
    r.meta[0:n_u, :] = jnp.broadcast_to(base[:n_u], (n_u, 128))
    r.meta[8 : 8 + n_u, :] = jnp.broadcast_to(most, (n_u, 128))
    mine_valid = r.picked[pl.ds(u, 1), :] < r.lengths[pl.ds(u, 1), :]
    mine_weight = jnp.where(mine_valid, r.advantages[pl.ds(u, 1), :], 0.0)
    r.meta[16:17, :] = jnp.broadcast_to(
        jnp.sum(jnp.where(mine_valid, 1.0, 0.0), axis=1, keepdims=True), (1, 128)
    )
    r.weight_wide[...] = jnp.broadcast_to(column_of(mine_weight), r.weight_wide.shape)
    my_length = r.lengths[pl.ds(u, 1), :]
    for row in range(n_u):
        here = slice(row * slots, (row + 1) * slots)
        r.row_ids[here, :] = jnp.sum(found[row], axis=1, keepdims=True).astype(jnp.int32) - 1
        entry = jnp.sum(found[n_u + row], axis=1, keepdims=True) - 1.0
        block = jnp.floor((entry + 0.5) * (1.0 / width))
        inside = entry - block * width
        token = (entry >= 0.0) & (inside < block_len)
        position = (block * block_len + inside).astype(jnp.int32)
        key_pos = jnp.where(token, position, 1 << 30)
        r.key_pos[here, :] = key_pos
        r.key_lim[here, :] = jnp.where(key_pos < my_length, key_pos, 1 << 30)
        r.positions[here, :] = jnp.where(token, position, 0)
        target = (block * picks + inside - block_len).astype(jnp.int32)
        r.target_of[here, :] = jnp.where((entry >= 0.0) & (inside >= block_len), target, -1)
    r.positions[places:, :] = column_of(r.slot_picked[...].astype(f32)).astype(jnp.int32)

    far.finish()
    share = r.scales.shape[1]
    for row in range(n_u):
        for k in range(n_b):
            at = (row * n_b + k) * share
            r.gains[:, at : at + share] = r.far[row, k].astype(bf16).astype(f32)
    r.gain_attn[...] = r.gains[:, :MODEL_WIDTH]
    r.gain_mlp[...] = r.gains[:, MODEL_WIDTH : 2 * MODEL_WIDTH]
    r.gain_final[...] = r.gains[:, 2 * MODEL_WIDTH : 3 * MODEL_WIDTH]
    r.gain_query[...] = r.gains[:, 3 * MODEL_WIDTH : 3 * MODEL_WIDTH + HEAD_WIDTH]
    r.gain_key[...] = r.gains[:, 3 * MODEL_WIDTH + HEAD_WIDTH :]


def totals_body(r, links, s):
    lane = lax.broadcasted_iota(jnp.int32, (1, 128), 1)
    squares = r.tails[0:1, 0:1] + jnp.sum(r.table_squares[...], axis=1, keepdims=True)
    row = jnp.where(lane == 0, squares, 0.0)
    row = jnp.where(lane == 1, r.counts[0:1, :], row)
    r.mine[...] = jnp.where(lane == 2, r.tails[1:2, 0:1], row)
    links.near(r.mine, r.all).finish()
    total = sum_blocks(r.all)
    count = total[:, 1:2]
    norm = jnp.sqrt(total[:, 0:1]) / count
    factor = jnp.minimum(1.0, clip_limit / norm) / count
    row = jnp.where(lane == 0, factor, r.steps[...])
    row = jnp.where(lane == 3, total[:, 2:3] / count, row)
    r.numbers[...] = jnp.where(lane == 4, norm, row)


def head_of(ref, head):
    share = ref.shape[2] // HEAD_WIDTH
    at = head % share * HEAD_WIDTH
    return ref[head // share, :, at : at + HEAD_WIDTH]


def cuts_of(head, n_u, n_b):
    cut = QUERY_WIDTH // (n_u * n_b)
    heads_row, pieces = QUERY_HEADS // n_u, HEAD_WIDTH // cut
    row = head // heads_row
    return [
        (head % heads_row * pieces + t, slice(row * cut, (row + 1) * cut), slice(t * cut, (t + 1) * cut))
        for t in range(pieces)
    ]


def ff_cuts(n_u, n_b):
    cut = FF // (n_u * n_b)
    return [
        (
            k,
            slice((half * n_u + row) * cut, (half * n_u + row + 1) * cut),
            slice(half * FF + (row * n_b + k) * cut, half * FF + (row * n_b + k + 1) * cut),
        )
        for k in range(n_b)
        for half in range(2)
        for row in range(n_u)
    ]


def rise_body(n_u, n_b, r, links, s):
    u, b = lax.axis_index(ULY), lax.axis_index(BLK)
    n_z = n_b // 2
    z, c = b // 2, lax.rem(b, 2)
    score_scale = HEAD_WIDTH ** (-0.5)

    def along_z(step):
        return remote(
            r.kv_in,
            r.kv_weight.at[u, z, c],
            s.z_send.at[step],
            s.z_recv.at[step],
            {BLK: lax.rem(z + step, n_z) * 2 + c},
        )

    def own_copy():
        return pltpu.make_async_copy(r.kv_in, r.kv_weight.at[u, z, c], s.own.at[0])

    def block(hop, step):
        return r.kv_weight.at[lax.rem(u - hop + n_u, n_u), lax.rem(z - step + n_z, n_z), c]

    def across(hop, step):
        place = block(0, step)
        return remote(
            place,
            place,
            s.xy_send.at[hop, step],
            s.xy_recv.at[hop, step],
            {ULY: lax.rem(u + hop, n_u)},
        )

    def to_core(hop, step):
        place = block(hop, step)
        return remote(
            place,
            place,
            s.core_send.at[hop, step],
            s.core_recv.at[hop, step],
            {BLK: z * 2 + 1 - c},
        )

    places = r.key_raw.shape[0]
    half = KEY_VALUE_HEADS * HEAD_WIDTH
    r.kv_in[...] = r.inflow[:, QUERY_WIDTH:].astype(bf16)
    own_copy().start()
    rows = links.rows(r.rows_in, r.arrived)
    q_share = r.q_in.shape[2]
    for k in range(n_b):
        r.q_in[k] = r.inflow[:, k * q_share : (k + 1) * q_share].astype(bf16)
    q_split = links.q_split(r.q_in, r.q_part)
    each(n_z, lambda step: along_z(step).start(), 1)
    own_copy().wait()
    each(n_u, lambda hop: across(hop, 0).start(), 1)
    to_core(0, 0).start()
    for k, there, here in ff_cuts(n_u, n_b):
        r.ff_in[k, :, there] = r.expand[:, here].astype(bf16)
    ff_split = links.ff_split(r.ff_in, r.ff_part)
    r.out_in[...] = r.outflow[...].astype(bf16)
    r.down_in[...] = r.contract[...].astype(bf16)
    q_split.finish()
    q_all = links.q_all(r.q_part, r.q_weight)
    rows.finish()

    arrived = flat_rows_of(r.arrived)
    pick_hot = jnp.where(r.key_pos[...] == r.slot_picked[...], 1.0, 0.0).astype(bf16)
    pick_lane = lax.broadcasted_iota(jnp.int32, pick_hot.shape, 1)
    target_hot = jnp.where(r.target_of[...] == pick_lane, 1.0, 0.0).astype(bf16)
    r.pick_send[...] = mm_outer(pick_hot, arrived).astype(bf16).reshape(r.pick_send.shape)
    picked = links.picks(r.pick_send, r.pick_got)
    r.aim_send[...] = mm_outer(target_hot, arrived).astype(bf16).reshape(r.aim_send.shape)

    def pass_on(step):
        along_z(step).wait_recv()
        each(n_u, lambda hop: across(hop, step).start(), 1)
        to_core(0, step).start()

    each(n_z, pass_on, 1)
    wide = arrived.astype(f32)
    r.normed_keys[...] = (wide * inverse_root(wide) * r.gain_attn[...]).astype(bf16)
    picked.finish()
    mine = sum_blocks(r.pick_got)
    r.pick_rows[:, :MODEL_WIDTH] = mine
    r.normed_mine[...] = (mine * inverse_root(mine) * r.gain_attn[...]).astype(bf16)
    links.normed(r.normed_mine, r.normed_slot).finish()
    q_all.finish()
    raw = mm(flat_rows_of(r.normed_slot), r.q_weight[...].reshape(MODEL_WIDTH, -1))
    r.query_raw[...] = raw
    for k in range(raw.shape[1] // HEAD_WIDTH):
        part = slice(k * HEAD_WIDTH, (k + 1) * HEAD_WIDTH)
        head = raw[:, part]
        r.query_mine[:, part] = turned(
            head * inverse_root(head) * r.gain_query[...], r.rope_cos[places:], r.rope_sin[places:]
        ).astype(bf16)
    queries = links.queries(r.query_mine, r.query_all)

    def share(step):
        def one(hop):
            across(hop, step).wait_recv()
            to_core(hop, step).start()

        each(n_u, one, 1)

    each(n_z, share)
    out_all = links.out_all(r.out_in, r.out_weight)
    ff_split.finish()
    ff_all = links.ff_all(r.ff_part, r.ff_weight)
    down_all = links.down_all(r.down_in, r.down_weight)
    each(n_z, lambda step: each(n_u, lambda hop: to_core(hop, step).wait_recv()))

    wide_head = 2 * HEAD_WIDTH

    def project(k):
        for first in (0, half):
            at = pl.multiple_of(first + k * wide_head, wide_head)
            weight = r.kv_weight[:, :, :, :, pl.ds(at, wide_head)].reshape(MODEL_WIDTH, wide_head)
            got = mm(r.normed_keys[...], weight)
            here = pl.ds(pl.multiple_of(k * wide_head, wide_head), wide_head)
            if first:
                r.values[:, here] = got.astype(bf16)
            else:
                r.key_raw[:, here] = got
                turned_both = []
                for j in range(2):
                    head = got[:, j * HEAD_WIDTH : (j + 1) * HEAD_WIDTH]
                    turned_both.append(
                        turned(
                            head * inverse_root(head) * r.gain_key[...],
                            r.rope_cos[:places],
                            r.rope_sin[:places],
                        )
                    )
                r.key_rot[:, here] = jnp.concatenate(turned_both, axis=1).astype(bf16)

    each(KEY_VALUE_HEADS // 2, project)
    queries.finish()
    allowed = r.key_lim[...] <= r.slot_picked[...]
    for head in range(QUERY_HEADS):
        at = head // (QUERY_HEADS // KEY_VALUE_HEADS) * HEAD_WIDTH
        part = slice(at, at + HEAD_WIDTH)
        scores = mm_back(r.key_rot[:, part], head_of(r.query_all, head)) * score_scale
        scores = jnp.where(allowed, scores, masked_score)
        top = jnp.max(scores, axis=0, keepdims=True)
        weights = jnp.where(allowed, jnp.exp(scores - top), 0.0)
        r.stats[head : head + 1, :] = top
        r.stats[QUERY_HEADS + head : QUERY_HEADS + head + 1, :] = jnp.sum(
            weights, axis=0, keepdims=True
        )
        out = mm_outer(weights.astype(bf16), r.values[:, part]).astype(bf16)
        for target, there, here in cuts_of(head, n_u, n_b):
            r.part_send[target, :, there] = out[:, here]

    picks = r.after_attn.shape[0]
    out_cut = r.attended.shape[1] // n_u
    heads_row = QUERY_HEADS // n_u
    cut_head = (b * out_cut) // HEAD_WIDTH
    sent = links.parts(r.part_send, r.part_got)
    links.stats(r.stats, r.stats_all).finish()
    full_max = r.stats_all[0, :QUERY_HEADS]
    for k in range(1, n_b):
        full_max = jnp.maximum(full_max, r.stats_all[k, :QUERY_HEADS])
    full_sum = jnp.zeros_like(full_max)
    for k in range(n_b):
        full_sum += r.stats_all[k, QUERY_HEADS:] * jnp.exp(
            r.stats_all[k, :QUERY_HEADS] - full_max
        )
    r.log_total[...] = full_max + jnp.log(full_sum)
    for row in range(n_u):
        head = row * heads_row + cut_head
        row_log = r.log_total[pl.ds(head, 1), :]
        for k in range(n_b):
            r.shares[k * n_u + row : k * n_u + row + 1, :] = jnp.exp(
                r.stats_all[k, pl.ds(head, 1), :] - row_log
            )
    columns = r.shares[...].T
    sent.finish()
    attended = jnp.zeros(r.attended.shape, f32)
    for k in range(n_b):
        attended += r.part_got[k].astype(f32) * lanes_of(
            [columns[:, k * n_u + row : k * n_u + row + 1] for row in range(n_u)], out_cut, n_u
        )
    r.attended[...] = attended
    out_all.finish()

    def to_picks(which, send, rows):
        r.partial[...] = rows.astype(bf16).reshape(r.partial.shape)
        landing = r.partial_got.at[which]
        send(r.partial, landing).finish()
        return sum_blocks(landing)

    after_attn = r.pick_rows[:, :MODEL_WIDTH] + to_picks(
        0, links.sum_out, mm(attended.astype(bf16), flat_rows_of(r.out_weight))
    )
    r.after_attn[...] = after_attn
    r.normed_mine[...] = (after_attn * inverse_root(after_attn) * r.gain_mlp[...]).astype(bf16)
    links.normed_mlp(r.normed_mine, r.normed_mlp).finish()
    ff_all.finish()
    gate_up = mm(flat_rows_of(r.normed_mlp), r.ff_weight[...].reshape(MODEL_WIDTH, -1))
    r.gate_up[...] = gate_up
    half = gate_up.shape[1] // 2
    gate_part, up_part = gate_up[:, :half], gate_up[:, half:]
    activated = (gate_part * jax.nn.sigmoid(gate_part) * up_part).astype(bf16)
    down_all.finish()
    after_mlp = after_attn + to_picks(1, links.sum_mlp, mm(activated, flat_rows_of(r.down_weight)))
    r.after_mlp[...] = after_mlp
    r.final_mine[...] = (after_mlp * inverse_root(after_mlp) * r.gain_final[...]).astype(bf16)
    links.final(r.final_mine, r.final_slot).finish()
    final_all = links.final_all(r.final_slot, r.final_all)
    aims = links.aims(r.aim_send, r.aim_got)
    aims.finish()
    r.pick_rows[:, MODEL_WIDTH:] = sum_blocks(r.aim_got)
    final_all.finish()
    each(n_z, lambda step: along_z(step).wait_send(), 1)
    each(n_z, lambda step: each(n_u, lambda hop: across(hop, step).wait_send(), 1))
    each(n_z, lambda step: each(n_u, lambda hop: to_core(hop, step).wait_send()))


def fall_body(n_u, n_b, r, links, s):
    u, b = lax.axis_index(ULY), lax.axis_index(BLK)
    n_z = n_b // 2
    z, c = b // 2, lax.rem(b, 2)
    score_scale = HEAD_WIDTH ** (-0.5)
    picks = r.after_mlp.shape[0]
    places = r.key_raw.shape[0]
    r.factors[...] = jnp.zeros_like(r.factors)
    head_rows = links.head_rows(r.head_rows, r.rows_got)
    links.head_stats(r.head_stats, r.stats_got).finish()
    tops = r.stats_got[0, 0:1, :]
    for k in range(1, n_u):
        tops = jnp.maximum(tops, r.stats_got[k, 0:1, :])
    total = jnp.zeros_like(tops)
    for k in range(n_u):
        factor = jnp.exp(r.stats_got[k, 0:1, :] - tops)
        r.factors[k : k + 1, :] = factor
        total += r.stats_got[k, 1:2, :] * factor
    r.slot_stats[...] = jnp.zeros_like(r.slot_stats)
    r.slot_stats[0:1, :] = tops
    r.slot_stats[1:2, :] = total
    slot_part = links.slot_stats(r.slot_stats, r.slot_got)
    by_row = r.factors[...].T
    head_rows.finish()
    rows = r.rows_got[0].astype(f32) * by_row[:, 0:1]
    for k in range(1, n_u):
        rows += r.rows_got[k].astype(f32) * by_row[:, k : k + 1]
    r.partial[...] = rows.astype(bf16).reshape(r.partial.shape)
    back = links.slot_rows(r.partial, r.partial_got.at[0])
    slot_part.finish()
    tops = r.slot_got[0, 0:1, :]
    for k in range(1, n_b):
        tops = jnp.maximum(tops, r.slot_got[k, 0:1, :])
    total = jnp.zeros_like(tops)
    for k in range(n_b):
        factor = jnp.exp(r.slot_got[k, 0:1, :] - tops)
        r.factors[k : k + 1, :] = factor
        total += r.slot_got[k, 1:2, :] * factor
    log_norm = tops + jnp.log(total)
    for k in range(n_b):
        r.factors[k : k + 1, :] = r.factors[k : k + 1, :] / total
    r.factors[n_b : n_b + 1, :] = log_norm
    r.norms_mine[...] = jnp.broadcast_to(log_norm, r.norms_mine.shape)
    norms_part = links.norms(r.norms_mine, r.norms_all)
    r.columns[...] = r.factors[...].T
    mine = r.columns[pl.ds(pl.multiple_of(b * picks, picks), picks), :]
    back.finish()
    target_rows = r.pick_rows[:, MODEL_WIDTH:]
    grad_final = -target_rows
    for k in range(n_b):
        grad_final += r.partial_got[0, k].astype(f32) * mine[:, k : k + 1]
    grad_final = grad_final * r.weights[:, 0:1]
    target_logit = jnp.sum(
        r.final_mine[...].astype(f32) * target_rows, axis=-1, keepdims=True
    )
    r.terms[...] = r.weights[...] * (target_logit - mine[:, n_b : n_b + 1])
    grad_mlp, gain_final = norm_back_rows(r.after_mlp[...], r.gain_final[...], grad_final)
    r.mine_low[...] = grad_mlp.astype(bf16)
    links.branch(r.mine_low, r.grad_all).finish()
    branch = flat_rows_of(r.grad_all)
    gate_up = r.gate_up[...]
    half = gate_up.shape[1] // 2
    gate_part, up_part = gate_up[:, :half], gate_up[:, half:]
    sigmoid_gate = jax.nn.sigmoid(gate_part)
    grad_act = mm_back(branch, flat_rows_of(r.down_weight))
    grad_gate = grad_act * up_part * sigmoid_gate * (1.0 + gate_part * (1.0 - sigmoid_gate))
    grad_up = grad_act * gate_part * sigmoid_gate
    grad_gate_up = jnp.concatenate([grad_gate, grad_up], axis=1).astype(bf16)
    r.partial[...] = (
        mm_back(grad_gate_up, r.ff_weight[...].reshape(MODEL_WIDTH, -1))
        .astype(bf16)
        .reshape(r.partial.shape)
    )
    back = links.sum_ff(r.partial, r.partial_got.at[1])
    activated = (gate_part * sigmoid_gate * up_part).astype(bf16)
    r.grad_down[...] = mm_outer(activated, branch).astype(bf16).reshape(r.grad_down.shape)
    down_part = links.down(r.grad_down, r.down_got)
    r.grad_ff[...] = (
        mm_outer(flat_rows_of(r.normed_mlp), grad_gate_up).astype(bf16).reshape(r.grad_ff.shape)
    )
    ff_part = links.ff(r.grad_ff, r.ff_got)
    back.finish()
    grad_mid, gain_mlp = norm_back_rows(
        r.after_attn[...], r.gain_mlp[...], sum_blocks(r.partial_got.at[1])
    )
    grad_attn = grad_mlp + grad_mid
    r.mine_low[...] = grad_attn.astype(bf16)
    links.branch_attn(r.mine_low, r.branch_all).finish()
    branch = flat_rows_of(r.branch_all)
    grad_low = mm_back(branch, flat_rows_of(r.out_weight)).astype(bf16)
    r.attended_mine[...] = grad_low
    last = links.attended(r.attended_mine, r.attended_all)
    out_cut = r.attended.shape[1] // n_u
    product = r.attended[...] * grad_low.astype(f32)
    group = lax.broadcasted_iota(jnp.int32, product.shape, 1) // out_cut
    lane = lax.broadcasted_iota(jnp.int32, r.deltas.shape, 1)
    sums = jnp.zeros(r.deltas.shape, f32)
    for row in range(n_u):
        one = jnp.sum(jnp.where(group == row, product, 0.0), axis=-1, keepdims=True)
        sums = jnp.where(lane == row, one, sums)
    r.deltas[...] = sums
    r.delta_mine[...] = r.deltas[...].T[:8, :]
    delta_part = links.deltas(r.delta_mine, r.delta_all)
    r.grad_out[...] = (
        mm_outer(r.attended[...].astype(bf16), branch).astype(bf16).reshape(r.grad_out.shape)
    )
    out_part = links.out(r.grad_out, r.out_got)
    wide = flat_rows_of(r.arrived).astype(f32)
    r.normed_keys[...] = (wide * inverse_root(wide) * r.gain_attn[...]).astype(bf16)
    last.finish()
    delta_part.finish()

    ff_part.finish()
    r.ff_sum[...] = sum_blocks(r.ff_got).astype(bf16)
    ff_last = links.ff_cols(r.ff_sum, r.ff_out)

    allowed = r.key_lim[...] <= r.slot_picked[...]
    width = KEY_VALUE_HEADS * HEAD_WIDTH
    r.gain_key_row[...] = jnp.zeros((1, HEAD_WIDTH), f32)
    heads_each = QUERY_HEADS // KEY_VALUE_HEADS
    for kv_head in range(KEY_VALUE_HEADS):
        part = slice(kv_head * HEAD_WIDTH, (kv_head + 1) * HEAD_WIDTH)
        key, value = r.key_rot[:, part], r.values[:, part]
        grad_key = jnp.zeros(key.shape, f32)
        grad_value = jnp.zeros(key.shape, f32)
        for head in range(kv_head * heads_each, (kv_head + 1) * heads_each):
            query = head_of(r.query_all, head)
            cuts = cuts_of(head, n_u, n_b)
            upstream = jnp.concatenate([r.attended_all[at, :, there] for at, there, _ in cuts], 1)
            row = head // (QUERY_HEADS // n_u)
            delta = sum(r.delta_all[at, row : row + 1, :] for at, _, _ in cuts)
            scores = mm_back(key, query) * score_scale
            probs = jnp.where(allowed, jnp.exp(scores - r.log_total[head : head + 1, :]), 0.0)
            grad_probs = mm_back(value, upstream)
            grad_scores = (probs * (grad_probs - delta) * score_scale).astype(bf16)
            grad_query = mm_outer(grad_scores, key).astype(bf16)
            share = r.query_send.shape[2] // HEAD_WIDTH
            at = head % share * HEAD_WIDTH
            r.query_send[head // share, :, at : at + HEAD_WIDTH] = grad_query
            grad_key += mm(grad_scores, query)
            grad_value += mm(probs.astype(bf16), upstream)
        grad_head, gain_head = norm_back_rows(
            r.key_raw[:, part],
            r.gain_key[...],
            turned(grad_key.astype(bf16).astype(f32), r.rope_cos[:places], -r.rope_sin[:places]),
        )
        r.gain_key_row[...] += gain_head
        r.grad_kv[:, part] = grad_head.astype(bf16)
        r.grad_kv[:, width + kv_head * HEAD_WIDTH : width + (kv_head + 1) * HEAD_WIDTH] = (
            grad_value.astype(bf16)
        )
    query_part = links.grad_queries(r.query_send, r.query_got)

    def place(hop, step):
        return (lax.rem(u + hop, n_u), lax.rem(z + step, n_z))

    def to_core(hop, step):
        row, line = place(hop, step)
        return remote(
            r.kv_grad.at[row, line, 1 - c],
            r.kv_core.at[hop, step],
            s.core_send.at[hop, step],
            s.core_recv.at[hop, step],
            {BLK: z * 2 + 1 - c},
        )

    def across(hop, step):
        return remote(
            r.kv_core.at[hop, step],
            r.kv_cross.at[hop, step],
            s.xy_send.at[hop, step],
            s.xy_recv.at[hop, step],
            {ULY: lax.rem(u + hop, n_u)},
        )

    def along_z(step):
        return remote(
            r.kv_plane.at[step],
            r.kv_line.at[step],
            s.z_send.at[step],
            s.z_recv.at[step],
            {BLK: lax.rem(z + step, n_z) * 2 + c},
        )

    block_rows = MODEL_WIDTH // n_u

    def weight_grad(k):
        hop = lax.rem(k + 1, n_u)
        row = lax.rem(u + hop, n_u)
        columns = pl.ds(pl.multiple_of(row * block_rows, block_rows), block_rows)
        r.kv_grad[row] = (
            mm_outer(r.normed_keys[:, columns], r.grad_kv[...])
            .astype(bf16)
            .reshape(r.kv_grad.shape[1:])
        )
        each(n_z, lambda step: to_core(hop, step).start())

    each(n_u, weight_grad)
    def add_pair(hop, step):
        row, line = place(hop, step)
        to_core(hop, step).wait_recv()
        r.kv_core[hop, step] = (
            r.kv_grad[row, line, c].astype(f32) + r.kv_core[hop, step].astype(f32)
        ).astype(bf16)

    def send_pairs(k):
        step = lax.rem(k + 1, n_z)

        def one(hop):
            add_pair(hop, step)
            across(hop, step).start()

        each(n_u, one, 1)
        add_pair(0, step)

    each(n_z, send_pairs)
    down_part.finish()
    r.down_out[...] = sum_blocks(r.down_got)
    out_part.finish()
    r.out_out[...] = sum_blocks(r.out_got)
    query_part.finish()
    upstream = sum_blocks(r.query_got).astype(bf16).astype(f32)
    r.gain_query_row[...] = jnp.zeros((1, HEAD_WIDTH), f32)
    for k in range(upstream.shape[1] // HEAD_WIDTH):
        part = slice(k * HEAD_WIDTH, (k + 1) * HEAD_WIDTH)
        grad_head, gain_head = norm_back_rows(
            r.query_raw[:, part],
            r.gain_query[...],
            turned(upstream[:, part], r.rope_cos[places:], -r.rope_sin[places:]),
        )
        r.grad_low[:, part] = grad_head.astype(bf16)
        r.gain_query_row[...] += gain_head
    r.partial[...] = (
        mm_back(r.grad_low[...], r.q_weight[...].reshape(MODEL_WIDTH, -1))
        .astype(bf16)
        .reshape(r.partial.shape)
    )
    back = links.sum_query(r.partial, r.partial_got.at[2])

    r.grad_q[...] = (
        mm_outer(flat_rows_of(r.normed_slot), r.grad_low[...]).astype(bf16).reshape(r.grad_q.shape)
    )
    q_part = links.q(r.grad_q, r.q_got)
    back.finish()
    grad_mine, gain_attn = norm_back_rows(
        r.pick_rows[:, :MODEL_WIDTH], r.gain_attn[...], sum_blocks(r.partial_got.at[2])
    )
    r.mine_low[...] = (grad_attn + grad_mine).astype(bf16)
    pick_part = links.pick_back(r.mine_low, r.pick_back)

    def row_grad(k):
        columns = pl.ds(pl.multiple_of(k * block_rows, block_rows), block_rows)
        r.grad_wide[:, columns] = mm_back(
            r.grad_kv[...], r.kv_weight[k].reshape(block_rows, -1)
        )

    each(n_u, row_grad)
    grad_rows, gain_keys = norm_back_rows(wide, r.gain_attn[...], r.grad_wide[...])
    def plane_sum(step):
        total = r.kv_core[0, step].astype(f32)
        for hop in range(1, n_u):
            across(hop, step).wait_recv()
            total = total + r.kv_cross[hop, step].astype(f32)
        return total

    def add_plane(step):
        r.kv_plane[step] = plane_sum(step).astype(bf16)
        along_z(step).start()

    each(n_z, add_plane, 1)
    pick_part.finish()
    pick_hot = jnp.where(r.key_pos[...] == r.slot_picked[...], 1.0, 0.0).astype(bf16)
    r.rows_send[...] = (
        (grad_rows + mm(pick_hot, flat_rows_of(r.pick_back)))
        .astype(bf16)
        .reshape(r.rows_send.shape)
    )
    rows_part = links.rows(r.rows_send, r.rows_back)

    r.gain_mlp_row[...] = gain_mlp
    r.gain_final_row[...] = gain_final
    r.gain_picks_row[...] = gain_attn
    r.gain_rows_row[...] = gain_keys
    r.gains_mine[...] = jnp.zeros_like(r.gains_mine)
    lines = MODEL_WIDTH // 128
    for j in range(lines):
        part = slice(j * 128, (j + 1) * 128)
        r.gains_mine[j : j + 1, :] = r.gain_picks_row[:, part] + r.gain_rows_row[:, part]
        r.gains_mine[lines + j : lines + j + 1, :] = r.gain_mlp_row[:, part]
        r.gains_mine[2 * lines + j : 2 * lines + j + 1, :] = r.gain_final_row[:, part]
    r.gains_mine[3 * lines : 3 * lines + 1, :] = r.gain_query_row[...]
    r.gains_mine[3 * lines + 1 : 3 * lines + 2, :] = r.gain_key_row[...]
    gains_part = links.gains_blk(r.gains_mine, r.gains_got)

    gains_part.finish()
    r.gains_slot[...] = sum_blocks(r.gains_got)
    gains_last = links.gains_ulysses(r.gains_slot, r.gains_all)
    q_part.finish()
    r.q_sum[...] = sum_blocks(r.q_got).astype(bf16)
    q_last = links.q_cols(r.q_sum, r.q_out)

    total = plane_sum(0)
    for step in range(1, n_z):
        along_z(step).wait_recv()
        total = total + r.kv_line[step].astype(f32)
    r.inflow_out[:, QUERY_WIDTH:] = total
    gains_last.finish()
    gains = sum_blocks(r.gains_all)
    for part in (norms_part, ff_last, q_last, rows_part):
        part.finish()
    q_share = r.q_out.shape[2]
    for k in range(n_b):
        r.inflow_out[:, k * q_share : (k + 1) * q_share] = r.q_out[k].astype(f32)
    for k, there, here in ff_cuts(n_u, n_b):
        r.expand_out[:, here] = r.ff_out[k, :, there].astype(f32)
    squares = jnp.sum(gains * gains) / (n_u * n_b)
    for ref in (r.inflow_out, r.expand_out, r.out_out, r.down_out):
        squares += jnp.sum(ref[...] * ref[...])
    r.tails[...] = jnp.zeros_like(r.tails)
    r.tails[0:1, :] = jnp.full((1, 128), squares, f32)
    r.tails[1:2, :] = jnp.full((1, 128), -jnp.sum(r.terms[:, 0:1]), f32)
    for row in range(n_u):
        at = slice(row * n_b * picks, (row + 1) * n_b * picks)
        r.norms_row[:, at] = r.norms_all[row, 0:1, :]
    for k in range(gains.shape[0] - 6):
        r.gains_line[:, k * 128 : (k + 1) * 128] = gains[k : k + 1, :]
    share = r.gains_out.shape[1]
    me = u * n_b + b
    own = jnp.zeros((1, share), f32)
    for k in range(n_u * n_b):
        own = jnp.where(me == k, r.gains_line[:, k * share : (k + 1) * share], own)
    r.gains_out[...] = own
    each(n_z, lambda step: each(n_u, lambda hop: to_core(hop, step).wait_send()))
    each(n_z, lambda step: each(n_u, lambda hop: across(hop, step).wait_send(), 1))
    each(n_z, lambda step: along_z(step).wait_send(), 1)


def lookup_kernel(slots, fills_ref, ids_ref, table_ref, rows_ref, wide, sem):
    wide[...] = jnp.zeros_like(wide)

    def row_copy(place, row):
        return pltpu.make_async_copy(
            table_ref.at[pl.ds(row, 1), :], wide.at[pl.ds(place, 1), :], sem
        )

    def of_peer(peer, total):
        fill = fills_ref[peer]

        def fetch(k, carry):
            place = peer * slots + k
            row_copy(place, ids_ref[place]).start()
            return carry

        lax.fori_loop(0, fill, fetch, 0)
        return total + fill

    total = lax.fori_loop(0, fills_ref.shape[0], of_peer, 0)

    def drain(k, carry):
        row_copy(0, 0).wait()
        return carry

    lax.fori_loop(0, total, drain, 0)
    rows_ref[...] = wide[...].astype(rows_ref.dtype)


def lookup(fills, ids, table, slots):
    places = ids.shape[0]
    return pl.pallas_call(
        functools.partial(lookup_kernel, slots),
        out_shape=jax.ShapeDtypeStruct((places, table.shape[1]), bf16),
        in_specs=[
            pl.BlockSpec(memory_space=pltpu.SMEM),
            pl.BlockSpec(memory_space=pltpu.SMEM),
            pl.BlockSpec(memory_space=pl.ANY),
        ],
        out_specs=VMEM,
        scratch_shapes=[
            pltpu.VMEM((places, table.shape[1]), f32),
            pltpu.SemaphoreType.DMA,
        ],
        compiler_params=pltpu.CompilerParams(vmem_limit_bytes=40 * 1024 * 1024),
        name="lookup",
    )(fills, ids, table)


def table_tile(share, count=9):
    return -(-share // (count * 16)) * 16


def head_kernel(share, finals, table, logits, rows, stats, mixed, top, total):
    tile = table.shape[0]
    step = pl.program_id(0)
    known = step * tile + lax.broadcasted_iota(jnp.int32, (tile, 1), 0) < share
    low = jnp.where(known, table[...], 0.0).astype(bf16)
    scores = mm_back(low, finals[...])
    logits[...] = scores
    scores = jnp.where(known, scores, masked_score)

    @pl.when(step == 0)
    def _():
        top[...] = jnp.full(top.shape, masked_score, f32)
        total[...] = jnp.zeros_like(total)
        mixed[...] = jnp.zeros_like(mixed)

    new_top = jnp.maximum(top[...], jnp.max(scores, axis=0, keepdims=True))
    shrink = jnp.exp(top[...] - new_top)
    weights = jnp.exp(scores - new_top)
    top[...] = new_top
    total[...] = total[...] * shrink + jnp.sum(weights, axis=0, keepdims=True)
    mixed[...] = mixed[...] * shrink + mm_outer(low, weights.astype(bf16))

    @pl.when(step == pl.num_programs(0) - 1)
    def _():
        rows[...] = mixed[...].T.astype(bf16)
        stats[...] = jnp.zeros_like(stats)
        width = stats.shape[2]
        for k in range(stats.shape[0]):
            at = slice(k * width, (k + 1) * width)
            stats[k, 0:1, :] = top[:, at]
            stats[k, 1:2, :] = total[:, at]


def head_call(finals, table, n_u):
    share, width = table.shape
    picks = finals.shape[0]
    tile = table_tile(share, 6)
    stats = (n_u, 8, picks // n_u)
    return pl.pallas_call(
        functools.partial(head_kernel, share),
        grid=(pl.cdiv(share, tile),),
        out_shape=[
            jax.ShapeDtypeStruct((share, picks), f32),
            jax.ShapeDtypeStruct((picks, width), bf16),
            jax.ShapeDtypeStruct(stats, f32),
        ],
        in_specs=[
            pl.BlockSpec((picks, width), lambda i: (0, 0)),
            pl.BlockSpec((tile, width), lambda i: (i, 0)),
        ],
        out_specs=[
            pl.BlockSpec((tile, picks), lambda i: (i, 0)),
            pl.BlockSpec((picks, width), lambda i: (0, 0)),
            pl.BlockSpec(stats, lambda i: (0, 0, 0)),
        ],
        scratch_shapes=[
            pltpu.VMEM((width, picks), f32),
            pltpu.VMEM((1, picks), f32),
            pltpu.VMEM((1, picks), f32),
        ],
        compiler_params=pltpu.CompilerParams(vmem_limit_bytes=44 * 1024 * 1024),
        name="head",
    )(finals, table)


def table_grad_kernel(
    limit, logits, finals, norms, weights, targets, rows, row_ids, grad_out, squares
):
    tile = grad_out.shape[0]
    start = pl.program_id(0) * tile
    ids = start + lax.broadcasted_iota(jnp.int32, (tile, 1), 0)
    grad_logits = (
        weights[...]
        * (jnp.exp(logits[...] - norms[...]) - jnp.where(targets[...] == ids, 1.0, 0.0))
    ).astype(bf16)
    hot = jnp.where(row_ids[...] == ids, 1.0, 0.0).astype(bf16)
    grad = mm(grad_logits, finals[...]) + mm(hot, rows[...])
    grad_out[...] = grad.astype(bf16)

    @pl.when(pl.program_id(0) == 0)
    def _():
        squares[...] = jnp.zeros_like(squares)

    squares[...] += jnp.sum(jnp.where(ids < limit, grad * grad, 0.0), axis=0, keepdims=True)


def table_grad_call(logits, finals, norms, weights, targets, rows, row_ids):
    share, picks = logits.shape
    places, width = rows.shape
    tile = table_tile(share)
    whole = lambda *shape: pl.BlockSpec(shape, lambda i: (0, 0))
    return pl.pallas_call(
        functools.partial(table_grad_kernel, share),
        grid=(pl.cdiv(share, tile),),
        out_shape=[
            jax.ShapeDtypeStruct((share, width), bf16),
            jax.ShapeDtypeStruct((1, width), f32),
        ],
        in_specs=[
            pl.BlockSpec((tile, picks), lambda i: (i, 0)),
            whole(picks, width),
            whole(1, picks),
            whole(1, picks),
            whole(1, picks),
            whole(places, width),
            whole(1, places),
        ],
        out_specs=[
            pl.BlockSpec((tile, width), lambda i: (i, 0)),
            whole(1, width),
        ],
        compiler_params=pltpu.CompilerParams(vmem_limit_bytes=32 * 1024 * 1024),
        cost_estimate=pl.CostEstimate(
            flops=2 * share * width * (picks + places),
            bytes_accessed=share * (4 * picks + 2 * width),
            transcendentals=share * picks,
        ),
        name="table_grad",
    )(logits, finals, norms, weights, targets, rows, row_ids)


def adam_kernel(rate, decay, numbers, weight, first, second, grad, change, new_first, new_second):
    gradient = grad[...].astype(f32) * numbers[:, 0:1]
    mean = beta_first * first[...] + (1.0 - beta_first) * gradient
    square = beta_second * second[...] + (1.0 - beta_second) * gradient * gradient
    new_first[...] = mean
    new_second[...] = square
    change[...] = -rate * (
        mean * numbers[:, 1:2] / (jnp.sqrt(square * numbers[:, 2:3]) + adam_eps)
        + decay * weight[...]
    )


def layer_adam_kernel(rates, decays, numbers, *refs):
    count = len(rates)
    for k in range(count):
        weight, first, second, grad = refs[4 * k : 4 * k + 4]
        adam_kernel(rates[k], decays[k], numbers, weight, first, second, grad, *refs[4 * count + 3 * k :][:3])


def layer_adam_call(numbers, groups, rates, decays):
    arrays = [array for group in groups for array in group]
    return pl.pallas_call(
        functools.partial(layer_adam_kernel, rates, decays),
        out_shape=[
            jax.ShapeDtypeStruct(group[0].shape, f32) for group in groups for _ in range(3)
        ],
        in_specs=[VMEM] * (1 + len(arrays)),
        out_specs=[VMEM] * (3 * len(groups)),
        compiler_params=pltpu.CompilerParams(vmem_limit_bytes=32 * 1024 * 1024),
        name="layer_adam",
    )(numbers, *arrays)


def adam_call(numbers, weight, first, second, grad, rate, decay):
    share, width = weight.shape
    tile = table_tile(share)
    block = pl.BlockSpec((tile, width), lambda i: (i, 0))
    return pl.pallas_call(
        functools.partial(adam_kernel, rate, decay),
        grid=(pl.cdiv(share, tile),),
        out_shape=[jax.ShapeDtypeStruct((share, width), f32)] * 3,
        in_specs=[pl.BlockSpec((1, 128), lambda i: (0, 0))] + [block] * 4,
        out_specs=[block] * 3,
        compiler_params=pltpu.CompilerParams(vmem_limit_bytes=40 * 1024 * 1024),
        name="adam",
    )(numbers, weight, first, second, grad)


def local(
    tokens,
    lengths,
    picked,
    targets,
    advantages,
    step_count,
    embedding,
    first_embedding,
    second_embedding,
    inflow,
    inflow_first_moment,
    inflow_second_moment,
    outflow,
    first_outflow,
    second_outflow,
    expand,
    first_expand,
    second_expand,
    contract,
    first_contract,
    second_contract,
    scales,
    first_scales,
    second_scales,
):
    exchange = Exchanger()
    n_u, n_b = lax.axis_size(ULY), lax.axis_size(BLK)
    n_all = n_u * n_b
    n_z = n_b // 2
    u, b = lax.axis_index(ULY), lax.axis_index(BLK)
    me = u * n_b + b
    slot_count, block_len = tokens.shape
    assert slot_count == n_u and n_b % 2 == 0
    picks = picked.shape[1]
    slot_picks = picks * n_b
    all_picks = slot_picks * n_u
    row_share = embedding.shape[0]
    group = QUERY_HEADS // KEY_VALUE_HEADS
    score_scale = HEAD_WIDTH ** (-0.5)
    in_rows, out_share, ff_share = inflow.shape[0], outflow.shape[0], contract.shape[0]
    q_share = QUERY_WIDTH // n_b
    heads_share = q_share // HEAD_WIDTH
    ff_mine = n_u * ff_share
    out_cut = QUERY_WIDTH // n_all
    scale_share = scales.shape[0]

    width = KEY_VALUE_HEADS * HEAD_WIDTH
    wants_mean = n_b * (block_len + picks) / n_all
    slots = -(-int(wants_mean + 5.2 * math.sqrt(wants_mean)) // 16) * 16
    places = n_u * slots
    blk_g = (BLK, WHOLE)
    column = ((places, 1), jnp.int32)
    row_wide = ((1, MODEL_WIDTH), f32)
    head_wide = ((1, HEAD_WIDTH), f32)
    def begin_call():
        return named_call(
            exchange,
            functools.partial(begin_body, n_u, n_b, row_share, slots),
            dict(
                tokens=blk_g,
                targets=blk_g,
                picked=blk_g,
                advantages=blk_g,
                near=blk_g,
                far=(ULY, WHOLE),
            ),
            {},
            dict(
                tokens=tokens,
                targets=targets,
                picked=picked,
                advantages=advantages,
                lengths=lengths[:, None],
                scales=scales[None, :],
            ),
            dict(
                tokens_all=((n_b,) + tokens.shape, jnp.int32),
                targets_all=((n_b,) + targets.shape, jnp.int32),
                slot_picked=((1, slot_picks), jnp.int32),
                weights=((1, all_picks), f32),
                target_ids=((1, all_picks), jnp.int32),
                weight_wide=((picks, 128), f32),
                row_ids=column,
                key_pos=column,
                key_lim=column,
                target_of=column,
                positions=((places + slot_picks, 1), jnp.int32),
                meta=((24, 128), f32),
                gain_attn=row_wide,
                gain_mlp=row_wide,
                gain_final=row_wide,
                gain_query=head_wide,
                gain_key=head_wide,
            ),
            dict(
                picked_all=((n_b,) + picked.shape, jnp.int32),
                advantages_all=((n_b,) + advantages.shape, f32),
                near=((n_b, 1, scale_share), f32),
                far=((n_u, n_b, 1, scale_share), f32),
                wants=((n_u, block_len + picks), jnp.int32),
                masks=((2 * n_u, block_len + picks), f32),
                labels=((2 * n_u, block_len + picks), f32),
                ranks=((2 * n_u, block_len + picks), f32),
                gains=((1, n_all * scale_share), f32),
            ),
            "begin",
        )

    begin = begin_call()
    gain_rows = [
        begin.gain_attn,
        begin.gain_mlp,
        begin.gain_final,
        begin.gain_query,
        begin.gain_key,
    ]
    gain_attn, gain_query, gain_key = begin.gain_attn[0], begin.gain_query[0], begin.gain_key[0]
    slot_picked = begin.slot_picked[0]
    rounds = (jnp.max(begin.meta[8 : 8 + n_u, 0]).astype(jnp.int32) + slots - 1) // slots
    count_local = begin.meta[16, 0]
    half = HEAD_WIDTH // 2
    lane = jnp.arange(HEAD_WIDTH, dtype=jnp.int32)
    frequency = rope_base ** (-((lane % half).astype(f32) * 2.0 / HEAD_WIDTH))
    angles = begin.positions.astype(f32) * frequency[None, :]
    rope_cos = jnp.cos(angles)
    rope_sin = jnp.sin(angles) * jnp.where(lane < half, -1.0, 1.0)[None, :]
    query_cos, query_sin = rope_cos[places:], rope_sin[places:]
    ff_width = 2 * ff_mine
    own_cut = n_u * out_cut
    rows_low = (picks, MODEL_WIDTH)
    slot_low = (n_b, picks, MODEL_WIDTH)
    stat_rows = (8, slot_picks)
    weight_wide = begin.weight_wide

    def fetch(fills, row_ids):
        rows = lookup(fills, jnp.maximum(row_ids, 0), embedding, slots)
        return rows.reshape(n_u, slots, MODEL_WIDTH)

    def widen_ff(array):
        return (
            array.astype(f32)
            .reshape(n_b, in_rows, 2, n_u, ff_share)
            .transpose(1, 2, 3, 0, 4)
            .reshape(in_rows, 2 * FF)
        )

    def head_of_table(final_all):
        logits, head_rows, head_stats = head_call(final_all, embedding, n_u)
        return (logits, head_rows.reshape(n_u, slot_picks, MODEL_WIDTH), head_stats)

    def usual_way():
        fills = jnp.minimum(begin.meta[:n_u, 0].astype(jnp.int32), slots)
        lined = dict(
            key_pos=begin.key_pos,
            key_lim=begin.key_lim,
            slot_picked=begin.slot_picked,
            gain_attn=gain_rows[0],
            gain_mlp=gain_rows[1],
            gain_final=gain_rows[2],
            gain_query=gain_rows[3],
            gain_key=gain_rows[4],
            rope_cos=rope_cos,
            rope_sin=rope_sin,
        )
        kv_block = (in_rows, 2 * width)
        kv_shape = (n_u, n_z, 2) + kv_block
        q_shape = (n_u, n_b, in_rows, q_share)
        ff_shape = (n_u, n_b, in_rows, ff_width)
        out_shape = (n_u, out_share, MODEL_WIDTH)
        down_shape = (n_u, ff_share, MODEL_WIDTH)
        rows_shape = (n_u, slots, MODEL_WIDTH)
        blk_s, blk_g = (BLK, SPLIT), (BLK, WHOLE)
        uly_s, uly_g = (ULY, SPLIT), (ULY, WHOLE)
        rise = named_call(
            exchange,
            functools.partial(rise_body, n_u, n_b),
            dict(
                rows=uly_s,
                q_split=blk_s,
                ff_split=blk_s,
                picks=blk_s,
                aims=blk_s,
                q_all=uly_g,
                normed=blk_g,
                queries=blk_g,
                out_all=uly_g,
                ff_all=uly_g,
                down_all=uly_g,
                parts=blk_s,
                stats=blk_g,
                sum_out=blk_s,
                normed_mlp=blk_g,
                sum_mlp=blk_s,
                final=blk_g,
                final_all=uly_g,
            ),
            dict(
                z_send=(n_z,),
                z_recv=(n_z,),
                own=(1,),
                xy_send=(n_u, n_z),
                xy_recv=(n_u, n_z),
                core_send=(n_u, n_z),
                core_recv=(n_u, n_z),
            ),
            dict(
                rows_in=fetch(fills, begin.row_ids.reshape(-1)),
                inflow=inflow,
                expand=expand,
                outflow=outflow,
                contract=contract,
                target_of=begin.target_of,
                **lined,
            ),
            dict(
                arrived=(rows_shape, bf16),
                kv_weight=(kv_shape, bf16),
                q_weight=(q_shape, bf16),
                ff_weight=(ff_shape, bf16),
                out_weight=(out_shape, bf16),
                down_weight=(down_shape, bf16),
                pick_rows=((picks, 2 * MODEL_WIDTH), f32),
                normed_slot=(slot_low, bf16),
                query_raw=((slot_picks, q_share), f32),
                query_all=((n_b, slot_picks, q_share), bf16),
                key_raw=((places, width), f32),
                key_rot=((places, width), bf16),
                values=((places, width), bf16),
                attended=((slot_picks, own_cut), f32),
                log_total=((QUERY_HEADS, slot_picks), f32),
                after_attn=(rows_low, f32),
                normed_mlp=(slot_low, bf16),
                gate_up=((slot_picks, ff_width), f32),
                after_mlp=(rows_low, f32),
                final_mine=(rows_low, bf16),
                final_all=((n_u,) + slot_low, bf16),
            ),
            dict(
                kv_in=(kv_block, bf16),
                q_in=(q_shape[1:], bf16),
                ff_in=(ff_shape[1:], bf16),
                out_in=(out_shape[1:], bf16),
                down_in=(down_shape[1:], bf16),
                q_part=(q_shape[1:], bf16),
                ff_part=(ff_shape[1:], bf16),
                pick_send=(slot_low, bf16),
                pick_got=(slot_low, bf16),
                aim_send=(slot_low, bf16),
                aim_got=(slot_low, bf16),
                normed_mine=(rows_low, bf16),
                normed_keys=((places, MODEL_WIDTH), bf16),
                query_mine=((slot_picks, q_share), bf16),
                part_send=((n_b, slot_picks, own_cut), bf16),
                part_got=((n_b, slot_picks, own_cut), bf16),
                stats=((2 * QUERY_HEADS, slot_picks), f32),
                stats_all=((n_b, 2 * QUERY_HEADS, slot_picks), f32),
                shares=((n_b * n_u, slot_picks), f32),
                partial=(slot_low, bf16),
                partial_got=((2,) + slot_low, bf16),
                final_slot=(slot_low, bf16),
            ),
            "rise",
        )
        final_all = rise.final_all.reshape(all_picks, MODEL_WIDTH)
        logits, head_rows, head_stats = head_of_table(final_all)
        fall = named_call(
            exchange,
            functools.partial(fall_body, n_u, n_b),
            dict(
                head_rows=uly_s,
                head_stats=uly_s,
                slot_stats=blk_g,
                slot_rows=blk_s,
                norms=uly_g,
                branch=blk_g,
                sum_ff=blk_s,
                down=uly_s,
                ff=uly_s,
                branch_attn=blk_g,
                attended=blk_g,
                deltas=blk_g,
                out=uly_s,
                grad_queries=blk_s,
                sum_query=blk_s,
                q=uly_s,
                pick_back=blk_g,
                rows=uly_s,
                gains_blk=blk_g,
                gains_ulysses=uly_g,
                ff_cols=blk_s,
                q_cols=blk_s,
            ),
            dict(
                core_send=(n_u, n_z),
                core_recv=(n_u, n_z),
                xy_send=(n_u, n_z),
                xy_recv=(n_u, n_z),
                z_send=(n_z,),
                z_recv=(n_z,),
            ),
            dict(
                head_rows=head_rows,
                head_stats=head_stats,
                weights=weight_wide,
                arrived=rise.arrived,
                kv_weight=rise.kv_weight,
                q_weight=rise.q_weight,
                ff_weight=rise.ff_weight,
                out_weight=rise.out_weight,
                down_weight=rise.down_weight,
                pick_rows=rise.pick_rows,
                normed_slot=rise.normed_slot,
                query_raw=rise.query_raw,
                query_all=rise.query_all,
                key_raw=rise.key_raw,
                key_rot=rise.key_rot,
                values=rise.values,
                attended=rise.attended,
                log_total=rise.log_total,
                after_attn=rise.after_attn,
                normed_mlp=rise.normed_mlp,
                gate_up=rise.gate_up,
                after_mlp=rise.after_mlp,
                final_mine=rise.final_mine,
                **lined,
            ),
            dict(
                rows_back=(rows_shape, bf16),
                inflow_out=(inflow.shape, f32),
                expand_out=(expand.shape, f32),
                out_out=(out_shape[1:], f32),
                down_out=(down_shape[1:], f32),
                gains_out=((1, scale_share), f32),
                tails=((8, 128), f32),
                norms_row=((1, all_picks), f32),
            ),
            dict(
                rows_got=((n_u, slot_picks, MODEL_WIDTH), bf16),
                stats_got=((n_u,) + stat_rows, f32),
                slot_stats=(stat_rows, f32),
                slot_got=((n_b,) + stat_rows, f32),
                factors=((n_b + 8, slot_picks), f32),
                columns=((slot_picks, n_b + 8), f32),
                norms_mine=(stat_rows, f32),
                partial=(slot_low, bf16),
                partial_got=((3,) + slot_low, bf16),
                mine_low=(rows_low, bf16),
                grad_all=(slot_low, bf16),
                branch_all=(slot_low, bf16),
                grad_down=(down_shape, bf16),
                down_got=(down_shape, bf16),
                grad_ff=(ff_shape, bf16),
                ff_got=(ff_shape, bf16),
                grad_out=(out_shape, bf16),
                out_got=(out_shape, bf16),
                attended_mine=((slot_picks, own_cut), bf16),
                attended_all=((n_b, slot_picks, own_cut), bf16),
                deltas=((slot_picks, 128), f32),
                delta_mine=(stat_rows, f32),
                delta_all=((n_b,) + stat_rows, f32),
                normed_keys=((places, MODEL_WIDTH), bf16),
                query_send=((n_b, slot_picks, q_share), bf16),
                query_got=((n_b, slot_picks, q_share), bf16),
                grad_kv=((places, 2 * width), bf16),
                kv_grad=(kv_shape, bf16),
                kv_core=((n_u, n_z) + kv_block, bf16),
                kv_cross=((n_u, n_z) + kv_block, bf16),
                kv_plane=((n_z,) + kv_block, bf16),
                kv_line=((n_z,) + kv_block, bf16),
                grad_low=((slot_picks, q_share), bf16),
                grad_q=(q_shape, bf16),
                q_got=(q_shape, bf16),
                q_sum=(q_shape[1:], bf16),
                pick_back=(slot_low, bf16),
                grad_wide=((places, MODEL_WIDTH), f32),
                rows_send=(rows_shape, bf16),
                gain_mlp_row=((1, MODEL_WIDTH), f32),
                gain_final_row=((1, MODEL_WIDTH), f32),
                gain_picks_row=((1, MODEL_WIDTH), f32),
                gain_rows_row=((1, MODEL_WIDTH), f32),
                gain_query_row=((1, HEAD_WIDTH), f32),
                gain_key_row=((1, HEAD_WIDTH), f32),
                norms_all=((n_u,) + stat_rows, f32),
                terms=((picks, 128), f32),
                gains_line=((1, n_all * scale_share), f32),
                gains_mine=((32, 128), f32),
                gains_got=((n_b, 32, 128), f32),
                gains_slot=((32, 128), f32),
                gains_all=((n_u, 32, 128), f32),
                ff_sum=(ff_shape[1:], bf16),
                q_out=(q_shape[1:], bf16),
                ff_out=(ff_shape[1:], bf16),
            ),
            "fall",
        )
        table_grad, table_squares = table_grad_call(
            logits,
            final_all,
            fall.norms_row,
            begin.weights,
            begin.target_ids,
            fall.rows_back.reshape(places, MODEL_WIDTH),
            begin.row_ids.reshape(1, places),
        )
        return (
            fall.tails,
            table_squares,
            table_grad,
            fall.inflow_out,
            fall.out_out,
            fall.expand_out,
            fall.down_out,
            fall.gains_out,
        )

    def long_way():
        inflow_low = inflow.astype(bf16)
        q_cols = inflow_low[:, :QUERY_WIDTH].reshape(in_rows, n_b, q_share).transpose(1, 0, 2)
        ff_cols = (
            expand.astype(bf16)
            .reshape(in_rows, 2, n_u, n_b, ff_share)
            .transpose(3, 0, 1, 2, 4)
            .reshape(n_b, in_rows, 2 * ff_mine)
        )
        wants_block = block_len + picks
        wants_count = n_b * wants_block
        wants = (
            jnp.concatenate([begin.tokens_all, begin.targets_all], axis=2)
            .transpose(1, 0, 2)
            .reshape(n_u, wants_count)
        )
        my_length = lax.dynamic_index_in_dim(lengths, u, 0, keepdims=False)
        owners = wants // row_share
        own_owners = lax.dynamic_index_in_dim(owners, u, 0, keepdims=True)
        sent_mask = owners == me
        got_mask = own_owners == jnp.arange(n_u, dtype=jnp.int32)[:, None] * n_b + b
        masks = jnp.concatenate([sent_mask, got_mask], axis=0)
        totals_sent = jnp.sum(sent_mask.astype(f32), axis=1).astype(jnp.int32)
        lanes = math.gcd(wants_count, 128)
        blocks = masks.astype(bf16).reshape(2 * n_u, wants_count // lanes, lanes)
        before = (jnp.arange(lanes)[:, None] < jnp.arange(lanes)[None, :]).astype(bf16)
        block_sums = jnp.sum(blocks.astype(f32), axis=-1)
        chunk = jnp.arange(wants_count // lanes)
        block_base = mm(block_sums.astype(bf16), (chunk[:, None] < chunk[None, :]).astype(bf16))
        ranks = (
            mm(blocks.reshape(-1, lanes), before).reshape(blocks.shape) + block_base[:, :, None]
        ).reshape(2 * n_u, wants_count)
        ranks = jnp.where(masks, ranks.astype(jnp.int32), -1)
        labels = jnp.concatenate(
            [
                wants - me * row_share,
                jnp.broadcast_to(
                    jnp.arange(wants_count, dtype=jnp.int32)[None, :], (n_u, wants_count)
                ),
            ],
            axis=0,
        )

        def slot_tables(turn, hot):
            slot_rank = turn * slots + jnp.arange(slots, dtype=jnp.int32)
            hit = ranks[:, None, :] == slot_rank[None, :, None]
            found = jnp.sum(jnp.where(hit, labels[:, None, :] + 1, 0), axis=-1) - 1
            fills = jnp.clip(totals_sent - turn * slots, 0, slots)
            row_ids = found[:n_u].reshape(-1)
            entry = found[n_u:].reshape(-1)
            block, inside = entry // wants_block, entry % wants_block
            is_token = (entry >= 0) & (inside < block_len)
            key_pos = jnp.where(is_token, block * block_len + inside, 1 << 30)
            target_of = jnp.where(
                (entry >= 0) & (inside >= block_len), block * picks + inside - block_len, -1
            )
            if not hot:
                return (row_ids, fills, key_pos, None, target_of)
            pick_hot = (slot_picked[:, None] == key_pos[None, :]).astype(bf16)
            target_hot = (jnp.arange(slot_picks)[:, None] == target_of[None, :]).astype(bf16)
            return (row_ids, fills, key_pos, pick_hot, target_hot)

        row_ids, fills, key_pos, pick_hot, target_hot = slot_tables(jnp.int32(0), True)

        arrived, kv_weight, q_weight, ff_split = start_call(
            exchange, fetch(fills, row_ids), inflow_low[:, QUERY_WIDTH:], q_cols, ff_cols
        )
        arrived = arrived.reshape(places, MODEL_WIDTH)
        kv_weight = kv_weight.reshape(MODEL_WIDTH, -1)
        q_weight = q_weight.reshape(MODEL_WIDTH, q_share)
        def picked_rows(pick_hot, target_hot, arrived):
            return jnp.concatenate([mm(pick_hot, arrived), mm(target_hot, arrived)], axis=1)

        refetch_id = [exchange.next_id() for _ in range(5)]

        def refetch(turn, which):
            tables = slot_tables(turn, True)
            (got,) = exchange.many(
                ((ULY, SPLIT),), fetch(tables[1], tables[0]), collective_id=refetch_id[which]
            )
            return (tables, got.reshape(places, MODEL_WIDTH))

        def more(state):
            return state[0] < rounds

        def picks_turn(state):
            tables, got = refetch(state[0], 0)
            return (state[0] + 1, state[1] + picked_rows(tables[3], tables[4], got))

        pick_part = picked_rows(pick_hot, target_hot, arrived)
        _, pick_part = lax.while_loop(more, picks_turn, (jnp.int32(1), pick_part))
        got_picks, normed_slot, query_raw, query_all, ff_all, out_all, down_all = fused_call(
            exchange,
            functools.partial(query_body, n_b),
            ((BLK, SPLIT), (BLK, WHOLE), (BLK, WHOLE)) + ((ULY, WHOLE),) * 3,
            (
                pick_part.astype(bf16).reshape(n_b, picks, 2 * MODEL_WIDTH),
                gain_rows[0],
                gain_rows[3],
                q_weight,
                query_cos,
                query_sin,
                ff_split,
                outflow.astype(bf16),
                contract.astype(bf16),
            ),
            (
                ((picks, 2 * MODEL_WIDTH), f32),
                (slot_low, bf16),
                ((slot_picks, q_share), f32),
                ((n_b, slot_picks, q_share), bf16),
                ((n_u, n_b, in_rows, ff_width), bf16),
                ((n_u, out_share, MODEL_WIDTH), bf16),
                ((n_u, ff_share, MODEL_WIDTH), bf16),
            ),
            (
                ((n_b, picks, 2 * MODEL_WIDTH), bf16),
                (rows_low, bf16),
                ((slot_picks, q_share), bf16),
            ),
            "queries",
        )
        ff_weight = ff_all.reshape(MODEL_WIDTH, ff_width)
        out_weight = out_all.reshape(n_u * out_share, MODEL_WIDTH)
        down_weight = down_all.reshape(ff_mine, MODEL_WIDTH)

        def keys_of(arrived, key_pos):
            embedded = arrived.astype(f32)
            normed = (embedded * inverse_root(embedded) * gain_attn).astype(bf16)
            mixed = mm(normed, kv_weight)
            half = KEY_VALUE_HEADS * HEAD_WIDTH
            key_raw = mixed[:, :half].reshape(places, KEY_VALUE_HEADS, HEAD_WIDTH)
            values = mixed[:, half:].reshape(places, KEY_VALUE_HEADS, HEAD_WIDTH)
            angle_tables = rope_angles(jnp.where(key_pos < (1 << 30), key_pos, 0))
            key_rot = rotate(key_raw * inverse_root(key_raw) * gain_key, angle_tables, 1.0)
            return (
                embedded,
                normed,
                key_raw,
                angle_tables,
                key_rot.astype(bf16).transpose(1, 0, 2),
                values.astype(bf16).transpose(1, 0, 2),
            )

        query_pos = jnp.tile(slot_picked, group)

        def allowed_of(key_pos):
            return ((key_pos[None, :] <= query_pos[:, None]) & (key_pos[None, :] < my_length))[None]

        def scores_of(query_groups, key_rot, allowed):
            scores = (
                jnp.einsum("kqd,kjd->kqj", query_groups, key_rot, preferred_element_type=f32)
                * score_scale
            )
            return jnp.where(allowed, scores, masked_score)

        def attend(scores, allowed, values):
            part_max = jnp.max(scores, axis=-1, keepdims=True)
            weights = jnp.where(allowed, jnp.exp(scores - part_max), 0.0)
            out = jnp.einsum("kqj,kjd->kqd", weights.astype(bf16), values, preferred_element_type=f32)
            return (part_max, jnp.sum(weights, axis=-1, keepdims=True), out)

        keys = keys_of(arrived, key_pos)

        query_groups = (
            query_all.reshape(n_b, slot_picks, heads_share, HEAD_WIDTH)
            .transpose(0, 2, 1, 3)
            .reshape(KEY_VALUE_HEADS, group * slot_picks, HEAD_WIDTH)
        )
        allowed = allowed_of(key_pos)
        scores = scores_of(query_groups, keys[4], allowed)

        def attend_turn(state):
            turn, top, total, out = state
            tables, got = refetch(turn, 1)
            keys_now = keys_of(got, tables[2])
            allowed_now = allowed_of(tables[2])
            new = attend(scores_of(query_groups, keys_now[4], allowed_now), allowed_now, keys_now[5])
            both = jnp.maximum(top, new[0])
            old_factor, new_factor = jnp.exp(top - both), jnp.exp(new[0] - both)
            return (
                turn + 1,
                both,
                total * old_factor + new[1] * new_factor,
                out * old_factor + new[2] * new_factor,
            )

        _, part_max, part_sum, part_out = lax.while_loop(
            more, attend_turn, (jnp.int32(1),) + attend(scores, allowed, keys[5])
        )
        part_send = (
            part_out.astype(bf16)
            .reshape(QUERY_HEADS, slot_picks, HEAD_WIDTH)
            .transpose(1, 0, 2)
            .reshape(slot_picks, n_u, n_b, out_cut)
            .transpose(2, 0, 1, 3)
            .reshape(n_b, slot_picks, n_u * out_cut)
        )
        stats = jnp.stack([part_max[..., 0], part_sum[..., 0]]).reshape(2 * QUERY_HEADS, slot_picks)
        (
            attended,
            log_total,
            after_attn,
            normed_mlp,
            gate_up,
            after_mlp,
            final_mine,
            final_all,
        ) = fused_call(
            exchange,
            functools.partial(forward_body, n_u, n_b),
            ((BLK, SPLIT), (BLK, WHOLE), (BLK, SPLIT), (BLK, WHOLE), (BLK, SPLIT), (BLK, WHOLE))
            + ((ULY, WHOLE),),
            (
                part_send,
                stats,
                got_picks,
                out_weight,
                ff_weight,
                down_weight,
                gain_rows[1],
                gain_rows[2],
            ),
            (
                ((slot_picks, own_cut), f32),
                ((QUERY_HEADS, slot_picks), f32),
                (rows_low, f32),
                (slot_low, bf16),
                ((slot_picks, ff_width), f32),
                (rows_low, f32),
                (rows_low, bf16),
                ((n_u,) + slot_low, bf16),
            ),
            (
                ((n_b, slot_picks, own_cut), bf16),
                ((n_b, 2 * QUERY_HEADS, slot_picks), f32),
                ((n_b * n_u, slot_picks), f32),
                (slot_low, bf16),
                ((2,) + slot_low, bf16),
                (rows_low, bf16),
                (slot_low, bf16),
            ),
            "forward",
        )

        final_all = final_all.reshape(all_picks, MODEL_WIDTH)
        logits, head_rows, head_stats = head_of_table(final_all)
        (
            norms_all,
            terms,
            grad_gain_mlp,
            grad_gain_final,
            grad_ff,
            grad_out,
            grad_down,
            grad_after_attn,
            _,
            got_attended,
            got_delta,
        ) = fused_call(
            exchange,
            functools.partial(backward_body, n_u, n_b),
            (
                (ULY, SPLIT),
                (ULY, SPLIT),
                (BLK, SPLIT),
                (BLK, WHOLE),
                (ULY, WHOLE),
                (BLK, WHOLE),
                (BLK, SPLIT),
                (BLK, WHOLE),
                (BLK, WHOLE),
                (BLK, WHOLE),
            ),
            (
                head_rows,
                head_stats,
                final_mine,
                got_picks,
                weight_wide,
                after_mlp,
                after_attn,
                gate_up,
                normed_mlp,
                attended,
                out_weight,
                ff_weight,
                down_weight,
                gain_rows[1],
                gain_rows[2],
            ),
            (
                ((n_u,) + stat_rows, f32),
                ((picks, 128), f32),
                ((1, MODEL_WIDTH), f32),
                ((1, MODEL_WIDTH), f32),
                ((n_u, n_b, in_rows, ff_width), bf16),
                ((n_u, out_share, MODEL_WIDTH), bf16),
                ((n_u, ff_share, MODEL_WIDTH), bf16),
                (rows_low, f32),
                (slot_low, bf16),
                ((n_b, slot_picks, own_cut), bf16),
                ((n_b,) + stat_rows, f32),
            ),
            (
                ((n_u, slot_picks, MODEL_WIDTH), bf16),
                ((n_u,) + stat_rows, f32),
                (stat_rows, f32),
                ((n_b,) + stat_rows, f32),
                ((n_b + 8, slot_picks), f32),
                ((slot_picks, n_b + 8), f32),
                (stat_rows, f32),
                (slot_low, bf16),
                ((2,) + slot_low, bf16),
                (rows_low, bf16),
                (slot_low, bf16),
                ((slot_picks, own_cut), bf16),
                ((slot_picks, 128), f32),
                (stat_rows, f32),
            ),
            "backward",
        )
        loss_local = -jnp.sum(terms[:, 0])
        grad_heads = (
            got_attended.reshape(n_b, slot_picks, n_u, out_cut)
            .transpose(1, 2, 0, 3)
            .reshape(slot_picks, QUERY_HEADS, HEAD_WIDTH)
            .transpose(1, 0, 2)
            .reshape(KEY_VALUE_HEADS, group * slot_picks, HEAD_WIDTH)
        )
        row_delta = jnp.sum(
            got_delta[:, :n_u].transpose(1, 0, 2).reshape(QUERY_HEADS, HEAD_WIDTH // out_cut, slot_picks), axis=1
        ).reshape(KEY_VALUE_HEADS, group * slot_picks, 1)
        log_groups = log_total.reshape(KEY_VALUE_HEADS, group * slot_picks, 1)

        def score_grads(scores, allowed, values):
            probs = jnp.where(allowed, jnp.exp(scores - log_groups), 0.0)
            grad_probs = jnp.einsum("kqd,kjd->kqj", grad_heads, values, preferred_element_type=f32)
            return (probs, (probs * (grad_probs - row_delta) * score_scale).astype(bf16))

        def query_grads(grad_scores, key_rot):
            return jnp.einsum("kqj,kjd->kqd", grad_scores, key_rot, preferred_element_type=f32)

        def key_grads(probs, grad_scores, keys):
            grad_key = jnp.einsum(
                "kqj,kqd->kjd", grad_scores, query_groups, preferred_element_type=f32
            )
            grad_value = jnp.einsum(
                "kqj,kqd->kjd", probs.astype(bf16), grad_heads, preferred_element_type=f32
            )
            upstream = rotate(
                grad_key.astype(bf16).astype(f32).transpose(1, 0, 2), keys[3], -1.0
            )
            grad_raw, grad_gain = norm_back(keys[2], gain_key, upstream)
            grad_kv = jnp.concatenate(
                [
                    grad_raw.reshape(places, -1).astype(bf16),
                    grad_value.astype(bf16).transpose(1, 0, 2).reshape(places, -1),
                ],
                axis=1,
            )
            return (grad_kv, grad_gain)

        def row_grads(grad_kv, keys):
            return norm_back(keys[0], gain_attn, mm_back(grad_kv, kv_weight))

        def redo(turn, which):
            tables, got = refetch(turn, which)
            keys_now = keys_of(got, tables[2])
            allowed_now = allowed_of(tables[2])
            scores_now = scores_of(query_groups, keys_now[4], allowed_now)
            return (tables, keys_now) + score_grads(scores_now, allowed_now, keys_now[5])

        def query_turn(state):
            _, keys_now, _, grad_scores_now = redo(state[0], 2)
            return (state[0] + 1, state[1] + query_grads(grad_scores_now, keys_now[4]))

        probs, grad_scores = score_grads(scores, allowed, keys[5])
        _, grad_query_part = lax.while_loop(
            more, query_turn, (jnp.int32(1), query_grads(grad_scores, keys[4]))
        )
        query_send = (
            grad_query_part.astype(bf16)
            .reshape(n_b, heads_share, slot_picks, HEAD_WIDTH)
            .transpose(0, 2, 1, 3)
            .reshape(n_b, slot_picks, q_share)
        )
        (
            grad_gain_query,
            grad_gain_picks,
            grad_q,
            pick_back,
            sum_ff,
            sum_outflow,
            sum_contract,
        ) = fused_call(
            exchange,
            query_back_body,
            ((BLK, SPLIT), (BLK, SPLIT), (BLK, WHOLE)) + ((ULY, SPLIT),) * 3,
            (
                query_send,
                query_raw,
                query_cos,
                query_sin,
                gain_rows[3],
                q_weight,
                normed_slot,
                got_picks,
                gain_rows[0],
                grad_after_attn,
                grad_ff,
                grad_out,
                grad_down,
            ),
            (
                ((1, HEAD_WIDTH), f32),
                ((1, MODEL_WIDTH), f32),
                ((n_u, n_b, in_rows, q_share), bf16),
                (slot_low, bf16),
                ((n_b, in_rows, ff_width), bf16),
                ((out_share, MODEL_WIDTH), f32),
                ((ff_share, MODEL_WIDTH), f32),
            ),
            (
                ((n_b, slot_picks, q_share), bf16),
                ((slot_picks, q_share), bf16),
                (slot_low, bf16),
                (slot_low, bf16),
                (rows_low, bf16),
                ((n_u, n_b, in_rows, ff_width), bf16),
                ((n_u, out_share, MODEL_WIDTH), bf16),
                ((n_u, ff_share, MODEL_WIDTH), bf16),
            ),
            "query_grads",
        )
        pick_back = pick_back.reshape(slot_picks, MODEL_WIDTH)

        grad_kv, grad_gain_key = key_grads(probs, grad_scores, keys)
        grad_kv_weight = mm_outer(keys[1], grad_kv)
        grad_rows, grad_gain_attn = row_grads(grad_kv, keys)

        def weight_turn(state):
            turn, weight_sum, key_sum, attn_sum = state
            _, keys_now, probs_now, grad_scores_now = redo(turn, 3)
            grad_kv_now, gain_key_now = key_grads(probs_now, grad_scores_now, keys_now)
            _, gain_attn_now = row_grads(grad_kv_now, keys_now)
            return (
                turn + 1,
                weight_sum + mm_outer(keys_now[1], grad_kv_now),
                key_sum + gain_key_now,
                attn_sum + gain_attn_now,
            )

        _, grad_kv_weight, grad_gain_key, grad_gain_attn = lax.while_loop(
            more, weight_turn, (jnp.int32(1), grad_kv_weight, grad_gain_key, grad_gain_attn)
        )
        grad_scales = jnp.concatenate(
            [
                grad_gain_attn + grad_gain_picks[0],
                grad_gain_mlp[0],
                grad_gain_final[0],
                grad_gain_query[0],
                grad_gain_key,
            ]
        )

        token_rows = (grad_rows + mm_outer(pick_hot, pick_back)).astype(bf16)
        sum_kv, rows_back, got_q, got_ff, got_scales = settle_call(
            exchange,
            grad_kv_weight.astype(bf16).reshape(n_u, n_z, 2, in_rows, -1),
            token_rows.reshape(n_u, slots, MODEL_WIDTH),
            grad_q,
            sum_ff,
            jnp.pad(
                grad_scales.reshape(n_all, scale_share), ((0, 0), (0, 128 - scale_share))
            ).reshape(n_all, 1, 128),
        )
        sum_q = got_q.astype(f32).transpose(1, 0, 2).reshape(in_rows, QUERY_WIDTH)
        sum_inflow = jnp.concatenate([sum_q, sum_kv], axis=1)
        sum_expand = widen_ff(got_ff)
        sum_scales = jnp.sum(got_scales, axis=0)[0, :scale_share]

        table_grad, table_squares = table_grad_call(
            logits,
            final_all,
            norms_all[:, 0].reshape(1, all_picks),
            begin.weights,
            begin.target_ids,
            rows_back.reshape(places, MODEL_WIDTH),
            row_ids.reshape(1, places),
        )
        return_id = exchange.next_id()

        def return_turn(state):
            turn, so_far, _ = state
            tables, keys_now, probs_now, grad_scores_now = redo(turn, 4)
            grad_kv_now, _ = key_grads(probs_now, grad_scores_now, keys_now)
            rows_now, _ = row_grads(grad_kv_now, keys_now)
            rows_now = (rows_now + mm_outer(tables[3], pick_back)).astype(bf16)
            (back,) = exchange.many(
                ((ULY, SPLIT),),
                rows_now.reshape(n_u, slots, MODEL_WIDTH),
                collective_id=return_id,
            )
            hot = (
                jnp.arange(row_share, dtype=jnp.int32)[:, None] == tables[0][None, :]
            ).astype(bf16)
            grown = so_far.astype(f32) + mm(hot, back.reshape(places, MODEL_WIDTH))
            return (turn + 1, grown.astype(bf16), jnp.sum(grown * grown, axis=0, keepdims=True))

        _, table_grad, table_squares = lax.while_loop(
            more, return_turn, (jnp.int32(1), table_grad, table_squares)
        )
        squares = jnp.zeros((), f32)
        for grad_piece in (sum_inflow, sum_outflow, sum_expand, sum_contract, sum_scales):
            squares = squares + jnp.sum(grad_piece * grad_piece)
        tails = jnp.pad(jnp.stack([squares, loss_local]), (0, 6))
        return (
            jnp.broadcast_to(tails[:, None], (8, 128)),
            table_squares,
            table_grad,
            sum_inflow,
            sum_outflow,
            sum_expand,
            sum_contract,
            sum_scales[None, :],
        )

    step_float = step_count[0].astype(f32)
    first_scale = 1.0 / (1.0 - beta_first**step_float)
    second_scale = 1.0 / (1.0 - beta_second**step_float)

    steps = jnp.pad(jnp.stack([first_scale, second_scale]), (1, 125)).reshape(1, 128)

    def finish(tails, table_squares, table_grad, *layer_grads):
        numbers = named_call(
            exchange,
            totals_body,
            dict(near=(ALL, WHOLE)),
            {},
            dict(
                tails=tails,
                table_squares=table_squares,
                counts=begin.meta[16:],
                steps=steps,
            ),
            dict(numbers=((1, 128), f32)),
            dict(mine=((1, 128), f32), all=((n_all, 1, 128), f32)),
            "totals",
            8,
        ).numbers
        outputs = [numbers[0, 3], numbers[0, 4]]
        outputs += adam_call(
            numbers,
            embedding,
            first_embedding,
            second_embedding,
            table_grad,
            learning_rates[0],
            weight_decays[0],
        )
        outputs += layer_adam_call(
            numbers,
            (
                (inflow, inflow_first_moment, inflow_second_moment, layer_grads[0]),
                (outflow, first_outflow, second_outflow, layer_grads[1]),
                (expand, first_expand, second_expand, layer_grads[2]),
                (contract, first_contract, second_contract, layer_grads[3]),
                (scales[None, :], first_scales[None, :], second_scales[None, :], layer_grads[4]),
            ),
            learning_rates[1:],
            weight_decays[1:],
        )
        outputs[-3:] = [array[0] for array in outputs[-3:]]
        return tuple(outputs)

    _, outputs = lax.while_loop(
        lambda state: state[0],
        lambda state: (jnp.bool_(False), finish(*long_way())),
        (rounds > 1, finish(*usual_way())),
    )
    return outputs


def solution(mesh):
    rows = P((ULY, BLK), None)
    flat_rows = P((ULY, BLK))
    column = P(None, BLK)
    return jax.shard_map(
        local,
        mesh=mesh,
        in_specs=(column, P(), column, column, column, P()) + (rows,) * 15 + (flat_rows,) * 3,
        out_specs=(P(), P()) + (rows,) * 15 + (flat_rows,) * 3,
        check_vma=False,
    )
```
